32 devices in a mesh: seq: 8 (over z, core), dp: 4 (over y, x).
Axes of the slice: x: 2, y: 2, z: 4, core: 2. Of those that a mesh axis runs over, the one named last changes fastest.
Arguments:
- state: bfloat16 [4, 2048, 1024], P('dp', 'seq'), may hold values from -6 to 6
- embedded: bfloat16 [4, 2048, 1024], P('dp', 'seq'), may hold values from -6 to 6
- cotangent: bfloat16 [4, 2048, 1024], P('dp', 'seq'), may hold values from -6 to 6
- w_adapt: bfloat16 [2048, 1024], replicated, may hold values from -0.125 to 0.125
- w_qkv: bfloat16 [1024, 3072], replicated, may hold values from -0.25 to 0.25
- w_out: bfloat16 [1024, 1024], replicated, may hold values from -0.1875 to 0.1875
- w_gate: bfloat16 [1024, 2816], replicated, may hold values from -0.1875 to 0.1875
- w_up: bfloat16 [1024, 2816], replicated, may hold values from -0.1875 to 0.1875
- w_down: bfloat16 [2816, 1024], replicated, may hold values from -0.109375 to 0.109375
- gains: bfloat16 [4, 1024], replicated, may hold values from 0.5 to 1.5
Outputs:
- layer_out: bfloat16 [4, 2048, 1024], P('dp', 'seq')
- grad_state: float32 [4, 2048, 1024], P('dp', 'seq')
- grad_embedded: float32 [4, 2048, 1024], P('dp', 'seq')
- grad_adapt: float32 [2048, 1024], P(('seq', 'dp'))
- grad_qkv: float32 [1024, 3072], P(('seq', 'dp'))
- grad_out: float32 [1024, 1024], P(('seq', 'dp'))
- grad_gate: float32 [1024, 2816], P(('seq', 'dp'))
- grad_up: float32 [1024, 2816], P(('seq', 'dp'))
- grad_down: float32 [2816, 1024], P(('seq', 'dp'))
- grad_gains: float32 [4, 1024], P(None, ('seq', 'dp'))
The draws below stay inside these ranges and needn't reach their ends.
All inputs are finite; a program needn't handle non-finite values.
Results may differ from the reference program's by a relative error of at most 0.025.
Values may be sent and summed in bfloat16 or wider, within the bound.
A program may use at most 256 MiB of HBM per device.

```python
import math
import jax
import jax.numpy as jnp
from jax import lax

D = 1024
FF = 2816
HEADS = 8
HEAD_DIM = 128
LEN = 2048
BATCH = 4


def steps_of(key, dims, cuts, smallest, top_value):
    gain = 1.0
    for position, shards_of in cuts:
        steps = jax.random.uniform(jax.random.fold_in(jax.random.fold_in(key, 6), position), (shards_of,), jnp.float32, smallest / len(cuts), top_value / len(cuts))
        gain = gain * jnp.repeat(jnp.exp(steps), dims[position] // shards_of).reshape((-1,) + (1,) * (len(dims) - 1 - position))
    return gain


def noise(stream_key, dims, scale, bound, shards=(), kind=jnp.bfloat16):
    array = jax.random.normal(stream_key, dims, jnp.float32) * scale
    if len(shards) > 0:
        array = steps_of(stream_key, dims, shards, -0.22, 0.18) * array
    return jnp.clip(array, min=-bound, max=bound).astype(kind)


def setup_inputs(seed: int = 0) -> dict:
    key_list = jax.random.split(jax.random.key(seed), 11)
    state = noise(key_list[0], (BATCH, LEN, D), 1.0, 6.0, ((0, 4), (1, 8)))
    embedded = noise(key_list[1], (BATCH, LEN, D), 1.0, 6.0, ((0, 4), (1, 8)))
    cotangent = noise(key_list[2], (BATCH, LEN, D), 1.0, 6.0, ((0, 4), (1, 8)))
    w_adapt = noise(key_list[3], (2 * D, D), (2 * D) ** -0.5, 0.125)
    w_qkv = noise(key_list[4], (D, 3 * D), (D // 2) ** -0.5, 0.25)
    w_out = noise(key_list[5], (D, D), D ** -0.5, 0.1875)
    w_gate = noise(key_list[6], (D, FF), D ** -0.5, 0.1875)
    w_up = noise(key_list[7], (D, FF), D ** -0.5, 0.1875)
    w_down = noise(key_list[8], (FF, D), FF ** -0.5, 0.109375)
    gains = jnp.clip(1.0 + 0.1 * jax.random.normal(key_list[9], (4, D), jnp.float32), 0.5, 1.5).astype(jnp.bfloat16)
    return dict(state=state, embedded=embedded, cotangent=cotangent, w_adapt=w_adapt, w_qkv=w_qkv, w_out=w_out, w_gate=w_gate, w_up=w_up, w_down=w_down, gains=gains)


norm_eps = 1e-06
rope_base = 50000.0
masked_score = -1e+30

@jax.custom_vjp
def low(v):
    return lax.optimization_barrier(v.astype(jnp.bfloat16)).astype(jnp.float32)

@jax.custom_vjp
def low_back(v):
    return v

def low_keep(v):
    return (low(v), None)

def low_pass(kept, grad):
    return (grad,)

def back_keep(v):
    return (v, None)

def back_low(kept, grad):
    return (low(grad),)
low.defvjp(low_keep, low_pass)
low_back.defvjp(back_keep, back_low)

def mean_norm(values_in, gain_row):
    return values_in * lax.rsqrt(lax.optimization_barrier(jnp.mean(values_in * values_in, axis=-1, keepdims=True)) + norm_eps) * gain_row

def angle_tables(positions):
    half_dim = HEAD_DIM // 2
    freqs = jnp.exp(jnp.arange(half_dim, dtype=jnp.float32) * (-2.0 * math.log(rope_base) / HEAD_DIM))
    angles = positions.astype(jnp.float32)[:, None] * freqs[None, :]
    return (jnp.cos(angles)[:, None, :], jnp.sin(angles)[:, None, :])

def rotate(heads_in, cos_table, sin_table):
    half_dim = heads_in.shape[-1] // 2
    lower_half = heads_in[..., :half_dim]
    upper_half = heads_in[..., half_dim:]
    return jnp.concatenate([lower_half * cos_table - upper_half * sin_table, upper_half * cos_table + lower_half * sin_table], axis=-1)

def attend(queries, key_heads, value_heads):
    length = queries.shape[0]
    tile_size = math.gcd(length, 512)
    score_scale = 1.0 / math.sqrt(HEAD_DIM)
    columns = jnp.arange(length, dtype=jnp.int32)

    def one_tile(start_row):
        query_tile = lax.dynamic_slice_in_dim(queries, start_row, tile_size, 0)
        scores = jnp.einsum('qhd,khd->hqk', query_tile, key_heads, precision=lax.Precision.HIGHEST) * score_scale
        scores = low_back(scores)
        query_spots = start_row + jnp.arange(tile_size, dtype=jnp.int32)
        allowed = query_spots[:, None] >= columns[None, :]
        scores = jnp.where(allowed[None], scores, masked_score)
        weights = low(jax.nn.softmax(scores, axis=-1))
        return jnp.einsum('hqk,khd->qhd', weights, value_heads, precision=lax.Precision.HIGHEST)
    starts = jnp.arange(length // tile_size, dtype=jnp.int32) * tile_size
    outputs = lax.map(jax.checkpoint(one_tile), starts)
    return outputs.reshape(length, HEADS, HEAD_DIM)

def one_layer(joined, w_adapt, w_qkv, w_out, w_gate, w_up, w_down, gains, cos_table, sin_table):
    highest = lax.Precision.HIGHEST
    length = joined.shape[0]
    resid = low_back(jnp.dot(joined, w_adapt, precision=highest))
    normed = low(mean_norm(resid, gains[0]))
    packed = low_back(jnp.dot(normed, w_qkv, precision=highest))
    queries = packed[:, :D].reshape(length, HEADS, HEAD_DIM)
    key_heads = packed[:, D:2 * D].reshape(length, HEADS, HEAD_DIM)
    value_heads = packed[:, 2 * D:].reshape(length, HEADS, HEAD_DIM)
    queries = low(rotate(queries, cos_table, sin_table))
    key_heads = low(rotate(key_heads, cos_table, sin_table))
    value_heads = low(value_heads)
    attended = low(low_back(attend(queries, key_heads, value_heads))).reshape(length, D)
    branch = low_back(jnp.dot(attended, w_out, precision=highest))
    middle = resid + mean_norm(branch, gains[1])
    normed_mid = low(mean_norm(middle, gains[2]))
    gate_pre = low_back(jnp.dot(normed_mid, w_gate, precision=highest))
    up_pre = low_back(jnp.dot(normed_mid, w_up, precision=highest))
    hidden = low(jax.nn.silu(gate_pre) * up_pre)
    down_out = low_back(jnp.dot(hidden, w_down, precision=highest))
    return middle + mean_norm(down_out, gains[3])

def reference(state, embedded, cotangent, w_adapt, w_qkv, w_out, w_gate, w_up, w_down, gains):
    weights = tuple((item.astype(jnp.float32) for item in (w_adapt, w_qkv, w_out, w_gate, w_up, w_down, gains)))
    joined = jnp.concatenate([state, embedded], axis=-1).astype(jnp.float32)
    cos_table, sin_table = angle_tables(jnp.arange(joined.shape[1], dtype=jnp.int32))

    def forward_all(joined_all, adapt_f, qkv_f, out_f, gate_f, up_f, down_f, gains_f):

        def one_sequence(sequence):
            return one_layer(sequence, adapt_f, qkv_f, out_f, gate_f, up_f, down_f, gains_f, cos_table, sin_table)
        return lax.map(jax.checkpoint(one_sequence), joined_all)
    layer_out, pullback = jax.vjp(forward_all, joined, *weights)
    gradients = pullback(cotangent.astype(jnp.float32))
    grad_joined = gradients[0]
    return (layer_out.astype(jnp.bfloat16), grad_joined[..., :D], grad_joined[..., D:], gradients[1], gradients[2], gradients[3], gradients[4], gradients[5], gradients[6], gradients[7])
```

```python
import functools
import math

import jax
import jax.numpy as jnp
import numpy as np
from jax import lax
from jax.experimental import pallas as pl
from jax.experimental.pallas import tpu as pltpu
from jax.sharding import PartitionSpec as P

HEADS = 8
HEAD_DIM = 128
norm_eps = 1e-06
rope_base = 50000.0
F32 = jnp.float32
BF16 = jnp.bfloat16
NEG = -1e30
SCORE_SCALE = 1.0 / math.sqrt(HEAD_DIM)
LOG2E = 1.0 / math.log(2.0)


def mean_norm(values_in, gain_row):
    return (
        values_in
        * lax.rsqrt(jnp.mean(values_in * values_in, axis=-1, keepdims=True) + norm_eps)
        * gain_row
    )


def norm_back(values_in, gain_row, upstream):
    inverse = lax.rsqrt(jnp.mean(values_in * values_in, axis=-1, keepdims=True) + norm_eps)
    scaled = upstream * gain_row
    value_grad = inverse * scaled - values_in * (inverse * inverse * inverse) * jnp.mean(
        values_in * scaled, axis=-1, keepdims=True
    )
    gain_grad = jnp.sum(upstream * values_in * inverse, axis=0)
    return (value_grad, gain_grad)


def angle_tables(length):
    half_dim = HEAD_DIM // 2
    freqs = np.exp(
        np.arange(half_dim, dtype=np.float32) * np.float32(-2.0 * math.log(rope_base) / HEAD_DIM)
    ).astype(np.float32)
    angles = np.arange(length, dtype=np.float32)[:, None] * freqs[None, :]
    return np.cos(angles).astype(np.float32), np.sin(angles).astype(np.float32)


def rotate(heads_in, cos_table, sin_table):
    half_dim = heads_in.shape[-1] // 2
    lower_half = heads_in[..., :half_dim]
    upper_half = heads_in[..., half_dim:]
    return jnp.concatenate(
        [
            lower_half * cos_table - upper_half * sin_table,
            upper_half * cos_table + lower_half * sin_table,
        ],
        axis=-1,
    )


def dot(a, b):
    return lax.dot_general(a, b, (((1,), (0,)), ((), ())), preferred_element_type=F32)


def dot_tn(a, b):
    return lax.dot_general(a, b, (((0,), (0,)), ((), ())), preferred_element_type=F32)


def dot_nt(a, b):
    return lax.dot_general(a, b, (((1,), (1,)), ((), ())), preferred_element_type=F32)


def span(low, high, body, unrolled):
    if unrolled:
        for i in range(low, high):
            body(i)
    else:
        lax.fori_loop(low, high, lambda i, c: (body(i), c)[1], 0)


def causal_fill(block, fill):
    kv = lax.broadcasted_iota(jnp.int32, block.shape, 0)
    q = lax.broadcasted_iota(jnp.int32, block.shape, 1)
    return jnp.where(q >= kv, block, fill)


def attention_kernel(x_ref, o_ref, ot_ref, ls_ref, vt_ref, s_ref):
    n, hp, _, rows, _ = x_ref.shape
    unrolled = n <= 8
    factor = SCORE_SCALE * LOG2E
    for h in range(hp):
        for j in range(n):
            vt_ref[j] = x_ref[j, h, 2].astype(F32).T.astype(BF16)

        def query_block(i):
            q = x_ref[i, h, 0]
            diag = causal_fill(dot_nt(x_ref[i, h, 1], q), NEG)

            def first(j, peak):
                s = dot_nt(x_ref[j, h, 1], q)
                s_ref[j] = s
                return jnp.maximum(peak, jnp.max(s, axis=0, keepdims=True))

            peak = jnp.max(diag, axis=0, keepdims=True)
            if unrolled:
                for j in range(i):
                    peak = first(j, peak)
            else:
                peak = lax.fori_loop(0, i, first, peak)
            shift = peak * factor
            p = jnp.exp2(diag * factor - shift)
            total = jnp.sum(p, axis=0, keepdims=True)
            acc = dot(vt_ref[i], p.astype(BF16))

            def second(j, state):
                total, acc = state
                p = jnp.exp2(s_ref[j] * factor - shift)
                return (
                    total + jnp.sum(p, axis=0, keepdims=True),
                    acc + dot(vt_ref[j], p.astype(BF16)),
                )

            state = (total, acc)
            if unrolled:
                for j in range(i):
                    state = second(j, state)
            else:
                state = lax.fori_loop(0, i, second, state)
            total, acc = state
            acc = acc / total
            ot_ref[i, h] = acc
            o_ref[i, h] = acc.T.astype(BF16)
            ls_ref[i, h] = shift + jnp.log2(total)

        span(0, n, query_block, unrolled)


def attention(x):
    n, hp, _, rows, dim = x.shape
    pairs = n * (n + 1) // 2 * rows * rows * hp
    return pl.pallas_call(
        attention_kernel,
        name="attention",
        out_shape=(
            jax.ShapeDtypeStruct((n, hp, rows, dim), BF16),
            jax.ShapeDtypeStruct((n, hp, dim, rows), F32),
            jax.ShapeDtypeStruct((n, hp, 1, rows), F32),
        ),
        scratch_shapes=[
            pltpu.VMEM((n, dim, rows), BF16),
            pltpu.VMEM((n, rows, rows), F32),
        ],
        compiler_params=pltpu.CompilerParams(vmem_limit_bytes=40 << 20),
        cost_estimate=pl.CostEstimate(
            flops=pairs * dim * 8, bytes_accessed=x.size * 4, transcendentals=pairs
        ),
    )(x)


def attention_back_kernel(
    x_ref, g_ref, ot_ref, ls_ref, cos_ref, sin_ref, out_ref, kt_ref, dqt_ref, delta_ref
):
    n, hp, _, rows, _ = x_ref.shape
    unrolled = n <= 8
    factor = SCORE_SCALE * LOG2E
    for h in range(hp):
        for j in range(n):
            kt_ref[j] = x_ref[j, h, 1].astype(F32).T.astype(BF16)
            delta_ref[j] = jnp.sum(
                g_ref[j, h].astype(F32).T * ot_ref[j, h], axis=0, keepdims=True
            )

        def unrotated(value, i):
            turned = pl.ds(i * rows, rows)
            cos, sin = cos_ref[turned], sin_ref[turned]
            return rotate(value * SCORE_SCALE, cos, -sin).astype(BF16)

        def pair(i, j, diagonal):
            q, g = x_ref[i, h, 0], g_ref[i, h]
            p = jnp.exp2(dot_nt(x_ref[j, h, 1], q) * factor - ls_ref[i, h])
            if diagonal:
                p = causal_fill(p, 0.0)
            dv = dot(p.astype(BF16), g)
            ds = (p * (dot_nt(x_ref[j, h, 2], g) - delta_ref[i])).astype(BF16)
            dk = dot(ds, q)
            dqt = dot(kt_ref[j], ds)
            return dv, dk, dqt

        def key_block(j):
            dv, dk, dqt = pair(j, j, True)
            if unrolled:
                dqt_ref[j] = dqt if j == 0 else dqt_ref[j] + dqt
            else:
                dqt_ref[j] = jnp.where(j == 0, 0.0, dqt_ref[j]) + dqt

            def step(i, state):
                dv, dk = state
                v, k, t = pair(i, j, False)
                if unrolled:
                    dqt_ref[i] = t if j == 0 else dqt_ref[i] + t
                else:
                    dqt_ref[i] = jnp.where(j == 0, 0.0, dqt_ref[i]) + t
                return dv + v, dk + k

            state = (dv, dk)
            if unrolled:
                for i in range(j + 1, n):
                    state = step(i, state)
            else:
                state = lax.fori_loop(j + 1, n, step, state)
            dv, dk = state
            out_ref[j, h, 0] = unrotated(dqt_ref[j].T, j)
            out_ref[j, h, 1] = unrotated(dk, j)
            out_ref[j, h, 2] = dv.astype(BF16)

        span(0, n, key_block, unrolled)


def attention_back(x, g, ot, ls, cos, sin):
    n, hp, _, rows, dim = x.shape
    pairs = n * (n + 1) // 2 * rows * rows * hp
    return pl.pallas_call(
        attention_back_kernel,
        name="attention_back",
        out_shape=jax.ShapeDtypeStruct(x.shape, BF16),
        scratch_shapes=[
            pltpu.VMEM((n, dim, rows), BF16),
            pltpu.VMEM((n, dim, rows), F32),
            pltpu.VMEM((n, 1, rows), F32),
        ],
        compiler_params=pltpu.CompilerParams(vmem_limit_bytes=40 << 20),
        cost_estimate=pl.CostEstimate(
            flops=pairs * dim * 20, bytes_accessed=x.size * 6, transcendentals=pairs
        ),
    )(x, g, ot, ls, cos, sin)


def xor_permute(value, axis, mask):
    return lax.ppermute(value, axis, [(i, i ^ mask) for i in range(lax.axis_size(axis))])


def quadrants(left):
    n, parts = lax.axis_size("seq"), lax.axis_size("dp")
    tokens, rows = left.shape
    shard = rows // (n * parts)
    split = left.reshape(tokens, n, parts, shard).transpose(2, 0, 1, 3)
    split = split.reshape(parts, tokens, n * shard)
    me = lax.axis_index("dp")
    return jnp.concatenate(
        [lax.dynamic_index_in_dim(split, me ^ m, 0, keepdims=True) for m in range(parts)]
    )


def other_core(left, right):
    core = lax.axis_index("seq") % 2
    half = right.shape[1] // 2
    mine = lax.dynamic_slice_in_dim(right, core * half, half, 1)
    theirs = lax.dynamic_slice_in_dim(right, (1 - core) * half, half, 1)
    left_in = xor_permute(left, "seq", 1)
    right_in = xor_permute(theirs, "seq", 1)
    return jnp.concatenate([left, left_in], axis=1), jnp.concatenate([mine, right_in], axis=0)


def scattered_sum(left, right, bits):
    n, parts = lax.axis_size("seq"), lax.axis_size("dp")
    cols = right.shape[1]
    left, right = other_core(quadrants(left), right)
    got = {}
    masks = list(range(parts))
    for bit in bits:
        outgoing = [m for m in masks if m >> bit & 1]
        masks = [m for m in masks if not m >> bit & 1]
        blocks = []
        for m in outgoing:
            block = dot_tn(left[m], right)
            for more in got.get(m, ()):
                block = block + more.astype(F32)
            blocks.append(block.astype(BF16))
        incoming = xor_permute(jnp.stack(blocks), "dp", 1 << bit)
        for k, m in enumerate(outgoing):
            got.setdefault(m ^ (1 << bit), []).append(incoming[k])
    block = dot_tn(left[0], right)
    for more in got.get(0, ()):
        block = block + more.astype(F32)
    shard = block.shape[0] // n
    block = block.astype(BF16).reshape(n, shard, cols // 2)
    block = lax.all_to_all(block, "seq", 0, 0)
    block = jnp.sum(block.reshape(n // 2, 2, shard, cols // 2).astype(F32), axis=0)
    return block.transpose(1, 0, 2).reshape(shard, cols)


def local(state, embedded, cotangent, w_adapt, w_qkv, w_out, w_gate, w_up, w_down, gains):
    seq_count, rows, width = state.shape
    n, parts = lax.axis_size("seq"), lax.axis_size("dp")
    tokens = seq_count * rows
    me = lax.axis_index("seq")
    bits = list(range(parts.bit_length() - 1))
    copies = max(1, n // HEADS)
    held = max(1, HEADS // n)
    owners = n // copies
    cos_np, sin_np = angle_tables(n * rows)
    cos_all, sin_all = jnp.asarray(cos_np), jnp.asarray(sin_np)
    cos = lax.dynamic_slice_in_dim(cos_all, me * rows, rows, 0)[:, None, :]
    sin = lax.dynamic_slice_in_dim(sin_all, me * rows, rows, 0)[:, None, :]
    gain_rows = gains.astype(F32)
    state, embedded = state.reshape(tokens, width), embedded.reshape(tokens, width)

    def to_heads(flat):
        return flat.reshape(tokens, HEADS, HEAD_DIM)

    def to_owner(parts_in):
        sent = jnp.stack(parts_in).reshape(len(parts_in), tokens, owners, held, HEAD_DIM)
        sent = sent.transpose(2, 3, 0, 1, 4)
        if copies > 1:
            sent = jnp.repeat(sent, copies, axis=0)
        return lax.all_to_all(sent, "seq", 0, 0)

    def from_owner(value):
        back = lax.all_to_all(value, "seq", 0, 0)[::copies]
        back = back.reshape(HEADS, -1, tokens, HEAD_DIM)
        return back.transpose(2, 1, 0, 3).reshape(tokens, -1)

    resid = dot(state, w_adapt[:width]) + dot(embedded, w_adapt[width:])
    normed = mean_norm(resid, gain_rows[0]).astype(BF16)
    packed = dot(normed, w_qkv)
    queries = rotate(to_heads(packed[:, :width]), cos, sin).astype(BF16)
    keys = rotate(to_heads(packed[:, width : 2 * width]), cos, sin).astype(BF16)
    values = to_heads(packed[:, 2 * width :]).astype(BF16)
    qkv = to_owner((queries, keys, values))
    attended, attended_t, logsum = attention(qkv)
    attended = from_owner(attended[:, :, None])
    branch = dot(attended, w_out)
    middle = resid + mean_norm(branch, gain_rows[1])
    normed_mid = mean_norm(middle, gain_rows[2]).astype(BF16)
    gate_pre = dot(normed_mid, w_gate)
    up_pre = dot(normed_mid, w_up)
    sigmoid_gate = jax.nn.sigmoid(gate_pre)
    silu_gate = gate_pre * sigmoid_gate
    hidden = (silu_gate * up_pre).astype(BF16)
    down_out = dot(hidden, w_down)
    layer_out = middle + mean_norm(down_out, gain_rows[3])
    out_grad = cotangent.astype(F32).reshape(tokens, width)
    down_grad, gain_grad3 = norm_back(down_out, gain_rows[3], out_grad)
    down_low = down_grad.astype(BF16)
    hidden_grad = dot_nt(down_low, w_down)
    gate_low = (
        hidden_grad * up_pre * sigmoid_gate * (1.0 + gate_pre * (1.0 - sigmoid_gate))
    ).astype(BF16)
    up_low = (hidden_grad * silu_gate).astype(BF16)
    mid_norm_grad = dot_nt(gate_low, w_gate) + dot_nt(up_low, w_up)
    middle_part, gain_grad2 = norm_back(middle, gain_rows[2], mid_norm_grad)
    middle_grad = out_grad + middle_part
    branch_grad, gain_grad1 = norm_back(branch, gain_rows[1], middle_grad)
    branch_low = branch_grad.astype(BF16)
    attended_grad = dot_nt(branch_low, w_out).astype(BF16)
    upstream = to_owner((to_heads(attended_grad),))[:, :, 0]
    packed_grad = attention_back(qkv, upstream, attended_t, logsum, cos_all, sin_all)
    packed_low = from_owner(packed_grad)
    normed_grad = dot_nt(packed_low, w_qkv)
    resid_part, gain_grad0 = norm_back(resid, gain_rows[0], normed_grad)
    resid_low = (middle_grad + resid_part).astype(BF16)
    grad_state = dot_nt(resid_low, w_adapt[:width])
    grad_embedded = dot_nt(resid_low, w_adapt[width:])
    flipped = bits[::-1]
    joined = jnp.concatenate([state, embedded], axis=-1)
    grad_down = scattered_sum(hidden, down_low, bits)
    grad_gate = scattered_sum(normed_mid, gate_low, flipped)
    grad_up = scattered_sum(normed_mid, up_low, bits)
    grad_out = scattered_sum(attended, branch_low, flipped)
    grad_qkv = scattered_sum(normed, packed_low, flipped)
    grad_adapt = scattered_sum(joined, resid_low, bits)
    grad_gains = jnp.stack([gain_grad0, gain_grad1, gain_grad2, gain_grad3])
    grad_gains = lax.psum_scatter(grad_gains, ("seq", "dp"), scatter_dimension=1, tiled=True)
    shape = (seq_count, rows, width)
    return (
        layer_out.reshape(shape).astype(BF16),
        grad_state.reshape(shape),
        grad_embedded.reshape(shape),
        grad_adapt,
        grad_qkv,
        grad_out,
        grad_gate,
        grad_up,
        grad_down,
        grad_gains,
    )


def solution(mesh):
    tokens = P("dp", "seq", None)
    rows = P(("seq", "dp"), None)
    return jax.shard_map(
        local,
        mesh=mesh,
        in_specs=(tokens,) * 3 + (P(),) * 7,
        out_specs=(tokens,) * 3 + (rows,) * 6 + (P(None, ("seq", "dp")),),
        check_vma=False,
    )
```

```python
import functools
import math

import jax
import jax.numpy as jnp
import numpy as np
from jax import lax
from jax.experimental import pallas as pl
from jax.experimental.pallas import tpu as pltpu
from jax.sharding import PartitionSpec as P

HEADS = 8
HEAD_DIM = 128
norm_eps = 1e-06
rope_base = 50000.0
F32 = jnp.float32
BF16 = jnp.bfloat16
NEG = -1e30
SCORE_SCALE = 1.0 / math.sqrt(HEAD_DIM)
LOG2E = 1.0 / math.log(2.0)


def mean_norm(values_in, gain_row):
    return (
        values_in
        * lax.rsqrt(jnp.mean(values_in * values_in, axis=-1, keepdims=True) + norm_eps)
        * gain_row
    )


def norm_back(values_in, gain_row, upstream):
    inverse = lax.rsqrt(jnp.mean(values_in * values_in, axis=-1, keepdims=True) + norm_eps)
    scaled = upstream * gain_row
    value_grad = inverse * scaled - values_in * (inverse * inverse * inverse) * jnp.mean(
        values_in * scaled, axis=-1, keepdims=True
    )
    gain_grad = jnp.sum(upstream * values_in * inverse, axis=0)
    return (value_grad, gain_grad)


def angle_tables(length):
    half_dim = HEAD_DIM // 2
    freqs = np.exp(
        np.arange(half_dim, dtype=np.float32) * np.float32(-2.0 * math.log(rope_base) / HEAD_DIM)
    ).astype(np.float32)
    angles = np.arange(length, dtype=np.float32)[:, None] * freqs[None, :]
    return np.cos(angles).astype(np.float32), np.sin(angles).astype(np.float32)


def rotate(heads_in, cos_table, sin_table):
    half_dim = heads_in.shape[-1] // 2
    lower_half = heads_in[..., :half_dim]
    upper_half = heads_in[..., half_dim:]
    return jnp.concatenate(
        [
            lower_half * cos_table - upper_half * sin_table,
            upper_half * cos_table + lower_half * sin_table,
        ],
        axis=-1,
    )


def dot(a, b):
    return lax.dot_general(a, b, (((1,), (0,)), ((), ())), preferred_element_type=F32)


def dot_tn(a, b):
    return lax.dot_general(a, b, (((0,), (0,)), ((), ())), preferred_element_type=F32)


def dot_nt(a, b):
    return lax.dot_general(a, b, (((1,), (1,)), ((), ())), preferred_element_type=F32)


def span(low, high, body, unrolled):
    if unrolled:
        for i in range(low, high):
            body(i)
    else:
        lax.fori_loop(low, high, lambda i, c: (body(i), c)[1], 0)


def causal_fill(block, fill):
    kv = lax.broadcasted_iota(jnp.int32, block.shape, 0)
    q = lax.broadcasted_iota(jnp.int32, block.shape, 1)
    return jnp.where(q >= kv, block, fill)


def attention_kernel(x_ref, o_ref, ot_ref, ls_ref, vt_ref, s_ref):
    n, hp, _, rows, _ = x_ref.shape
    unrolled = n <= 8
    factor = SCORE_SCALE * LOG2E
    for h in range(hp):
        for j in range(n):
            vt_ref[j] = x_ref[j, h, 2].astype(F32).T.astype(BF16)

        def query_block(i):
            q = x_ref[i, h, 0]
            diag = causal_fill(dot_nt(x_ref[i, h, 1], q), NEG)

            def first(j, peak):
                s = dot_nt(x_ref[j, h, 1], q)
                s_ref[j] = s
                return jnp.maximum(peak, jnp.max(s, axis=0, keepdims=True))

            peak = jnp.max(diag, axis=0, keepdims=True)
            if unrolled:
                for j in range(i):
                    peak = first(j, peak)
            else:
                peak = lax.fori_loop(0, i, first, peak)
            shift = peak * factor
            p = jnp.exp2(diag * factor - shift)
            total = jnp.sum(p, axis=0, keepdims=True)
            acc = dot(vt_ref[i], p.astype(BF16))

            def second(j, state):
                total, acc = state
                p = jnp.exp2(s_ref[j] * factor - shift)
                return (
                    total + jnp.sum(p, axis=0, keepdims=True),
                    acc + dot(vt_ref[j], p.astype(BF16)),
                )

            state = (total, acc)
            if unrolled:
                for j in range(i):
                    state = second(j, state)
            else:
                state = lax.fori_loop(0, i, second, state)
            total, acc = state
            acc = acc / total
            ot_ref[i, h] = acc
            o_ref[i, h] = acc.T.astype(BF16)
            ls_ref[i, h] = shift + jnp.log2(total)

        span(0, n, query_block, unrolled)


def attention(x):
    n, hp, _, rows, dim = x.shape
    pairs = n * (n + 1) // 2 * rows * rows * hp
    return pl.pallas_call(
        attention_kernel,
        name="attention",
        out_shape=(
            jax.ShapeDtypeStruct((n, hp, rows, dim), BF16),
            jax.ShapeDtypeStruct((n, hp, dim, rows), F32),
            jax.ShapeDtypeStruct((n, hp, 1, rows), F32),
        ),
        scratch_shapes=[
            pltpu.VMEM((n, dim, rows), BF16),
            pltpu.VMEM((n, rows, rows), F32),
        ],
        compiler_params=pltpu.CompilerParams(vmem_limit_bytes=40 << 20),
        cost_estimate=pl.CostEstimate(
            flops=pairs * dim * 8, bytes_accessed=x.size * 4, transcendentals=pairs
        ),
    )(x)


def attention_back_kernel(
    x_ref, g_ref, ot_ref, ls_ref, cos_ref, sin_ref, out_ref, kt_ref, dqt_ref, delta_ref
):
    n, hp, _, rows, _ = x_ref.shape
    unrolled = n <= 8
    factor = SCORE_SCALE * LOG2E
    for h in range(hp):
        for j in range(n):
            kt_ref[j] = x_ref[j, h, 1].astype(F32).T.astype(BF16)
            delta_ref[j] = jnp.sum(
                g_ref[j, h].astype(F32).T * ot_ref[j, h], axis=0, keepdims=True
            )

        def unrotated(value, i):
            turned = pl.ds(i * rows, rows)
            cos, sin = cos_ref[turned], sin_ref[turned]
            return rotate(value * SCORE_SCALE, cos, -sin).astype(BF16)

        def pair(i, j, diagonal):
            q, g = x_ref[i, h, 0], g_ref[i, h]
            p = jnp.exp2(dot_nt(x_ref[j, h, 1], q) * factor - ls_ref[i, h])
            if diagonal:
                p = causal_fill(p, 0.0)
            dv = dot(p.astype(BF16), g)
            ds = (p * (dot_nt(x_ref[j, h, 2], g) - delta_ref[i])).astype(BF16)
            dk = dot(ds, q)
            dqt = dot(kt_ref[j], ds)
            return dv, dk, dqt

        def key_block(j):
            dv, dk, dqt = pair(j, j, True)
            if unrolled:
                dqt_ref[j] = dqt if j == 0 else dqt_ref[j] + dqt
            else:
                dqt_ref[j] = jnp.where(j == 0, 0.0, dqt_ref[j]) + dqt

            def step(i, state):
                dv, dk = state
                v, k, t = pair(i, j, False)
                if unrolled:
                    dqt_ref[i] = t if j == 0 else dqt_ref[i] + t
                else:
                    dqt_ref[i] = jnp.where(j == 0, 0.0, dqt_ref[i]) + t
                return dv + v, dk + k

            state = (dv, dk)
            if unrolled:
                for i in range(j + 1, n):
                    state = step(i, state)
            else:
                state = lax.fori_loop(j + 1, n, step, state)
            dv, dk = state
            out_ref[j, h, 0] = unrotated(dqt_ref[j].T, j)
            out_ref[j, h, 1] = unrotated(dk, j)
            out_ref[j, h, 2] = dv.astype(BF16)

        span(0, n, key_block, unrolled)


def attention_back(x, g, ot, ls, cos, sin):
    n, hp, _, rows, dim = x.shape
    pairs = n * (n + 1) // 2 * rows * rows * hp
    return pl.pallas_call(
        attention_back_kernel,
        name="attention_back",
        out_shape=jax.ShapeDtypeStruct(x.shape, BF16),
        scratch_shapes=[
            pltpu.VMEM((n, dim, rows), BF16),
            pltpu.VMEM((n, dim, rows), F32),
            pltpu.VMEM((n, 1, rows), F32),
        ],
        compiler_params=pltpu.CompilerParams(vmem_limit_bytes=40 << 20),
        cost_estimate=pl.CostEstimate(
            flops=pairs * dim * 20, bytes_accessed=x.size * 6, transcendentals=pairs
        ),
    )(x, g, ot, ls, cos, sin)


def xor_permute(value, axis, mask):
    return lax.ppermute(value, axis, [(i, i ^ mask) for i in range(lax.axis_size(axis))])


def quadrants(left):
    n, parts = lax.axis_size("seq"), lax.axis_size("dp")
    tokens, rows = left.shape
    shard = rows // (n * parts)
    split = left.reshape(tokens, n, parts, shard).transpose(2, 0, 1, 3)
    split = split.reshape(parts, tokens, n * shard)
    me = lax.axis_index("dp")
    return jnp.concatenate(
        [lax.dynamic_index_in_dim(split, me ^ m, 0, keepdims=True) for m in range(parts)]
    )


def other_core(left, right):
    core = lax.axis_index("seq") % 2
    half = right.shape[1] // 2
    mine = lax.dynamic_slice_in_dim(right, core * half, half, 1)
    theirs = lax.dynamic_slice_in_dim(right, (1 - core) * half, half, 1)
    left_in = xor_permute(left, "seq", 1)
    right_in = xor_permute(theirs, "seq", 1)
    return jnp.concatenate([left, left_in], axis=1), jnp.concatenate([mine, right_in], axis=0)


def scattered_sum(left, right, bits):
    n, parts = lax.axis_size("seq"), lax.axis_size("dp")
    cols = right.shape[1]
    left, right = other_core(quadrants(left), right)
    got = {}
    masks = list(range(parts))
    for bit in bits:
        outgoing = [m for m in masks if m >> bit & 1]
        masks = [m for m in masks if not m >> bit & 1]
        blocks = []
        for m in outgoing:
            block = dot_tn(left[m], right)
            for more in got.get(m, ()):
                block = block + more.astype(F32)
            blocks.append(block.astype(BF16))
        incoming = xor_permute(jnp.stack(blocks), "dp", 1 << bit)
        for k, m in enumerate(outgoing):
            got.setdefault(m ^ (1 << bit), []).append(incoming[k])
    block = dot_tn(left[0], right)
    for more in got.get(0, ()):
        block = block + more.astype(F32)
    shard = block.shape[0] // n
    block = block.astype(BF16).reshape(n, shard, cols // 2)
    block = lax.all_to_all(block, "seq", 0, 0)
    block = jnp.sum(block.reshape(n // 2, 2, shard, cols // 2).astype(F32), axis=0)
    return block.transpose(1, 0, 2).reshape(shard, cols)


def small_sum(value):
    value = value.reshape(value.shape[0], -1, value.shape[1])
    for axis in ("seq", "dp"):
        size = lax.axis_size(axis)
        me = lax.axis_index(axis)
        for bit in reversed(range(size.bit_length() - 1)):
            half = value.shape[2] // 2
            mine = (me >> bit) & 1
            kept = lax.dynamic_slice_in_dim(value, mine * half, half, 2)
            sent = lax.dynamic_slice_in_dim(value, (1 - mine) * half, half, 2)
            value = kept + xor_permute(sent, axis, 1 << bit)
    return value[:, 0]


def local(state, embedded, cotangent, w_adapt, w_qkv, w_out, w_gate, w_up, w_down, gains):
    seq_count, rows, width = state.shape
    n, parts = lax.axis_size("seq"), lax.axis_size("dp")
    tokens = seq_count * rows
    me = lax.axis_index("seq")
    bits = list(range(parts.bit_length() - 1))
    copies = max(1, n // HEADS)
    held = max(1, HEADS // n)
    owners = n // copies
    cos_np, sin_np = angle_tables(n * rows)
    cos_all, sin_all = jnp.asarray(cos_np), jnp.asarray(sin_np)
    cos = lax.dynamic_slice_in_dim(cos_all, me * rows, rows, 0)[:, None, :]
    sin = lax.dynamic_slice_in_dim(sin_all, me * rows, rows, 0)[:, None, :]
    gain_rows = gains.astype(F32)
    state, embedded = state.reshape(tokens, width), embedded.reshape(tokens, width)

    def to_heads(flat):
        return flat.reshape(tokens, HEADS, HEAD_DIM)

    def to_owner(parts_in):
        sent = jnp.stack(parts_in).reshape(len(parts_in), tokens, owners, held, HEAD_DIM)
        sent = sent.transpose(2, 3, 0, 1, 4)
        if copies > 1:
            sent = jnp.repeat(sent, copies, axis=0)
        return lax.all_to_all(sent, "seq", 0, 0)

    def from_owner(value):
        back = lax.all_to_all(value, "seq", 0, 0)[::copies]
        back = back.reshape(HEADS, -1, tokens, HEAD_DIM)
        return back.transpose(2, 1, 0, 3).reshape(tokens, -1)

    resid = dot(state, w_adapt[:width]) + dot(embedded, w_adapt[width:])
    normed = mean_norm(resid, gain_rows[0]).astype(BF16)
    packed = dot(normed, w_qkv)
    queries = rotate(to_heads(packed[:, :width]), cos, sin).astype(BF16)
    keys = rotate(to_heads(packed[:, width : 2 * width]), cos, sin).astype(BF16)
    values = to_heads(packed[:, 2 * width :]).astype(BF16)
    qkv = to_owner((queries, keys, values))
    attended, attended_t, logsum = attention(qkv)
    attended = from_owner(attended[:, :, None])
    branch = dot(attended, w_out)
    middle = resid + mean_norm(branch, gain_rows[1])
    normed_mid = mean_norm(middle, gain_rows[2]).astype(BF16)
    gate_pre = dot(normed_mid, w_gate)
    up_pre = dot(normed_mid, w_up)
    sigmoid_gate = jax.nn.sigmoid(gate_pre)
    silu_gate = gate_pre * sigmoid_gate
    hidden = (silu_gate * up_pre).astype(BF16)
    down_out = dot(hidden, w_down)
    layer_out = middle + mean_norm(down_out, gain_rows[3])
    out_grad = cotangent.astype(F32).reshape(tokens, width)
    down_grad, gain_grad3 = norm_back(down_out, gain_rows[3], out_grad)
    down_low = down_grad.astype(BF16)
    hidden_grad = dot_nt(down_low, w_down)
    gate_low = (
        hidden_grad * up_pre * sigmoid_gate * (1.0 + gate_pre * (1.0 - sigmoid_gate))
    ).astype(BF16)
    up_low = (hidden_grad * silu_gate).astype(BF16)
    mid_norm_grad = dot_nt(gate_low, w_gate) + dot_nt(up_low, w_up)
    middle_part, gain_grad2 = norm_back(middle, gain_rows[2], mid_norm_grad)
    middle_grad = out_grad + middle_part
    branch_grad, gain_grad1 = norm_back(branch, gain_rows[1], middle_grad)
    branch_low = branch_grad.astype(BF16)
    attended_grad = dot_nt(branch_low, w_out).astype(BF16)
    upstream = to_owner((to_heads(attended_grad),))[:, :, 0]
    packed_grad = attention_back(qkv, upstream, attended_t, logsum, cos_all, sin_all)
    packed_low = from_owner(packed_grad)
    normed_grad = dot_nt(packed_low, w_qkv)
    resid_part, gain_grad0 = norm_back(resid, gain_rows[0], normed_grad)
    resid_low = (middle_grad + resid_part).astype(BF16)
    grad_state = dot_nt(resid_low, w_adapt[:width])
    grad_embedded = dot_nt(resid_low, w_adapt[width:])
    flipped = bits[::-1]
    joined = jnp.concatenate([state, embedded], axis=-1)
    grad_down = scattered_sum(hidden, down_low, bits)
    grad_gate = scattered_sum(normed_mid, gate_low, flipped)
    grad_up = scattered_sum(normed_mid, up_low, bits)
    grad_out = scattered_sum(attended, branch_low, flipped)
    grad_qkv = scattered_sum(normed, packed_low, flipped)
    grad_adapt = scattered_sum(joined, resid_low, bits)
    grad_gains = jnp.stack([gain_grad0, gain_grad1, gain_grad2, gain_grad3])
    grad_gains = small_sum(grad_gains)
    shape = (seq_count, rows, width)
    return (
        layer_out.reshape(shape).astype(BF16),
        grad_state.reshape(shape),
        grad_embedded.reshape(shape),
        grad_adapt,
        grad_qkv,
        grad_out,
        grad_gate,
        grad_up,
        grad_down,
        grad_gains,
    )


def solution(mesh):
    tokens = P("dp", "seq", None)
    rows = P(("seq", "dp"), None)
    return jax.shard_map(
        local,
        mesh=mesh,
        in_specs=(tokens,) * 3 + (P(),) * 7,
        out_specs=(tokens,) * 3 + (rows,) * 6 + (P(None, ("seq", "dp")),),
        check_vma=False,
    )
```

```python
import functools
import math

import jax
import jax.numpy as jnp
import numpy as np
from jax import lax
from jax.experimental import pallas as pl
from jax.experimental.pallas import tpu as pltpu
from jax.sharding import PartitionSpec as P

HEADS = 8
HEAD_DIM = 128
norm_eps = 1e-06
rope_base = 50000.0
F32 = jnp.float32
BF16 = jnp.bfloat16
MESH = pl.DeviceIdType.MESH
NEG = -1e30
SCORE_SCALE = 1.0 / math.sqrt(HEAD_DIM)
LOG2E = 1.0 / math.log(2.0)


def mean_norm(values_in, gain_row):
    return (
        values_in
        * lax.rsqrt(jnp.mean(values_in * values_in, axis=-1, keepdims=True) + norm_eps)
        * gain_row
    )


def norm_back(values_in, gain_row, upstream):
    inverse = lax.rsqrt(jnp.mean(values_in * values_in, axis=-1, keepdims=True) + norm_eps)
    scaled = upstream * gain_row
    value_grad = inverse * scaled - values_in * (inverse * inverse * inverse) * jnp.mean(
        values_in * scaled, axis=-1, keepdims=True
    )
    gain_grad = jnp.sum(upstream * values_in * inverse, axis=0)
    return (value_grad, gain_grad)


def angle_tables(length):
    half_dim = HEAD_DIM // 2
    freqs = np.exp(
        np.arange(half_dim, dtype=np.float32) * np.float32(-2.0 * math.log(rope_base) / HEAD_DIM)
    ).astype(np.float32)
    angles = np.arange(length, dtype=np.float32)[:, None] * freqs[None, :]
    return np.cos(angles).astype(np.float32), np.sin(angles).astype(np.float32)


def rotate(heads_in, cos_table, sin_table):
    half_dim = heads_in.shape[-1] // 2
    lower_half = heads_in[..., :half_dim]
    upper_half = heads_in[..., half_dim:]
    return jnp.concatenate(
        [
            lower_half * cos_table - upper_half * sin_table,
            upper_half * cos_table + lower_half * sin_table,
        ],
        axis=-1,
    )


def dot(a, b):
    return lax.dot_general(a, b, (((1,), (0,)), ((), ())), preferred_element_type=F32)


def dot_tn(a, b):
    return lax.dot_general(a, b, (((0,), (0,)), ((), ())), preferred_element_type=F32)


def dot_nt(a, b):
    return lax.dot_general(a, b, (((1,), (1,)), ((), ())), preferred_element_type=F32)


def span(low, high, body, unrolled):
    if unrolled:
        for i in range(low, high):
            body(i)
    else:
        lax.fori_loop(low, high, lambda i, c: (body(i), c)[1], 0)


def causal_fill(block, fill):
    kv = lax.broadcasted_iota(jnp.int32, block.shape, 0)
    q = lax.broadcasted_iota(jnp.int32, block.shape, 1)
    return jnp.where(q >= kv, block, fill)


def attention_kernel(x_ref, o_ref, ot_ref, ls_ref, vt_ref, s_ref):
    n, hp, _, rows, _ = x_ref.shape
    unrolled = n <= 8
    factor = SCORE_SCALE * LOG2E
    for h in range(hp):
        for j in range(n):
            vt_ref[j] = x_ref[j, h, 2].astype(F32).T.astype(BF16)

        def query_block(i):
            q = x_ref[i, h, 0]
            diag = causal_fill(dot_nt(x_ref[i, h, 1], q), NEG)

            def first(j, peak):
                s = dot_nt(x_ref[j, h, 1], q)
                s_ref[j] = s
                return jnp.maximum(peak, jnp.max(s, axis=0, keepdims=True))

            peak = jnp.max(diag, axis=0, keepdims=True)
            if unrolled:
                for j in range(i):
                    peak = first(j, peak)
            else:
                peak = lax.fori_loop(0, i, first, peak)
            shift = peak * factor
            p = jnp.exp2(diag * factor - shift)
            total = jnp.sum(p, axis=0, keepdims=True)
            acc = dot(vt_ref[i], p.astype(BF16))

            def second(j, state):
                total, acc = state
                p = jnp.exp2(s_ref[j] * factor - shift)
                return (
                    total + jnp.sum(p, axis=0, keepdims=True),
                    acc + dot(vt_ref[j], p.astype(BF16)),
                )

            state = (total, acc)
            if unrolled:
                for j in range(i):
                    state = second(j, state)
            else:
                state = lax.fori_loop(0, i, second, state)
            total, acc = state
            acc = acc / total
            ot_ref[i, h] = acc
            o_ref[i, h] = acc.T.astype(BF16)
            ls_ref[i, h] = shift + jnp.log2(total)

        span(0, n, query_block, unrolled)


def attention(x):
    n, hp, _, rows, dim = x.shape
    pairs = n * (n + 1) // 2 * rows * rows * hp
    return pl.pallas_call(
        attention_kernel,
        name="attention",
        out_shape=(
            jax.ShapeDtypeStruct((n, hp, rows, dim), BF16),
            jax.ShapeDtypeStruct((n, hp, dim, rows), F32),
            jax.ShapeDtypeStruct((n, hp, 1, rows), F32),
        ),
        scratch_shapes=[
            pltpu.VMEM((n, dim, rows), BF16),
            pltpu.VMEM((n, rows, rows), F32),
        ],
        compiler_params=pltpu.CompilerParams(vmem_limit_bytes=40 << 20),
        cost_estimate=pl.CostEstimate(
            flops=pairs * dim * 8, bytes_accessed=x.size * 4, transcendentals=pairs
        ),
    )(x)


def attention_back_kernel(
    x_ref, g_ref, ot_ref, ls_ref, cos_ref, sin_ref, out_ref, kt_ref, dqt_ref, delta_ref
):
    n, hp, _, rows, _ = x_ref.shape
    unrolled = n <= 8
    factor = SCORE_SCALE * LOG2E
    for h in range(hp):
        for j in range(n):
            kt_ref[j] = x_ref[j, h, 1].astype(F32).T.astype(BF16)
            delta_ref[j] = jnp.sum(
                g_ref[j, h].astype(F32).T * ot_ref[j, h], axis=0, keepdims=True
            )

        def unrotated(value, i):
            turned = pl.ds(i * rows, rows)
            cos, sin = cos_ref[turned], sin_ref[turned]
            return rotate(value * SCORE_SCALE, cos, -sin).astype(BF16)

        def pair(i, j, diagonal):
            q, g = x_ref[i, h, 0], g_ref[i, h]
            p = jnp.exp2(dot_nt(x_ref[j, h, 1], q) * factor - ls_ref[i, h])
            if diagonal:
                p = causal_fill(p, 0.0)
            dv = dot(p.astype(BF16), g)
            ds = (p * (dot_nt(x_ref[j, h, 2], g) - delta_ref[i])).astype(BF16)
            dk = dot(ds, q)
            dqt = dot(kt_ref[j], ds)
            return dv, dk, dqt

        def key_block(j):
            dv, dk, dqt = pair(j, j, True)
            if unrolled:
                dqt_ref[j] = dqt if j == 0 else dqt_ref[j] + dqt
            else:
                dqt_ref[j] = jnp.where(j == 0, 0.0, dqt_ref[j]) + dqt

            def step(i, state):
                dv, dk = state
                v, k, t = pair(i, j, False)
                if unrolled:
                    dqt_ref[i] = t if j == 0 else dqt_ref[i] + t
                else:
                    dqt_ref[i] = jnp.where(j == 0, 0.0, dqt_ref[i]) + t
                return dv + v, dk + k

            state = (dv, dk)
            if unrolled:
                for i in range(j + 1, n):
                    state = step(i, state)
            else:
                state = lax.fori_loop(j + 1, n, step, state)
            dv, dk = state
            out_ref[j, h, 0] = unrotated(dqt_ref[j].T, j)
            out_ref[j, h, 1] = unrotated(dk, j)
            out_ref[j, h, 2] = dv.astype(BF16)

        span(0, n, key_block, unrolled)


def attention_back(x, g, ot, ls, cos, sin):
    n, hp, _, rows, dim = x.shape
    pairs = n * (n + 1) // 2 * rows * rows * hp
    return pl.pallas_call(
        attention_back_kernel,
        name="attention_back",
        out_shape=jax.ShapeDtypeStruct(x.shape, BF16),
        scratch_shapes=[
            pltpu.VMEM((n, dim, rows), BF16),
            pltpu.VMEM((n, dim, rows), F32),
            pltpu.VMEM((n, 1, rows), F32),
        ],
        compiler_params=pltpu.CompilerParams(vmem_limit_bytes=40 << 20),
        cost_estimate=pl.CostEstimate(
            flops=pairs * dim * 20, bytes_accessed=x.size * 6, transcendentals=pairs
        ),
    )(x, g, ot, ls, cos, sin)


def seq_device(index):
    return {"seq": index}


def greet(peers):
    barrier = pltpu.get_barrier_semaphore()
    for device in peers:
        pl.semaphore_signal(barrier, inc=1, device_id=device, device_id_type=MESH)


def greeted(count):
    pl.semaphore_wait(pltpu.get_barrier_semaphore(), count)


def remote(src, dst, send, recv, device):
    return pltpu.make_async_remote_copy(
        src_ref=src,
        dst_ref=dst,
        send_sem=send,
        recv_sem=recv,
        device_id=device,
        device_id_type=MESH,
    )


def front_kernel(
    state_ref,
    embedded_ref,
    wa_ref,
    wq_ref,
    gain_ref,
    cos_ref,
    sin_ref,
    resid_out,
    normed_out,
    att_out,
    x_out,
    ot_out,
    ls_out,
    wa,
    wq,
    joined,
    resid,
    normed,
    sent,
    x,
    vt,
    scores,
    ot,
    o_sent,
    att,
    load_sem,
    store_sem,
    send_sem,
    recv_sem,
    o_send_sem,
    o_recv_sem,
):
    n, rows, width = HEADS, state_ref.shape[0], state_ref.shape[1]
    me = lax.axis_index("seq")
    peers = [seq_device((me + k) % n) for k in range(1, n)]
    greet(peers)
    loads = [
        pltpu.make_async_copy(state_ref, joined.at[0], load_sem.at[0]),
        pltpu.make_async_copy(wa_ref.at[pl.ds(0, width)], wa.at[0], load_sem.at[1]),
        pltpu.make_async_copy(embedded_ref, joined.at[1], load_sem.at[2]),
        pltpu.make_async_copy(wa_ref.at[pl.ds(width, width)], wa.at[1], load_sem.at[3]),
        pltpu.make_async_copy(wq_ref, wq, load_sem.at[4]),
    ]
    for copy in loads:
        copy.start()
    tile = 256
    for half in range(2):
        loads[2 * half].wait()
        loads[2 * half + 1].wait()

        def adapt(t, c):
            cols = pl.ds(pl.multiple_of(t * tile, tile), tile)
            block = dot(joined[half], wa[half, :, cols])
            resid[:, cols] = block if half == 0 else resid[:, cols] + block
            return c

        lax.fori_loop(0, width // tile, adapt, 0)
    normed[...] = mean_norm(resid[...], gain_ref[0:1, :]).astype(BF16)
    stores = [
        pltpu.make_async_copy(resid, resid_out, store_sem.at[0]),
        pltpu.make_async_copy(normed, normed_out, store_sem.at[1]),
    ]
    for copy in stores:
        copy.start()
    loads[4].wait()
    cos, sin = cos_ref[...], sin_ref[...]
    pairs = n // 2
    order = [2, 1, 3, 0] if pairs == 4 else list(range(pairs - 1, -1, -1))
    sends = []
    for k in order:
        chip = (me // 2 + k) % pairs
        for part in range(3):
            cols = pl.ds(pl.multiple_of(part * width + chip * 2 * HEAD_DIM, 2 * HEAD_DIM), 2 * HEAD_DIM)
            block = dot(normed[...], wq[:, cols])
            for core in range(2):
                head = block[:, core * HEAD_DIM : (core + 1) * HEAD_DIM]
                if part < 2:
                    head = rotate(head, cos, sin)
                sent[2 * chip + core, part] = head.astype(BF16)
        if k == order[0]:
            greeted(n - 1)
        for core in range(2):
            owner = 2 * chip + core
            if k == 0:
                continue
            copy = remote(sent.at[owner], x.at[me], send_sem.at[owner], recv_sem.at[me], seq_device(owner))
            copy.start()
            sends.append(copy)
    mate = me + 1 - 2 * (me % 2)
    copy = remote(sent.at[mate], x.at[me], send_sem.at[mate], recv_sem.at[me], seq_device(mate))
    copy.start()
    sends.append(copy)
    x[me] = sent[me]
    factor = SCORE_SCALE * LOG2E
    for i in range(n):

        @pl.when(me != i)
        def arrive():
            remote(sent.at[0], x.at[i], send_sem.at[0], recv_sem.at[i], seq_device(i)).wait_recv()

        vt[i] = x[i, 2].astype(F32).T.astype(BF16)
        q = x[i, 0]
        diag = causal_fill(dot_nt(x[i, 1], q), NEG)
        peak = jnp.max(diag, axis=0, keepdims=True)
        for j in range(i):
            block = dot_nt(x[j, 1], q)
            scores[j] = block
            peak = jnp.maximum(peak, jnp.max(block, axis=0, keepdims=True))
        shift = peak * factor
        p = jnp.exp2(diag * factor - shift)
        total = jnp.sum(p, axis=0, keepdims=True)
        acc = dot(vt[i], p.astype(BF16))
        for j in range(i):
            p = jnp.exp2(scores[j] * factor - shift)
            total = total + jnp.sum(p, axis=0, keepdims=True)
            acc = acc + dot(vt[j], p.astype(BF16))
        acc = acc / total
        ot[i] = acc
        o_sent[i] = acc.T.astype(BF16)
        ls_out[i] = shift + jnp.log2(total)
        mine = pl.ds(pl.multiple_of(me * HEAD_DIM, HEAD_DIM), HEAD_DIM)

        @pl.when(me != i)
        def give():
            remote(o_sent.at[i], att.at[:, mine], o_send_sem.at[i], o_recv_sem.at[me], seq_device(i)).start()

        @pl.when(me == i)
        def keep():
            att[:, mine] = o_sent[i]

    stores.append(pltpu.make_async_copy(x, x_out, store_sem.at[2]))
    stores.append(pltpu.make_async_copy(ot, ot_out, store_sem.at[3]))
    for copy in stores[2:]:
        copy.start()
    for copy in sends:
        copy.wait_send()
    for i in range(n):

        @pl.when(me != i)
        def finish():
            cols = pl.ds(i * HEAD_DIM, HEAD_DIM)
            copy = remote(o_sent.at[i], att.at[:, cols], o_send_sem.at[i], o_recv_sem.at[i], seq_device(i))
            copy.wait_send()
            copy.wait_recv()

    att_out[...] = att[...]
    for copy in stores:
        copy.wait()


def front(state, embedded, w_adapt, w_qkv, gain_rows, cos, sin):
    n = HEADS
    rows, width = state.shape
    hbm = pl.BlockSpec(memory_space=pl.ANY)
    vmem = pl.BlockSpec(memory_space=pltpu.VMEM)
    return pl.pallas_call(
        front_kernel,
        name="front",
        out_shape=(
            jax.ShapeDtypeStruct((rows, width), F32),
            jax.ShapeDtypeStruct((rows, width), BF16),
            jax.ShapeDtypeStruct((rows, width), BF16),
            jax.ShapeDtypeStruct((n, 3, rows, HEAD_DIM), BF16),
            jax.ShapeDtypeStruct((n, HEAD_DIM, rows), F32),
            jax.ShapeDtypeStruct((n, 1, rows), F32),
        ),
        in_specs=[hbm, hbm, hbm, hbm, vmem, vmem, vmem],
        out_specs=(hbm, hbm, vmem, hbm, hbm, vmem),
        scratch_shapes=[
            pltpu.VMEM((2, width, width), BF16),
            pltpu.VMEM((width, 3 * width), BF16),
            pltpu.VMEM((2, rows, width), BF16),
            pltpu.VMEM((rows, width), F32),
            pltpu.VMEM((rows, width), BF16),
            pltpu.VMEM((n, 3, rows, HEAD_DIM), BF16),
            pltpu.VMEM((n, 3, rows, HEAD_DIM), BF16),
            pltpu.VMEM((n, HEAD_DIM, rows), BF16),
            pltpu.VMEM((n, rows, rows), F32),
            pltpu.VMEM((n, HEAD_DIM, rows), F32),
            pltpu.VMEM((n, rows, HEAD_DIM), BF16),
            pltpu.VMEM((rows, width), BF16),
            pltpu.SemaphoreType.DMA((5,)),
            pltpu.SemaphoreType.DMA((4,)),
            pltpu.SemaphoreType.DMA((n,)),
            pltpu.SemaphoreType.DMA((n,)),
            pltpu.SemaphoreType.DMA((n,)),
            pltpu.SemaphoreType.DMA((n,)),
        ],
        compiler_params=pltpu.CompilerParams(
            collective_id=1, has_side_effects=True, vmem_limit_bytes=48 << 20
        ),
    )(state, embedded, w_adapt, w_qkv, gain_rows, cos, sin)


def xor_permute(value, axis, mask):
    return lax.ppermute(value, axis, [(i, i ^ mask) for i in range(lax.axis_size(axis))])


def quadrants(left):
    n, parts = lax.axis_size("seq"), lax.axis_size("dp")
    tokens, rows = left.shape
    shard = rows // (n * parts)
    split = left.reshape(tokens, n, parts, shard).transpose(2, 0, 1, 3)
    split = split.reshape(parts, tokens, n * shard)
    me = lax.axis_index("dp")
    return jnp.concatenate(
        [lax.dynamic_index_in_dim(split, me ^ m, 0, keepdims=True) for m in range(parts)]
    )


def other_core(left, right):
    core = lax.axis_index("seq") % 2
    half = right.shape[1] // 2
    mine = lax.dynamic_slice_in_dim(right, core * half, half, 1)
    theirs = lax.dynamic_slice_in_dim(right, (1 - core) * half, half, 1)
    left_in = xor_permute(left, "seq", 1)
    right_in = xor_permute(theirs, "seq", 1)
    return jnp.concatenate([left, left_in], axis=1), jnp.concatenate([mine, right_in], axis=0)


def scattered_sum(left, right, bits):
    n, parts = lax.axis_size("seq"), lax.axis_size("dp")
    cols = right.shape[1]
    left, right = other_core(quadrants(left), right)
    got = {}
    masks = list(range(parts))
    for bit in bits:
        outgoing = [m for m in masks if m >> bit & 1]
        masks = [m for m in masks if not m >> bit & 1]
        blocks = []
        for m in outgoing:
            block = dot_tn(left[m], right)
            for more in got.get(m, ()):
                block = block + more.astype(F32)
            blocks.append(block.astype(BF16))
        incoming = xor_permute(jnp.stack(blocks), "dp", 1 << bit)
        for k, m in enumerate(outgoing):
            got.setdefault(m ^ (1 << bit), []).append(incoming[k])
    block = dot_tn(left[0], right)
    for more in got.get(0, ()):
        block = block + more.astype(F32)
    shard = block.shape[0] // n
    block = block.astype(BF16).reshape(n, shard, cols // 2)
    block = lax.all_to_all(block, "seq", 0, 0)
    block = jnp.sum(block.reshape(n // 2, 2, shard, cols // 2).astype(F32), axis=0)
    return block.transpose(1, 0, 2).reshape(shard, cols)


def small_sum(value):
    value = value.reshape(value.shape[0], -1, value.shape[1])
    for axis in ("seq", "dp"):
        size = lax.axis_size(axis)
        me = lax.axis_index(axis)
        for bit in reversed(range(size.bit_length() - 1)):
            half = value.shape[2] // 2
            mine = (me >> bit) & 1
            kept = lax.dynamic_slice_in_dim(value, mine * half, half, 2)
            sent = lax.dynamic_slice_in_dim(value, (1 - mine) * half, half, 2)
            value = kept + xor_permute(sent, axis, 1 << bit)
    return value[:, 0]


def local(state, embedded, cotangent, w_adapt, w_qkv, w_out, w_gate, w_up, w_down, gains):
    seq_count, rows, width = state.shape
    n, parts = lax.axis_size("seq"), lax.axis_size("dp")
    tokens = seq_count * rows
    me = lax.axis_index("seq")
    bits = list(range(parts.bit_length() - 1))
    copies = max(1, n // HEADS)
    held = max(1, HEADS // n)
    owners = n // copies
    cos_np, sin_np = angle_tables(n * rows)
    cos_all, sin_all = jnp.asarray(cos_np), jnp.asarray(sin_np)
    cos = lax.dynamic_slice_in_dim(cos_all, me * rows, rows, 0)[:, None, :]
    sin = lax.dynamic_slice_in_dim(sin_all, me * rows, rows, 0)[:, None, :]
    gain_rows = gains.astype(F32)
    state, embedded = state.reshape(tokens, width), embedded.reshape(tokens, width)

    def to_heads(flat):
        return flat.reshape(tokens, HEADS, HEAD_DIM)

    def to_owner(parts_in):
        sent = jnp.stack(parts_in).reshape(len(parts_in), tokens, owners, held, HEAD_DIM)
        sent = sent.transpose(2, 3, 0, 1, 4)
        if copies > 1:
            sent = jnp.repeat(sent, copies, axis=0)
        return lax.all_to_all(sent, "seq", 0, 0)

    def from_owner(value):
        back = lax.all_to_all(value, "seq", 0, 0)[::copies]
        back = back.reshape(HEADS, -1, tokens, HEAD_DIM)
        return back.transpose(2, 1, 0, 3).reshape(tokens, -1)

    if n == HEADS and seq_count == 1:
        resid, normed, attended, qkv, attended_t, logsum = front(
            state, embedded, w_adapt, w_qkv, gain_rows, cos[:, 0], sin[:, 0]
        )
        qkv, attended_t, logsum = qkv[:, None], attended_t[:, None], logsum[:, None]
    else:
        resid = dot(state, w_adapt[:width]) + dot(embedded, w_adapt[width:])
        normed = mean_norm(resid, gain_rows[0]).astype(BF16)
        packed = dot(normed, w_qkv)
        queries = rotate(to_heads(packed[:, :width]), cos, sin).astype(BF16)
        keys = rotate(to_heads(packed[:, width : 2 * width]), cos, sin).astype(BF16)
        values = to_heads(packed[:, 2 * width :]).astype(BF16)
        qkv = to_owner((queries, keys, values))
        attended, attended_t, logsum = attention(qkv)
        attended = from_owner(attended[:, :, None])
    branch = dot(attended, w_out)
    middle = resid + mean_norm(branch, gain_rows[1])
    normed_mid = mean_norm(middle, gain_rows[2]).astype(BF16)
    gate_pre = dot(normed_mid, w_gate)
    up_pre = dot(normed_mid, w_up)
    sigmoid_gate = jax.nn.sigmoid(gate_pre)
    silu_gate = gate_pre * sigmoid_gate
    hidden = (silu_gate * up_pre).astype(BF16)
    down_out = dot(hidden, w_down)
    layer_out = middle + mean_norm(down_out, gain_rows[3])
    out_grad = cotangent.astype(F32).reshape(tokens, width)
    down_grad, gain_grad3 = norm_back(down_out, gain_rows[3], out_grad)
    down_low = down_grad.astype(BF16)
    hidden_grad = dot_nt(down_low, w_down)
    gate_low = (
        hidden_grad * up_pre * sigmoid_gate * (1.0 + gate_pre * (1.0 - sigmoid_gate))
    ).astype(BF16)
    up_low = (hidden_grad * silu_gate).astype(BF16)
    mid_norm_grad = dot_nt(gate_low, w_gate) + dot_nt(up_low, w_up)
    middle_part, gain_grad2 = norm_back(middle, gain_rows[2], mid_norm_grad)
    middle_grad = out_grad + middle_part
    branch_grad, gain_grad1 = norm_back(branch, gain_rows[1], middle_grad)
    branch_low = branch_grad.astype(BF16)
    attended_grad = dot_nt(branch_low, w_out).astype(BF16)
    upstream = to_owner((to_heads(attended_grad),))[:, :, 0]
    packed_grad = attention_back(qkv, upstream, attended_t, logsum, cos_all, sin_all)
    packed_low = from_owner(packed_grad)
    normed_grad = dot_nt(packed_low, w_qkv)
    resid_part, gain_grad0 = norm_back(resid, gain_rows[0], normed_grad)
    resid_low = (middle_grad + resid_part).astype(BF16)
    grad_state = dot_nt(resid_low, w_adapt[:width])
    grad_embedded = dot_nt(resid_low, w_adapt[width:])
    flipped = bits[::-1]
    joined = jnp.concatenate([state, embedded], axis=-1)
    grad_down = scattered_sum(hidden, down_low, bits)
    grad_gate = scattered_sum(normed_mid, gate_low, flipped)
    grad_up = scattered_sum(normed_mid, up_low, bits)
    grad_out = scattered_sum(attended, branch_low, flipped)
    grad_qkv = scattered_sum(normed, packed_low, flipped)
    grad_adapt = scattered_sum(joined, resid_low, bits)
    grad_gains = jnp.stack([gain_grad0, gain_grad1, gain_grad2, gain_grad3])
    grad_gains = small_sum(grad_gains)
    shape = (seq_count, rows, width)
    return (
        layer_out.reshape(shape).astype(BF16),
        grad_state.reshape(shape),
        grad_embedded.reshape(shape),
        grad_adapt,
        grad_qkv,
        grad_out,
        grad_gate,
        grad_up,
        grad_down,
        grad_gains,
    )


def solution(mesh):
    tokens = P("dp", "seq", None)
    rows = P(("seq", "dp"), None)
    return jax.shard_map(
        local,
        mesh=mesh,
        in_specs=(tokens,) * 3 + (P(),) * 7,
        out_specs=(tokens,) * 3 + (rows,) * 6 + (P(None, ("seq", "dp")),),
        check_vma=False,
    )
```

```python
import functools
import math

import jax
import jax.numpy as jnp
import numpy as np
from jax import lax
from jax.experimental import pallas as pl
from jax.experimental.pallas import tpu as pltpu
from jax.sharding import PartitionSpec as P

HEADS = 8
HEAD_DIM = 128
norm_eps = 1e-06
rope_base = 50000.0
F32 = jnp.float32
BF16 = jnp.bfloat16
MESH = pl.DeviceIdType.MESH
NEG = -1e30
SCORE_SCALE = 1.0 / math.sqrt(HEAD_DIM)
LOG2E = 1.0 / math.log(2.0)


def mean_norm(values_in, gain_row):
    return (
        values_in
        * lax.rsqrt(jnp.mean(values_in * values_in, axis=-1, keepdims=True) + norm_eps)
        * gain_row
    )


def norm_back(values_in, gain_row, upstream):
    inverse = lax.rsqrt(jnp.mean(values_in * values_in, axis=-1, keepdims=True) + norm_eps)
    scaled = upstream * gain_row
    value_grad = inverse * scaled - values_in * (inverse * inverse * inverse) * jnp.mean(
        values_in * scaled, axis=-1, keepdims=True
    )
    gain_grad = jnp.sum(upstream * values_in * inverse, axis=0)
    return (value_grad, gain_grad)


def angle_tables(length):
    half_dim = HEAD_DIM // 2
    freqs = np.exp(
        np.arange(half_dim, dtype=np.float32) * np.float32(-2.0 * math.log(rope_base) / HEAD_DIM)
    ).astype(np.float32)
    angles = np.arange(length, dtype=np.float32)[:, None] * freqs[None, :]
    return np.cos(angles).astype(np.float32), np.sin(angles).astype(np.float32)


def rotate(heads_in, cos_table, sin_table):
    half_dim = heads_in.shape[-1] // 2
    lower_half = heads_in[..., :half_dim]
    upper_half = heads_in[..., half_dim:]
    return jnp.concatenate(
        [
            lower_half * cos_table - upper_half * sin_table,
            upper_half * cos_table + lower_half * sin_table,
        ],
        axis=-1,
    )


def dot(a, b):
    return lax.dot_general(a, b, (((1,), (0,)), ((), ())), preferred_element_type=F32)


def dot_tn(a, b):
    return lax.dot_general(a, b, (((0,), (0,)), ((), ())), preferred_element_type=F32)


def dot_nt(a, b):
    return lax.dot_general(a, b, (((1,), (1,)), ((), ())), preferred_element_type=F32)


def span(low, high, body, unrolled):
    if unrolled:
        for i in range(low, high):
            body(i)
    else:
        lax.fori_loop(low, high, lambda i, c: (body(i), c)[1], 0)


def causal_fill(block, fill):
    kv = lax.broadcasted_iota(jnp.int32, block.shape, 0)
    q = lax.broadcasted_iota(jnp.int32, block.shape, 1)
    return jnp.where(q >= kv, block, fill)


def attention_kernel(x_ref, o_ref, ot_ref, ls_ref, vt_ref, s_ref):
    n, hp, _, rows, _ = x_ref.shape
    unrolled = n <= 8
    factor = SCORE_SCALE * LOG2E
    for h in range(hp):
        for j in range(n):
            vt_ref[j] = x_ref[j, h, 2].astype(F32).T.astype(BF16)

        def query_block(i):
            q = x_ref[i, h, 0]
            diag = causal_fill(dot_nt(x_ref[i, h, 1], q), NEG)

            def first(j, peak):
                s = dot_nt(x_ref[j, h, 1], q)
                s_ref[j] = s
                return jnp.maximum(peak, jnp.max(s, axis=0, keepdims=True))

            peak = jnp.max(diag, axis=0, keepdims=True)
            if unrolled:
                for j in range(i):
                    peak = first(j, peak)
            else:
                peak = lax.fori_loop(0, i, first, peak)
            shift = peak * factor
            p = jnp.exp2(diag * factor - shift)
            total = jnp.sum(p, axis=0, keepdims=True)
            acc = dot(vt_ref[i], p.astype(BF16))

            def second(j, state):
                total, acc = state
                p = jnp.exp2(s_ref[j] * factor - shift)
                return (
                    total + jnp.sum(p, axis=0, keepdims=True),
                    acc + dot(vt_ref[j], p.astype(BF16)),
                )

            state = (total, acc)
            if unrolled:
                for j in range(i):
                    state = second(j, state)
            else:
                state = lax.fori_loop(0, i, second, state)
            total, acc = state
            acc = acc / total
            ot_ref[i, h] = acc
            o_ref[i, h] = acc.T.astype(BF16)
            ls_ref[i, h] = shift + jnp.log2(total)

        span(0, n, query_block, unrolled)


def attention(x):
    n, hp, _, rows, dim = x.shape
    pairs = n * (n + 1) // 2 * rows * rows * hp
    return pl.pallas_call(
        attention_kernel,
        name="attention",
        out_shape=(
            jax.ShapeDtypeStruct((n, hp, rows, dim), BF16),
            jax.ShapeDtypeStruct((n, hp, dim, rows), F32),
            jax.ShapeDtypeStruct((n, hp, 1, rows), F32),
        ),
        scratch_shapes=[
            pltpu.VMEM((n, dim, rows), BF16),
            pltpu.VMEM((n, rows, rows), F32),
        ],
        compiler_params=pltpu.CompilerParams(vmem_limit_bytes=40 << 20),
        cost_estimate=pl.CostEstimate(
            flops=pairs * dim * 8, bytes_accessed=x.size * 4, transcendentals=pairs
        ),
    )(x)


def attention_back_kernel(
    x_ref, g_ref, ot_ref, ls_ref, cos_ref, sin_ref, out_ref, kt_ref, dqt_ref, delta_ref
):
    n, hp, _, rows, _ = x_ref.shape
    unrolled = n <= 8
    factor = SCORE_SCALE * LOG2E
    for h in range(hp):
        for j in range(n):
            kt_ref[j] = x_ref[j, h, 1].astype(F32).T.astype(BF16)
            delta_ref[j] = jnp.sum(
                g_ref[j, h].astype(F32).T * ot_ref[j, h], axis=0, keepdims=True
            )

        def unrotated(value, i):
            turned = pl.ds(i * rows, rows)
            cos, sin = cos_ref[turned], sin_ref[turned]
            return rotate(value * SCORE_SCALE, cos, -sin).astype(BF16)

        def pair(i, j, diagonal):
            q, g = x_ref[i, h, 0], g_ref[i, h]
            p = jnp.exp2(dot_nt(x_ref[j, h, 1], q) * factor - ls_ref[i, h])
            if diagonal:
                p = causal_fill(p, 0.0)
            dv = dot(p.astype(BF16), g)
            ds = (p * (dot_nt(x_ref[j, h, 2], g) - delta_ref[i])).astype(BF16)
            dk = dot(ds, q)
            dqt = dot(kt_ref[j], ds)
            return dv, dk, dqt

        def key_block(j):
            dv, dk, dqt = pair(j, j, True)
            if unrolled:
                dqt_ref[j] = dqt if j == 0 else dqt_ref[j] + dqt
            else:
                dqt_ref[j] = jnp.where(j == 0, 0.0, dqt_ref[j]) + dqt

            def step(i, state):
                dv, dk = state
                v, k, t = pair(i, j, False)
                if unrolled:
                    dqt_ref[i] = t if j == 0 else dqt_ref[i] + t
                else:
                    dqt_ref[i] = jnp.where(j == 0, 0.0, dqt_ref[i]) + t
                return dv + v, dk + k

            state = (dv, dk)
            if unrolled:
                for i in range(j + 1, n):
                    state = step(i, state)
            else:
                state = lax.fori_loop(j + 1, n, step, state)
            dv, dk = state
            out_ref[j, h, 0] = unrotated(dqt_ref[j].T, j)
            out_ref[j, h, 1] = unrotated(dk, j)
            out_ref[j, h, 2] = dv.astype(BF16)

        span(0, n, key_block, unrolled)


def attention_back(x, g, ot, ls, cos, sin):
    n, hp, _, rows, dim = x.shape
    pairs = n * (n + 1) // 2 * rows * rows * hp
    return pl.pallas_call(
        attention_back_kernel,
        name="attention_back",
        out_shape=jax.ShapeDtypeStruct(x.shape, BF16),
        scratch_shapes=[
            pltpu.VMEM((n, dim, rows), BF16),
            pltpu.VMEM((n, dim, rows), F32),
            pltpu.VMEM((n, 1, rows), F32),
        ],
        compiler_params=pltpu.CompilerParams(vmem_limit_bytes=40 << 20),
        cost_estimate=pl.CostEstimate(
            flops=pairs * dim * 20, bytes_accessed=x.size * 6, transcendentals=pairs
        ),
    )(x, g, ot, ls, cos, sin)


def seq_device(index):
    return {"seq": index}


def greet(peers):
    barrier = pltpu.get_barrier_semaphore()
    for device in peers:
        pl.semaphore_signal(barrier, inc=1, device_id=device, device_id_type=MESH)


def greeted(count):
    pl.semaphore_wait(pltpu.get_barrier_semaphore(), count)


def remote(src, dst, send, recv, device):
    return pltpu.make_async_remote_copy(
        src_ref=src,
        dst_ref=dst,
        send_sem=send,
        recv_sem=recv,
        device_id=device,
        device_id_type=MESH,
    )


def front_kernel(
    state_ref,
    embedded_ref,
    wa_ref,
    wq_ref,
    gain_ref,
    cos_ref,
    sin_ref,
    resid_out,
    normed_out,
    att_out,
    x_out,
    ot_out,
    ls_out,
    wa,
    wq,
    joined,
    resid,
    normed,
    sent,
    x,
    vt,
    scores,
    ot,
    o_sent,
    att,
    load_sem,
    store_sem,
    send_sem,
    recv_sem,
    o_send_sem,
    o_recv_sem,
):
    n, rows, width = HEADS, state_ref.shape[0], state_ref.shape[1]
    me = lax.axis_index("seq")
    peers = [seq_device((me + k) % n) for k in range(1, n)]
    greet(peers)
    loads = [
        pltpu.make_async_copy(state_ref, joined.at[0], load_sem.at[0]),
        pltpu.make_async_copy(wa_ref.at[pl.ds(0, width)], wa.at[0], load_sem.at[1]),
        pltpu.make_async_copy(embedded_ref, joined.at[1], load_sem.at[2]),
        pltpu.make_async_copy(wa_ref.at[pl.ds(width, width)], wa.at[1], load_sem.at[3]),
        pltpu.make_async_copy(wq_ref, wq, load_sem.at[4]),
    ]
    for copy in loads:
        copy.start()
    tile = 256
    for half in range(2):
        loads[2 * half].wait()
        loads[2 * half + 1].wait()

        def adapt(t, c):
            cols = pl.ds(pl.multiple_of(t * tile, tile), tile)
            block = dot(joined[half], wa[half, :, cols])
            resid[:, cols] = block if half == 0 else resid[:, cols] + block
            return c

        lax.fori_loop(0, width // tile, adapt, 0)
    normed[...] = mean_norm(resid[...], gain_ref[0:1, :]).astype(BF16)
    stores = [
        pltpu.make_async_copy(resid, resid_out, store_sem.at[0]),
        pltpu.make_async_copy(normed, normed_out, store_sem.at[1]),
    ]
    for copy in stores:
        copy.start()
    loads[4].wait()
    cos, sin = cos_ref[...], sin_ref[...]
    pairs = n // 2
    order = [2, 1, 3, 0] if pairs == 4 else list(range(pairs - 1, -1, -1))
    sends = []
    for k in order:
        chip = (me // 2 + k) % pairs
        for part in range(3):
            cols = pl.ds(pl.multiple_of(part * width + chip * 2 * HEAD_DIM, 2 * HEAD_DIM), 2 * HEAD_DIM)
            block = dot(normed[...], wq[:, cols])
            for core in range(2):
                head = block[:, core * HEAD_DIM : (core + 1) * HEAD_DIM]
                if part < 2:
                    head = rotate(head, cos, sin)
                sent[2 * chip + core, part] = head.astype(BF16)
        if k == order[0]:
            greeted(n - 1)
        for core in range(2):
            owner = 2 * chip + core
            if k == 0:
                continue
            copy = remote(sent.at[owner], x.at[me], send_sem.at[owner], recv_sem.at[me], seq_device(owner))
            copy.start()
            sends.append(copy)
    mate = me + 1 - 2 * (me % 2)
    copy = remote(sent.at[mate], x.at[me], send_sem.at[mate], recv_sem.at[me], seq_device(mate))
    copy.start()
    sends.append(copy)
    x[me] = sent[me]
    factor = SCORE_SCALE * LOG2E
    for i in range(n):

        @pl.when(me != i)
        def arrive():
            remote(sent.at[0], x.at[i], send_sem.at[0], recv_sem.at[i], seq_device(i)).wait_recv()

        vt[i] = x[i, 2].astype(F32).T.astype(BF16)
        q = x[i, 0]
        diag = causal_fill(dot_nt(x[i, 1], q), NEG)
        peak = jnp.max(diag, axis=0, keepdims=True)
        for j in range(i):
            block = dot_nt(x[j, 1], q)
            scores[j] = block
            peak = jnp.maximum(peak, jnp.max(block, axis=0, keepdims=True))
        shift = peak * factor
        p = jnp.exp2(diag * factor - shift)
        total = jnp.sum(p, axis=0, keepdims=True)
        acc = dot(vt[i], p.astype(BF16))
        for j in range(i):
            p = jnp.exp2(scores[j] * factor - shift)
            total = total + jnp.sum(p, axis=0, keepdims=True)
            acc = acc + dot(vt[j], p.astype(BF16))
        acc = acc / total
        ot[i] = acc
        o_sent[i] = acc.T.astype(BF16)
        ls_out[i] = shift + jnp.log2(total)
        mine = pl.ds(pl.multiple_of(me * HEAD_DIM, HEAD_DIM), HEAD_DIM)

        @pl.when(me != i)
        def give():
            remote(o_sent.at[i], att.at[:, mine], o_send_sem.at[i], o_recv_sem.at[me], seq_device(i)).start()

        @pl.when(me == i)
        def keep():
            att[:, mine] = o_sent[i]

    stores.append(pltpu.make_async_copy(x, x_out, store_sem.at[2]))
    stores.append(pltpu.make_async_copy(ot, ot_out, store_sem.at[3]))
    for copy in stores[2:]:
        copy.start()
    for copy in sends:
        copy.wait_send()
    for i in range(n):

        @pl.when(me != i)
        def finish():
            cols = pl.ds(i * HEAD_DIM, HEAD_DIM)
            copy = remote(o_sent.at[i], att.at[:, cols], o_send_sem.at[i], o_recv_sem.at[i], seq_device(i))
            copy.wait_send()
            copy.wait_recv()

    att_out[...] = att[...]
    for copy in stores:
        copy.wait()


def front(state, embedded, w_adapt, w_qkv, gain_rows, cos, sin):
    n = HEADS
    rows, width = state.shape
    hbm = pl.BlockSpec(memory_space=pl.ANY)
    vmem = pl.BlockSpec(memory_space=pltpu.VMEM)
    return pl.pallas_call(
        front_kernel,
        name="front",
        out_shape=(
            jax.ShapeDtypeStruct((rows, width), F32),
            jax.ShapeDtypeStruct((rows, width), BF16),
            jax.ShapeDtypeStruct((rows, width), BF16),
            jax.ShapeDtypeStruct((n, 3, rows, HEAD_DIM), BF16),
            jax.ShapeDtypeStruct((n, HEAD_DIM, rows), F32),
            jax.ShapeDtypeStruct((n, 1, rows), F32),
        ),
        in_specs=[hbm, hbm, hbm, hbm, vmem, vmem, vmem],
        out_specs=(hbm, hbm, vmem, hbm, hbm, vmem),
        scratch_shapes=[
            pltpu.VMEM((2, width, width), BF16),
            pltpu.VMEM((width, 3 * width), BF16),
            pltpu.VMEM((2, rows, width), BF16),
            pltpu.VMEM((rows, width), F32),
            pltpu.VMEM((rows, width), BF16),
            pltpu.VMEM((n, 3, rows, HEAD_DIM), BF16),
            pltpu.VMEM((n, 3, rows, HEAD_DIM), BF16),
            pltpu.VMEM((n, HEAD_DIM, rows), BF16),
            pltpu.VMEM((n, rows, rows), F32),
            pltpu.VMEM((n, HEAD_DIM, rows), F32),
            pltpu.VMEM((n, rows, HEAD_DIM), BF16),
            pltpu.VMEM((rows, width), BF16),
            pltpu.SemaphoreType.DMA((5,)),
            pltpu.SemaphoreType.DMA((4,)),
            pltpu.SemaphoreType.DMA((n,)),
            pltpu.SemaphoreType.DMA((n,)),
            pltpu.SemaphoreType.DMA((n,)),
            pltpu.SemaphoreType.DMA((n,)),
        ],
        compiler_params=pltpu.CompilerParams(
            collective_id=1, has_side_effects=True, vmem_limit_bytes=48 << 20
        ),
    )(state, embedded, w_adapt, w_qkv, gain_rows, cos, sin)


def flipped(bit, value):
    return value + (1 - 2 * ((value // (1 << bit)) % 2)) * (1 << bit)


UNITS = (
    ("down", 0, 0, 0, 512, 0),
    ("gate", 1, 1, 0, 1408, 1),
    ("up_a", 1, 2, 0, 512, 0),
    ("up_b", 1, 2, 512, 896, 1),
    ("out", 2, 3, 0, 512, 0),
)


def unit_slots(first, dp):
    slots = []
    for q in range(4):
        turned = [(dp + q) % 2, (dp // 2 + q // 2) % 2]
        slots.append(turned[first] * 2 + turned[1 - first])
    return slots


def transposed_into(source, target):
    tile = 256

    def step(t, c):
        at = pl.multiple_of(t * tile, tile)
        target[pl.ds(at, tile), :] = source[:, pl.ds(at, tile)].T
        return c

    lax.fori_loop(0, source.shape[1] // tile, step, 0)


def weight_blocks(left, right, column, width, slots, out, work):
    total = left.shape[1]
    shard = total // 32
    for begin in range(0, width, 256):
        wide = min(256, width - begin)
        cols = pl.ds(column + begin, wide)
        work[0:total, 0:wide] = dot(left[0], right[0, :, cols]) + dot(left[1], right[1, :, cols])
        for z in range(4):
            for q in range(4):
                pieces = [
                    work[pl.ds((8 * z + 4 * core + q) * shard, shard), 0:wide] for core in range(2)
                ]
                out[slots[q], pl.ds(2 * z * shard, 2 * shard), pl.ds(begin, wide)] = (
                    jnp.concatenate(pieces, axis=0).astype(BF16)
                )


def add_into(target, more):
    rows = target.shape[0]
    chunk = 16
    while rows % (chunk * 2) == 0 and chunk < 64:
        chunk *= 2

    def step(t, c):
        at = pl.ds(pl.multiple_of(t * chunk, chunk), chunk)
        target[at, :] = (target[at, :].astype(F32) + more[at, :].astype(F32)).astype(BF16)
        return c

    lax.fori_loop(0, rows // chunk, step, 0)


def back_kernel(*refs):
    refs = list(refs)

    def take(count):
        taken, refs[:count] = refs[:count], []
        return taken

    lefts_in, rights_in = take(3), take(4)
    (dout_ref, x_ref, ot_ref, ls_ref, cos_ref, sin_ref) = take(6)
    (packed_out,) = take(1)
    kept_out = take(5)
    held, turned, halves = take(3), take(3), take(4)
    sums, arrived = take(5), take(5)
    (work, g, kt, dqt, delta, dsent, packed) = take(7)
    (load_sem, store_sem, g_send, g_recv, d_send, d_recv, m_send, m_recv, s_send, s_recv) = take(10)
    n, rows = HEADS, dout_ref.shape[0]
    me = lax.axis_index("seq")
    dp = lax.axis_index("dp")
    core = me % 2
    mate = flipped(0, me)
    across = [{"dp": flipped(0, dp)}, {"dp": flipped(1, dp)}]
    greet([seq_device((me + k) % n) for k in range(1, n)] + across)
    loads = []
    for k in range(3):
        loads.append(pltpu.make_async_copy(lefts_in[k], held[k], load_sem.at[k]))
    for k in range(4):
        half = halves[k].shape[2]
        mine = pl.ds(pl.multiple_of(core * half, 128), half)
        loads.append(
            pltpu.make_async_copy(rights_in[k].at[:, mine], halves[k].at[0], load_sem.at[3 + k])
        )
    for copy in loads:
        copy.start()
    greeted(n + 1)
    sends = []
    my_cols = pl.ds(pl.multiple_of(me * HEAD_DIM, HEAD_DIM), HEAD_DIM)
    for k in (4, 5, 3, 2, 6, 7, 1):
        owner = (me + k) % n
        cols = pl.ds(pl.multiple_of(owner * HEAD_DIM, HEAD_DIM), HEAD_DIM)
        copy = remote(dout_ref.at[:, cols], g.at[me], g_send.at[owner], g_recv.at[me], seq_device(owner))
        copy.start()
        sends.append(copy)
    own = pltpu.make_async_copy(dout_ref.at[:, my_cols], g.at[me], load_sem.at[7])
    own.start()
    mates = {}

    def to_mate(key, slot, src, dst):
        copy = remote(src, dst, m_send.at[slot], m_recv.at[slot], seq_device(mate))
        copy.start()
        sends.append(copy)
        mates[key] = copy

    for k in range(4):
        half = halves[k].shape[2]
        theirs = pl.ds(pl.multiple_of((1 - core) * half, 128), half)
        to_mate(("right", k), 3 + k, rights_in[k].at[:, theirs], halves[k].at[1])
    for k in range(3):
        loads[k].wait()
        transposed_into(held[k], turned[k].at[0])
        to_mate(("left", k), k, turned[k].at[0], turned[k].at[1])
    loaded = set()
    steps = []
    for u, (name, left, right, column, width, first) in enumerate(UNITS):
        if ("left", left) not in loaded:
            loaded.add(("left", left))
            mates[("left", left)].wait_recv()
        if ("right", right) not in loaded:
            loaded.add(("right", right))
            loads[3 + right].wait()
            mates[("right", right)].wait_recv()
        weight_blocks(
            turned[left], halves[right], column, width, unit_slots(first, dp), sums[u], work
        )
        pair = []
        for k in range(2):
            copy = remote(
                sums[u].at[2 + k],
                arrived[u].at[k],
                s_send.at[2 * u + k],
                s_recv.at[2 * u + k],
                across[first],
            )
            copy.start()
            sends.append(copy)
            pair.append(copy)
        steps.append(pair)
    own.wait()
    for i in range(n):

        @pl.when(me != i)
        def arrive():
            remote(g.at[0], g.at[i], g_send.at[0], g_recv.at[i], seq_device(i)).wait_recv()

    factor = SCORE_SCALE * LOG2E
    for j in range(n):
        kt[j] = x_ref[j, 1].astype(F32).T.astype(BF16)
        delta[j] = jnp.sum(g[j].astype(F32).T * ot_ref[j], axis=0, keepdims=True)
    for j in range(n):
        dk = dv = None
        for i in range(j, n):
            q, up = x_ref[i, 0], g[i]
            p = jnp.exp2(dot_nt(x_ref[j, 1], q) * factor - ls_ref[i])
            if i == j:
                p = causal_fill(p, 0.0)
            v = dot(p.astype(BF16), up)
            ds = (p * (dot_nt(x_ref[j, 2], up) - delta[i])).astype(BF16)
            k = dot(ds, q)
            t = dot(kt[j], ds)
            dqt[i] = t if j == 0 else dqt[i] + t
            dv, dk = (v, k) if i == j else (dv + v, dk + k)
        here = pl.ds(j * rows, rows)
        cos, sin = cos_ref[here], -sin_ref[here]
        dsent[j, 0] = rotate(dqt[j].T * SCORE_SCALE, cos, sin).astype(BF16)
        dsent[j, 1] = rotate(dk * SCORE_SCALE, cos, sin).astype(BF16)
        dsent[j, 2] = dv.astype(BF16)

        @pl.when(me != j)
        def give():
            remote(dsent.at[j], packed.at[:, :, my_cols], d_send.at[j], d_recv.at[me], seq_device(j)).start()

        @pl.when(me == j)
        def keep():
            packed[:, :, my_cols] = dsent[j]

    stores = []
    for u, pair in enumerate(steps):
        for k in range(2):
            pair[k].wait_recv()
            add_into(sums[u].at[k], arrived[u].at[k])
        copy = pltpu.make_async_copy(sums[u].at[pl.ds(0, 2)], kept_out[u], store_sem.at[u])
        copy.start()
        stores.append(copy)
    for j in range(n):

        @pl.when(me != j)
        def finish():
            cols = pl.ds(j * HEAD_DIM, HEAD_DIM)
            copy = remote(dsent.at[j], packed.at[:, :, cols], d_send.at[j], d_recv.at[j], seq_device(j))
            copy.wait_send()
            copy.wait_recv()

    last = pltpu.make_async_copy(packed, packed_out, store_sem.at[5])
    last.start()
    for copy in sends:
        copy.wait_send()
    for copy in stores:
        copy.wait()
    last.wait()


def back(lefts, rights, dout, x, ot, ls, cos, sin):
    n = HEADS
    rows, width = dout.shape
    hbm = pl.BlockSpec(memory_space=pl.ANY)
    vmem = pl.BlockSpec(memory_space=pltpu.VMEM)
    heights = [lefts[unit[1]].shape[1] // 4 for unit in UNITS]
    kept = [(2, height, unit[4]) for height, unit in zip(heights, UNITS)]
    dma = pltpu.SemaphoreType.DMA
    return pl.pallas_call(
        back_kernel,
        name="back",
        out_shape=[jax.ShapeDtypeStruct((3, rows, width), BF16)]
        + [jax.ShapeDtypeStruct(shape, BF16) for shape in kept],
        in_specs=[hbm] * 8 + [vmem] * 5,
        out_specs=[hbm] * 6,
        scratch_shapes=[pltpu.VMEM(left.shape, BF16) for left in lefts]
        + [pltpu.VMEM((2, left.shape[1], rows), BF16) for left in lefts]
        + [pltpu.VMEM((2, rows, right.shape[1] // 2), BF16) for right in rights]
        + [pltpu.VMEM((4,) + shape[1:], BF16) for shape in kept]
        + [pltpu.VMEM(shape, BF16) for shape in kept]
        + [
            pltpu.VMEM((max(left.shape[1] for left in lefts), 256), F32),
            pltpu.VMEM((n, rows, HEAD_DIM), BF16),
            pltpu.VMEM((n, HEAD_DIM, rows), BF16),
            pltpu.VMEM((n, HEAD_DIM, rows), F32),
            pltpu.VMEM((n, 1, rows), F32),
            pltpu.VMEM((n, 3, rows, HEAD_DIM), BF16),
            pltpu.VMEM((3, rows, width), BF16),
            dma((8,)),
            dma((6,)),
            dma((n,)),
            dma((n,)),
            dma((n,)),
            dma((n,)),
            dma((7,)),
            dma((7,)),
            dma((10,)),
            dma((10,)),
        ],
        compiler_params=pltpu.CompilerParams(
            collective_id=2, has_side_effects=True, vmem_limit_bytes=56 << 20
        ),
    )(*lefts, *rights, dout, x, ot, ls, cos, sin)


TAIL = (
    ("down", 5, 0, 512, 512, 0, 0, True),
    ("gate", 3, 0, 1408, 1408, 0, 1, True),
    ("up_a", 4, 0, 512, 1408, 0, 0, True),
    ("up_b", 4, 512, 896, 1408, 0, 1, True),
    ("out", 2, 0, 512, 512, 0, 0, True),
    ("query", 1, 0, 512, 512, 0, 0, False),
    ("key", 1, 0, 512, 512, 1024, 0, False),
    ("value", 1, 0, 512, 512, 2048, 1, False),
    ("adapt_a", 0, 0, 256, 512, 0, 0, False),
    ("adapt_b", 0, 256, 256, 512, 0, 1, False),
)


def tail_kernel(*refs):
    refs = list(refs)

    def take(count):
        taken, refs[:count] = refs[:count], []
        return taken

    count = len(TAIL)
    begun = 5
    kept_in = take(begun)
    packed_in, normed_in, state_in, embedded_in, wq_in, wa_in = take(6)
    resid, above, gain_rows, gain_parts = take(4)
    grad_joined = take(2)
    outs = take(6)
    (gains_out,) = take(1)
    sums = take(count)
    arrived1 = take(count - begun)
    arrived2, planes, arrived3, arrived4, finals = (
        take(count),
        take(count),
        take(count),
        take(count),
        take(count),
    )
    (wq, wa, packed, held, turned_n, turned_j, halves, low, work, gain_buf, gain_got) = take(11)
    (load_sem, m_send, m_recv, s1_send, s1_recv, s2_send, s2_recv, z1_send, z1_recv) = take(9)
    (z2_send, z2_recv, c_send, c_recv, gain_send, gain_recv) = take(6)
    rows, width = resid.shape
    me = lax.axis_index("seq")
    dp = lax.axis_index("dp")
    core = me % 2
    z_low, z_high = (me // 2) % 2, me // 4
    mate = seq_device(flipped(0, me))
    across = [{"dp": flipped(0, dp)}, {"dp": flipped(1, dp)}]
    beside = [seq_device(flipped(1, me)), seq_device(flipped(2, me))]
    partners = [mate] + across + beside
    greet(partners)
    loads = {}

    def load(key, slot, src, dst):
        loads[key] = pltpu.make_async_copy(src, dst, load_sem.at[slot])
        loads[key].start()

    load("packed", 0, packed_in, packed)
    load("normed", 1, normed_in, held.at[0])
    load("wq", 2, wq_in, wq)
    load("state", 3, state_in, held.at[1])
    load("embedded", 4, embedded_in, held.at[2])
    for u in range(begun):
        load(u, 5 + u, kept_in[u].at[0], sums[u].at[0])
    load("wa", 10, wa_in, wa)
    greeted(len(partners))
    sends = []

    def send(src, dst, send_sem, recv_sem, device):
        copy = remote(src, dst, send_sem, recv_sem, device)
        copy.start()
        sends.append(copy)
        return copy

    second, first, third, fourth, cores = {}, {}, {}, {}, {}

    def send_second(u, src):
        bit = 1 - TAIL[u][6]
        second[u] = send(src, arrived2[u], s2_send.at[u], s2_recv.at[u], across[bit])

    for u in (4, 3, 2, 1, 0):
        send_second(u, kept_in[u].at[1])
    lefts = {}
    loads["packed"].wait()
    theirs = pl.ds(pl.multiple_of((1 - core) * 512, 512), 512)
    mine = pl.ds(pl.multiple_of(core * 512, 512), 512)
    for p in range(3):
        lefts["right", p] = send(
            packed.at[p, :, theirs], halves.at[p, 1], m_send.at[p], m_recv.at[p], mate
        )
    loads["normed"].wait()
    transposed_into(held.at[0], turned_n.at[0])
    lefts["normed"] = send(turned_n.at[0], turned_n.at[1], m_send.at[3], m_recv.at[3], mate)
    for p in range(3):
        halves[p, 0] = packed[p, :, mine]
    loads["wq"].wait()
    tile = 256

    def back_tile(t, c):
        at = pl.ds(pl.multiple_of(t * tile, tile), tile)
        block = dot_nt(packed[0], wq[at, pl.ds(0, width)])
        block += dot_nt(packed[1], wq[at, pl.ds(width, width)])
        block += dot_nt(packed[2], wq[at, pl.ds(2 * width, width)])
        work[0:rows, at] = block
        return c

    lax.fori_loop(0, width // tile, back_tile, 0)
    part, gain0 = norm_back(resid[...], gain_rows[0:1, :], work[0:rows, 0:width])
    low[...] = (above[...] + part).astype(BF16)
    gain_buf[0] = gain_parts[...]
    gain_buf[0, 0:1, :] = gain0[None, :]
    lefts["right", 3] = send(low.at[:, theirs], halves.at[3, 1], m_send.at[4], m_recv.at[4], mate)
    halves[3, 0] = low[:, mine]

    gain_steps = {}

    def send_gain(k):
        gain_steps[k] = send(
            gain_buf.at[k], gain_got.at[k], gain_send.at[k], gain_recv.at[k], partners[k]
        )

    def add_gain(k):
        gain_steps[k].wait_recv()
        total = gain_buf[k] + gain_got[k]
        if k == 4:
            gains_out[...] = total
        else:
            gain_buf[k + 1] = total
            send_gain(k + 1)

    send_gain(0)

    def send_first(u, left, p):
        name, out, column, wide, half, base, bit, _ = TAIL[u]
        weight_blocks(left, halves.at[p], column, wide, unit_slots(bit, dp), sums[u], work)
        first[u] = [
            send(
                sums[u].at[2 + k],
                arrived1[u - begun].at[k],
                s1_send.at[2 * (u - begun) + k],
                s1_recv.at[2 * (u - begun) + k],
                across[bit],
            )
            for k in (1, 0)
        ][::-1]

    lefts["normed"].wait_recv()
    for p in (2, 1, 0):
        lefts["right", p].wait_recv()
        send_first(5 + p, turned_n, p)
    loads["state"].wait()
    transposed_into(held.at[1], turned_j.at[0, pl.ds(0, width)])
    loads["embedded"].wait()
    transposed_into(held.at[2], turned_j.at[0, pl.ds(width, width)])
    lefts["joined"] = send(turned_j.at[0], turned_j.at[1], m_send.at[5], m_recv.at[5], mate)
    add_gain(0)
    loads["wa"].wait()

    def out_tile(t, c):
        at = pl.ds(pl.multiple_of(t * tile, tile), tile)
        for k in range(2):
            from_row = pl.ds(pl.multiple_of(k * width + t * tile, tile), tile)
            grad_joined[k][:, at] = dot_nt(low[...], wa[from_row, :])
        return c

    lefts["right", 3].wait_recv()
    lefts["joined"].wait_recv()
    send_first(9, turned_j, 3)
    send_first(8, turned_j, 3)
    add_gain(1)
    lax.fori_loop(0, width // tile, out_tile, 0)

    def phase_b(u):
        for k in (1, 0):
            first[u][k].wait_recv()
            add_into(sums[u].at[k], arrived1[u - begun].at[k])
            if k == 1:
                send_second(u, sums[u].at[1])

    def phase_c(u):
        second[u].wait_recv()
        if u < begun:
            loads[u].wait()
        tall = planes[u].shape[2]
        for z in range(4):
            at = pl.ds(z * tall, tall)
            planes[u][z % 2, z // 2] = (
                sums[u][0, at, :].astype(F32) + arrived2[u][at, :].astype(F32)
            ).astype(BF16)
        third[u] = send(
            planes[u].at[1 - z_low], arrived3[u], z1_send.at[u], z1_recv.at[u], beside[0]
        )

    def phase_d(u):
        third[u].wait_recv()
        for k in range(2):
            planes[u][z_low, k] = (
                planes[u][z_low, k].astype(F32) + arrived3[u][k].astype(F32)
            ).astype(BF16)
        fourth[u] = send(
            planes[u].at[z_low, 1 - z_high], arrived4[u], z2_send.at[u], z2_recv.at[u], beside[1]
        )

    def phase_e(u):
        name, out, column, wide, half, base, bit, _ = TAIL[u]
        fourth[u].wait_recv()
        shard = planes[u].shape[2] // 2
        finals[u][...] = planes[u][z_low, z_high].astype(F32) + arrived4[u][...].astype(F32)
        cols = pl.ds(pl.multiple_of(base + core * half + column, 128), wide)
        cores[u] = send(
            finals[u].at[pl.ds(pl.multiple_of((1 - core) * shard, 8), shard)],
            outs[out].at[:, cols],
            c_send.at[u],
            c_recv.at[u],
            mate,
        )
        outs[out][:, cols] = finals[u][pl.ds(pl.multiple_of(core * shard, 8), shard), :]

    def phase_f(u):
        cores[u].wait_recv()

    todo = (
        ("C", 4), ("C", 3), ("C", 2), ("D", 4), ("G", 2), ("D", 3), ("C", 1),
        ("D", 2), ("C", 0), ("E", 4), ("E", 3), ("E", 2), ("G", 3), ("D", 1),
        ("D", 0), ("B", 7), ("B", 6), ("B", 5), ("E", 1), ("E", 0), ("G", 4),
        ("B", 9), ("B", 8), ("C", 7), ("C", 6), ("C", 5), ("D", 7), ("D", 6),
        ("C", 9), ("D", 5), ("E", 7), ("C", 8), ("E", 6), ("D", 9), ("E", 5),
        ("D", 8), ("E", 9), ("E", 8),
    )
    phases = {"B": phase_b, "C": phase_c, "D": phase_d, "E": phase_e, "G": add_gain}
    for phase, u in todo:
        phases[phase](u)
    for u in range(count):
        phase_f(u)
    for copy in sends:
        copy.wait_send()


def tail(kept, packed, normed, state, embedded, w_qkv, w_adapt, resid, above, gain_rows, gain_parts):
    rows, width = normed.shape
    hbm = pl.BlockSpec(memory_space=pl.ANY)
    vmem = pl.BlockSpec(memory_space=pltpu.VMEM)
    dma = pltpu.SemaphoreType.DMA
    count, begun = len(TAIL), len(kept)
    heights = [value.shape[1] for value in kept] + [width // 4] * 3 + [width // 2] * 2
    wides = [unit[3] for unit in TAIL]
    ff = 2 * kept[1].shape[2]
    shapes = [
        (2 * width // 32, width),
        (width // 32, 3 * width),
        (width // 32, width),
        (width // 32, ff),
        (width // 32, ff),
        (ff // 32, width),
    ]
    scratch = [
        pltpu.VMEM((1 if u < begun else 4, heights[u], wides[u]), BF16) for u in range(count)
    ]
    scratch += [pltpu.VMEM((2, heights[u], wides[u]), BF16) for u in range(begun, count)]
    scratch += [pltpu.VMEM((heights[u], wides[u]), BF16) for u in range(count)]
    scratch += [pltpu.VMEM((2, 2, heights[u] // 4, wides[u]), BF16) for u in range(count)]
    scratch += [pltpu.VMEM((2, heights[u] // 4, wides[u]), BF16) for u in range(count)]
    scratch += [pltpu.VMEM((heights[u] // 4, wides[u]), BF16) for u in range(count)]
    scratch += [pltpu.VMEM((heights[u] // 4, wides[u]), F32) for u in range(count)]
    scratch += [
        pltpu.VMEM(w_qkv.shape, BF16),
        pltpu.VMEM(w_adapt.shape, BF16),
        pltpu.VMEM(packed.shape, BF16),
        pltpu.VMEM((3, rows, width), BF16),
        pltpu.VMEM((2, width, rows), BF16),
        pltpu.VMEM((2, 2 * width, rows), BF16),
        pltpu.VMEM((4, 2, rows, width // 2), BF16),
        pltpu.VMEM((rows, width), BF16),
        pltpu.VMEM((2 * width, width), F32),
        pltpu.VMEM((5, 8, width), F32),
        pltpu.VMEM((5, 8, width), F32),
    ]
    scratch += [dma((11,)), dma((6,)), dma((6,))]
    scratch += [dma((2 * (count - begun),)) for _ in range(2)]
    scratch += [dma((count,)) for _ in range(8)]
    scratch += [dma((5,)) for _ in range(2)]
    return pl.pallas_call(
        tail_kernel,
        name="tail",
        out_shape=[jax.ShapeDtypeStruct((rows, width), F32)] * 2
        + [jax.ShapeDtypeStruct(shape, F32) for shape in shapes]
        + [jax.ShapeDtypeStruct((8, width), F32)],
        in_specs=[hbm] * (begun + 6) + [vmem] * 4,
        out_specs=[vmem] * 9,
        scratch_shapes=scratch,
        compiler_params=pltpu.CompilerParams(
            collective_id=3, has_side_effects=True, vmem_limit_bytes=60 << 20
        ),
    )(*kept, packed, normed, state, embedded, w_qkv, w_adapt, resid, above, gain_rows, gain_parts)


def xor_permute(value, axis, mask):
    return lax.ppermute(value, axis, [(i, i ^ mask) for i in range(lax.axis_size(axis))])


def quadrants(left):
    n, parts = lax.axis_size("seq"), lax.axis_size("dp")
    tokens, rows = left.shape
    shard = rows // (n * parts)
    split = left.reshape(tokens, n, parts, shard).transpose(2, 0, 1, 3)
    split = split.reshape(parts, tokens, n * shard)
    me = lax.axis_index("dp")
    return jnp.concatenate(
        [lax.dynamic_index_in_dim(split, me ^ m, 0, keepdims=True) for m in range(parts)]
    )


def other_core(left, right):
    core = lax.axis_index("seq") % 2
    half = right.shape[1] // 2
    mine = lax.dynamic_slice_in_dim(right, core * half, half, 1)
    theirs = lax.dynamic_slice_in_dim(right, (1 - core) * half, half, 1)
    left_in = xor_permute(left, "seq", 1)
    right_in = xor_permute(theirs, "seq", 1)
    return jnp.concatenate([left, left_in], axis=1), jnp.concatenate([mine, right_in], axis=0)


def scattered_sum(left, right, bits):
    n, parts = lax.axis_size("seq"), lax.axis_size("dp")
    cols = right.shape[1]
    left, right = other_core(quadrants(left), right)
    got = {}
    masks = list(range(parts))
    for bit in bits:
        outgoing = [m for m in masks if m >> bit & 1]
        masks = [m for m in masks if not m >> bit & 1]
        blocks = []
        for m in outgoing:
            block = dot_tn(left[m], right)
            for more in got.get(m, ()):
                block = block + more.astype(F32)
            blocks.append(block.astype(BF16))
        incoming = xor_permute(jnp.stack(blocks), "dp", 1 << bit)
        for k, m in enumerate(outgoing):
            got.setdefault(m ^ (1 << bit), []).append(incoming[k])
    block = dot_tn(left[0], right)
    for more in got.get(0, ()):
        block = block + more.astype(F32)
    shard = block.shape[0] // n
    block = block.astype(BF16).reshape(n, shard, cols // 2)
    block = lax.all_to_all(block, "seq", 0, 0)
    block = jnp.sum(block.reshape(n // 2, 2, shard, cols // 2).astype(F32), axis=0)
    return block.transpose(1, 0, 2).reshape(shard, cols)


def small_sum(value):
    value = value.reshape(value.shape[0], -1, value.shape[1])
    for axis in ("seq", "dp"):
        size = lax.axis_size(axis)
        me = lax.axis_index(axis)
        for bit in reversed(range(size.bit_length() - 1)):
            half = value.shape[2] // 2
            mine = (me >> bit) & 1
            kept = lax.dynamic_slice_in_dim(value, mine * half, half, 2)
            sent = lax.dynamic_slice_in_dim(value, (1 - mine) * half, half, 2)
            value = kept + xor_permute(sent, axis, 1 << bit)
    return value[:, 0]


def local(state, embedded, cotangent, w_adapt, w_qkv, w_out, w_gate, w_up, w_down, gains):
    seq_count, rows, width = state.shape
    n, parts = lax.axis_size("seq"), lax.axis_size("dp")
    tokens = seq_count * rows
    me = lax.axis_index("seq")
    bits = list(range(parts.bit_length() - 1))
    copies = max(1, n // HEADS)
    held = max(1, HEADS // n)
    owners = n // copies
    cos_np, sin_np = angle_tables(n * rows)
    cos_all, sin_all = jnp.asarray(cos_np), jnp.asarray(sin_np)
    cos = lax.dynamic_slice_in_dim(cos_all, me * rows, rows, 0)[:, None, :]
    sin = lax.dynamic_slice_in_dim(sin_all, me * rows, rows, 0)[:, None, :]
    gain_rows = gains.astype(F32)
    state, embedded = state.reshape(tokens, width), embedded.reshape(tokens, width)

    def to_heads(flat):
        return flat.reshape(tokens, HEADS, HEAD_DIM)

    def to_owner(parts_in):
        sent = jnp.stack(parts_in).reshape(len(parts_in), tokens, owners, held, HEAD_DIM)
        sent = sent.transpose(2, 3, 0, 1, 4)
        if copies > 1:
            sent = jnp.repeat(sent, copies, axis=0)
        return lax.all_to_all(sent, "seq", 0, 0)

    def from_owner(value):
        back = lax.all_to_all(value, "seq", 0, 0)[::copies]
        back = back.reshape(HEADS, -1, tokens, HEAD_DIM)
        return back.transpose(2, 1, 0, 3).reshape(tokens, -1)

    if n == HEADS and seq_count == 1:
        resid, normed, attended, qkv, attended_t, logsum = front(
            state, embedded, w_adapt, w_qkv, gain_rows, cos[:, 0], sin[:, 0]
        )
        qkv, attended_t, logsum = qkv[:, None], attended_t[:, None], logsum[:, None]
    else:
        resid = dot(state, w_adapt[:width]) + dot(embedded, w_adapt[width:])
        normed = mean_norm(resid, gain_rows[0]).astype(BF16)
        packed = dot(normed, w_qkv)
        queries = rotate(to_heads(packed[:, :width]), cos, sin).astype(BF16)
        keys = rotate(to_heads(packed[:, width : 2 * width]), cos, sin).astype(BF16)
        values = to_heads(packed[:, 2 * width :]).astype(BF16)
        qkv = to_owner((queries, keys, values))
        attended, attended_t, logsum = attention(qkv)
        attended = from_owner(attended[:, :, None])
    branch = dot(attended, w_out)
    middle = resid + mean_norm(branch, gain_rows[1])
    normed_mid = mean_norm(middle, gain_rows[2]).astype(BF16)
    gate_pre = dot(normed_mid, w_gate)
    up_pre = dot(normed_mid, w_up)
    sigmoid_gate = jax.nn.sigmoid(gate_pre)
    silu_gate = gate_pre * sigmoid_gate
    hidden = (silu_gate * up_pre).astype(BF16)
    down_out = dot(hidden, w_down)
    layer_out = middle + mean_norm(down_out, gain_rows[3])
    out_grad = cotangent.astype(F32).reshape(tokens, width)
    down_grad, gain_grad3 = norm_back(down_out, gain_rows[3], out_grad)
    down_low = down_grad.astype(BF16)
    hidden_grad = dot_nt(down_low, w_down)
    gate_low = (
        hidden_grad * up_pre * sigmoid_gate * (1.0 + gate_pre * (1.0 - sigmoid_gate))
    ).astype(BF16)
    up_low = (hidden_grad * silu_gate).astype(BF16)
    mid_norm_grad = dot_nt(gate_low, w_gate) + dot_nt(up_low, w_up)
    middle_part, gain_grad2 = norm_back(middle, gain_rows[2], mid_norm_grad)
    middle_grad = out_grad + middle_part
    branch_grad, gain_grad1 = norm_back(branch, gain_rows[1], middle_grad)
    branch_low = branch_grad.astype(BF16)
    attended_grad = dot_nt(branch_low, w_out).astype(BF16)
    shape = (seq_count, rows, width)
    if n == HEADS and parts == 4 and seq_count == 1:
        packed_low, *kept = back(
            (hidden, normed_mid, attended),
            (down_low, gate_low, up_low, branch_low),
            attended_grad,
            qkv[:, 0],
            attended_t[:, 0],
            logsum[:, 0],
            cos_all,
            sin_all,
        )
        nothing = jnp.zeros_like(gain_grad1)
        gain_parts = jnp.stack([nothing, gain_grad1, gain_grad2, gain_grad3] + [nothing] * 4)
        grad_state, grad_embedded, *sums, gains_sum = tail(
            kept,
            packed_low,
            normed,
            state,
            embedded,
            w_qkv,
            w_adapt,
            resid,
            middle_grad,
            gain_rows,
            gain_parts,
        )
        share = width // (n * parts)
        at = (me * parts + lax.axis_index("dp")) * share
        return (
            layer_out.reshape(shape).astype(BF16),
            grad_state.reshape(shape),
            grad_embedded.reshape(shape),
            *sums,
            lax.dynamic_slice_in_dim(gains_sum[:4], at, share, 1),
        )
    upstream = to_owner((to_heads(attended_grad),))[:, :, 0]
    packed_grad = attention_back(qkv, upstream, attended_t, logsum, cos_all, sin_all)
    packed_low = from_owner(packed_grad)
    normed_grad = dot_nt(packed_low, w_qkv)
    resid_part, gain_grad0 = norm_back(resid, gain_rows[0], normed_grad)
    resid_low = (middle_grad + resid_part).astype(BF16)
    grad_state = dot_nt(resid_low, w_adapt[:width])
    grad_embedded = dot_nt(resid_low, w_adapt[width:])
    flipped = bits[::-1]
    joined = jnp.concatenate([state, embedded], axis=-1)
    grad_down = scattered_sum(hidden, down_low, bits)
    grad_gate = scattered_sum(normed_mid, gate_low, flipped)
    grad_up = scattered_sum(normed_mid, up_low, bits)
    grad_out = scattered_sum(attended, branch_low, flipped)
    grad_qkv = scattered_sum(normed, packed_low, flipped)
    grad_adapt = scattered_sum(joined, resid_low, bits)
    grad_gains = jnp.stack([gain_grad0, gain_grad1, gain_grad2, gain_grad3])
    grad_gains = small_sum(grad_gains)
    return (
        layer_out.reshape(shape).astype(BF16),
        grad_state.reshape(shape),
        grad_embedded.reshape(shape),
        grad_adapt,
        grad_qkv,
        grad_out,
        grad_gate,
        grad_up,
        grad_down,
        grad_gains,
    )


def solution(mesh):
    tokens = P("dp", "seq", None)
    rows = P(("seq", "dp"), None)
    return jax.shard_map(
        local,
        mesh=mesh,
        in_specs=(tokens,) * 3 + (P(),) * 7,
        out_specs=(tokens,) * 3 + (rows,) * 6 + (P(None, ("seq", "dp")),),
        check_vma=False,
    )
```

```python
import functools
import math

import jax
import jax.numpy as jnp
import numpy as np
from jax import lax
from jax.experimental import pallas as pl
from jax.experimental.pallas import tpu as pltpu
from jax.sharding import PartitionSpec as P

HEADS = 8
HEAD_DIM = 128
norm_eps = 1e-06
rope_base = 50000.0
F32 = jnp.float32
BF16 = jnp.bfloat16
MESH = pl.DeviceIdType.MESH
NEG = -1e30
SCORE_SCALE = 1.0 / math.sqrt(HEAD_DIM)
LOG2E = 1.0 / math.log(2.0)


def mean_norm(values_in, gain_row):
    return (
        values_in
        * lax.rsqrt(jnp.mean(values_in * values_in, axis=-1, keepdims=True) + norm_eps)
        * gain_row
    )


def norm_back(values_in, gain_row, upstream):
    inverse = lax.rsqrt(jnp.mean(values_in * values_in, axis=-1, keepdims=True) + norm_eps)
    scaled = upstream * gain_row
    value_grad = inverse * scaled - values_in * (inverse * inverse * inverse) * jnp.mean(
        values_in * scaled, axis=-1, keepdims=True
    )
    gain_grad = jnp.sum(upstream * values_in * inverse, axis=0)
    return (value_grad, gain_grad)


def angle_tables(length):
    half_dim = HEAD_DIM // 2
    freqs = np.exp(
        np.arange(half_dim, dtype=np.float32) * np.float32(-2.0 * math.log(rope_base) / HEAD_DIM)
    ).astype(np.float32)
    angles = np.arange(length, dtype=np.float32)[:, None] * freqs[None, :]
    return np.cos(angles).astype(np.float32), np.sin(angles).astype(np.float32)


def rotate(heads_in, cos_table, sin_table):
    half_dim = heads_in.shape[-1] // 2
    lower_half = heads_in[..., :half_dim]
    upper_half = heads_in[..., half_dim:]
    return jnp.concatenate(
        [
            lower_half * cos_table - upper_half * sin_table,
            upper_half * cos_table + lower_half * sin_table,
        ],
        axis=-1,
    )


def dot(a, b):
    return lax.dot_general(a, b, (((1,), (0,)), ((), ())), preferred_element_type=F32)


def dot_tn(a, b):
    return lax.dot_general(a, b, (((0,), (0,)), ((), ())), preferred_element_type=F32)


def dot_nt(a, b):
    return lax.dot_general(a, b, (((1,), (1,)), ((), ())), preferred_element_type=F32)


def span(low, high, body, unrolled):
    if unrolled:
        for i in range(low, high):
            body(i)
    else:
        lax.fori_loop(low, high, lambda i, c: (body(i), c)[1], 0)


def causal_fill(block, fill):
    kv = lax.broadcasted_iota(jnp.int32, block.shape, 0)
    q = lax.broadcasted_iota(jnp.int32, block.shape, 1)
    return jnp.where(q >= kv, block, fill)


def attention_kernel(x_ref, o_ref, ot_ref, ls_ref, vt_ref, s_ref):
    n, hp, _, rows, _ = x_ref.shape
    unrolled = n <= 8
    factor = SCORE_SCALE * LOG2E
    for h in range(hp):
        for j in range(n):
            vt_ref[j] = x_ref[j, h, 2].astype(F32).T.astype(BF16)

        def query_block(i):
            q = x_ref[i, h, 0]
            diag = causal_fill(dot_nt(x_ref[i, h, 1], q), NEG)

            def first(j, peak):
                s = dot_nt(x_ref[j, h, 1], q)
                s_ref[j] = s
                return jnp.maximum(peak, jnp.max(s, axis=0, keepdims=True))

            peak = jnp.max(diag, axis=0, keepdims=True)
            if unrolled:
                for j in range(i):
                    peak = first(j, peak)
            else:
                peak = lax.fori_loop(0, i, first, peak)
            shift = peak * factor
            p = jnp.exp2(diag * factor - shift)
            total = jnp.sum(p, axis=0, keepdims=True)
            acc = dot(vt_ref[i], p.astype(BF16))

            def second(j, state):
                total, acc = state
                p = jnp.exp2(s_ref[j] * factor - shift)
                return (
                    total + jnp.sum(p, axis=0, keepdims=True),
                    acc + dot(vt_ref[j], p.astype(BF16)),
                )

            state = (total, acc)
            if unrolled:
                for j in range(i):
                    state = second(j, state)
            else:
                state = lax.fori_loop(0, i, second, state)
            total, acc = state
            acc = acc / total
            ot_ref[i, h] = acc
            o_ref[i, h] = acc.T.astype(BF16)
            ls_ref[i, h] = shift + jnp.log2(total)

        span(0, n, query_block, unrolled)


def attention(x):
    n, hp, _, rows, dim = x.shape
    pairs = n * (n + 1) // 2 * rows * rows * hp
    return pl.pallas_call(
        attention_kernel,
        name="attention",
        out_shape=(
            jax.ShapeDtypeStruct((n, hp, rows, dim), BF16),
            jax.ShapeDtypeStruct((n, hp, dim, rows), F32),
            jax.ShapeDtypeStruct((n, hp, 1, rows), F32),
        ),
        scratch_shapes=[
            pltpu.VMEM((n, dim, rows), BF16),
            pltpu.VMEM((n, rows, rows), F32),
        ],
        compiler_params=pltpu.CompilerParams(vmem_limit_bytes=40 << 20),
        cost_estimate=pl.CostEstimate(
            flops=pairs * dim * 8, bytes_accessed=x.size * 4, transcendentals=pairs
        ),
    )(x)


def attention_back_kernel(
    x_ref, g_ref, ot_ref, ls_ref, cos_ref, sin_ref, out_ref, kt_ref, dqt_ref, delta_ref
):
    n, hp, _, rows, _ = x_ref.shape
    unrolled = n <= 8
    factor = SCORE_SCALE * LOG2E
    for h in range(hp):
        for j in range(n):
            kt_ref[j] = x_ref[j, h, 1].astype(F32).T.astype(BF16)
            delta_ref[j] = jnp.sum(
                g_ref[j, h].astype(F32).T * ot_ref[j, h], axis=0, keepdims=True
            )

        def unrotated(value, i):
            turned = pl.ds(i * rows, rows)
            cos, sin = cos_ref[turned], sin_ref[turned]
            return rotate(value * SCORE_SCALE, cos, -sin).astype(BF16)

        def pair(i, j, diagonal):
            q, g = x_ref[i, h, 0], g_ref[i, h]
            p = jnp.exp2(dot_nt(x_ref[j, h, 1], q) * factor - ls_ref[i, h])
            if diagonal:
                p = causal_fill(p, 0.0)
            dv = dot(p.astype(BF16), g)
            ds = (p * (dot_nt(x_ref[j, h, 2], g) - delta_ref[i])).astype(BF16)
            dk = dot(ds, q)
            dqt = dot(kt_ref[j], ds)
            return dv, dk, dqt

        def key_block(j):
            dv, dk, dqt = pair(j, j, True)
            if unrolled:
                dqt_ref[j] = dqt if j == 0 else dqt_ref[j] + dqt
            else:
                dqt_ref[j] = jnp.where(j == 0, 0.0, dqt_ref[j]) + dqt

            def step(i, state):
                dv, dk = state
                v, k, t = pair(i, j, False)
                if unrolled:
                    dqt_ref[i] = t if j == 0 else dqt_ref[i] + t
                else:
                    dqt_ref[i] = jnp.where(j == 0, 0.0, dqt_ref[i]) + t
                return dv + v, dk + k

            state = (dv, dk)
            if unrolled:
                for i in range(j + 1, n):
                    state = step(i, state)
            else:
                state = lax.fori_loop(j + 1, n, step, state)
            dv, dk = state
            out_ref[j, h, 0] = unrotated(dqt_ref[j].T, j)
            out_ref[j, h, 1] = unrotated(dk, j)
            out_ref[j, h, 2] = dv.astype(BF16)

        span(0, n, key_block, unrolled)


def attention_back(x, g, ot, ls, cos, sin):
    n, hp, _, rows, dim = x.shape
    pairs = n * (n + 1) // 2 * rows * rows * hp
    return pl.pallas_call(
        attention_back_kernel,
        name="attention_back",
        out_shape=jax.ShapeDtypeStruct(x.shape, BF16),
        scratch_shapes=[
            pltpu.VMEM((n, dim, rows), BF16),
            pltpu.VMEM((n, dim, rows), F32),
            pltpu.VMEM((n, 1, rows), F32),
        ],
        compiler_params=pltpu.CompilerParams(vmem_limit_bytes=40 << 20),
        cost_estimate=pl.CostEstimate(
            flops=pairs * dim * 20, bytes_accessed=x.size * 6, transcendentals=pairs
        ),
    )(x, g, ot, ls, cos, sin)


def seq_device(index):
    return {"seq": index}


def greet(peers):
    barrier = pltpu.get_barrier_semaphore()
    for device in peers:
        pl.semaphore_signal(barrier, inc=1, device_id=device, device_id_type=MESH)


def greeted(count):
    pl.semaphore_wait(pltpu.get_barrier_semaphore(), count)


def remote(src, dst, send, recv, device):
    return pltpu.make_async_remote_copy(
        src_ref=src,
        dst_ref=dst,
        send_sem=send,
        recv_sem=recv,
        device_id=device,
        device_id_type=MESH,
    )


def front_kernel(
    state_ref,
    embedded_ref,
    wa_ref,
    wq_ref,
    gain_ref,
    cos_ref,
    sin_ref,
    resid_out,
    normed_out,
    att_out,
    x_out,
    ot_out,
    ls_out,
    ltn_out,
    ltj_out,
    wa,
    wq,
    joined,
    resid,
    normed,
    sent,
    x,
    vt,
    scores,
    ot,
    o_sent,
    att,
    ltn,
    ltj,
    load_sem,
    store_sem,
    send_sem,
    recv_sem,
    o_send_sem,
    o_recv_sem,
    l_send_sem,
    l_recv_sem,
):
    n, rows, width = HEADS, state_ref.shape[0], state_ref.shape[1]
    me = lax.axis_index("seq")
    dp = lax.axis_index("dp")
    peers = [seq_device((me + k) % n) for k in range(1, n)]
    across = [{"dp": flipped(0, dp)}, {"dp": flipped(1, dp)}]
    near = seq_device(flipped(0, me))
    greet(peers + across)
    loads = [
        pltpu.make_async_copy(state_ref, joined.at[0], load_sem.at[0]),
        pltpu.make_async_copy(wa_ref.at[pl.ds(0, width)], wa.at[0], load_sem.at[1]),
        pltpu.make_async_copy(embedded_ref, joined.at[1], load_sem.at[2]),
        pltpu.make_async_copy(wa_ref.at[pl.ds(width, width)], wa.at[1], load_sem.at[3]),
        pltpu.make_async_copy(wq_ref, wq, load_sem.at[4]),
    ]
    for copy in loads:
        copy.start()
    tile = 256
    for half in range(2):
        loads[2 * half].wait()
        loads[2 * half + 1].wait()

        def adapt(t, c):
            cols = pl.ds(pl.multiple_of(t * tile, tile), tile)
            block = dot(joined[half], wa[half, :, cols])
            resid[:, cols] = block if half == 0 else resid[:, cols] + block
            return c

        lax.fori_loop(0, width // tile, adapt, 0)
    normed[...] = mean_norm(resid[...], gain_ref[0:1, :]).astype(BF16)
    stores = [
        pltpu.make_async_copy(resid, resid_out, store_sem.at[0]),
        pltpu.make_async_copy(normed, normed_out, store_sem.at[1]),
    ]
    for copy in stores:
        copy.start()
    loads[4].wait()
    lefts = []

    def share(source, out, slot, device):
        k = len(lefts)
        copy = remote(source, out.at[slot], l_send_sem.at[k], l_recv_sem.at[k], device)
        copy.start()
        lefts.append(copy)
    cos, sin = cos_ref[...], sin_ref[...]
    pairs = n // 2
    order = [2, 1, 3, 0] if pairs == 4 else list(range(pairs - 1, -1, -1))
    sends = []
    for k in order:
        chip = (me // 2 + k) % pairs
        for part in range(3):
            cols = pl.ds(pl.multiple_of(part * width + chip * 2 * HEAD_DIM, 2 * HEAD_DIM), 2 * HEAD_DIM)
            block = dot(normed[...], wq[:, cols])
            for core in range(2):
                head = block[:, core * HEAD_DIM : (core + 1) * HEAD_DIM]
                if part < 2:
                    head = rotate(head, cos, sin)
                sent[2 * chip + core, part] = head.astype(BF16)
        if k == order[0]:
            greeted(n + 1)
        for core in range(2):
            owner = 2 * chip + core
            if k == 0:
                continue
            copy = remote(sent.at[owner], x.at[me], send_sem.at[owner], recv_sem.at[me], seq_device(owner))
            copy.start()
            sends.append(copy)
    mate = me + 1 - 2 * (me % 2)
    copy = remote(sent.at[mate], x.at[me], send_sem.at[mate], recv_sem.at[me], seq_device(mate))
    copy.start()
    sends.append(copy)
    x[me] = sent[me]
    transposed_into(normed, ltn)
    for half in range(2):
        transposed_into(joined.at[half], ltj.at[pl.ds(half * width, width)])
    stores.append(pltpu.make_async_copy(ltn, ltn_out.at[0], store_sem.at[4]))
    stores.append(pltpu.make_async_copy(ltj, ltj_out.at[0], store_sem.at[5]))
    for copy in stores[2:]:
        copy.start()
    share(ltn, ltn_out, 2, across[0])
    share(ltn, ltn_out, 4, across[1])
    share(ltj, ltj_out, 2, across[1])
    share(ltn, ltn_out, 1, near)
    share(ltj, ltj_out, 1, near)
    factor = SCORE_SCALE * LOG2E
    for i in range(n):

        @pl.when(me != i)
        def arrive():
            remote(sent.at[0], x.at[i], send_sem.at[0], recv_sem.at[i], seq_device(i)).wait_recv()

        vt[i] = x[i, 2].astype(F32).T.astype(BF16)
        q = x[i, 0]
        diag = causal_fill(dot_nt(x[i, 1], q), NEG)
        peak = jnp.max(diag, axis=0, keepdims=True)
        for j in range(i):
            block = dot_nt(x[j, 1], q)
            scores[j] = block
            peak = jnp.maximum(peak, jnp.max(block, axis=0, keepdims=True))
        shift = peak * factor
        p = jnp.exp2(diag * factor - shift)
        total = jnp.sum(p, axis=0, keepdims=True)
        acc = dot(vt[i], p.astype(BF16))
        for j in range(i):
            p = jnp.exp2(scores[j] * factor - shift)
            total = total + jnp.sum(p, axis=0, keepdims=True)
            acc = acc + dot(vt[j], p.astype(BF16))
        acc = acc / total
        ot[i] = acc
        o_sent[i] = acc.T.astype(BF16)
        ls_out[i] = shift + jnp.log2(total)
        mine = pl.ds(pl.multiple_of(me * HEAD_DIM, HEAD_DIM), HEAD_DIM)

        @pl.when(me != i)
        def give():
            remote(o_sent.at[i], att.at[:, mine], o_send_sem.at[i], o_recv_sem.at[me], seq_device(i)).start()

        @pl.when(me == i)
        def keep():
            att[:, mine] = o_sent[i]

    stores.append(pltpu.make_async_copy(x, x_out, store_sem.at[2]))
    stores.append(pltpu.make_async_copy(ot, ot_out, store_sem.at[3]))
    for copy in stores[4:]:
        copy.start()
    for k, out, slot in ((0, ltn_out, 2), (1, ltn_out, 4), (2, ltj_out, 2)):
        lefts[k].wait_recv()
        share(out.at[slot], out, slot + 1, near)
    for copy in sends:
        copy.wait_send()
    for i in range(n):

        @pl.when(me != i)
        def finish():
            cols = pl.ds(i * HEAD_DIM, HEAD_DIM)
            copy = remote(o_sent.at[i], att.at[:, cols], o_send_sem.at[i], o_recv_sem.at[i], seq_device(i))
            copy.wait_send()
            copy.wait_recv()

    att_out[...] = att[...]
    for copy in stores:
        copy.wait()
    for k, copy in enumerate(lefts):
        copy.wait_send()
        if k > 2:
            copy.wait_recv()


def front(state, embedded, w_adapt, w_qkv, gain_rows, cos, sin):
    n = HEADS
    rows, width = state.shape
    hbm = pl.BlockSpec(memory_space=pl.ANY)
    vmem = pl.BlockSpec(memory_space=pltpu.VMEM)
    return pl.pallas_call(
        front_kernel,
        name="front",
        out_shape=(
            jax.ShapeDtypeStruct((rows, width), F32),
            jax.ShapeDtypeStruct((rows, width), BF16),
            jax.ShapeDtypeStruct((rows, width), BF16),
            jax.ShapeDtypeStruct((n, 3, rows, HEAD_DIM), BF16),
            jax.ShapeDtypeStruct((n, HEAD_DIM, rows), F32),
            jax.ShapeDtypeStruct((n, 1, rows), F32),
            jax.ShapeDtypeStruct((6, width, rows), BF16),
            jax.ShapeDtypeStruct((4, 2 * width, rows), BF16),
        ),
        in_specs=[hbm, hbm, hbm, hbm, vmem, vmem, vmem],
        out_specs=(hbm, hbm, vmem, hbm, hbm, vmem, hbm, hbm),
        scratch_shapes=[
            pltpu.VMEM((2, width, width), BF16),
            pltpu.VMEM((width, 3 * width), BF16),
            pltpu.VMEM((2, rows, width), BF16),
            pltpu.VMEM((rows, width), F32),
            pltpu.VMEM((rows, width), BF16),
            pltpu.VMEM((n, 3, rows, HEAD_DIM), BF16),
            pltpu.VMEM((n, 3, rows, HEAD_DIM), BF16),
            pltpu.VMEM((n, HEAD_DIM, rows), BF16),
            pltpu.VMEM((n, rows, rows), F32),
            pltpu.VMEM((n, HEAD_DIM, rows), F32),
            pltpu.VMEM((n, rows, HEAD_DIM), BF16),
            pltpu.VMEM((rows, width), BF16),
            pltpu.VMEM((width, rows), BF16),
            pltpu.VMEM((2 * width, rows), BF16),
            pltpu.SemaphoreType.DMA((5,)),
            pltpu.SemaphoreType.DMA((6,)),
            pltpu.SemaphoreType.DMA((n,)),
            pltpu.SemaphoreType.DMA((n,)),
            pltpu.SemaphoreType.DMA((n,)),
            pltpu.SemaphoreType.DMA((n,)),
            pltpu.SemaphoreType.DMA((8,)),
            pltpu.SemaphoreType.DMA((8,)),
        ],
        compiler_params=pltpu.CompilerParams(
            collective_id=1, has_side_effects=True, vmem_limit_bytes=48 << 20
        ),
    )(state, embedded, w_adapt, w_qkv, gain_rows, cos, sin)


def flipped(bit, value):
    return value + (1 - 2 * ((value // (1 << bit)) % 2)) * (1 << bit)


UNITS = (
    ("down", 0, 0, 0, 512, 0),
    ("gate", 1, 1, 0, 1408, 1),
    ("up_a", 1, 2, 0, 512, 0),
    ("up_b", 1, 2, 512, 896, 1),
    ("out", 2, 3, 0, 512, 0),
)


def unit_slots(first, dp):
    slots = []
    for q in range(4):
        turned = [(dp + q) % 2, (dp // 2 + q // 2) % 2]
        slots.append(turned[first] * 2 + turned[1 - first])
    return slots


def transposed_into(source, target):
    tile = 256

    def step(t, c):
        at = pl.multiple_of(t * tile, tile)
        target[pl.ds(at, tile), :] = source[:, pl.ds(at, tile)].T
        return c

    lax.fori_loop(0, source.shape[1] // tile, step, 0)


def weight_blocks(left, right, column, width, slots, out, work):
    total = left.shape[1]
    shard = total // 32
    for begin in range(0, width, 256):
        wide = min(256, width - begin)
        cols = pl.ds(column + begin, wide)
        work[0:total, 0:wide] = dot(left[0], right[0, :, cols]) + dot(left[1], right[1, :, cols])
        for z in range(4):
            for q in range(4):
                pieces = [
                    work[pl.ds((8 * z + 4 * core + q) * shard, shard), 0:wide] for core in range(2)
                ]
                out[slots[q], pl.ds(2 * z * shard, 2 * shard), pl.ds(begin, wide)] = (
                    jnp.concatenate(pieces, axis=0).astype(BF16)
                )


def add_into(target, more):
    rows = target.shape[0]
    chunk = 16
    while rows % (chunk * 2) == 0 and chunk < 64:
        chunk *= 2

    def step(t, c):
        at = pl.ds(pl.multiple_of(t * chunk, chunk), chunk)
        target[at, :] = (target[at, :].astype(F32) + more[at, :].astype(F32)).astype(BF16)
        return c

    lax.fori_loop(0, rows // chunk, step, 0)


def back_kernel(*refs):
    refs = list(refs)

    def take(count):
        taken, refs[:count] = refs[:count], []
        return taken

    lefts_in, rights_in = take(3), take(4)
    (dout_ref, x_ref, ot_ref, ls_ref, cos_ref, sin_ref) = take(6)
    (packed_out,) = take(1)
    kept_out = take(5)
    held, turned, halves = take(3), take(3), take(4)
    sums, arrived = take(5), take(5)
    (work, g, kt, dqt, delta, dsent, packed) = take(7)
    (load_sem, store_sem, g_send, g_recv, d_send, d_recv, m_send, m_recv, s_send, s_recv) = take(10)
    n, rows = HEADS, dout_ref.shape[0]
    me = lax.axis_index("seq")
    dp = lax.axis_index("dp")
    core = me % 2
    mate = flipped(0, me)
    across = [{"dp": flipped(0, dp)}, {"dp": flipped(1, dp)}]
    greet([seq_device((me + k) % n) for k in range(1, n)] + across)
    loads = []
    for k in range(3):
        loads.append(pltpu.make_async_copy(lefts_in[k], held[k], load_sem.at[k]))
    for k in range(4):
        half = halves[k].shape[2]
        mine = pl.ds(pl.multiple_of(core * half, 128), half)
        loads.append(
            pltpu.make_async_copy(rights_in[k].at[:, mine], halves[k].at[0], load_sem.at[3 + k])
        )
    for copy in loads:
        copy.start()
    greeted(n + 1)
    sends = []
    my_cols = pl.ds(pl.multiple_of(me * HEAD_DIM, HEAD_DIM), HEAD_DIM)
    for k in (4, 5, 3, 2, 6, 7, 1):
        owner = (me + k) % n
        cols = pl.ds(pl.multiple_of(owner * HEAD_DIM, HEAD_DIM), HEAD_DIM)
        copy = remote(dout_ref.at[:, cols], g.at[me], g_send.at[owner], g_recv.at[me], seq_device(owner))
        copy.start()
        sends.append(copy)
    own = pltpu.make_async_copy(dout_ref.at[:, my_cols], g.at[me], load_sem.at[7])
    own.start()
    mates = {}

    def to_mate(key, slot, src, dst):
        copy = remote(src, dst, m_send.at[slot], m_recv.at[slot], seq_device(mate))
        copy.start()
        sends.append(copy)
        mates[key] = copy

    for k in range(4):
        half = halves[k].shape[2]
        theirs = pl.ds(pl.multiple_of((1 - core) * half, 128), half)
        to_mate(("right", k), 3 + k, rights_in[k].at[:, theirs], halves[k].at[1])
    for k in range(3):
        loads[k].wait()
        transposed_into(held[k], turned[k].at[0])
        to_mate(("left", k), k, turned[k].at[0], turned[k].at[1])
    loaded = set()
    steps = []
    for u, (name, left, right, column, width, first) in enumerate(UNITS):
        if ("left", left) not in loaded:
            loaded.add(("left", left))
            mates[("left", left)].wait_recv()
        if ("right", right) not in loaded:
            loaded.add(("right", right))
            loads[3 + right].wait()
            mates[("right", right)].wait_recv()
        weight_blocks(
            turned[left], halves[right], column, width, unit_slots(first, dp), sums[u], work
        )
        pair = []
        for k in range(2):
            copy = remote(
                sums[u].at[2 + k],
                arrived[u].at[k],
                s_send.at[2 * u + k],
                s_recv.at[2 * u + k],
                across[first],
            )
            copy.start()
            sends.append(copy)
            pair.append(copy)
        steps.append(pair)
    own.wait()
    for i in range(n):

        @pl.when(me != i)
        def arrive():
            remote(g.at[0], g.at[i], g_send.at[0], g_recv.at[i], seq_device(i)).wait_recv()

    factor = SCORE_SCALE * LOG2E
    for j in range(n):
        kt[j] = x_ref[j, 1].astype(F32).T.astype(BF16)
        delta[j] = jnp.sum(g[j].astype(F32).T * ot_ref[j], axis=0, keepdims=True)
    for j in range(n):
        dk = dv = None
        for i in range(j, n):
            q, up = x_ref[i, 0], g[i]
            p = jnp.exp2(dot_nt(x_ref[j, 1], q) * factor - ls_ref[i])
            if i == j:
                p = causal_fill(p, 0.0)
            v = dot(p.astype(BF16), up)
            ds = (p * (dot_nt(x_ref[j, 2], up) - delta[i])).astype(BF16)
            k = dot(ds, q)
            t = dot(kt[j], ds)
            dqt[i] = t if j == 0 else dqt[i] + t
            dv, dk = (v, k) if i == j else (dv + v, dk + k)
        here = pl.ds(j * rows, rows)
        cos, sin = cos_ref[here], -sin_ref[here]
        dsent[j, 0] = rotate(dqt[j].T * SCORE_SCALE, cos, sin).astype(BF16)
        dsent[j, 1] = rotate(dk * SCORE_SCALE, cos, sin).astype(BF16)
        dsent[j, 2] = dv.astype(BF16)

        @pl.when(me != j)
        def give():
            remote(dsent.at[j], packed.at[:, :, my_cols], d_send.at[j], d_recv.at[me], seq_device(j)).start()

        @pl.when(me == j)
        def keep():
            packed[:, :, my_cols] = dsent[j]

    stores = []
    for u, pair in enumerate(steps):
        for k in range(2):
            pair[k].wait_recv()
            add_into(sums[u].at[k], arrived[u].at[k])
        copy = pltpu.make_async_copy(sums[u].at[pl.ds(0, 2)], kept_out[u], store_sem.at[u])
        copy.start()
        stores.append(copy)
    for j in range(n):

        @pl.when(me != j)
        def finish():
            cols = pl.ds(j * HEAD_DIM, HEAD_DIM)
            copy = remote(dsent.at[j], packed.at[:, :, cols], d_send.at[j], d_recv.at[j], seq_device(j))
            copy.wait_send()
            copy.wait_recv()

    last = pltpu.make_async_copy(packed, packed_out, store_sem.at[5])
    last.start()
    for copy in sends:
        copy.wait_send()
    for copy in stores:
        copy.wait()
    last.wait()


def back(lefts, rights, dout, x, ot, ls, cos, sin):
    n = HEADS
    rows, width = dout.shape
    hbm = pl.BlockSpec(memory_space=pl.ANY)
    vmem = pl.BlockSpec(memory_space=pltpu.VMEM)
    heights = [lefts[unit[1]].shape[1] // 4 for unit in UNITS]
    kept = [(2, height, unit[4]) for height, unit in zip(heights, UNITS)]
    dma = pltpu.SemaphoreType.DMA
    return pl.pallas_call(
        back_kernel,
        name="back",
        out_shape=[jax.ShapeDtypeStruct((3, rows, width), BF16)]
        + [jax.ShapeDtypeStruct(shape, BF16) for shape in kept],
        in_specs=[hbm] * 8 + [vmem] * 5,
        out_specs=[hbm] * 6,
        scratch_shapes=[pltpu.VMEM(left.shape, BF16) for left in lefts]
        + [pltpu.VMEM((2, left.shape[1], rows), BF16) for left in lefts]
        + [pltpu.VMEM((2, rows, right.shape[1] // 2), BF16) for right in rights]
        + [pltpu.VMEM((4,) + shape[1:], BF16) for shape in kept]
        + [pltpu.VMEM(shape, BF16) for shape in kept]
        + [
            pltpu.VMEM((max(left.shape[1] for left in lefts), 256), F32),
            pltpu.VMEM((n, rows, HEAD_DIM), BF16),
            pltpu.VMEM((n, HEAD_DIM, rows), BF16),
            pltpu.VMEM((n, HEAD_DIM, rows), F32),
            pltpu.VMEM((n, 1, rows), F32),
            pltpu.VMEM((n, 3, rows, HEAD_DIM), BF16),
            pltpu.VMEM((3, rows, width), BF16),
            dma((8,)),
            dma((6,)),
            dma((n,)),
            dma((n,)),
            dma((n,)),
            dma((n,)),
            dma((7,)),
            dma((7,)),
            dma((10,)),
            dma((10,)),
        ],
        compiler_params=pltpu.CompilerParams(
            collective_id=2, has_side_effects=True, vmem_limit_bytes=56 << 20
        ),
    )(*lefts, *rights, dout, x, ot, ls, cos, sin)


BEGUN = (
    (0, 5, 0, 256, 0, 512, 1),
    (0, 5, 256, 256, 256, 512, 1),
    (1, 3, 0, 512, 0, 1408, 0),
    (1, 3, 512, 512, 512, 1408, 0),
    (1, 3, 1024, 384, 1024, 1408, 0),
    (2, 4, 0, 512, 0, 1408, 1),
    (3, 4, 0, 512, 512, 1408, 0),
    (3, 4, 512, 384, 1024, 1408, 0),
    (4, 2, 0, 512, 0, 512, 1),
)
FRESH = ((1, 0, 0), (1, 1024, 0), (1, 2048, 1), (0, 0, 1))
SCHEDULE = (
    ("U", 9), ("U", 10), ("U", 11), ("S", 8), ("P", 0), ("U", 12), ("S", 2), ("W", 9),
    ("W", 11), ("O", 0), ("S", 9), ("S", 7), ("W", 10), ("C", 8), ("1", 8), ("S", 6),
    ("S", 1), ("C", 2), ("1", 2), ("W", 12), ("S", 12), ("D", 8), ("G", 0), ("2", 8),
    ("S", 5), ("C", 7), ("1", 7), ("C", 9), ("1", 9), ("D", 2), ("G", 1), ("2", 2),
    ("E", 8), ("S", 3), ("D", 7), ("2", 7), ("C", 6), ("G", 2), ("1", 6), ("E", 2),
    ("S", 0), ("C", 1), ("1", 1), ("E", 7), ("G", 3), ("D", 9), ("2", 9), ("S", 10),
    ("D", 6), ("2", 6), ("E", 9), ("G", 4), ("C", 5), ("1", 5), ("S", 11), ("C", 12),
    ("1", 12), ("E", 6), ("D", 1), ("2", 1), ("S", 4), ("C", 3), ("1", 3), ("D", 5),
    ("2", 5), ("C", 0), ("E", 1), ("E", 5), ("C", 11), ("C", 10), ("1", 0), ("D", 12),
    ("2", 12), ("C", 4), ("1", 10), ("D", 3), ("2", 3), ("E", 12), ("1", 11), ("D", 0),
    ("2", 0), ("E", 3), ("1", 4), ("D", 10), ("2", 10), ("E", 0), ("D", 11), ("2", 11),
    ("E", 10), ("D", 4), ("2", 4), ("E", 11), ("E", 4),
)


def dealt_blocks(left, slots, right, spread, bit, out, work):
    total = left.shape[1]
    shard = total // 32
    block = dot(left[slots[0]], right[0])
    for k in range(1, 4):
        block += dot(left[slots[k]], right[k])
    work[0:total, :] = block
    for z in range(4):
        for other in range(2):
            pieces = []
            for core in range(2):
                for b in range(2):
                    q = (b << bit) | (other << (1 - bit))
                    pieces.append(work[pl.ds((8 * z + 4 * core + q) * shard, shard), :])
            out[spread[other], pl.ds(4 * z * shard, 4 * shard), :] = jnp.concatenate(
                pieces, axis=0
            ).astype(BF16)


def tail_kernel(*refs):
    refs = list(refs)

    def take(count):
        taken, refs[:count] = refs[:count], []
        return taken

    begun, fresh = len(BEGUN), len(FRESH)
    count = begun + fresh
    kept_in = take(5)
    packed_in, ltn_in, ltj_in, wq_in, wa_in = take(5)
    resid, above, gain_rows, gain_parts = take(4)
    grad_joined = take(2)
    outs = take(6)
    (gains_out,) = take(1)
    held = take(5)
    sums = take(fresh)
    arrived2, planes, arrived3, arrived4, finals = (
        take(count),
        take(count),
        take(count),
        take(count),
        take(count),
    )
    (wq, wa, packed, ltn, ltj, dealt, low, work, back_sum, gain_buf, gain_got) = take(11)
    (load_sem, u_send, u_recv, s_send, s_recv, z1_send, z1_recv) = take(7)
    (z2_send, z2_recv, c_send, c_recv, gain_send, gain_recv) = take(6)
    rows, width = resid.shape
    me = lax.axis_index("seq")
    dp = lax.axis_index("dp")
    core = me % 2
    bits = [dp % 2, dp // 2]
    z_low, z_high = (me // 2) % 2, me // 4
    mate = flipped(0, me)
    near = seq_device(mate)
    across = [{"dp": flipped(0, dp)}, {"dp": flipped(1, dp)}]
    diagonal = [{"seq": mate, "dp": flipped(0, dp)}, {"seq": mate, "dp": flipped(1, dp)}]
    beside = [seq_device(flipped(1, me)), seq_device(flipped(2, me))]
    greet([near] + across + diagonal + beside)
    loads = {}

    def load(key, src, dst):
        loads[key] = pltpu.make_async_copy(src, dst, load_sem.at[len(loads)])
        loads[key].start()

    load("packed", packed_in, packed)
    load("wq", wq_in, wq)
    load("ltn", ltn_in, ltn)
    for u in (4, 3, 2, 1, 0):
        load(u, kept_in[u].at[0], held[u])
    load("ltj", ltj_in, ltj)
    load("wa", wa_in, wa)
    greeted(7)
    sends = []

    def send(src, dst, send_sem, recv_sem, device):
        copy = remote(src, dst, send_sem, recv_sem, device)
        copy.start()
        sends.append(copy)
        return copy

    dealing, second, third, fourth, finished, taken = {}, {}, {}, {}, {}, set()

    def ready(key):
        if key not in taken:
            taken.add(key)
            loads[key].wait()

    def start_columns(u):
        k = u - begun
        bit = FRESH[k][2]
        source = low if k == 3 else packed.at[k]
        if k < 3:
            ready("packed")

        def columns(other_core, other_bit):
            place = (core + (1 - 2 * core) * other_core) * 2
            place = place + bits[bit] + (1 - 2 * bits[bit]) * other_bit
            return pl.ds(pl.multiple_of(place * 256, 256), 256)

        dealing[u] = [
            send(
                source.at[:, columns(*there)],
                dealt.at[k, slot],
                u_send.at[3 * k + slot - 1],
                u_recv.at[3 * k + slot - 1],
                device,
            )
            for there, slot, device in (
                ((0, 1), 2, across[bit]),
                ((1, 1), 3, diagonal[bit]),
                ((1, 0), 1, near),
            )
        ]
        dealt[k, 0] = source[:, columns(0, 0)]

    def start_second(u):
        if u < begun:
            array, out, at, wide, column, half, bit = BEGUN[u]
            src = kept_in[array].at[1, :, pl.ds(at, wide)]
        else:
            bit = 1 - FRESH[u - begun][2]
            src = sums[u - begun].at[1]
        second[u] = send(src, arrived2[u], s_send.at[u], s_recv.at[u], across[bit])

    def multiply(u):
        k = u - begun
        out, column, bit = FRESH[k]
        slots = (0, 1, 2, 3) if (bit == 0 or k == 3) else (0, 1, 4, 5)
        left = ltj if k == 3 else ltn
        ready("ltj" if k == 3 else "ltn")
        for copy in dealing[u]:
            copy.wait_recv()
        spread = [(bits[1 - bit] + other) % 2 for other in range(2)]
        dealt_blocks(left, slots, dealt.at[k], spread, bit, sums[k], work)

    def take_second(u):
        second[u].wait_recv()
        tall = planes[u].shape[2]
        for z in range(4):
            at = pl.ds(z * tall, tall)
            if u < begun:
                array, begin, wide = BEGUN[u][0], BEGUN[u][2], BEGUN[u][3]
                ready(array)
                mine = held[array][at, pl.ds(begin, wide)]
            else:
                mine = sums[u - begun][0, at, :]
            planes[u][z % 2, z // 2] = (
                mine.astype(F32) + arrived2[u][at, :].astype(F32)
            ).astype(BF16)

    def start_third(u):
        third[u] = send(
            planes[u].at[1 - z_low], arrived3[u], z1_send.at[u], z1_recv.at[u], beside[0]
        )

    def take_third(u):
        third[u].wait_recv()
        for k in range(2):
            planes[u][z_low, k] = (
                planes[u][z_low, k].astype(F32) + arrived3[u][k].astype(F32)
            ).astype(BF16)

    def start_fourth(u):
        fourth[u] = send(
            planes[u].at[z_low, 1 - z_high], arrived4[u], z2_send.at[u], z2_recv.at[u], beside[1]
        )

    def take_fourth(u):
        fourth[u].wait_recv()
        finals[u][...] = planes[u][z_low, z_high].astype(F32) + arrived4[u][...].astype(F32)
        if u < begun:
            array, out, begin, wide, column, half, bit = BEGUN[u]
            cols = pl.ds(pl.multiple_of(core * half + column, 128), wide)
            owners = [(core, core), (1 - core, near)]
            shard = planes[u].shape[2] // 2
        else:
            out, column, bit = FRESH[u - begun]
            cols = pl.ds(pl.multiple_of((core * 2 + bits[bit]) * 256 + column, 256), 256)
            here, there = bits[bit], 1 - bits[bit]
            owners = [
                (core * 2 + here, None),
                ((1 - core) * 2 + here, near),
                (core * 2 + there, across[bit]),
                ((1 - core) * 2 + there, diagonal[bit]),
            ]
            shard = planes[u].shape[2] // 4
        finished[u] = []
        for k, (place, device) in enumerate(owners):
            at = pl.ds(pl.multiple_of(place * shard, 8), shard)
            if k == 0:
                outs[out][:, cols] = finals[u][at, :]
            else:
                sem = u if k == 1 else count + 2 * (u - begun) + k - 2
                finished[u].append(
                    send(
                        finals[u].at[at], outs[out].at[:, cols], c_send.at[sem], c_recv.at[sem], device
                    )
                )

    gain_steps = {}
    gain_partners = [near] + across + beside

    def send_gain(k):
        gain_steps[k] = send(
            gain_buf.at[k], gain_got.at[k], gain_send.at[k], gain_recv.at[k], gain_partners[k]
        )

    def add_gain(k):
        gain_steps[k].wait_recv()
        total = gain_buf[k] + gain_got[k]
        if k == 4:
            gains_out[...] = total
        else:
            gain_buf[k + 1] = total
            send_gain(k + 1)

    tile = 256

    def dense_back(_):
        ready("packed")
        ready("wq")

        def back_tile(t, c):
            at = pl.ds(pl.multiple_of(t * tile, tile), tile)
            block = dot_nt(packed[0], wq[at, pl.ds(0, width)])
            block += dot_nt(packed[1], wq[at, pl.ds(width, width)])
            block += dot_nt(packed[2], wq[at, pl.ds(2 * width, width)])
            back_sum[:, at] = block
            return c

        lax.fori_loop(0, width // tile, back_tile, 0)
        part, gain0 = norm_back(resid[...], gain_rows[0:1, :], back_sum[...])
        low[...] = (above[...] + part).astype(BF16)
        gain_buf[0] = gain_parts[...]
        gain_buf[0, 0:1, :] = gain0[None, :]
        send_gain(0)

    def dense_out(_):
        ready("wa")

        def out_tile(t, c):
            at = pl.ds(pl.multiple_of(t * tile, tile), tile)
            for k in range(2):
                from_row = pl.ds(pl.multiple_of(k * width + t * tile, tile), tile)
                grad_joined[k][:, at] = dot_nt(low[...], wa[from_row, :])
            return c

        lax.fori_loop(0, width // tile, out_tile, 0)

    actions = {
        "U": start_columns,
        "S": start_second,
        "1": start_third,
        "2": start_fourth,
        "W": multiply,
        "C": take_second,
        "D": take_third,
        "E": take_fourth,
        "G": add_gain,
        "P": dense_back,
        "O": dense_out,
    }
    for action, u in SCHEDULE:
        actions[action](u)
    for u in range(count):
        for copy in finished[u]:
            copy.wait_recv()
    for copy in sends:
        copy.wait_send()


def tail(kept, packed, left_n, left_j, w_qkv, w_adapt, resid, above, gain_rows, gain_parts):
    rows, width = resid.shape
    hbm = pl.BlockSpec(memory_space=pl.ANY)
    vmem = pl.BlockSpec(memory_space=pltpu.VMEM)
    dma = pltpu.SemaphoreType.DMA
    begun, fresh = len(BEGUN), len(FRESH)
    count = begun + fresh
    heights = [kept[unit[0]].shape[1] for unit in BEGUN] + [width // 2] * 3 + [width]
    wides = [unit[3] for unit in BEGUN] + [256] * fresh
    ff = 2 * kept[1].shape[2]
    shapes = [
        (2 * width // 32, width),
        (width // 32, 3 * width),
        (width // 32, width),
        (width // 32, ff),
        (width // 32, ff),
        (ff // 32, width),
    ]
    every = list(zip(heights, wides))
    scratch = [pltpu.VMEM(value.shape[1:], BF16) for value in kept]
    scratch += [pltpu.VMEM((2, height, wide), BF16) for height, wide in every[begun:]]
    scratch += [pltpu.VMEM((height, wide), BF16) for height, wide in every]
    scratch += [pltpu.VMEM((2, 2, height // 4, wide), BF16) for height, wide in every]
    scratch += [pltpu.VMEM((2, height // 4, wide), BF16) for height, wide in every]
    scratch += [pltpu.VMEM((height // 4, wide), BF16) for height, wide in every]
    scratch += [pltpu.VMEM((height // 4, wide), F32) for height, wide in every]
    scratch += [
        pltpu.VMEM(w_qkv.shape, BF16),
        pltpu.VMEM(w_adapt.shape, BF16),
        pltpu.VMEM(packed.shape, BF16),
        pltpu.VMEM(left_n.shape, BF16),
        pltpu.VMEM(left_j.shape, BF16),
        pltpu.VMEM((4, 4, rows, 256), BF16),
        pltpu.VMEM((rows, width), BF16),
        pltpu.VMEM((2 * width, 256), F32),
        pltpu.VMEM((rows, width), F32),
        pltpu.VMEM((5, 8, width), F32),
        pltpu.VMEM((5, 8, width), F32),
    ]
    scratch += [dma((10,)), dma((3 * fresh,)), dma((3 * fresh,))]
    scratch += [dma((count,)) for _ in range(6)]
    scratch += [dma((count + 2 * fresh,)) for _ in range(2)]
    scratch += [dma((5,)) for _ in range(2)]
    return pl.pallas_call(
        tail_kernel,
        name="tail",
        out_shape=[jax.ShapeDtypeStruct((rows, width), F32)] * 2
        + [jax.ShapeDtypeStruct(shape, F32) for shape in shapes]
        + [jax.ShapeDtypeStruct((8, width), F32)],
        in_specs=[hbm] * 10 + [vmem] * 4,
        out_specs=[vmem] * 9,
        scratch_shapes=scratch,
        compiler_params=pltpu.CompilerParams(
            collective_id=3, has_side_effects=True, vmem_limit_bytes=60 << 20
        ),
    )(*kept, packed, left_n, left_j, w_qkv, w_adapt, resid, above, gain_rows, gain_parts)


def xor_permute(value, axis, mask):
    return lax.ppermute(value, axis, [(i, i ^ mask) for i in range(lax.axis_size(axis))])


def quadrants(left):
    n, parts = lax.axis_size("seq"), lax.axis_size("dp")
    tokens, rows = left.shape
    shard = rows // (n * parts)
    split = left.reshape(tokens, n, parts, shard).transpose(2, 0, 1, 3)
    split = split.reshape(parts, tokens, n * shard)
    me = lax.axis_index("dp")
    return jnp.concatenate(
        [lax.dynamic_index_in_dim(split, me ^ m, 0, keepdims=True) for m in range(parts)]
    )


def other_core(left, right):
    core = lax.axis_index("seq") % 2
    half = right.shape[1] // 2
    mine = lax.dynamic_slice_in_dim(right, core * half, half, 1)
    theirs = lax.dynamic_slice_in_dim(right, (1 - core) * half, half, 1)
    left_in = xor_permute(left, "seq", 1)
    right_in = xor_permute(theirs, "seq", 1)
    return jnp.concatenate([left, left_in], axis=1), jnp.concatenate([mine, right_in], axis=0)


def scattered_sum(left, right, bits):
    n, parts = lax.axis_size("seq"), lax.axis_size("dp")
    cols = right.shape[1]
    left, right = other_core(quadrants(left), right)
    got = {}
    masks = list(range(parts))
    for bit in bits:
        outgoing = [m for m in masks if m >> bit & 1]
        masks = [m for m in masks if not m >> bit & 1]
        blocks = []
        for m in outgoing:
            block = dot_tn(left[m], right)
            for more in got.get(m, ()):
                block = block + more.astype(F32)
            blocks.append(block.astype(BF16))
        incoming = xor_permute(jnp.stack(blocks), "dp", 1 << bit)
        for k, m in enumerate(outgoing):
            got.setdefault(m ^ (1 << bit), []).append(incoming[k])
    block = dot_tn(left[0], right)
    for more in got.get(0, ()):
        block = block + more.astype(F32)
    shard = block.shape[0] // n
    block = block.astype(BF16).reshape(n, shard, cols // 2)
    block = lax.all_to_all(block, "seq", 0, 0)
    block = jnp.sum(block.reshape(n // 2, 2, shard, cols // 2).astype(F32), axis=0)
    return block.transpose(1, 0, 2).reshape(shard, cols)


def small_sum(value):
    value = value.reshape(value.shape[0], -1, value.shape[1])
    for axis in ("seq", "dp"):
        size = lax.axis_size(axis)
        me = lax.axis_index(axis)
        for bit in reversed(range(size.bit_length() - 1)):
            half = value.shape[2] // 2
            mine = (me >> bit) & 1
            kept = lax.dynamic_slice_in_dim(value, mine * half, half, 2)
            sent = lax.dynamic_slice_in_dim(value, (1 - mine) * half, half, 2)
            value = kept + xor_permute(sent, axis, 1 << bit)
    return value[:, 0]


def local(state, embedded, cotangent, w_adapt, w_qkv, w_out, w_gate, w_up, w_down, gains):
    seq_count, rows, width = state.shape
    n, parts = lax.axis_size("seq"), lax.axis_size("dp")
    tokens = seq_count * rows
    me = lax.axis_index("seq")
    bits = list(range(parts.bit_length() - 1))
    copies = max(1, n // HEADS)
    held = max(1, HEADS // n)
    owners = n // copies
    cos_np, sin_np = angle_tables(n * rows)
    cos_all, sin_all = jnp.asarray(cos_np), jnp.asarray(sin_np)
    cos = lax.dynamic_slice_in_dim(cos_all, me * rows, rows, 0)[:, None, :]
    sin = lax.dynamic_slice_in_dim(sin_all, me * rows, rows, 0)[:, None, :]
    gain_rows = gains.astype(F32)
    state, embedded = state.reshape(tokens, width), embedded.reshape(tokens, width)

    def to_heads(flat):
        return flat.reshape(tokens, HEADS, HEAD_DIM)

    def to_owner(parts_in):
        sent = jnp.stack(parts_in).reshape(len(parts_in), tokens, owners, held, HEAD_DIM)
        sent = sent.transpose(2, 3, 0, 1, 4)
        if copies > 1:
            sent = jnp.repeat(sent, copies, axis=0)
        return lax.all_to_all(sent, "seq", 0, 0)

    def from_owner(value):
        back = lax.all_to_all(value, "seq", 0, 0)[::copies]
        back = back.reshape(HEADS, -1, tokens, HEAD_DIM)
        return back.transpose(2, 1, 0, 3).reshape(tokens, -1)

    if n == HEADS and seq_count == 1:
        resid, normed, attended, qkv, attended_t, logsum, left_n, left_j = front(
            state, embedded, w_adapt, w_qkv, gain_rows, cos[:, 0], sin[:, 0]
        )
        qkv, attended_t, logsum = qkv[:, None], attended_t[:, None], logsum[:, None]
    else:
        resid = dot(state, w_adapt[:width]) + dot(embedded, w_adapt[width:])
        normed = mean_norm(resid, gain_rows[0]).astype(BF16)
        packed = dot(normed, w_qkv)
        queries = rotate(to_heads(packed[:, :width]), cos, sin).astype(BF16)
        keys = rotate(to_heads(packed[:, width : 2 * width]), cos, sin).astype(BF16)
        values = to_heads(packed[:, 2 * width :]).astype(BF16)
        qkv = to_owner((queries, keys, values))
        attended, attended_t, logsum = attention(qkv)
        attended = from_owner(attended[:, :, None])
    branch = dot(attended, w_out)
    middle = resid + mean_norm(branch, gain_rows[1])
    normed_mid = mean_norm(middle, gain_rows[2]).astype(BF16)
    gate_pre = dot(normed_mid, w_gate)
    up_pre = dot(normed_mid, w_up)
    sigmoid_gate = jax.nn.sigmoid(gate_pre)
    silu_gate = gate_pre * sigmoid_gate
    hidden = (silu_gate * up_pre).astype(BF16)
    down_out = dot(hidden, w_down)
    layer_out = middle + mean_norm(down_out, gain_rows[3])
    out_grad = cotangent.astype(F32).reshape(tokens, width)
    down_grad, gain_grad3 = norm_back(down_out, gain_rows[3], out_grad)
    down_low = down_grad.astype(BF16)
    hidden_grad = dot_nt(down_low, w_down)
    gate_low = (
        hidden_grad * up_pre * sigmoid_gate * (1.0 + gate_pre * (1.0 - sigmoid_gate))
    ).astype(BF16)
    up_low = (hidden_grad * silu_gate).astype(BF16)
    mid_norm_grad = dot_nt(gate_low, w_gate) + dot_nt(up_low, w_up)
    middle_part, gain_grad2 = norm_back(middle, gain_rows[2], mid_norm_grad)
    middle_grad = out_grad + middle_part
    branch_grad, gain_grad1 = norm_back(branch, gain_rows[1], middle_grad)
    branch_low = branch_grad.astype(BF16)
    attended_grad = dot_nt(branch_low, w_out).astype(BF16)
    shape = (seq_count, rows, width)
    if n == HEADS and parts == 4 and seq_count == 1:
        packed_low, *kept = back(
            (hidden, normed_mid, attended),
            (down_low, gate_low, up_low, branch_low),
            attended_grad,
            qkv[:, 0],
            attended_t[:, 0],
            logsum[:, 0],
            cos_all,
            sin_all,
        )
        nothing = jnp.zeros_like(gain_grad1)
        gain_parts = jnp.stack([nothing, gain_grad1, gain_grad2, gain_grad3] + [nothing] * 4)
        grad_state, grad_embedded, *sums, gains_sum = tail(
            kept,
            packed_low,
            left_n,
            left_j,
            w_qkv,
            w_adapt,
            resid,
            middle_grad,
            gain_rows,
            gain_parts,
        )
        share = width // (n * parts)
        at = (me * parts + lax.axis_index("dp")) * share
        return (
            layer_out.reshape(shape).astype(BF16),
            grad_state.reshape(shape),
            grad_embedded.reshape(shape),
            *sums,
            lax.dynamic_slice_in_dim(gains_sum[:4], at, share, 1),
        )
    upstream = to_owner((to_heads(attended_grad),))[:, :, 0]
    packed_grad = attention_back(qkv, upstream, attended_t, logsum, cos_all, sin_all)
    packed_low = from_owner(packed_grad)
    normed_grad = dot_nt(packed_low, w_qkv)
    resid_part, gain_grad0 = norm_back(resid, gain_rows[0], normed_grad)
    resid_low = (middle_grad + resid_part).astype(BF16)
    grad_state = dot_nt(resid_low, w_adapt[:width])
    grad_embedded = dot_nt(resid_low, w_adapt[width:])
    flipped = bits[::-1]
    joined = jnp.concatenate([state, embedded], axis=-1)
    grad_down = scattered_sum(hidden, down_low, bits)
    grad_gate = scattered_sum(normed_mid, gate_low, flipped)
    grad_up = scattered_sum(normed_mid, up_low, bits)
    grad_out = scattered_sum(attended, branch_low, flipped)
    grad_qkv = scattered_sum(normed, packed_low, flipped)
    grad_adapt = scattered_sum(joined, resid_low, bits)
    grad_gains = jnp.stack([gain_grad0, gain_grad1, gain_grad2, gain_grad3])
    grad_gains = small_sum(grad_gains)
    return (
        layer_out.reshape(shape).astype(BF16),
        grad_state.reshape(shape),
        grad_embedded.reshape(shape),
        grad_adapt,
        grad_qkv,
        grad_out,
        grad_gate,
        grad_up,
        grad_down,
        grad_gains,
    )


def solution(mesh):
    tokens = P("dp", "seq", None)
    rows = P(("seq", "dp"), None)
    return jax.shard_map(
        local,
        mesh=mesh,
        in_specs=(tokens,) * 3 + (P(),) * 7,
        out_specs=(tokens,) * 3 + (rows,) * 6 + (P(None, ("seq", "dp")),),
        check_vma=False,
    )
```

```python
import functools
import math

import jax
import jax.numpy as jnp
import numpy as np
from jax import lax
from jax.experimental import pallas as pl
from jax.experimental.pallas import tpu as pltpu
from jax.sharding import PartitionSpec as P

HEADS = 8
HEAD_DIM = 128
norm_eps = 1e-06
rope_base = 50000.0
F32 = jnp.float32
BF16 = jnp.bfloat16
MESH = pl.DeviceIdType.MESH
NEG = -1e30
SCORE_SCALE = 1.0 / math.sqrt(HEAD_DIM)
LOG2E = 1.0 / math.log(2.0)


def mean_norm(values_in, gain_row):
    return (
        values_in
        * lax.rsqrt(jnp.mean(values_in * values_in, axis=-1, keepdims=True) + norm_eps)
        * gain_row
    )


def norm_back(values_in, gain_row, upstream):
    inverse = lax.rsqrt(jnp.mean(values_in * values_in, axis=-1, keepdims=True) + norm_eps)
    scaled = upstream * gain_row
    value_grad = inverse * scaled - values_in * (inverse * inverse * inverse) * jnp.mean(
        values_in * scaled, axis=-1, keepdims=True
    )
    gain_grad = jnp.sum(upstream * values_in * inverse, axis=0)
    return (value_grad, gain_grad)


def angle_tables(length):
    half_dim = HEAD_DIM // 2
    freqs = np.exp(
        np.arange(half_dim, dtype=np.float32) * np.float32(-2.0 * math.log(rope_base) / HEAD_DIM)
    ).astype(np.float32)
    angles = np.arange(length, dtype=np.float32)[:, None] * freqs[None, :]
    return np.cos(angles).astype(np.float32), np.sin(angles).astype(np.float32)


def rotate(heads_in, cos_table, sin_table):
    half_dim = heads_in.shape[-1] // 2
    lower_half = heads_in[..., :half_dim]
    upper_half = heads_in[..., half_dim:]
    return jnp.concatenate(
        [
            lower_half * cos_table - upper_half * sin_table,
            upper_half * cos_table + lower_half * sin_table,
        ],
        axis=-1,
    )


def dot(a, b):
    return lax.dot_general(a, b, (((1,), (0,)), ((), ())), preferred_element_type=F32)


def dot_tn(a, b):
    return lax.dot_general(a, b, (((0,), (0,)), ((), ())), preferred_element_type=F32)


def dot_nt(a, b):
    return lax.dot_general(a, b, (((1,), (1,)), ((), ())), preferred_element_type=F32)


def span(low, high, body, unrolled):
    if unrolled:
        for i in range(low, high):
            body(i)
    else:
        lax.fori_loop(low, high, lambda i, c: (body(i), c)[1], 0)


def causal_fill(block, fill):
    kv = lax.broadcasted_iota(jnp.int32, block.shape, 0)
    q = lax.broadcasted_iota(jnp.int32, block.shape, 1)
    return jnp.where(q >= kv, block, fill)


def attention_kernel(x_ref, o_ref, ot_ref, ls_ref, vt_ref, s_ref):
    n, hp, _, rows, _ = x_ref.shape
    unrolled = n <= 8
    factor = SCORE_SCALE * LOG2E
    for h in range(hp):
        for j in range(n):
            vt_ref[j] = x_ref[j, h, 2].astype(F32).T.astype(BF16)

        def query_block(i):
            q = x_ref[i, h, 0]
            diag = causal_fill(dot_nt(x_ref[i, h, 1], q), NEG)

            def first(j, peak):
                s = dot_nt(x_ref[j, h, 1], q)
                s_ref[j] = s
                return jnp.maximum(peak, jnp.max(s, axis=0, keepdims=True))

            peak = jnp.max(diag, axis=0, keepdims=True)
            if unrolled:
                for j in range(i):
                    peak = first(j, peak)
            else:
                peak = lax.fori_loop(0, i, first, peak)
            shift = peak * factor
            p = jnp.exp2(diag * factor - shift)
            total = jnp.sum(p, axis=0, keepdims=True)
            acc = dot(vt_ref[i], p.astype(BF16))

            def second(j, state):
                total, acc = state
                p = jnp.exp2(s_ref[j] * factor - shift)
                return (
                    total + jnp.sum(p, axis=0, keepdims=True),
                    acc + dot(vt_ref[j], p.astype(BF16)),
                )

            state = (total, acc)
            if unrolled:
                for j in range(i):
                    state = second(j, state)
            else:
                state = lax.fori_loop(0, i, second, state)
            total, acc = state
            acc = acc / total
            ot_ref[i, h] = acc
            o_ref[i, h] = acc.T.astype(BF16)
            ls_ref[i, h] = shift + jnp.log2(total)

        span(0, n, query_block, unrolled)


def attention(x):
    n, hp, _, rows, dim = x.shape
    pairs = n * (n + 1) // 2 * rows * rows * hp
    return pl.pallas_call(
        attention_kernel,
        name="attention",
        out_shape=(
            jax.ShapeDtypeStruct((n, hp, rows, dim), BF16),
            jax.ShapeDtypeStruct((n, hp, dim, rows), F32),
            jax.ShapeDtypeStruct((n, hp, 1, rows), F32),
        ),
        scratch_shapes=[
            pltpu.VMEM((n, dim, rows), BF16),
            pltpu.VMEM((n, rows, rows), F32),
        ],
        compiler_params=pltpu.CompilerParams(vmem_limit_bytes=40 << 20),
        cost_estimate=pl.CostEstimate(
            flops=pairs * dim * 8, bytes_accessed=x.size * 4, transcendentals=pairs
        ),
    )(x)


def attention_back_kernel(
    x_ref, g_ref, ot_ref, ls_ref, cos_ref, sin_ref, out_ref, kt_ref, dqt_ref, delta_ref
):
    n, hp, _, rows, _ = x_ref.shape
    unrolled = n <= 8
    factor = SCORE_SCALE * LOG2E
    for h in range(hp):
        for j in range(n):
            kt_ref[j] = x_ref[j, h, 1].astype(F32).T.astype(BF16)
            delta_ref[j] = jnp.sum(
                g_ref[j, h].astype(F32).T * ot_ref[j, h], axis=0, keepdims=True
            )

        def unrotated(value, i):
            turned = pl.ds(i * rows, rows)
            cos, sin = cos_ref[turned], sin_ref[turned]
            return rotate(value * SCORE_SCALE, cos, -sin).astype(BF16)

        def pair(i, j, diagonal):
            q, g = x_ref[i, h, 0], g_ref[i, h]
            p = jnp.exp2(dot_nt(x_ref[j, h, 1], q) * factor - ls_ref[i, h])
            if diagonal:
                p = causal_fill(p, 0.0)
            dv = dot(p.astype(BF16), g)
            ds = (p * (dot_nt(x_ref[j, h, 2], g) - delta_ref[i])).astype(BF16)
            dk = dot(ds, q)
            dqt = dot(kt_ref[j], ds)
            return dv, dk, dqt

        def key_block(j):
            dv, dk, dqt = pair(j, j, True)
            if unrolled:
                dqt_ref[j] = dqt if j == 0 else dqt_ref[j] + dqt
            else:
                dqt_ref[j] = jnp.where(j == 0, 0.0, dqt_ref[j]) + dqt

            def step(i, state):
                dv, dk = state
                v, k, t = pair(i, j, False)
                if unrolled:
                    dqt_ref[i] = t if j == 0 else dqt_ref[i] + t
                else:
                    dqt_ref[i] = jnp.where(j == 0, 0.0, dqt_ref[i]) + t
                return dv + v, dk + k

            state = (dv, dk)
            if unrolled:
                for i in range(j + 1, n):
                    state = step(i, state)
            else:
                state = lax.fori_loop(j + 1, n, step, state)
            dv, dk = state
            out_ref[j, h, 0] = unrotated(dqt_ref[j].T, j)
            out_ref[j, h, 1] = unrotated(dk, j)
            out_ref[j, h, 2] = dv.astype(BF16)

        span(0, n, key_block, unrolled)


def attention_back(x, g, ot, ls, cos, sin):
    n, hp, _, rows, dim = x.shape
    pairs = n * (n + 1) // 2 * rows * rows * hp
    return pl.pallas_call(
        attention_back_kernel,
        name="attention_back",
        out_shape=jax.ShapeDtypeStruct(x.shape, BF16),
        scratch_shapes=[
            pltpu.VMEM((n, dim, rows), BF16),
            pltpu.VMEM((n, dim, rows), F32),
            pltpu.VMEM((n, 1, rows), F32),
        ],
        compiler_params=pltpu.CompilerParams(vmem_limit_bytes=40 << 20),
        cost_estimate=pl.CostEstimate(
            flops=pairs * dim * 20, bytes_accessed=x.size * 6, transcendentals=pairs
        ),
    )(x, g, ot, ls, cos, sin)


def seq_device(index):
    return {"seq": index}


def greet(peers):
    barrier = pltpu.get_barrier_semaphore()
    for device in peers:
        pl.semaphore_signal(barrier, inc=1, device_id=device, device_id_type=MESH)


def greeted(count):
    pl.semaphore_wait(pltpu.get_barrier_semaphore(), count)


def remote(src, dst, send, recv, device):
    return pltpu.make_async_remote_copy(
        src_ref=src,
        dst_ref=dst,
        send_sem=send,
        recv_sem=recv,
        device_id=device,
        device_id_type=MESH,
    )


def front_kernel(
    state_ref,
    embedded_ref,
    wa_ref,
    wq_ref,
    gain_ref,
    cos_ref,
    sin_ref,
    resid_out,
    normed_out,
    att_out,
    x_out,
    ot_out,
    ls_out,
    ltn_out,
    ltj_out,
    wa,
    wq,
    joined,
    resid,
    normed,
    sent,
    x,
    vt,
    scores,
    ot,
    o_sent,
    att,
    ltn,
    ltj,
    load_sem,
    store_sem,
    send_sem,
    recv_sem,
    o_send_sem,
    o_recv_sem,
    l_send_sem,
    l_recv_sem,
):
    n, rows, width = HEADS, state_ref.shape[0], state_ref.shape[1]
    me = lax.axis_index("seq")
    dp = lax.axis_index("dp")
    peers = [seq_device((me + k) % n) for k in range(1, n)]
    across = [{"dp": flipped(0, dp)}, {"dp": flipped(1, dp)}]
    near = seq_device(flipped(0, me))
    greet(peers + across)
    loads = [
        pltpu.make_async_copy(state_ref, joined.at[0], load_sem.at[0]),
        pltpu.make_async_copy(wa_ref.at[pl.ds(0, width)], wa.at[0], load_sem.at[1]),
        pltpu.make_async_copy(embedded_ref, joined.at[1], load_sem.at[2]),
        pltpu.make_async_copy(wa_ref.at[pl.ds(width, width)], wa.at[1], load_sem.at[3]),
        pltpu.make_async_copy(wq_ref, wq, load_sem.at[4]),
    ]
    for copy in loads:
        copy.start()
    tile = 256
    for half in range(2):
        loads[2 * half].wait()
        loads[2 * half + 1].wait()

        for begin in range(0, width, tile):
            cols = pl.ds(begin, tile)
            block = dot(joined[half], wa[half, :, cols])
            resid[:, cols] = block if half == 0 else resid[:, cols] + block
    normed[...] = mean_norm(resid[...], gain_ref[0:1, :]).astype(BF16)
    stores = [
        pltpu.make_async_copy(resid, resid_out, store_sem.at[0]),
        pltpu.make_async_copy(normed, normed_out, store_sem.at[1]),
    ]
    for copy in stores:
        copy.start()
    loads[4].wait()
    lefts = []

    def share(source, out, slot, device):
        k = len(lefts)
        copy = remote(source, out.at[slot], l_send_sem.at[k], l_recv_sem.at[k], device)
        copy.start()
        lefts.append(copy)
    cos, sin = cos_ref[...], sin_ref[...]
    pairs = n // 2
    order = [2, 1, 3, 0] if pairs == 4 else list(range(pairs - 1, -1, -1))
    sends = []
    for k in order:
        chip = (me // 2 + k) % pairs
        for part in range(3):
            cols = pl.ds(pl.multiple_of(part * width + chip * 2 * HEAD_DIM, 2 * HEAD_DIM), 2 * HEAD_DIM)
            block = dot(normed[...], wq[:, cols])
            for core in range(2):
                head = block[:, core * HEAD_DIM : (core + 1) * HEAD_DIM]
                if part < 2:
                    head = rotate(head, cos, sin)
                sent[2 * chip + core, part] = head.astype(BF16)
        if k == order[0]:
            greeted(n + 1)
        for core in range(2):
            owner = 2 * chip + core
            if k == 0:
                continue
            copy = remote(sent.at[owner], x.at[me], send_sem.at[owner], recv_sem.at[me], seq_device(owner))
            copy.start()
            sends.append(copy)
    mate = me + 1 - 2 * (me % 2)
    copy = remote(sent.at[mate], x.at[me], send_sem.at[mate], recv_sem.at[me], seq_device(mate))
    copy.start()
    sends.append(copy)
    x[me] = sent[me]
    transposed_into(normed, ltn)
    for half in range(2):
        transposed_into(joined.at[half], ltj.at[pl.ds(half * width, width)])
    stores.append(pltpu.make_async_copy(ltn, ltn_out.at[0], store_sem.at[4]))
    stores.append(pltpu.make_async_copy(ltj, ltj_out.at[0], store_sem.at[5]))
    for copy in stores[2:]:
        copy.start()
    share(ltn, ltn_out, 2, across[0])
    share(ltn, ltn_out, 4, across[1])
    share(ltj, ltj_out, 2, across[1])
    share(ltn, ltn_out, 1, near)
    share(ltj, ltj_out, 1, near)
    factor = SCORE_SCALE * LOG2E
    for i in range(n):

        @pl.when(me != i)
        def arrive():
            remote(sent.at[0], x.at[i], send_sem.at[0], recv_sem.at[i], seq_device(i)).wait_recv()

        vt[i] = x[i, 2].astype(F32).T.astype(BF16)
        q = x[i, 0]
        diag = causal_fill(dot_nt(x[i, 1], q), NEG)
        peak = jnp.max(diag, axis=0, keepdims=True)
        for j in range(i):
            block = dot_nt(x[j, 1], q)
            scores[j] = block
            peak = jnp.maximum(peak, jnp.max(block, axis=0, keepdims=True))
        shift = peak * factor
        p = jnp.exp2(diag * factor - shift)
        total = jnp.sum(p, axis=0, keepdims=True)
        acc = dot(vt[i], p.astype(BF16))
        for j in range(i):
            p = jnp.exp2(scores[j] * factor - shift)
            total = total + jnp.sum(p, axis=0, keepdims=True)
            acc = acc + dot(vt[j], p.astype(BF16))
        acc = acc / total
        ot[i] = acc
        o_sent[i] = acc.T.astype(BF16)
        ls_out[i] = shift + jnp.log2(total)
        mine = pl.ds(pl.multiple_of(me * HEAD_DIM, HEAD_DIM), HEAD_DIM)

        @pl.when(me != i)
        def give():
            remote(o_sent.at[i], att.at[:, mine], o_send_sem.at[i], o_recv_sem.at[me], seq_device(i)).start()

        @pl.when(me == i)
        def keep():
            att[:, mine] = o_sent[i]

    stores.append(pltpu.make_async_copy(x, x_out, store_sem.at[2]))
    stores.append(pltpu.make_async_copy(ot, ot_out, store_sem.at[3]))
    for copy in stores[4:]:
        copy.start()
    for k, out, slot in ((0, ltn_out, 2), (1, ltn_out, 4), (2, ltj_out, 2)):
        lefts[k].wait_recv()
        share(out.at[slot], out, slot + 1, near)
    for copy in sends:
        copy.wait_send()
    for i in range(n):

        @pl.when(me != i)
        def finish():
            cols = pl.ds(i * HEAD_DIM, HEAD_DIM)
            copy = remote(o_sent.at[i], att.at[:, cols], o_send_sem.at[i], o_recv_sem.at[i], seq_device(i))
            copy.wait_send()
            copy.wait_recv()

    att_out[...] = att[...]
    for copy in stores:
        copy.wait()
    for k, copy in enumerate(lefts):
        copy.wait_send()
        if k > 2:
            copy.wait_recv()


def front(state, embedded, w_adapt, w_qkv, gain_rows, cos, sin):
    n = HEADS
    rows, width = state.shape
    hbm = pl.BlockSpec(memory_space=pl.ANY)
    vmem = pl.BlockSpec(memory_space=pltpu.VMEM)
    return pl.pallas_call(
        front_kernel,
        name="front",
        out_shape=(
            jax.ShapeDtypeStruct((rows, width), F32),
            jax.ShapeDtypeStruct((rows, width), BF16),
            jax.ShapeDtypeStruct((rows, width), BF16),
            jax.ShapeDtypeStruct((n, 3, rows, HEAD_DIM), BF16),
            jax.ShapeDtypeStruct((n, HEAD_DIM, rows), F32),
            jax.ShapeDtypeStruct((n, 1, rows), F32),
            jax.ShapeDtypeStruct((6, width, rows), BF16),
            jax.ShapeDtypeStruct((4, 2 * width, rows), BF16),
        ),
        in_specs=[hbm, hbm, hbm, hbm, vmem, vmem, vmem],
        out_specs=(hbm, hbm, vmem, hbm, hbm, vmem, hbm, hbm),
        scratch_shapes=[
            pltpu.VMEM((2, width, width), BF16),
            pltpu.VMEM((width, 3 * width), BF16),
            pltpu.VMEM((2, rows, width), BF16),
            pltpu.VMEM((rows, width), F32),
            pltpu.VMEM((rows, width), BF16),
            pltpu.VMEM((n, 3, rows, HEAD_DIM), BF16),
            pltpu.VMEM((n, 3, rows, HEAD_DIM), BF16),
            pltpu.VMEM((n, HEAD_DIM, rows), BF16),
            pltpu.VMEM((n, rows, rows), F32),
            pltpu.VMEM((n, HEAD_DIM, rows), F32),
            pltpu.VMEM((n, rows, HEAD_DIM), BF16),
            pltpu.VMEM((rows, width), BF16),
            pltpu.VMEM((width, rows), BF16),
            pltpu.VMEM((2 * width, rows), BF16),
            pltpu.SemaphoreType.DMA((5,)),
            pltpu.SemaphoreType.DMA((6,)),
            pltpu.SemaphoreType.DMA((n,)),
            pltpu.SemaphoreType.DMA((n,)),
            pltpu.SemaphoreType.DMA((n,)),
            pltpu.SemaphoreType.DMA((n,)),
            pltpu.SemaphoreType.DMA((8,)),
            pltpu.SemaphoreType.DMA((8,)),
        ],
        compiler_params=pltpu.CompilerParams(
            collective_id=1, has_side_effects=True, vmem_limit_bytes=48 << 20
        ),
    )(state, embedded, w_adapt, w_qkv, gain_rows, cos, sin)


def flipped(bit, value):
    return value + (1 - 2 * ((value // (1 << bit)) % 2)) * (1 << bit)


def unit_slots(first, dp):
    slots = []
    for q in range(4):
        turned = [(dp + q) % 2, (dp // 2 + q // 2) % 2]
        slots.append(turned[first] * 2 + turned[1 - first])
    return slots


def transposed_into(source, target):
    tile = 256
    for begin in range(0, source.shape[1], tile):
        target[pl.ds(begin, tile), :] = source[:, pl.ds(begin, tile)].T


def add_into(target, more):
    rows = target.shape[0]
    chunk = 16
    while rows % (chunk * 2) == 0 and chunk < 64:
        chunk *= 2

    def step(t, c):
        at = pl.ds(pl.multiple_of(t * chunk, chunk), chunk)
        target[at, :] = (target[at, :].astype(F32) + more[at, :].astype(F32)).astype(BF16)
        return c

    lax.fori_loop(0, rows // chunk, step, 0)


CHUNKS = ((0, 512), (512, 512), (1024, 384))


def z_place(z):
    return (z % 2) * 2 + z // 2


def transposed_blocks(source, target):
    tile = 256
    parts, size = target.shape[1], target.shape[2]
    for begin in range(0, source.shape[1], tile):
        block = source[:, pl.ds(begin, tile)].T
        for k in range(begin // size, (begin + tile - 1) // size + 1):
            low, high = max(begin, size * k), min(begin + tile, size * (k + 1))
            target[k // parts, k % parts, pl.ds(low - size * k, high - low), :] = block[
                low - begin : high - begin
            ]


def middle_kernel(*refs):
    refs = list(refs)

    def take(count):
        taken, refs[:count] = refs[:count], []
        return taken

    (att_in, resid_in, cot_in, gain_rows, wo_in, wg_in, wu_in, wd_in) = take(8)
    (x_in, ot_in, ls_ref, table_in) = take(4)
    (layer_out, above_out, gains_out, packed_out) = take(4)
    (kept_d, kept_g, kept_o) = take(3)
    (wo, wg, wu, wd, att, cot, resid, branch, mid, down) = take(10)
    (normed, hidden, gate_by, up_by, down_low, wide_low, branch_low, dout) = take(8)
    (left_n, left_h, left_m, left_a, right_g, right_d, right_b) = take(7)
    (got_g, got_d) = take(2)
    (work, x, ot, table, g, kt, dqt, delta, dsent, packed) = take(10)
    (load_sem, store_sem, g_send, g_recv, d_send, d_recv, m_send, m_recv, s_send, s_recv) = take(10)
    n, (rows, width) = HEADS, resid.shape
    ff = wg.shape[1]
    half, part = ff // 2, width // 2
    me = lax.axis_index("seq")
    dp = lax.axis_index("dp")
    core = me % 2
    mate = flipped(0, me)
    bits = [dp % 2, dp // 2]
    near = seq_device(mate)
    across = [{"dp": flipped(0, dp)}, {"dp": flipped(1, dp)}]
    diagonal = [{"seq": mate, "dp": flipped(0, dp)}, {"seq": mate, "dp": flipped(1, dp)}]
    greet([seq_device((me + k) % n) for k in range(1, n)] + across + diagonal)
    loads = {}
    for key, src, dst in (
        ("att", att_in, att),
        ("wo", wo_in, wo),
        ("resid", resid_in, resid),
        ("wg", wg_in, wg),
        ("wu", wu_in, wu),
        ("cot", cot_in, cot),
        ("wd", wd_in, wd),
        ("x", x_in, x),
        ("ot", ot_in, ot),
        ("table", table_in, table),
    ):
        copy = pltpu.make_async_copy(src, dst, load_sem.at[len(loads)])
        copy.start()
        loads[key] = copy
    tile = 256

    def tiles(total, body):
        for begin in range(0, total, tile):
            body(pl.ds(begin, tile))

    sends = []
    given = {}

    issued = []

    def give(key, src, dst, device):
        k = len(issued)
        copy = remote(src, dst, m_send.at[k], m_recv.at[k], device)
        copy.start()
        issued.append(key)
        sends.append(copy)
        given[key] = copy

    loads["att"].wait()
    loads["wo"].wait()

    def project(cols):
        branch[:, cols] = dot(att[...], wo[:, cols])

    tiles(width, project)
    loads["resid"].wait()
    mid[...] = resid[...] + mean_norm(branch[...], gain_rows[1:2, :])
    normed[...] = mean_norm(mid[...], gain_rows[2:3, :]).astype(BF16)
    transposed_into(normed, left_n.at[0])
    greeted(n + 3)
    give("n1", left_n.at[0], left_n.at[1], near)
    give("n2", left_n.at[0], left_n.at[2], across[0])
    loads["wg"].wait()
    loads["wu"].wait()

    def widen(cols):
        gate = dot(normed[...], wg[:, cols])
        up = dot(normed[...], wu[:, cols])
        bent = jax.nn.sigmoid(gate)
        silu = gate * bent
        hidden[:, cols] = (silu * up).astype(BF16)
        gate_by[:, cols] = (up * bent * (1.0 + gate * (1.0 - bent))).astype(BF16)
        up_by[:, cols] = silu.astype(BF16)

    tiles(ff, widen)
    loads["wd"].wait()

    def narrow(cols):
        down[:, cols] = dot(hidden[...], wd[:, cols])

    tiles(width, narrow)
    loads["cot"].wait()
    layer_out[...] = (mid[...] + mean_norm(down[...], gain_rows[3:4, :])).astype(BF16)
    grad, gain3 = norm_back(down[...], gain_rows[3:4, :], cot[...].astype(F32))
    down_low[...] = grad.astype(BF16)
    mine_d = pl.ds(pl.multiple_of(core * part, 128), part)
    theirs_d = pl.ds(pl.multiple_of((1 - core) * part, 128), part)
    give("d2", down_low.at[:, mine_d], right_d.at[1], across[1])
    give("d3", down_low.at[:, theirs_d], right_d.at[2], diagonal[1])
    give("d1", down_low.at[:, theirs_d], right_d.at[0], near)

    def widen_back(cols):
        block = dot_nt(down_low[...], wd[cols, :])
        wide_low[0, :, cols] = (block * gate_by[:, cols].astype(F32)).astype(BF16)
        wide_low[1, :, cols] = (block * up_by[:, cols].astype(F32)).astype(BF16)

    tiles(ff, widen_back)

    def chunk_of(c, which_core, which_bit):
        at, wide = CHUNKS[c]
        return wide_low.at[which_core, :, pl.ds(pl.multiple_of(which_bit * half + at, 128), wide)]

    for c, (at, wide) in enumerate(CHUNKS):
        cols = pl.ds(at, wide)
        give(("g2", c), chunk_of(c, core, 1 - bits[0]), right_g.at[1, :, cols], across[0])
        give(("g3", c), chunk_of(c, 1 - core, 1 - bits[0]), right_g.at[2, :, cols], diagonal[0])
        give(("g1", c), chunk_of(c, 1 - core, bits[0]), right_g.at[0, :, cols], near)

    def narrow_back(cols):
        down[:, cols] = dot_nt(wide_low[0], wg[cols, :]) + dot_nt(wide_low[1], wu[cols, :])

    tiles(width, narrow_back)
    grad, gain2 = norm_back(mid[...], gain_rows[2:3, :], down[...])
    resid[...] = cot[...].astype(F32) + grad
    grad, gain1 = norm_back(branch[...], gain_rows[1:2, :], resid[...])
    branch_low[...] = grad.astype(BF16)

    def project_back(cols):
        dout[:, cols] = dot_nt(branch_low[...], wo[cols, :]).astype(BF16)

    tiles(width, project_back)
    my_cols = pl.ds(pl.multiple_of(me * HEAD_DIM, HEAD_DIM), HEAD_DIM)
    for k in (4, 5, 3, 2, 6, 7, 1):
        owner = (me + k) % n
        cols = pl.ds(pl.multiple_of(owner * HEAD_DIM, HEAD_DIM), HEAD_DIM)
        copy = remote(dout.at[:, cols], g.at[me], g_send.at[owner], g_recv.at[me], seq_device(owner))
        copy.start()
        sends.append(copy)
    g[me] = dout[:, my_cols]
    transposed_blocks(hidden, left_h)
    give("h2", left_h.at[:, 1 - bits[1]], left_m.at[1], across[1])
    give("h1", left_h.at[:, bits[1]], left_m.at[0], near)
    given["n2"].wait_recv()
    give("n3", left_n.at[2], left_n.at[3], near)
    transposed_into(att, left_a.at[0])
    give("a1", left_a.at[0], left_a.at[1], near)
    give("b1", branch_low.at[:, theirs_d], right_b, near)
    stores = []

    def store(src, dst):
        copy = pltpu.make_async_copy(src, dst, store_sem.at[len(stores)])
        copy.start()
        stores.append(copy)

    store(resid, above_out)
    gains_out[...] = jnp.zeros_like(gains_out)
    gains_out[1:2, :] = gain1[None, :]
    gains_out[2:3, :] = gain2[None, :]
    gains_out[3:4, :] = gain3[None, :]
    seconds = {}

    def wide_sum(c):
        at, wide = CHUNKS[c]
        for key in ("n1", "n3"):
            if key in given:
                given.pop(key).wait_recv()
        for key in ("g1", "g2", "g3"):
            given[key, c].wait_recv()
        shard = width // 32
        spread = [(bits[1] + other) % 2 for other in range(2)]
        own = chunk_of(c, core, bits[0])
        for begin in range(0, wide, 256):
            step = min(256, wide - begin)
            cols = pl.ds(at + begin, step)
            block = dot(left_n[0], own[:, pl.ds(begin, step)])
            for k in range(1, 4):
                block += dot(left_n[k], right_g[k - 1, :, cols])
            work[0:width, 0:step] = block
            for z in range(4):
                for other in range(2):
                    pieces = [
                        work[pl.ds((8 * z + 4 * c2 + 2 * other + b) * shard, shard), 0:step]
                        for c2 in range(2)
                        for b in range(2)
                    ]
                    place = pl.multiple_of(spread[other] * part + z_place(z) * 4 * shard, 16)
                    wg[pl.ds(place, 4 * shard), cols] = jnp.concatenate(pieces, axis=0).astype(BF16)
        cols = pl.ds(at, wide)
        seconds[c] = remote(
            wg.at[pl.ds(part, part), cols], got_g.at[:, cols], s_send.at[c], s_recv.at[c], across[1]
        )
        seconds[c].start()
        sends.append(seconds[c])

    def down_sum():
        for key in ("h1", "h3", "d1", "d2", "d3"):
            given[key].wait_recv()
        tall = ff // 4
        shard = ff // 32
        spread = [(bits[0] + other) % 2 for other in range(2)]
        for begin in range(0, part, 256):
            cols = pl.ds(begin, 256)
            own = down_low.at[:, mine_d]
            block = dot(left_h[:, bits[1]].reshape(2 * tall, rows), own[:, cols])
            for k in range(3):
                block += dot(left_m[k].reshape(2 * tall, rows), right_d[k, :, cols])
            work[...] = block
            for z in range(4):
                for other in range(2):
                    pieces = [
                        work[pl.ds((4 * z + 2 * c2 + other) * shard, shard), :] for c2 in range(2)
                    ]
                    place = pl.multiple_of(spread[other] * tall + z_place(z) * 2 * shard, 16)
                    wd[pl.ds(place, 2 * shard), cols] = jnp.concatenate(pieces, axis=0).astype(BF16)
        cols = pl.ds(0, part)
        seconds["d"] = remote(
            wd.at[pl.ds(tall, tall), cols], got_d, s_send.at[3], s_recv.at[3], across[0]
        )
        seconds["d"].start()
        sends.append(seconds["d"])

    def out_sum():
        given["a1"].wait_recv()
        given["b1"].wait_recv()
        shard = width // 32
        slots = unit_slots(0, dp)
        for begin in range(0, part, 256):
            cols = pl.ds(begin, 256)
            block = dot(left_a[0], branch_low.at[:, mine_d][:, cols])
            work[0:width, :] = block + dot(left_a[1], right_b[:, cols])
            for z in range(4):
                for q in range(4):
                    pieces = [
                        work[pl.ds((8 * z + 4 * c2 + q) * shard, shard), :] for c2 in range(2)
                    ]
                    place = pl.multiple_of(slots[q] * (width // 4) + z_place(z) * 2 * shard, 16)
                    wu[pl.ds(place, 2 * shard), cols] = jnp.concatenate(pieces, axis=0).astype(BF16)
        store(wu.at[:, pl.ds(0, part)], kept_o)

    wide_sum(0)
    loads["x"].wait()
    loads["ot"].wait()
    loads["table"].wait()
    for i in range(n):

        @pl.when(me != i)
        def arrive():
            remote(g.at[0], g.at[i], g_send.at[0], g_recv.at[i], seq_device(i)).wait_recv()

    factor = SCORE_SCALE * LOG2E
    half_dim = HEAD_DIM // 2
    for j in range(n):
        kt[j] = x[j, 1].astype(F32).T.astype(BF16)
        delta[j] = jnp.sum(g[j].astype(F32).T * ot[j], axis=0, keepdims=True)
    for j in range(n):
        dk = dv = None
        for i in range(j, n):
            q, up = x[i, 0], g[i]
            p = jnp.exp2(dot_nt(x[j, 1], q) * factor - ls_ref[i])
            if i == j:
                p = causal_fill(p, 0.0)
            v = dot(p.astype(BF16), up)
            ds = (p * (dot_nt(x[j, 2], up) - delta[i])).astype(BF16)
            k = dot(ds, q)
            t = dot(kt[j], ds)
            dqt[i] = t if j == 0 else dqt[i] + t
            dv, dk = (v, k) if i == j else (dv + v, dk + k)
        here = pl.ds(j * rows, rows)
        cos, sin = table[here, 0:half_dim], -table[here, half_dim:HEAD_DIM]
        dsent[j, 0] = rotate(dqt[j].T * SCORE_SCALE, cos, sin).astype(BF16)
        dsent[j, 1] = rotate(dk * SCORE_SCALE, cos, sin).astype(BF16)
        dsent[j, 2] = dv.astype(BF16)

        @pl.when(me != j)
        def give_head():
            remote(dsent.at[j], packed.at[:, :, my_cols], d_send.at[j], d_recv.at[me], seq_device(j)).start()

        @pl.when(me == j)
        def keep_head():
            packed[:, :, my_cols] = dsent[j]

    wide_sum(1)
    given["h2"].wait_recv()
    give("h3", left_m.at[1], left_m.at[2], near)
    wide_sum(2)
    down_sum()
    out_sum()

    def finish_wide(c):
        at, wide = CHUNKS[c]
        cols = pl.ds(at, wide)
        seconds[c].wait_recv()
        add_into(wg.at[pl.ds(0, part), cols], got_g.at[:, cols])
        store(wg.at[pl.ds(0, part), cols], kept_g.at[:, cols])

    finish_wide(0)
    finish_wide(1)
    seconds["d"].wait_recv()
    mine = wd.at[pl.ds(0, ff // 4), pl.ds(0, part)]
    add_into(mine, got_d)
    store(mine, kept_d)
    for j in range(n):

        @pl.when(me != j)
        def finish():
            cols = pl.ds(j * HEAD_DIM, HEAD_DIM)
            copy = remote(dsent.at[j], packed.at[:, :, cols], d_send.at[j], d_recv.at[j], seq_device(j))
            copy.wait_send()
            copy.wait_recv()

    store(packed, packed_out)
    finish_wide(2)
    for copy in sends:
        copy.wait_send()
    for copy in stores:
        copy.wait()


def middle_block(att, resid, cot, gain_rows, w_out, w_gate, w_up, w_down, x, ot, ls, table):
    n = HEADS
    rows, width = resid.shape
    ff = w_gate.shape[1]
    half, part = ff // 2, width // 2
    hbm = pl.BlockSpec(memory_space=pl.ANY)
    vmem = pl.BlockSpec(memory_space=pltpu.VMEM)
    dma = pltpu.SemaphoreType.DMA
    low = pltpu.VMEM((rows, width), BF16)
    wide = pltpu.VMEM((rows, ff), BF16)
    full = pltpu.VMEM((rows, width), F32)
    scratch = [pltpu.VMEM(w.shape, BF16) for w in (w_out, w_gate, w_up, w_down)]
    scratch += [low, low, full, full, full, full]
    scratch += [low, wide, wide, wide, low, pltpu.VMEM((2, rows, ff), BF16), low, low]
    scratch += [
        pltpu.VMEM((4, width, rows), BF16),
        pltpu.VMEM((8, 2, ff // 16, rows), BF16),
        pltpu.VMEM((3, 8, ff // 16, rows), BF16),
        pltpu.VMEM((2, width, rows), BF16),
        pltpu.VMEM((3, rows, half), BF16),
        pltpu.VMEM((3, rows, part), BF16),
        pltpu.VMEM((rows, part), BF16),
        pltpu.VMEM((part, half), BF16),
        pltpu.VMEM((ff // 4, part), BF16),
        pltpu.VMEM((half, 256), F32),
        pltpu.VMEM(x.shape, BF16),
        pltpu.VMEM(ot.shape, F32),
        pltpu.VMEM(table.shape, F32),
        pltpu.VMEM((n, rows, HEAD_DIM), BF16),
        pltpu.VMEM((n, HEAD_DIM, rows), BF16),
        pltpu.VMEM((n, HEAD_DIM, rows), F32),
        pltpu.VMEM((n, 1, rows), F32),
        pltpu.VMEM((n, 3, rows, HEAD_DIM), BF16),
        pltpu.VMEM((3, rows, width), BF16),
        dma((10,)),
        dma((7,)),
        dma((n,)),
        dma((n,)),
        dma((n,)),
        dma((n,)),
        dma((20,)),
        dma((20,)),
        dma((4,)),
        dma((4,)),
    ]
    return pl.pallas_call(
        middle_kernel,
        name="middle",
        out_shape=[
            jax.ShapeDtypeStruct((rows, width), BF16),
            jax.ShapeDtypeStruct((rows, width), F32),
            jax.ShapeDtypeStruct((8, width), F32),
            jax.ShapeDtypeStruct((3, rows, width), BF16),
            jax.ShapeDtypeStruct((ff // 4, part), BF16),
            jax.ShapeDtypeStruct((part, half), BF16),
            jax.ShapeDtypeStruct((width, part), BF16),
        ],
        in_specs=[hbm] * 3 + [vmem] + [hbm] * 6 + [vmem] + [hbm],
        out_specs=[vmem, hbm, vmem, hbm] + [hbm] * 3,
        scratch_shapes=scratch,
        compiler_params=pltpu.CompilerParams(
            collective_id=2, has_side_effects=True, vmem_limit_bytes=62 << 20
        ),
    )(att, resid, cot, gain_rows, w_out, w_gate, w_up, w_down, x, ot, ls, table)


BEGUN = ((0, 0, 256), (0, 256, 256), (1, 0, 512), (1, 512, 512), (1, 1024, 384))
FRESH = ((1, 0, 0), (1, 1024, 0), (1, 2048, 1), (0, 0, 1))
SCHEDULE = (
    ("1", 1), ("1", 4), ("F", 5), ("U", 6), ("U", 8), ("P", 0), ("1", 3), ("U", 9),
    ("O", 0), ("W", 8), ("D", 1), ("2", 1), ("U", 7), ("1", 0), ("B", 5), ("S", 5),
    ("D", 4), ("2", 4), ("W", 9), ("E", 1), ("G", 0), ("S", 9), ("W", 6), ("S", 6),
    ("1", 2), ("C", 5), ("E", 4), ("D", 3), ("G", 1), ("2", 3), ("S", 8), ("1", 5),
    ("W", 7), ("S", 7), ("D", 0), ("2", 0), ("C", 6), ("E", 3), ("G", 2), ("1", 6),
    ("E", 0), ("C", 7), ("D", 2), ("G", 3), ("2", 2), ("C", 9), ("1", 9), ("D", 5),
    ("2", 5), ("1", 7), ("C", 8), ("G", 4), ("E", 2), ("D", 6), ("2", 6), ("E", 5),
    ("E", 6), ("1", 8), ("D", 9), ("2", 9), ("D", 7), ("2", 7), ("E", 9), ("D", 8),
    ("2", 8), ("E", 7), ("E", 8),
)


def dealt_blocks(left, slots, right, spread, bit, out, work):
    total = left.shape[1]
    shard = total // 32
    block = dot(left[slots[0]], right[0])
    for k in range(1, 4):
        block += dot(left[slots[k]], right[k])
    work[0:total, :] = block
    for z in range(4):
        for other in range(2):
            pieces = []
            for core in range(2):
                for b in range(2):
                    q = (b << bit) | (other << (1 - bit))
                    pieces.append(work[pl.ds((8 * z + 4 * core + q) * shard, shard), :])
            out[spread[other], pl.ds(z_place(z) * 4 * shard, 4 * shard), :] = jnp.concatenate(
                pieces, axis=0
            ).astype(BF16)


def tail_kernel(*refs):
    refs = list(refs)

    def take(count):
        taken, refs[:count] = refs[:count], []
        return taken

    begun, fresh = len(BEGUN), len(FRESH)
    single = begun
    first_fresh = begun + 1
    count = first_fresh + fresh
    kept_in = take(3)
    packed_in, ltn_in, ltj_in, wq_in, wa_in = take(5)
    resid, above, gain_rows, gain_parts = take(4)
    grad_joined = take(2)
    outs = take(5)
    (gains_out,) = take(1)
    held = take(2)
    sums, arrived2 = take(1 + fresh), take(1 + fresh)
    parts, arrived3, arrived4, finals = take(count), take(count), take(count), take(count)
    (got_o, wq, wa, packed, ltn, ltj, dealt, low, work, back_sum, gain_buf, gain_got) = take(12)
    (load_sem, u_send, u_recv, s_send, s_recv, z1_send, z1_recv) = take(7)
    (z2_send, z2_recv, c_send, c_recv, gain_send, gain_recv) = take(6)
    rows, width = resid.shape
    me = lax.axis_index("seq")
    dp = lax.axis_index("dp")
    core = me % 2
    bits = [dp % 2, dp // 2]
    z_low, z_high = (me // 2) % 2, me // 4
    mate = flipped(0, me)
    near = seq_device(mate)
    across = [{"dp": flipped(0, dp)}, {"dp": flipped(1, dp)}]
    diagonal = [{"seq": mate, "dp": flipped(0, dp)}, {"seq": mate, "dp": flipped(1, dp)}]
    beside = [seq_device(flipped(1, me)), seq_device(flipped(2, me))]
    greet([near] + across + diagonal + beside)
    loads = {}

    def load(key, src, dst):
        loads[key] = pltpu.make_async_copy(src, dst, load_sem.at[len(loads)])
        loads[key].start()

    load("packed", packed_in, packed)
    load("wq", wq_in, wq)
    greeted(7)
    sends = []

    def send(src, dst, send_sem, recv_sem, device):
        copy = remote(src, dst, send_sem, recv_sem, device)
        copy.start()
        sends.append(copy)
        return copy

    first, dealing, second, third, fourth, finished, taken = [], {}, {}, {}, {}, {}, set()

    def ready(key):
        if key not in taken:
            taken.add(key)
            loads[key].wait()

    def z_rows(u, which):
        tall = finals[u].shape[0]
        return pl.ds(pl.multiple_of(which * 2 * tall, 16), 2 * tall)

    def one_z(u, which):
        tall = finals[u].shape[0]
        return pl.ds(pl.multiple_of(which * tall, 16), tall)

    def start_first(u):
        first.append(send(kept_in[2].at[pl.ds(2, 2)], got_o, s_send.at[count], s_recv.at[count], across[0]))

    def take_first(u):
        first[0].wait_recv()
        ready("out")
        for k in (1, 0):
            add_into(sums[0].at[k], got_o.at[k])

    def start_columns(u):
        k = u - first_fresh
        bit = FRESH[k][2]
        source = low if k == 3 else packed.at[k]
        if k < 3:
            ready("packed")

        def columns(other_core, other_bit):
            place = (core + (1 - 2 * core) * other_core) * 2
            place = place + bits[bit] + (1 - 2 * bits[bit]) * other_bit
            return pl.ds(pl.multiple_of(place * 256, 256), 256)

        dealing[u] = [
            send(
                source.at[:, columns(*there)],
                dealt.at[k, slot],
                u_send.at[3 * k + slot - 1],
                u_recv.at[3 * k + slot - 1],
                device,
            )
            for there, slot, device in (
                ((0, 1), 2, across[bit]),
                ((1, 1), 3, diagonal[bit]),
                ((1, 0), 1, near),
            )
        ]
        dealt[k, 0] = source[:, columns(0, 0)]

    def start_second(u):
        k = u - single
        bit = 1 if k == 0 else 1 - FRESH[k - 1][2]
        second[u] = send(sums[k].at[1], arrived2[k], s_send.at[u], s_recv.at[u], across[bit])

    def multiply(u):
        k = u - first_fresh
        out, column, bit = FRESH[k]
        slots = (0, 1, 2, 3) if (bit == 0 or k == 3) else (0, 1, 4, 5)
        left = ltj if k == 3 else ltn
        ready("ltj" if k == 3 else "ltn")
        for copy in dealing[u]:
            copy.wait_recv()
        spread = [(bits[1 - bit] + other) % 2 for other in range(2)]
        dealt_blocks(left, slots, dealt.at[k], spread, bit, sums[1 + k], work)

    def take_second(u):
        second[u].wait_recv()
        add_into(sums[u - single].at[0], arrived2[u - single])

    def start_third(u):
        theirs = z_rows(u, 1 - z_low)
        if u < begun:
            array, at, wide = BEGUN[u]
            src = kept_in[array].at[theirs, pl.ds(at, wide)]
        else:
            src = sums[u - single].at[0, theirs]
        third[u] = send(src, arrived3[u], z1_send.at[u], z1_recv.at[u], beside[0])

    def take_third(u):
        third[u].wait_recv()
        if u < begun:
            array, at, wide = BEGUN[u]
            ready(array)
            mine = held[array][:, pl.ds(at, wide)]
        else:
            mine = sums[u - single][0, z_rows(u, z_low), :]
        parts[u][...] = (mine.astype(F32) + arrived3[u][...].astype(F32)).astype(BF16)

    def start_fourth(u):
        fourth[u] = send(
            parts[u].at[one_z(u, 1 - z_high)], arrived4[u], z2_send.at[u], z2_recv.at[u], beside[1]
        )

    def take_fourth(u):
        fourth[u].wait_recv()
        finals[u][...] = parts[u][one_z(u, z_high), :].astype(F32) + arrived4[u][...].astype(F32)
        if u < begun and BEGUN[u][0] == 1:
            at, wide = BEGUN[u][1:]
            bit = 0
            cols = pl.ds(pl.multiple_of(bits[0] * (outs[3].shape[2] // 2) + at, 128), wide)
            target = outs[3].at[core, :, cols]
        elif u <= single:
            out, at, wide = (2, 0, width // 2) if u == single else (4,) + BEGUN[u][1:]
            bit = None
            target = outs[out].at[:, pl.ds(pl.multiple_of(core * (width // 2) + at, 128), wide)]
        else:
            out, column, bit = FRESH[u - first_fresh]
            cols = pl.ds(pl.multiple_of((core * 2 + bits[bit]) * 256 + column, 256), 256)
            target = outs[out].at[:, cols]
        if bit is None:
            owners = [(core, None), (1 - core, near)]
        else:
            here, there = bits[bit], 1 - bits[bit]
            owners = [
                (core * 2 + here, None),
                ((1 - core) * 2 + here, near),
                (core * 2 + there, across[bit]),
                ((1 - core) * 2 + there, diagonal[bit]),
            ]
        shard = finals[u].shape[0] // len(owners)
        finished[u] = []
        for k, (place, device) in enumerate(owners):
            at = pl.ds(pl.multiple_of(place * shard, 8), shard)
            if k == 0:
                target[...] = finals[u][at, :]
            else:
                sem = 3 * u + k - 1
                finished[u].append(
                    send(finals[u].at[at], target, c_send.at[sem], c_recv.at[sem], device)
                )

    gain_steps = {}
    gain_partners = [near] + across + beside

    def send_gain(k):
        gain_steps[k] = send(
            gain_buf.at[k], gain_got.at[k], gain_send.at[k], gain_recv.at[k], gain_partners[k]
        )

    def add_gain(k):
        gain_steps[k].wait_recv()
        total = gain_buf[k] + gain_got[k]
        if k == 4:
            gains_out[...] = total
        else:
            gain_buf[k + 1] = total
            send_gain(k + 1)

    tile = 256

    def dense_back(_):
        ready("packed")
        ready("wq")
        for array in (0, 1):
            tall = 2 * finals[0 if array == 0 else 2].shape[0]
            mine = pl.ds(pl.multiple_of(z_low * tall, 16), tall)
            load(array, kept_in[array].at[mine], held[array])
        load("out", kept_in[2].at[pl.ds(0, 2)], sums[0])
        load("ltn", ltn_in, ltn)
        load("ltj", ltj_in, ltj)
        load("wa", wa_in, wa)
        for begin in range(0, width, tile):
            at = pl.ds(begin, tile)
            block = dot_nt(packed[0], wq[at, pl.ds(0, width)])
            block += dot_nt(packed[1], wq[at, pl.ds(width, width)])
            block += dot_nt(packed[2], wq[at, pl.ds(2 * width, width)])
            back_sum[:, at] = block
        part, gain0 = norm_back(resid[...], gain_rows[0:1, :], back_sum[...])
        low[...] = (above[...] + part).astype(BF16)
        gain_buf[0] = gain_parts[...]
        gain_buf[0, 0:1, :] = gain0[None, :]
        send_gain(0)

    def dense_out(_):
        ready("wa")
        for k in range(2):
            for begin in range(0, width, tile):
                from_row = pl.ds(k * width + begin, tile)
                grad_joined[k][:, pl.ds(begin, tile)] = dot_nt(low[...], wa[from_row, :])

    actions = {
        "F": start_first,
        "B": take_first,
        "U": start_columns,
        "S": start_second,
        "1": start_third,
        "2": start_fourth,
        "W": multiply,
        "C": take_second,
        "D": take_third,
        "E": take_fourth,
        "G": add_gain,
        "P": dense_back,
        "O": dense_out,
    }
    for action, u in SCHEDULE:
        actions[action](u)
    for u in range(count):
        for copy in finished[u]:
            copy.wait_recv()
    for copy in sends:
        copy.wait_send()


def tail(kept, packed, left_n, left_j, w_qkv, w_adapt, resid, above, gain_rows, gain_parts):
    rows, width = resid.shape
    hbm = pl.BlockSpec(memory_space=pl.ANY)
    vmem = pl.BlockSpec(memory_space=pltpu.VMEM)
    dma = pltpu.SemaphoreType.DMA
    fresh = len(FRESH)
    down, gate, out = kept
    every = [(kept[array].shape[0] // 4, wide) for array, _, wide in BEGUN]
    every += [(out.shape[1] // 4, out.shape[2])]
    every += [(width // 8, 256)] * 3 + [(width // 4, 256)]
    count = len(every)
    halved = every[len(BEGUN) :]
    shapes = [
        (2 * width // 32, width),
        (width // 32, 3 * width),
        (width // 32, width),
        (2, width // 32, 2 * gate.shape[1]),
        (gate.shape[1] // 16, width),
    ]
    scratch = [pltpu.VMEM((down.shape[0] // 2, down.shape[1]), BF16)]
    scratch += [pltpu.VMEM((gate.shape[0] // 2, gate.shape[1]), BF16)]
    scratch += [pltpu.VMEM((2, 4 * tall, wide), BF16) for tall, wide in halved]
    scratch += [pltpu.VMEM((4 * tall, wide), BF16) for tall, wide in halved]
    scratch += [pltpu.VMEM((2 * tall, wide), BF16) for tall, wide in every]
    scratch += [pltpu.VMEM((2 * tall, wide), BF16) for tall, wide in every]
    scratch += [pltpu.VMEM((tall, wide), BF16) for tall, wide in every]
    scratch += [pltpu.VMEM((tall, wide), F32) for tall, wide in every]
    scratch += [
        pltpu.VMEM((2,) + out.shape[1:], BF16),
        pltpu.VMEM(w_qkv.shape, BF16),
        pltpu.VMEM(w_adapt.shape, BF16),
        pltpu.VMEM(packed.shape, BF16),
        pltpu.VMEM(left_n.shape, BF16),
        pltpu.VMEM(left_j.shape, BF16),
        pltpu.VMEM((4, 4, rows, 256), BF16),
        pltpu.VMEM((rows, width), BF16),
        pltpu.VMEM((2 * width, 256), F32),
        pltpu.VMEM((rows, width), F32),
        pltpu.VMEM((5, 8, width), F32),
        pltpu.VMEM((5, 8, width), F32),
    ]
    scratch += [dma((8,)), dma((3 * fresh,)), dma((3 * fresh,))]
    scratch += [dma((count + 1,)) for _ in range(2)]
    scratch += [dma((count,)) for _ in range(4)]
    scratch += [dma((3 * count,)) for _ in range(2)]
    scratch += [dma((5,)) for _ in range(2)]
    return pl.pallas_call(
        tail_kernel,
        name="tail",
        out_shape=[jax.ShapeDtypeStruct((rows, width), F32)] * 2
        + [jax.ShapeDtypeStruct(shape, F32) for shape in shapes]
        + [jax.ShapeDtypeStruct((8, width), F32)],
        in_specs=[hbm] * 8 + [vmem] * 4,
        out_specs=[vmem] * 8,
        scratch_shapes=scratch,
        compiler_params=pltpu.CompilerParams(
            collective_id=3, has_side_effects=True, vmem_limit_bytes=60 << 20
        ),
    )(*kept, packed, left_n, left_j, w_qkv, w_adapt, resid, above, gain_rows, gain_parts)


def xor_permute(value, axis, mask):
    return lax.ppermute(value, axis, [(i, i ^ mask) for i in range(lax.axis_size(axis))])


def quadrants(left):
    n, parts = lax.axis_size("seq"), lax.axis_size("dp")
    tokens, rows = left.shape
    shard = rows // (n * parts)
    split = left.reshape(tokens, n, parts, shard).transpose(2, 0, 1, 3)
    split = split.reshape(parts, tokens, n * shard)
    me = lax.axis_index("dp")
    return jnp.concatenate(
        [lax.dynamic_index_in_dim(split, me ^ m, 0, keepdims=True) for m in range(parts)]
    )


def other_core(left, right):
    core = lax.axis_index("seq") % 2
    half = right.shape[1] // 2
    mine = lax.dynamic_slice_in_dim(right, core * half, half, 1)
    theirs = lax.dynamic_slice_in_dim(right, (1 - core) * half, half, 1)
    left_in = xor_permute(left, "seq", 1)
    right_in = xor_permute(theirs, "seq", 1)
    return jnp.concatenate([left, left_in], axis=1), jnp.concatenate([mine, right_in], axis=0)


def scattered_sum(left, right, bits):
    n, parts = lax.axis_size("seq"), lax.axis_size("dp")
    cols = right.shape[1]
    left, right = other_core(quadrants(left), right)
    got = {}
    masks = list(range(parts))
    for bit in bits:
        outgoing = [m for m in masks if m >> bit & 1]
        masks = [m for m in masks if not m >> bit & 1]
        blocks = []
        for m in outgoing:
            block = dot_tn(left[m], right)
            for more in got.get(m, ()):
                block = block + more.astype(F32)
            blocks.append(block.astype(BF16))
        incoming = xor_permute(jnp.stack(blocks), "dp", 1 << bit)
        for k, m in enumerate(outgoing):
            got.setdefault(m ^ (1 << bit), []).append(incoming[k])
    block = dot_tn(left[0], right)
    for more in got.get(0, ()):
        block = block + more.astype(F32)
    shard = block.shape[0] // n
    block = block.astype(BF16).reshape(n, shard, cols // 2)
    block = lax.all_to_all(block, "seq", 0, 0)
    block = jnp.sum(block.reshape(n // 2, 2, shard, cols // 2).astype(F32), axis=0)
    return block.transpose(1, 0, 2).reshape(shard, cols)


def small_sum(value):
    value = value.reshape(value.shape[0], -1, value.shape[1])
    for axis in ("seq", "dp"):
        size = lax.axis_size(axis)
        me = lax.axis_index(axis)
        for bit in reversed(range(size.bit_length() - 1)):
            half = value.shape[2] // 2
            mine = (me >> bit) & 1
            kept = lax.dynamic_slice_in_dim(value, mine * half, half, 2)
            sent = lax.dynamic_slice_in_dim(value, (1 - mine) * half, half, 2)
            value = kept + xor_permute(sent, axis, 1 << bit)
    return value[:, 0]


def local(state, embedded, cotangent, w_adapt, w_qkv, w_out, w_gate, w_up, w_down, gains):
    seq_count, rows, width = state.shape
    n, parts = lax.axis_size("seq"), lax.axis_size("dp")
    tokens = seq_count * rows
    me = lax.axis_index("seq")
    bits = list(range(parts.bit_length() - 1))
    copies = max(1, n // HEADS)
    held = max(1, HEADS // n)
    owners = n // copies
    cos_np, sin_np = angle_tables(n * rows)
    cos_all, sin_all = jnp.asarray(cos_np), jnp.asarray(sin_np)
    cos = lax.dynamic_slice_in_dim(cos_all, me * rows, rows, 0)[:, None, :]
    sin = lax.dynamic_slice_in_dim(sin_all, me * rows, rows, 0)[:, None, :]
    gain_rows = gains.astype(F32)
    state, embedded = state.reshape(tokens, width), embedded.reshape(tokens, width)

    def to_heads(flat):
        return flat.reshape(tokens, HEADS, HEAD_DIM)

    def to_owner(parts_in):
        sent = jnp.stack(parts_in).reshape(len(parts_in), tokens, owners, held, HEAD_DIM)
        sent = sent.transpose(2, 3, 0, 1, 4)
        if copies > 1:
            sent = jnp.repeat(sent, copies, axis=0)
        return lax.all_to_all(sent, "seq", 0, 0)

    def from_owner(value):
        back = lax.all_to_all(value, "seq", 0, 0)[::copies]
        back = back.reshape(HEADS, -1, tokens, HEAD_DIM)
        return back.transpose(2, 1, 0, 3).reshape(tokens, -1)

    if n == HEADS and seq_count == 1:
        resid, normed, attended, qkv, attended_t, logsum, left_n, left_j = front(
            state, embedded, w_adapt, w_qkv, gain_rows, cos[:, 0], sin[:, 0]
        )
        qkv, attended_t, logsum = qkv[:, None], attended_t[:, None], logsum[:, None]
    else:
        resid = dot(state, w_adapt[:width]) + dot(embedded, w_adapt[width:])
        normed = mean_norm(resid, gain_rows[0]).astype(BF16)
        packed = dot(normed, w_qkv)
        queries = rotate(to_heads(packed[:, :width]), cos, sin).astype(BF16)
        keys = rotate(to_heads(packed[:, width : 2 * width]), cos, sin).astype(BF16)
        values = to_heads(packed[:, 2 * width :]).astype(BF16)
        qkv = to_owner((queries, keys, values))
        attended, attended_t, logsum = attention(qkv)
        attended = from_owner(attended[:, :, None])
    shape = (seq_count, rows, width)
    if n == HEADS and parts == 4 and seq_count == 1:
        layer_out, middle_grad, gain_parts, packed_low, kept_d, kept_g, kept_o = middle_block(
            attended,
            resid,
            cotangent.reshape(tokens, width),
            gain_rows,
            w_out,
            w_gate,
            w_up,
            w_down,
            qkv[:, 0],
            attended_t[:, 0],
            logsum[:, 0],
            jnp.asarray(np.concatenate([cos_np, sin_np], axis=1)),
        )
        grad_state, grad_embedded, grad_adapt, grad_qkv, grad_out, grad_wide, grad_down, gains_sum = tail(
            (kept_d, kept_g, kept_o.reshape(4, width // 4, width // 2)),
            packed_low,
            left_n,
            left_j,
            w_qkv,
            w_adapt,
            resid,
            middle_grad,
            gain_rows,
            gain_parts,
        )
        share = width // (n * parts)
        at = (me * parts + lax.axis_index("dp")) * share
        return (
            layer_out.reshape(shape),
            grad_state.reshape(shape),
            grad_embedded.reshape(shape),
            grad_adapt,
            grad_qkv,
            grad_out,
            grad_wide[0],
            grad_wide[1],
            grad_down,
            lax.dynamic_slice_in_dim(gains_sum[:4], at, share, 1),
        )
    branch = dot(attended, w_out)
    middle = resid + mean_norm(branch, gain_rows[1])
    normed_mid = mean_norm(middle, gain_rows[2]).astype(BF16)
    gate_pre = dot(normed_mid, w_gate)
    up_pre = dot(normed_mid, w_up)
    sigmoid_gate = jax.nn.sigmoid(gate_pre)
    silu_gate = gate_pre * sigmoid_gate
    hidden = (silu_gate * up_pre).astype(BF16)
    down_out = dot(hidden, w_down)
    layer_out = middle + mean_norm(down_out, gain_rows[3])
    out_grad = cotangent.astype(F32).reshape(tokens, width)
    down_grad, gain_grad3 = norm_back(down_out, gain_rows[3], out_grad)
    down_low = down_grad.astype(BF16)
    hidden_grad = dot_nt(down_low, w_down)
    gate_low = (
        hidden_grad * up_pre * sigmoid_gate * (1.0 + gate_pre * (1.0 - sigmoid_gate))
    ).astype(BF16)
    up_low = (hidden_grad * silu_gate).astype(BF16)
    mid_norm_grad = dot_nt(gate_low, w_gate) + dot_nt(up_low, w_up)
    middle_part, gain_grad2 = norm_back(middle, gain_rows[2], mid_norm_grad)
    middle_grad = out_grad + middle_part
    branch_grad, gain_grad1 = norm_back(branch, gain_rows[1], middle_grad)
    branch_low = branch_grad.astype(BF16)
    attended_grad = dot_nt(branch_low, w_out).astype(BF16)
    upstream = to_owner((to_heads(attended_grad),))[:, :, 0]
    packed_grad = attention_back(qkv, upstream, attended_t, logsum, cos_all, sin_all)
    packed_low = from_owner(packed_grad)
    normed_grad = dot_nt(packed_low, w_qkv)
    resid_part, gain_grad0 = norm_back(resid, gain_rows[0], normed_grad)
    resid_low = (middle_grad + resid_part).astype(BF16)
    grad_state = dot_nt(resid_low, w_adapt[:width])
    grad_embedded = dot_nt(resid_low, w_adapt[width:])
    flipped = bits[::-1]
    joined = jnp.concatenate([state, embedded], axis=-1)
    grad_down = scattered_sum(hidden, down_low, bits)
    grad_gate = scattered_sum(normed_mid, gate_low, flipped)
    grad_up = scattered_sum(normed_mid, up_low, bits)
    grad_out = scattered_sum(attended, branch_low, flipped)
    grad_qkv = scattered_sum(normed, packed_low, flipped)
    grad_adapt = scattered_sum(joined, resid_low, bits)
    grad_gains = jnp.stack([gain_grad0, gain_grad1, gain_grad2, gain_grad3])
    grad_gains = small_sum(grad_gains)
    return (
        layer_out.reshape(shape).astype(BF16),
        grad_state.reshape(shape),
        grad_embedded.reshape(shape),
        grad_adapt,
        grad_qkv,
        grad_out,
        grad_gate,
        grad_up,
        grad_down,
        grad_gains,
    )


def solution(mesh):
    tokens = P("dp", "seq", None)
    rows = P(("seq", "dp"), None)
    return jax.shard_map(
        local,
        mesh=mesh,
        in_specs=(tokens,) * 3 + (P(),) * 7,
        out_specs=(tokens,) * 3 + (rows,) * 6 + (P(None, ("seq", "dp")),),
        check_vma=False,
    )
```

```python
import functools
import math

import jax
import jax.numpy as jnp
import numpy as np
from jax import lax
from jax.experimental import pallas as pl
from jax.experimental.pallas import tpu as pltpu
from jax.sharding import PartitionSpec as P

HEADS = 8
HEAD_DIM = 128
norm_eps = 1e-06
rope_base = 50000.0
F32 = jnp.float32
BF16 = jnp.bfloat16
MESH = pl.DeviceIdType.MESH
NEG = -1e30
SCORE_SCALE = 1.0 / math.sqrt(HEAD_DIM)
LOG2E = 1.0 / math.log(2.0)


def mean_norm(values_in, gain_row):
    return (
        values_in
        * lax.rsqrt(jnp.mean(values_in * values_in, axis=-1, keepdims=True) + norm_eps)
        * gain_row
    )


def norm_back(values_in, gain_row, upstream):
    inverse = lax.rsqrt(jnp.mean(values_in * values_in, axis=-1, keepdims=True) + norm_eps)
    scaled = upstream * gain_row
    value_grad = inverse * scaled - values_in * (inverse * inverse * inverse) * jnp.mean(
        values_in * scaled, axis=-1, keepdims=True
    )
    gain_grad = jnp.sum(upstream * values_in * inverse, axis=0)
    return (value_grad, gain_grad)


def angle_tables(length):
    half_dim = HEAD_DIM // 2
    freqs = np.exp(
        np.arange(half_dim, dtype=np.float32) * np.float32(-2.0 * math.log(rope_base) / HEAD_DIM)
    ).astype(np.float32)
    angles = np.arange(length, dtype=np.float32)[:, None] * freqs[None, :]
    return np.cos(angles).astype(np.float32), np.sin(angles).astype(np.float32)


def rotate(heads_in, cos_table, sin_table):
    half_dim = heads_in.shape[-1] // 2
    lower_half = heads_in[..., :half_dim]
    upper_half = heads_in[..., half_dim:]
    return jnp.concatenate(
        [
            lower_half * cos_table - upper_half * sin_table,
            upper_half * cos_table + lower_half * sin_table,
        ],
        axis=-1,
    )


def dot(a, b):
    return lax.dot_general(a, b, (((1,), (0,)), ((), ())), preferred_element_type=F32)


def dot_tn(a, b):
    return lax.dot_general(a, b, (((0,), (0,)), ((), ())), preferred_element_type=F32)


def dot_nt(a, b):
    return lax.dot_general(a, b, (((1,), (1,)), ((), ())), preferred_element_type=F32)


def span(low, high, body, unrolled):
    if unrolled:
        for i in range(low, high):
            body(i)
    else:
        lax.fori_loop(low, high, lambda i, c: (body(i), c)[1], 0)


def causal_fill(block, fill):
    kv = lax.broadcasted_iota(jnp.int32, block.shape, 0)
    q = lax.broadcasted_iota(jnp.int32, block.shape, 1)
    return jnp.where(q >= kv, block, fill)


def attention_kernel(x_ref, o_ref, ot_ref, ls_ref, vt_ref, s_ref):
    n, hp, _, rows, _ = x_ref.shape
    unrolled = n <= 8
    factor = SCORE_SCALE * LOG2E
    for h in range(hp):
        for j in range(n):
            vt_ref[j] = x_ref[j, h, 2].astype(F32).T.astype(BF16)

        def query_block(i):
            q = x_ref[i, h, 0]
            diag = causal_fill(dot_nt(x_ref[i, h, 1], q), NEG)

            def first(j, peak):
                s = dot_nt(x_ref[j, h, 1], q)
                s_ref[j] = s
                return jnp.maximum(peak, jnp.max(s, axis=0, keepdims=True))

            peak = jnp.max(diag, axis=0, keepdims=True)
            if unrolled:
                for j in range(i):
                    peak = first(j, peak)
            else:
                peak = lax.fori_loop(0, i, first, peak)
            shift = peak * factor
            p = jnp.exp2(diag * factor - shift)
            total = jnp.sum(p, axis=0, keepdims=True)
            acc = dot(vt_ref[i], p.astype(BF16))

            def second(j, state):
                total, acc = state
                p = jnp.exp2(s_ref[j] * factor - shift)
                return (
                    total + jnp.sum(p, axis=0, keepdims=True),
                    acc + dot(vt_ref[j], p.astype(BF16)),
                )

            state = (total, acc)
            if unrolled:
                for j in range(i):
                    state = second(j, state)
            else:
                state = lax.fori_loop(0, i, second, state)
            total, acc = state
            acc = acc / total
            ot_ref[i, h] = acc
            o_ref[i, h] = acc.T.astype(BF16)
            ls_ref[i, h] = shift + jnp.log2(total)

        span(0, n, query_block, unrolled)


def attention(x):
    n, hp, _, rows, dim = x.shape
    pairs = n * (n + 1) // 2 * rows * rows * hp
    return pl.pallas_call(
        attention_kernel,
        name="attention",
        out_shape=(
            jax.ShapeDtypeStruct((n, hp, rows, dim), BF16),
            jax.ShapeDtypeStruct((n, hp, dim, rows), F32),
            jax.ShapeDtypeStruct((n, hp, 1, rows), F32),
        ),
        scratch_shapes=[
            pltpu.VMEM((n, dim, rows), BF16),
            pltpu.VMEM((n, rows, rows), F32),
        ],
        compiler_params=pltpu.CompilerParams(vmem_limit_bytes=40 << 20),
        cost_estimate=pl.CostEstimate(
            flops=pairs * dim * 8, bytes_accessed=x.size * 4, transcendentals=pairs
        ),
    )(x)


def attention_back_kernel(
    x_ref, g_ref, ot_ref, ls_ref, cos_ref, sin_ref, out_ref, kt_ref, dqt_ref, delta_ref
):
    n, hp, _, rows, _ = x_ref.shape
    unrolled = n <= 8
    factor = SCORE_SCALE * LOG2E
    for h in range(hp):
        for j in range(n):
            kt_ref[j] = x_ref[j, h, 1].astype(F32).T.astype(BF16)
            delta_ref[j] = jnp.sum(
                g_ref[j, h].astype(F32).T * ot_ref[j, h], axis=0, keepdims=True
            )

        def unrotated(value, i):
            turned = pl.ds(i * rows, rows)
            cos, sin = cos_ref[turned], sin_ref[turned]
            return rotate(value * SCORE_SCALE, cos, -sin).astype(BF16)

        def pair(i, j, diagonal):
            q, g = x_ref[i, h, 0], g_ref[i, h]
            p = jnp.exp2(dot_nt(x_ref[j, h, 1], q) * factor - ls_ref[i, h])
            if diagonal:
                p = causal_fill(p, 0.0)
            dv = dot(p.astype(BF16), g)
            ds = (p * (dot_nt(x_ref[j, h, 2], g) - delta_ref[i])).astype(BF16)
            dk = dot(ds, q)
            dqt = dot(kt_ref[j], ds)
            return dv, dk, dqt

        def key_block(j):
            dv, dk, dqt = pair(j, j, True)
            if unrolled:
                dqt_ref[j] = dqt if j == 0 else dqt_ref[j] + dqt
            else:
                dqt_ref[j] = jnp.where(j == 0, 0.0, dqt_ref[j]) + dqt

            def step(i, state):
                dv, dk = state
                v, k, t = pair(i, j, False)
                if unrolled:
                    dqt_ref[i] = t if j == 0 else dqt_ref[i] + t
                else:
                    dqt_ref[i] = jnp.where(j == 0, 0.0, dqt_ref[i]) + t
                return dv + v, dk + k

            state = (dv, dk)
            if unrolled:
                for i in range(j + 1, n):
                    state = step(i, state)
            else:
                state = lax.fori_loop(j + 1, n, step, state)
            dv, dk = state
            out_ref[j, h, 0] = unrotated(dqt_ref[j].T, j)
            out_ref[j, h, 1] = unrotated(dk, j)
            out_ref[j, h, 2] = dv.astype(BF16)

        span(0, n, key_block, unrolled)


def attention_back(x, g, ot, ls, cos, sin):
    n, hp, _, rows, dim = x.shape
    pairs = n * (n + 1) // 2 * rows * rows * hp
    return pl.pallas_call(
        attention_back_kernel,
        name="attention_back",
        out_shape=jax.ShapeDtypeStruct(x.shape, BF16),
        scratch_shapes=[
            pltpu.VMEM((n, dim, rows), BF16),
            pltpu.VMEM((n, dim, rows), F32),
            pltpu.VMEM((n, 1, rows), F32),
        ],
        compiler_params=pltpu.CompilerParams(vmem_limit_bytes=40 << 20),
        cost_estimate=pl.CostEstimate(
            flops=pairs * dim * 20, bytes_accessed=x.size * 6, transcendentals=pairs
        ),
    )(x, g, ot, ls, cos, sin)


def seq_device(index):
    return {"seq": index}


def greet(peers):
    barrier = pltpu.get_barrier_semaphore()
    for device in peers:
        pl.semaphore_signal(barrier, inc=1, device_id=device, device_id_type=MESH)


def greeted(count):
    pl.semaphore_wait(pltpu.get_barrier_semaphore(), count)


def remote(src, dst, send, recv, device):
    return pltpu.make_async_remote_copy(
        src_ref=src,
        dst_ref=dst,
        send_sem=send,
        recv_sem=recv,
        device_id=device,
        device_id_type=MESH,
    )


def front_kernel(
    state_ref,
    embedded_ref,
    wa_ref,
    wq_ref,
    gain_ref,
    table_ref,
    resid_out,
    normed_out,
    att_out,
    x_out,
    ot_out,
    ls_out,
    ltn_out,
    ltj_out,
    wa,
    wq,
    joined,
    resid,
    normed,
    sent,
    x,
    vt,
    scores,
    ot,
    o_sent,
    att,
    ltn,
    ltj,
    table,
    load_sem,
    store_sem,
    send_sem,
    recv_sem,
    o_send_sem,
    o_recv_sem,
    l_send_sem,
    l_recv_sem,
):
    n, rows, width = HEADS, state_ref.shape[0], state_ref.shape[1]
    me = lax.axis_index("seq")
    dp = lax.axis_index("dp")
    peers = [seq_device((me + k) % n) for k in range(1, n)]
    across = [{"dp": flipped(0, dp)}, {"dp": flipped(1, dp)}]
    near = seq_device(flipped(0, me))
    greet(peers + across)
    loads = [
        pltpu.make_async_copy(state_ref, joined.at[0], load_sem.at[0]),
        pltpu.make_async_copy(wa_ref.at[pl.ds(0, width)], wa.at[0], load_sem.at[1]),
        pltpu.make_async_copy(embedded_ref, joined.at[1], load_sem.at[2]),
        pltpu.make_async_copy(wa_ref.at[pl.ds(width, width)], wa.at[1], load_sem.at[3]),
        pltpu.make_async_copy(wq_ref, wq, load_sem.at[4]),
        pltpu.make_async_copy(
            table_ref.at[pl.ds(pl.multiple_of(me * rows, 8), rows)], table, load_sem.at[5]
        ),
    ]
    for copy in loads:
        copy.start()
    tile = 256
    for half in range(2):
        loads[2 * half].wait()
        loads[2 * half + 1].wait()

        for begin in range(0, width, tile):
            cols = pl.ds(begin, tile)
            block = dot(joined[half], wa[half, :, cols])
            resid[:, cols] = block if half == 0 else resid[:, cols] + block
    normed[...] = mean_norm(resid[...], gain_ref[0:1, :].astype(F32)).astype(BF16)
    stores = [
        pltpu.make_async_copy(resid, resid_out, store_sem.at[0]),
        pltpu.make_async_copy(normed, normed_out, store_sem.at[1]),
    ]
    for copy in stores:
        copy.start()
    loads[4].wait()
    lefts = []

    def share(source, out, slot, device):
        k = len(lefts)
        copy = remote(source, out.at[slot], l_send_sem.at[k], l_recv_sem.at[k], device)
        copy.start()
        lefts.append(copy)
    loads[5].wait()
    cos, sin = table[:, 0 : HEAD_DIM // 2], table[:, HEAD_DIM // 2 : HEAD_DIM]
    pairs = n // 2
    order = [2, 1, 3, 0] if pairs == 4 else list(range(pairs - 1, -1, -1))
    sends = []
    for k in order:
        chip = (me // 2 + k) % pairs
        for part in range(3):
            cols = pl.ds(pl.multiple_of(part * width + chip * 2 * HEAD_DIM, 2 * HEAD_DIM), 2 * HEAD_DIM)
            block = dot(normed[...], wq[:, cols])
            for core in range(2):
                head = block[:, core * HEAD_DIM : (core + 1) * HEAD_DIM]
                if part < 2:
                    head = rotate(head, cos, sin)
                sent[2 * chip + core, part] = head.astype(BF16)
        if k == order[0]:
            greeted(n + 1)
        for core in range(2):
            owner = 2 * chip + core
            if k == 0:
                continue
            copy = remote(sent.at[owner], x.at[me], send_sem.at[owner], recv_sem.at[me], seq_device(owner))
            copy.start()
            sends.append(copy)
    mate = me + 1 - 2 * (me % 2)
    copy = remote(sent.at[mate], x.at[me], send_sem.at[mate], recv_sem.at[me], seq_device(mate))
    copy.start()
    sends.append(copy)
    x[me] = sent[me]
    transposed_into(normed, ltn)
    for half in range(2):
        transposed_into(joined.at[half], ltj.at[pl.ds(half * width, width)])
    stores.append(pltpu.make_async_copy(ltn, ltn_out.at[0], store_sem.at[4]))
    stores.append(pltpu.make_async_copy(ltj, ltj_out.at[0], store_sem.at[5]))
    for copy in stores[2:]:
        copy.start()
    share(ltn, ltn_out, 2, across[0])
    share(ltn, ltn_out, 4, across[1])
    share(ltj, ltj_out, 2, across[1])
    share(ltn, ltn_out, 1, near)
    share(ltj, ltj_out, 1, near)
    factor = SCORE_SCALE * LOG2E
    for i in range(n):

        @pl.when(me != i)
        def arrive():
            remote(sent.at[0], x.at[i], send_sem.at[0], recv_sem.at[i], seq_device(i)).wait_recv()

        vt[i] = x[i, 2].astype(F32).T.astype(BF16)
        q = x[i, 0]
        diag = causal_fill(dot_nt(x[i, 1], q), NEG)
        peak = jnp.max(diag, axis=0, keepdims=True)
        for j in range(i):
            block = dot_nt(x[j, 1], q)
            scores[j] = block
            peak = jnp.maximum(peak, jnp.max(block, axis=0, keepdims=True))
        shift = peak * factor
        p = jnp.exp2(diag * factor - shift)
        total = jnp.sum(p, axis=0, keepdims=True)
        acc = dot(vt[i], p.astype(BF16))
        for j in range(i):
            p = jnp.exp2(scores[j] * factor - shift)
            total = total + jnp.sum(p, axis=0, keepdims=True)
            acc = acc + dot(vt[j], p.astype(BF16))
        acc = acc / total
        ot[i] = acc
        o_sent[i] = acc.T.astype(BF16)
        ls_out[i] = shift + jnp.log2(total)
        mine = pl.ds(pl.multiple_of(me * HEAD_DIM, HEAD_DIM), HEAD_DIM)

        @pl.when(me != i)
        def give():
            remote(o_sent.at[i], att.at[:, mine], o_send_sem.at[i], o_recv_sem.at[me], seq_device(i)).start()

        @pl.when(me == i)
        def keep():
            att[:, mine] = o_sent[i]

    stores.append(pltpu.make_async_copy(x, x_out, store_sem.at[2]))
    stores.append(pltpu.make_async_copy(ot, ot_out, store_sem.at[3]))
    for copy in stores[4:]:
        copy.start()
    for k, out, slot in ((0, ltn_out, 2), (1, ltn_out, 4), (2, ltj_out, 2)):
        lefts[k].wait_recv()
        share(out.at[slot], out, slot + 1, near)
    for copy in sends:
        copy.wait_send()
    for i in range(n):

        @pl.when(me != i)
        def finish():
            cols = pl.ds(i * HEAD_DIM, HEAD_DIM)
            copy = remote(o_sent.at[i], att.at[:, cols], o_send_sem.at[i], o_recv_sem.at[i], seq_device(i))
            copy.wait_send()
            copy.wait_recv()

    att_out[...] = att[...]
    for copy in stores:
        copy.wait()
    for k, copy in enumerate(lefts):
        copy.wait_send()
        if k > 2:
            copy.wait_recv()


def front(state, embedded, w_adapt, w_qkv, gains, table):
    n = HEADS
    rows, width = state.shape
    hbm = pl.BlockSpec(memory_space=pl.ANY)
    vmem = pl.BlockSpec(memory_space=pltpu.VMEM)
    return pl.pallas_call(
        front_kernel,
        name="front",
        out_shape=(
            jax.ShapeDtypeStruct((rows, width), F32),
            jax.ShapeDtypeStruct((rows, width), BF16),
            jax.ShapeDtypeStruct((rows, width), BF16),
            jax.ShapeDtypeStruct((n, 3, rows, HEAD_DIM), BF16),
            jax.ShapeDtypeStruct((n, HEAD_DIM, rows), F32),
            jax.ShapeDtypeStruct((n, 1, rows), F32),
            jax.ShapeDtypeStruct((6, width, rows), BF16),
            jax.ShapeDtypeStruct((4, 2 * width, rows), BF16),
        ),
        in_specs=[hbm, hbm, hbm, hbm, vmem, hbm],
        out_specs=(hbm, hbm, vmem, hbm, hbm, vmem, hbm, hbm),
        scratch_shapes=[
            pltpu.VMEM((2, width, width), BF16),
            pltpu.VMEM((width, 3 * width), BF16),
            pltpu.VMEM((2, rows, width), BF16),
            pltpu.VMEM((rows, width), F32),
            pltpu.VMEM((rows, width), BF16),
            pltpu.VMEM((n, 3, rows, HEAD_DIM), BF16),
            pltpu.VMEM((n, 3, rows, HEAD_DIM), BF16),
            pltpu.VMEM((n, HEAD_DIM, rows), BF16),
            pltpu.VMEM((n, rows, rows), F32),
            pltpu.VMEM((n, HEAD_DIM, rows), F32),
            pltpu.VMEM((n, rows, HEAD_DIM), BF16),
            pltpu.VMEM((rows, width), BF16),
            pltpu.VMEM((width, rows), BF16),
            pltpu.VMEM((2 * width, rows), BF16),
            pltpu.VMEM((rows, HEAD_DIM), F32),
            pltpu.SemaphoreType.DMA((6,)),
            pltpu.SemaphoreType.DMA((6,)),
            pltpu.SemaphoreType.DMA((n,)),
            pltpu.SemaphoreType.DMA((n,)),
            pltpu.SemaphoreType.DMA((n,)),
            pltpu.SemaphoreType.DMA((n,)),
            pltpu.SemaphoreType.DMA((8,)),
            pltpu.SemaphoreType.DMA((8,)),
        ],
        compiler_params=pltpu.CompilerParams(
            collective_id=1, has_side_effects=True, vmem_limit_bytes=62 << 20
        ),
    )(state, embedded, w_adapt, w_qkv, gains, table)


def flipped(bit, value):
    return value + (1 - 2 * ((value // (1 << bit)) % 2)) * (1 << bit)


def unit_slots(first, dp):
    slots = []
    for q in range(4):
        turned = [(dp + q) % 2, (dp // 2 + q // 2) % 2]
        slots.append(turned[first] * 2 + turned[1 - first])
    return slots


def transposed_into(source, target):
    tile = 256
    for begin in range(0, source.shape[1], tile):
        target[pl.ds(begin, tile), :] = source[:, pl.ds(begin, tile)].T


def add_into(target, more):
    rows = target.shape[0]
    chunk = 16
    while rows % (chunk * 2) == 0 and chunk < 64:
        chunk *= 2

    def step(t, c):
        at = pl.ds(pl.multiple_of(t * chunk, chunk), chunk)
        target[at, :] = (target[at, :].astype(F32) + more[at, :].astype(F32)).astype(BF16)
        return c

    lax.fori_loop(0, rows // chunk, step, 0)


CHUNKS = ((0, 512), (512, 512), (1024, 384))


def z_place(z):
    return (z % 2) * 2 + z // 2


def transposed_blocks(source, target):
    tile = 256
    parts, size = target.shape[1], target.shape[2]
    for begin in range(0, source.shape[1], tile):
        block = source[:, pl.ds(begin, tile)].T
        for k in range(begin // size, (begin + tile - 1) // size + 1):
            low, high = max(begin, size * k), min(begin + tile, size * (k + 1))
            target[k // parts, k % parts, pl.ds(low - size * k, high - low), :] = block[
                low - begin : high - begin
            ]


def middle_kernel(*refs):
    refs = list(refs)

    def take(count):
        taken, refs[:count] = refs[:count], []
        return taken

    (att_in, resid_in, cot_in, gain_rows, wo_in, wg_in, wu_in, wd_in) = take(8)
    (x_in, ot_in, ls_ref, table_in) = take(4)
    (layer_out, above_out, gains_out, packed_out) = take(4)
    (kept_d, kept_g, kept_h, kept_o) = take(4)
    (wo, wg, wu, wd, att, cot, resid, branch, mid, down) = take(10)
    (normed, hidden, gate_by, up_by, down_low, wide_low, branch_low, dout) = take(8)
    (left_n, left_h, left_m, left_a, right_g, right_d, right_b) = take(7)
    (got_g, got_d) = take(2)
    (work, x, ot, table, g, kt, dqt, delta, dsent, packed) = take(10)
    (load_sem, store_sem, g_send, g_recv, d_send, d_recv, m_send, m_recv, s_send, s_recv) = take(10)
    n, (rows, width) = HEADS, resid.shape
    ff = wg.shape[1]
    half, part = ff // 2, width // 2
    me = lax.axis_index("seq")
    dp = lax.axis_index("dp")
    core = me % 2
    mate = flipped(0, me)
    bits = [dp % 2, dp // 2]
    near = seq_device(mate)
    across = [{"dp": flipped(0, dp)}, {"dp": flipped(1, dp)}]
    diagonal = [{"seq": mate, "dp": flipped(0, dp)}, {"seq": mate, "dp": flipped(1, dp)}]
    greet([seq_device((me + k) % n) for k in range(1, n)] + across + diagonal)
    loads = {}
    for key, src, dst in (
        ("att", att_in, att),
        ("wo", wo_in, wo),
        ("resid", resid_in, resid),
        ("wg", wg_in, wg),
        ("wu", wu_in, wu),
        ("cot", cot_in, cot),
        ("wd", wd_in, wd),
        ("x", x_in, x),
        ("ot", ot_in, ot),
        ("table", table_in, table),
    ):
        copy = pltpu.make_async_copy(src, dst, load_sem.at[len(loads)])
        copy.start()
        loads[key] = copy
    tile = 256
    gains = [gain_rows[k : k + 1, :].astype(F32) for k in range(4)]

    def tiles(total, body):
        for begin in range(0, total, tile):
            body(pl.ds(begin, tile))

    sends = []
    given = {}

    issued = []

    def give(key, src, dst, device):
        k = len(issued)
        copy = remote(src, dst, m_send.at[k], m_recv.at[k], device)
        copy.start()
        issued.append(key)
        sends.append(copy)
        given[key] = copy

    loads["att"].wait()
    loads["wo"].wait()

    def project(cols):
        branch[:, cols] = dot(att[...], wo[:, cols])

    tiles(width, project)
    loads["resid"].wait()
    mid[...] = resid[...] + mean_norm(branch[...], gains[1])
    normed[...] = mean_norm(mid[...], gains[2]).astype(BF16)
    transposed_into(normed, left_n.at[0])
    greeted(n + 3)
    give("n1", left_n.at[0], left_n.at[1], near)
    give("n2", left_n.at[0], left_n.at[2], across[0])
    loads["wg"].wait()
    loads["wu"].wait()

    def widen(cols):
        gate = dot(normed[...], wg[:, cols])
        up = dot(normed[...], wu[:, cols])
        bent = jax.nn.sigmoid(gate)
        silu = gate * bent
        hidden[:, cols] = (silu * up).astype(BF16)
        gate_by[:, cols] = (up * bent * (1.0 + gate * (1.0 - bent))).astype(BF16)
        up_by[:, cols] = silu.astype(BF16)

    tiles(ff, widen)
    loads["wd"].wait()

    def narrow(cols):
        down[:, cols] = dot(hidden[...], wd[:, cols])

    tiles(width, narrow)
    loads["cot"].wait()
    layer_out[...] = (mid[...] + mean_norm(down[...], gains[3])).astype(BF16)
    grad, gain3 = norm_back(down[...], gains[3], cot[...].astype(F32))
    down_low[...] = grad.astype(BF16)
    mine_d = pl.ds(pl.multiple_of(core * part, 128), part)
    theirs_d = pl.ds(pl.multiple_of((1 - core) * part, 128), part)
    give("d2", down_low.at[:, mine_d], right_d.at[1], across[1])
    give("d3", down_low.at[:, theirs_d], right_d.at[2], diagonal[1])
    give("d1", down_low.at[:, theirs_d], right_d.at[0], near)

    def widen_back(cols):
        block = dot_nt(down_low[...], wd[cols, :])
        wide_low[0, :, cols] = (block * gate_by[:, cols].astype(F32)).astype(BF16)
        wide_low[1, :, cols] = (block * up_by[:, cols].astype(F32)).astype(BF16)

    tiles(ff, widen_back)

    def chunk_of(c, which_core, which_bit):
        at, wide = CHUNKS[c]
        return wide_low.at[which_core, :, pl.ds(pl.multiple_of(which_bit * half + at, 128), wide)]

    for c, (at, wide) in enumerate(CHUNKS):
        cols = pl.ds(at, wide)
        give(("g2", c), chunk_of(c, core, 1 - bits[0]), right_g.at[1, :, cols], across[0])
        give(("g3", c), chunk_of(c, 1 - core, 1 - bits[0]), right_g.at[2, :, cols], diagonal[0])
        give(("g1", c), chunk_of(c, 1 - core, bits[0]), right_g.at[0, :, cols], near)

    def narrow_back(cols):
        down[:, cols] = dot_nt(wide_low[0], wg[cols, :]) + dot_nt(wide_low[1], wu[cols, :])

    tiles(width, narrow_back)
    grad, gain2 = norm_back(mid[...], gains[2], down[...])
    resid[...] = cot[...].astype(F32) + grad
    grad, gain1 = norm_back(branch[...], gains[1], resid[...])
    branch_low[...] = grad.astype(BF16)

    def project_back(cols):
        dout[:, cols] = dot_nt(branch_low[...], wo[cols, :]).astype(BF16)

    tiles(width, project_back)
    my_cols = pl.ds(pl.multiple_of(me * HEAD_DIM, HEAD_DIM), HEAD_DIM)
    for k in (4, 5, 3, 2, 6, 7, 1):
        owner = (me + k) % n
        cols = pl.ds(pl.multiple_of(owner * HEAD_DIM, HEAD_DIM), HEAD_DIM)
        copy = remote(dout.at[:, cols], g.at[me], g_send.at[owner], g_recv.at[me], seq_device(owner))
        copy.start()
        sends.append(copy)
    g[me] = dout[:, my_cols]
    transposed_blocks(hidden, left_h)
    give("h2", left_h.at[:, 1 - bits[1]], left_m.at[1], across[1])
    give("h1", left_h.at[:, bits[1]], left_m.at[0], near)
    given["n2"].wait_recv()
    give("n3", left_n.at[2], left_n.at[3], near)
    transposed_into(att, left_a.at[0])
    give("a1", left_a.at[0], left_a.at[1], near)
    give("b1", branch_low.at[:, theirs_d], right_b, near)
    stores = []

    def store(src, dst):
        copy = pltpu.make_async_copy(src, dst, store_sem.at[len(stores)])
        copy.start()
        stores.append(copy)

    store(resid, above_out)
    gains_out[...] = jnp.zeros_like(gains_out)
    gains_out[1:2, :] = gain1[None, :]
    gains_out[2:3, :] = gain2[None, :]
    gains_out[3:4, :] = gain3[None, :]
    seconds = {}

    def wide_sum(c):
        at, wide = CHUNKS[c]
        for key in ("n1", "n3"):
            if key in given:
                given.pop(key).wait_recv()
        for key in ("g1", "g2", "g3"):
            given[key, c].wait_recv()
        shard = width // 32
        spread = [(bits[1] + other) % 2 for other in range(2)]
        own = chunk_of(c, core, bits[0])
        for begin in range(0, wide, 256):
            step = min(256, wide - begin)
            cols = pl.ds(at + begin, step)
            block = dot(left_n[0], own[:, pl.ds(begin, step)])
            for k in range(1, 4):
                block += dot(left_n[k], right_g[k - 1, :, cols])
            work[0:width, 0:step] = block
            for z in range(4):
                for other in range(2):
                    pieces = [
                        work[pl.ds((8 * z + 4 * c2 + 2 * other + b) * shard, shard), 0:step]
                        for c2 in range(2)
                        for b in range(2)
                    ]
                    place = pl.multiple_of(spread[other] * part + z_place(z) * 4 * shard, 16)
                    wg[pl.ds(place, 4 * shard), cols] = jnp.concatenate(pieces, axis=0).astype(BF16)
        cols = pl.ds(at, wide)
        if c == len(CHUNKS) - 1:
            store(wg.at[:, cols], kept_h)
            return
        seconds[c] = remote(
            wg.at[pl.ds(part, part), cols], got_g.at[:, cols], s_send.at[c], s_recv.at[c], across[1]
        )
        seconds[c].start()
        sends.append(seconds[c])

    def down_sum():
        for key in ("h1", "h3", "d1", "d2", "d3"):
            given[key].wait_recv()
        tall = ff // 4
        shard = ff // 32
        spread = [(bits[0] + other) % 2 for other in range(2)]
        for begin in range(0, part, 256):
            cols = pl.ds(begin, 256)
            own = down_low.at[:, mine_d]
            block = dot(left_h[:, bits[1]].reshape(2 * tall, rows), own[:, cols])
            for k in range(3):
                block += dot(left_m[k].reshape(2 * tall, rows), right_d[k, :, cols])
            work[...] = block
            for z in range(4):
                for other in range(2):
                    pieces = [
                        work[pl.ds((4 * z + 2 * c2 + other) * shard, shard), :] for c2 in range(2)
                    ]
                    place = pl.multiple_of(spread[other] * tall + z_place(z) * 2 * shard, 16)
                    wd[pl.ds(place, 2 * shard), cols] = jnp.concatenate(pieces, axis=0).astype(BF16)
        cols = pl.ds(0, part)
        seconds["d"] = remote(
            wd.at[pl.ds(tall, tall), cols], got_d, s_send.at[3], s_recv.at[3], across[0]
        )
        seconds["d"].start()
        sends.append(seconds["d"])

    def out_sum():
        given["a1"].wait_recv()
        given["b1"].wait_recv()
        shard = width // 32
        slots = unit_slots(0, dp)
        for begin in range(0, part, 256):
            cols = pl.ds(begin, 256)
            block = dot(left_a[0], branch_low.at[:, mine_d][:, cols])
            work[0:width, :] = block + dot(left_a[1], right_b[:, cols])
            for z in range(4):
                for q in range(4):
                    pieces = [
                        work[pl.ds((8 * z + 4 * c2 + q) * shard, shard), :] for c2 in range(2)
                    ]
                    place = pl.multiple_of(slots[q] * (width // 4) + z_place(z) * 2 * shard, 16)
                    wu[pl.ds(place, 2 * shard), cols] = jnp.concatenate(pieces, axis=0).astype(BF16)
        store(wu.at[:, pl.ds(0, part)], kept_o)

    loads["x"].wait()
    factor = SCORE_SCALE * LOG2E
    half_dim = HEAD_DIM // 2
    pairs = [(i, j) for j in range(n) for i in range(j, n)]
    across_blocks = ff // rows

    def probs(i, j):
        k = pairs.index((i, j))
        at, cols = k // across_blocks * rows, k % across_blocks * rows
        return wu.at[pl.ds(at, rows), pl.ds(cols, rows)]

    for j in range(n):
        kt[j] = x[j, 1].astype(F32).T.astype(BF16)
        for i in range(j, n):
            p = jnp.exp2(dot_nt(x[j, 1], x[i, 0]) * factor - ls_ref[i])
            if i == j:
                p = causal_fill(p, 0.0)
            probs(i, j)[...] = p.astype(BF16)
    wide_sum(0)
    loads["ot"].wait()
    loads["table"].wait()
    arrived, summed = set(), set()

    def upstream(i):
        if i not in arrived:
            arrived.add(i)

            @pl.when(me != i)
            def arrive():
                remote(g.at[0], g.at[i], g_send.at[0], g_recv.at[i], seq_device(i)).wait_recv()

            delta[i] = jnp.sum(g[i].astype(F32).T * ot[i], axis=0, keepdims=True)
        return g[i]

    def give_head(j, first, count, sem):
        span = pl.ds(first, count)

        @pl.when(me != j)
        def over():
            remote(
                dsent.at[j, span], packed.at[span, :, my_cols], d_send.at[sem], d_recv.at[sem - j + me], seq_device(j)
            ).start()

        @pl.when(me == j)
        def keep():
            packed[span, :, my_cols] = dsent[j, span]

    def unrotated(value, j):
        here = pl.ds(j * rows, rows)
        cos, sin = table[here, 0:half_dim], -table[here, half_dim:HEAD_DIM]
        return rotate(value * SCORE_SCALE, cos, sin).astype(BF16)

    order = [n - 1, n - 2, 0]
    for k in range(1, n // 2 - 1):
        order += [n - 2 - k, k]
    order += [n // 2 - 1]
    for j in order:
        dk = dv = None
        for i in range(j, n):
            up = upstream(i)
            p = probs(i, j)[...]
            v = dot(p, up)
            ds = (p.astype(F32) * (dot_nt(x[j, 2], up) - delta[i])).astype(BF16)
            k = dot(ds, x[i, 0])
            t = dot(kt[j], ds)
            dqt[i] = dqt[i] + t if i in summed else t
            summed.add(i)
            dv, dk = (v, k) if i == j else (dv + v, dk + k)
        dsent[j, 1] = unrotated(dk, j)
        dsent[j, 2] = dv.astype(BF16)
        give_head(j, 1, 2, j)
        if j < n // 2:
            dsent[j, 0] = unrotated(dqt[j].T, j)
            give_head(j, 0, 1, n + j)
    for j in range(n // 2, n):
        dsent[j, 0] = unrotated(dqt[j].T, j)
        give_head(j, 0, 1, n + j)

    wide_sum(1)
    given["h2"].wait_recv()
    give("h3", left_m.at[1], left_m.at[2], near)
    wide_sum(2)
    down_sum()
    out_sum()

    def finish_wide(c):
        at, wide = CHUNKS[c]
        cols = pl.ds(at, wide)
        seconds[c].wait_recv()
        add_into(wg.at[pl.ds(0, part), cols], got_g.at[:, cols])
        store(wg.at[pl.ds(0, part), cols], kept_g.at[:, cols])

    finish_wide(0)
    finish_wide(1)
    seconds["d"].wait_recv()
    mine = wd.at[pl.ds(0, ff // 4), pl.ds(0, part)]
    add_into(mine, got_d)
    store(mine, kept_d)
    for first, count in ((1, 2), (0, 1)):
        span = pl.ds(first, count)
        for j in range(n):

            @pl.when(me != j)
            def finish():
                cols = pl.ds(j * HEAD_DIM, HEAD_DIM)
                sem = j if first == 1 else n + j
                copy = remote(
                    dsent.at[j, span], packed.at[span, :, cols], d_send.at[sem], d_recv.at[sem], seq_device(j)
                )
                copy.wait_send()
                copy.wait_recv()

    store(packed, packed_out)
    for copy in sends:
        copy.wait_send()
    for copy in stores:
        copy.wait()


def middle_block(att, resid, cot, gain_rows, w_out, w_gate, w_up, w_down, x, ot, ls, table):
    n = HEADS
    rows, width = resid.shape
    ff = w_gate.shape[1]
    half, part = ff // 2, width // 2
    hbm = pl.BlockSpec(memory_space=pl.ANY)
    vmem = pl.BlockSpec(memory_space=pltpu.VMEM)
    dma = pltpu.SemaphoreType.DMA
    low = pltpu.VMEM((rows, width), BF16)
    wide = pltpu.VMEM((rows, ff), BF16)
    full = pltpu.VMEM((rows, width), F32)
    scratch = [pltpu.VMEM(w.shape, BF16) for w in (w_out, w_gate, w_up, w_down)]
    scratch += [low, low, full, full, full, full]
    scratch += [low, wide, wide, wide, low, pltpu.VMEM((2, rows, ff), BF16), low, low]
    scratch += [
        pltpu.VMEM((4, width, rows), BF16),
        pltpu.VMEM((8, 2, ff // 16, rows), BF16),
        pltpu.VMEM((3, 8, ff // 16, rows), BF16),
        pltpu.VMEM((2, width, rows), BF16),
        pltpu.VMEM((3, rows, half), BF16),
        pltpu.VMEM((3, rows, part), BF16),
        pltpu.VMEM((rows, part), BF16),
        pltpu.VMEM((part, CHUNKS[-1][0]), BF16),
        pltpu.VMEM((ff // 4, part), BF16),
        pltpu.VMEM((half, 256), F32),
        pltpu.VMEM(x.shape, BF16),
        pltpu.VMEM(ot.shape, F32),
        pltpu.VMEM(table.shape, F32),
        pltpu.VMEM((n, rows, HEAD_DIM), BF16),
        pltpu.VMEM((n, HEAD_DIM, rows), BF16),
        pltpu.VMEM((n, HEAD_DIM, rows), F32),
        pltpu.VMEM((n, 1, rows), F32),
        pltpu.VMEM((n, 3, rows, HEAD_DIM), BF16),
        pltpu.VMEM((3, rows, width), BF16),
        dma((10,)),
        dma((7,)),
        dma((n,)),
        dma((n,)),
        dma((2 * n,)),
        dma((2 * n,)),
        dma((20,)),
        dma((20,)),
        dma((4,)),
        dma((4,)),
    ]
    return pl.pallas_call(
        middle_kernel,
        name="middle",
        out_shape=[
            jax.ShapeDtypeStruct((rows, width), BF16),
            jax.ShapeDtypeStruct((rows, width), F32),
            jax.ShapeDtypeStruct((8, width), F32),
            jax.ShapeDtypeStruct((3, rows, width), BF16),
            jax.ShapeDtypeStruct((ff // 4, part), BF16),
            jax.ShapeDtypeStruct((part, CHUNKS[-1][0]), BF16),
            jax.ShapeDtypeStruct((width, CHUNKS[-1][1]), BF16),
            jax.ShapeDtypeStruct((width, part), BF16),
        ],
        in_specs=[hbm] * 3 + [vmem] + [hbm] * 6 + [vmem] + [hbm],
        out_specs=[vmem, hbm, vmem, hbm] + [hbm] * 4,
        scratch_shapes=scratch,
        compiler_params=pltpu.CompilerParams(
            collective_id=2, has_side_effects=True, vmem_limit_bytes=62 << 20
        ),
    )(att, resid, cot, gain_rows, w_out, w_gate, w_up, w_down, x, ot, ls, table)


BEGUN = ((1, 0, 512, None), (1, 512, 512, None), (0, 0, 256, None), (0, 256, 256, None), (2, 0, 384, 1))
FRESH = ((1, 0, 0), (1, 1024, 0), (1, 2048, 1), (0, 0, 1))
SCHEDULE = (
    ("1", 2), ("U", 7), ("1", 1), ("F", 5), ("U", 8), ("S", 4), ("P", 0), ("1", 3),
    ("U", 6), ("O", 0), ("U", 9), ("W", 7), ("W", 8), ("D", 2), ("2", 2), ("1", 0),
    ("S", 7), ("D", 1), ("2", 1), ("C", 4), ("G", 0), ("S", 8), ("E", 2), ("1", 4),
    ("B", 5), ("D", 3), ("2", 3), ("S", 5), ("W", 9), ("S", 9), ("E", 1), ("G", 1),
    ("W", 6), ("S", 6), ("E", 3), ("C", 7), ("1", 7), ("D", 0), ("G", 2), ("2", 0),
    ("C", 8), ("1", 8), ("C", 5), ("D", 4), ("G", 3), ("2", 4), ("E", 0), ("1", 5),
    ("D", 7), ("2", 7), ("C", 6), ("G", 4), ("E", 4), ("1", 6), ("C", 9), ("D", 8),
    ("2", 8), ("E", 7), ("1", 9), ("D", 5), ("2", 5), ("E", 8), ("D", 6), ("2", 6),
    ("E", 5), ("E", 6), ("D", 9), ("2", 9), ("E", 9),
)


def dealt_blocks(left, slots, right, spread, bit, out, work):
    total = left.shape[1]
    shard = total // 32
    block = dot(left[slots[0]], right[0])
    for k in range(1, 4):
        block += dot(left[slots[k]], right[k])
    work[0:total, :] = block
    for z in range(4):
        for other in range(2):
            pieces = []
            for core in range(2):
                for b in range(2):
                    q = (b << bit) | (other << (1 - bit))
                    pieces.append(work[pl.ds((8 * z + 4 * core + q) * shard, shard), :])
            out[spread[other], pl.ds(z_place(z) * 4 * shard, 4 * shard), :] = jnp.concatenate(
                pieces, axis=0
            ).astype(BF16)


def tail_kernel(*refs):
    refs = list(refs)

    def take(count):
        taken, refs[:count] = refs[:count], []
        return taken

    begun, fresh = len(BEGUN), len(FRESH)
    single = begun
    first_fresh = begun + 1
    count = first_fresh + fresh
    kept_in = take(4)
    packed_in, ltn_in, ltj_in, wq_in, wa_in = take(5)
    resid, above, gain_rows, gain_parts = take(4)
    grad_joined = take(2)
    outs = take(5)
    (gains_out,) = take(1)
    held = take(2)
    sums, arrived2 = [None] * 4 + take(count - 4), [None] * 4 + take(count - 4)
    parts, arrived3, arrived4, finals = take(count), take(count), take(count), take(count)
    (got_o, wq, wa, packed, ltn, ltj, dealt, low, work, back_sum, gain_buf, gain_got) = take(12)
    (load_sem, u_send, u_recv, s_send, s_recv, z1_send, z1_recv) = take(7)
    (z2_send, z2_recv, c_send, c_recv, gain_send, gain_recv) = take(6)
    rows, width = resid.shape
    me = lax.axis_index("seq")
    dp = lax.axis_index("dp")
    core = me % 2
    bits = [dp % 2, dp // 2]
    z_low, z_high = (me // 2) % 2, me // 4
    mate = flipped(0, me)
    near = seq_device(mate)
    across = [{"dp": flipped(0, dp)}, {"dp": flipped(1, dp)}]
    diagonal = [{"seq": mate, "dp": flipped(0, dp)}, {"seq": mate, "dp": flipped(1, dp)}]
    beside = [seq_device(flipped(1, me)), seq_device(flipped(2, me))]
    greet([near] + across + diagonal + beside)
    loads = {}

    def load(key, src, dst):
        loads[key] = pltpu.make_async_copy(src, dst, load_sem.at[len(loads)])
        loads[key].start()

    load("packed", packed_in, packed)
    load("wq", wq_in, wq)
    greeted(7)
    sends = []

    def send(src, dst, send_sem, recv_sem, device):
        copy = remote(src, dst, send_sem, recv_sem, device)
        copy.start()
        sends.append(copy)
        return copy

    first, dealing, second, third, fourth, finished, taken = [], {}, {}, {}, {}, {}, set()

    def ready(key):
        if key not in taken:
            taken.add(key)
            loads[key].wait()

    def z_rows(u, which):
        tall = finals[u].shape[0]
        return pl.ds(pl.multiple_of(which * 2 * tall, 16), 2 * tall)

    def one_z(u, which):
        tall = finals[u].shape[0]
        return pl.ds(pl.multiple_of(which * tall, 16), tall)

    def start_first(u):
        first.append(send(kept_in[3].at[pl.ds(2, 2)], got_o, s_send.at[count], s_recv.at[count], across[0]))

    def take_first(u):
        first[0].wait_recv()
        ready(single)
        for k in (1, 0):
            add_into(sums[single].at[k], got_o.at[k])

    def start_columns(u):
        k = u - first_fresh
        bit = FRESH[k][2]
        source = low if k == 3 else packed.at[k]
        if k < 3:
            ready("packed")

        def columns(other_core, other_bit):
            place = (core + (1 - 2 * core) * other_core) * 2
            place = place + bits[bit] + (1 - 2 * bits[bit]) * other_bit
            return pl.ds(pl.multiple_of(place * 256, 256), 256)

        dealing[u] = [
            send(
                source.at[:, columns(*there)],
                dealt.at[k, slot],
                u_send.at[3 * k + slot - 1],
                u_recv.at[3 * k + slot - 1],
                device,
            )
            for there, slot, device in (
                ((0, 1), 2, across[bit]),
                ((1, 1), 3, diagonal[bit]),
                ((1, 0), 1, near),
            )
        ]
        dealt[k, 0] = source[:, columns(0, 0)]

    def start_second(u):
        if u < begun:
            array, at, wide, bit = BEGUN[u]
            rows_in = kept_in[array].shape[0] // 2
            src = kept_in[array].at[pl.ds(rows_in, rows_in), pl.ds(at, wide)]
        else:
            bit = 1 if u == single else 1 - FRESH[u - first_fresh][2]
            src = sums[u].at[1]
        second[u] = send(src, arrived2[u], s_send.at[u], s_recv.at[u], across[bit])

    def multiply(u):
        k = u - first_fresh
        out, column, bit = FRESH[k]
        slots = (0, 1, 2, 3) if (bit == 0 or k == 3) else (0, 1, 4, 5)
        left = ltj if k == 3 else ltn
        ready("ltj" if k == 3 else "ltn")
        for copy in dealing[u]:
            copy.wait_recv()
        spread = [(bits[1 - bit] + other) % 2 for other in range(2)]
        dealt_blocks(left, slots, dealt.at[k], spread, bit, sums[u], work)

    def take_second(u):
        second[u].wait_recv()
        if u < begun:
            ready(u)
        add_into(sums[u].at[0], arrived2[u])

    def start_third(u):
        theirs = z_rows(u, 1 - z_low)
        if u < 4:
            array, at, wide, _ = BEGUN[u]
            src = kept_in[array].at[theirs, pl.ds(at, wide)]
        else:
            src = sums[u].at[0, theirs]
        third[u] = send(src, arrived3[u], z1_send.at[u], z1_recv.at[u], beside[0])

    def take_third(u):
        third[u].wait_recv()
        if u < 4:
            array, at, wide, _ = BEGUN[u]
            ready(array)
            mine = held[array][:, pl.ds(at, wide)]
        else:
            mine = sums[u][0, z_rows(u, z_low), :]
        parts[u][...] = (mine.astype(F32) + arrived3[u][...].astype(F32)).astype(BF16)

    def start_fourth(u):
        fourth[u] = send(
            parts[u].at[one_z(u, 1 - z_high)], arrived4[u], z2_send.at[u], z2_recv.at[u], beside[1]
        )

    def take_fourth(u):
        fourth[u].wait_recv()
        finals[u][...] = parts[u][one_z(u, z_high), :].astype(F32) + arrived4[u][...].astype(F32)
        if u in (0, 1, 4):
            at, wide = CHUNKS[min(u, 2)]
            bit = 0
            cols = pl.ds(pl.multiple_of(bits[0] * (outs[3].shape[2] // 2) + at, 128), wide)
            target = outs[3].at[core, :, cols]
        elif u <= single:
            out, at, wide = (2, 0, width // 2) if u == single else (4,) + BEGUN[u][1:3]
            bit = None
            target = outs[out].at[:, pl.ds(pl.multiple_of(core * (width // 2) + at, 128), wide)]
        else:
            out, column, bit = FRESH[u - first_fresh]
            cols = pl.ds(pl.multiple_of((core * 2 + bits[bit]) * 256 + column, 256), 256)
            target = outs[out].at[:, cols]
        if bit is None:
            owners = [(core, None), (1 - core, near)]
        else:
            here, there = bits[bit], 1 - bits[bit]
            owners = [
                (core * 2 + here, None),
                ((1 - core) * 2 + here, near),
                (core * 2 + there, across[bit]),
                ((1 - core) * 2 + there, diagonal[bit]),
            ]
        shard = finals[u].shape[0] // len(owners)
        finished[u] = []
        for k, (place, device) in enumerate(owners):
            at = pl.ds(pl.multiple_of(place * shard, 8), shard)
            if k == 0:
                target[...] = finals[u][at, :]
            else:
                sem = 3 * u + k - 1
                finished[u].append(
                    send(finals[u].at[at], target, c_send.at[sem], c_recv.at[sem], device)
                )

    gain_steps = {}
    gain_partners = [near] + across + beside

    def send_gain(k):
        gain_steps[k] = send(
            gain_buf.at[k], gain_got.at[k], gain_send.at[k], gain_recv.at[k], gain_partners[k]
        )

    def add_gain(k):
        gain_steps[k].wait_recv()
        total = gain_buf[k] + gain_got[k]
        if k == 4:
            gains_out[...] = total
        else:
            gain_buf[k + 1] = total
            send_gain(k + 1)

    tile = 256

    def dense_back(_):
        ready("packed")
        ready("wq")
        load(1, kept_in[1].at[z_rows(0, z_low)], held[1])
        load(0, kept_in[0].at[z_rows(2, z_low)], held[0])
        load(single, kept_in[3].at[pl.ds(0, 2)], sums[single])
        load(4, kept_in[2].at[pl.ds(0, kept_in[2].shape[0] // 2)], sums[4].at[0])
        load("ltn", ltn_in, ltn)
        load("ltj", ltj_in, ltj)
        load("wa", wa_in, wa)
        for begin in range(0, width, tile):
            at = pl.ds(begin, tile)
            block = dot_nt(packed[0], wq[at, pl.ds(0, width)])
            block += dot_nt(packed[1], wq[at, pl.ds(width, width)])
            block += dot_nt(packed[2], wq[at, pl.ds(2 * width, width)])
            back_sum[:, at] = block
        part, gain0 = norm_back(resid[...], gain_rows[0:1, :].astype(F32), back_sum[...])
        low[...] = (above[...] + part).astype(BF16)
        gain_buf[0] = gain_parts[...]
        gain_buf[0, 0:1, :] = gain0[None, :]
        send_gain(0)

    def dense_out(_):
        ready("wa")
        for k in range(2):
            for begin in range(0, width, tile):
                from_row = pl.ds(k * width + begin, tile)
                grad_joined[k][:, pl.ds(begin, tile)] = dot_nt(low[...], wa[from_row, :])

    actions = {
        "F": start_first,
        "B": take_first,
        "U": start_columns,
        "S": start_second,
        "1": start_third,
        "2": start_fourth,
        "W": multiply,
        "C": take_second,
        "D": take_third,
        "E": take_fourth,
        "G": add_gain,
        "P": dense_back,
        "O": dense_out,
    }
    for action, u in SCHEDULE:
        actions[action](u)
    for u in range(count):
        for copy in finished[u]:
            copy.wait_recv()
    for copy in sends:
        copy.wait_send()


def tail(kept, packed, left_n, left_j, w_qkv, w_adapt, resid, above, gain_rows, gain_parts):
    rows, width = resid.shape
    hbm = pl.BlockSpec(memory_space=pl.ANY)
    vmem = pl.BlockSpec(memory_space=pltpu.VMEM)
    dma = pltpu.SemaphoreType.DMA
    fresh = len(FRESH)
    down, gate, last, out = kept
    every = [
        (kept[array].shape[0] // (4 if bit is None else 8), wide) for array, _, wide, bit in BEGUN
    ]
    every += [(out.shape[1] // 4, out.shape[2])]
    every += [(width // 8, 256)] * 3 + [(width // 4, 256)]
    count = len(every)
    slots = [1] + [2] * (1 + fresh)
    shapes = [
        (2 * width // 32, width),
        (width // 32, 3 * width),
        (width // 32, width),
        (2, width // 32, 2 * (gate.shape[1] + last.shape[1])),
        (down.shape[0] // 8, width),
    ]
    scratch = [pltpu.VMEM((value.shape[0] // 2, value.shape[1]), BF16) for value in (down, gate)]
    scratch += [pltpu.VMEM((k, 4 * tall, wide), BF16) for k, (tall, wide) in zip(slots, every[4:])]
    scratch += [pltpu.VMEM((4 * tall, wide), BF16) for tall, wide in every[4:]]
    scratch += [pltpu.VMEM((2 * tall, wide), BF16) for tall, wide in every]
    scratch += [pltpu.VMEM((2 * tall, wide), BF16) for tall, wide in every]
    scratch += [pltpu.VMEM((tall, wide), BF16) for tall, wide in every]
    scratch += [pltpu.VMEM((tall, wide), F32) for tall, wide in every]
    scratch += [
        pltpu.VMEM((2,) + out.shape[1:], BF16),
        pltpu.VMEM(w_qkv.shape, BF16),
        pltpu.VMEM(w_adapt.shape, BF16),
        pltpu.VMEM(packed.shape, BF16),
        pltpu.VMEM(left_n.shape, BF16),
        pltpu.VMEM(left_j.shape, BF16),
        pltpu.VMEM((4, 4, rows, 256), BF16),
        pltpu.VMEM((rows, width), BF16),
        pltpu.VMEM((2 * width, 256), F32),
        pltpu.VMEM((rows, width), F32),
        pltpu.VMEM((5, 8, width), F32),
        pltpu.VMEM((5, 8, width), F32),
    ]
    scratch += [dma((10,)), dma((3 * fresh,)), dma((3 * fresh,))]
    scratch += [dma((count + 1,)) for _ in range(2)]
    scratch += [dma((count,)) for _ in range(4)]
    scratch += [dma((3 * count,)) for _ in range(2)]
    scratch += [dma((5,)) for _ in range(2)]
    return pl.pallas_call(
        tail_kernel,
        name="tail",
        out_shape=[jax.ShapeDtypeStruct((rows, width), F32)] * 2
        + [jax.ShapeDtypeStruct(shape, F32) for shape in shapes]
        + [jax.ShapeDtypeStruct((8, width), F32)],
        in_specs=[hbm] * 9 + [vmem] * 4,
        out_specs=[vmem] * 8,
        scratch_shapes=scratch,
        compiler_params=pltpu.CompilerParams(
            collective_id=3, has_side_effects=True, vmem_limit_bytes=62 << 20
        ),
    )(*kept, packed, left_n, left_j, w_qkv, w_adapt, resid, above, gain_rows, gain_parts)


def finish_kernel(*refs):
    sources, gain_ref, targets, gain_out, sem = refs[:8], refs[8], refs[9:18], refs[18], refs[19]
    wide = sources[6]
    pairs = list(zip(sources[:6], targets[:6]))
    pairs += [(wide.at[0], targets[6]), (wide.at[1], targets[7]), (sources[7], targets[8])]
    copies = [
        pltpu.make_async_copy(src, dst, sem.at[k]) for k, (src, dst) in enumerate(pairs)
    ]
    for copy in copies:
        copy.start()
    share = gain_out.shape[1]
    at = (lax.axis_index("seq") * lax.axis_size("dp") + lax.axis_index("dp")) * share
    block = gain_ref[:, pl.ds(pl.multiple_of(at // 128 * 128, 128), 128)]
    here = lax.broadcasted_iota(jnp.int32, (128, share), 0) - at % 128
    picked = here == lax.broadcasted_iota(jnp.int32, (128, share), 1)
    gain_out[...] = lax.dot_general(
        block,
        picked.astype(F32),
        (((1,), (0,)), ((), ())),
        precision=lax.Precision.HIGHEST,
        preferred_element_type=F32,
    )[:4]
    for copy in copies:
        copy.wait()


def finish(*values):
    hbm = pl.BlockSpec(memory_space=pl.ANY)
    vmem = pl.BlockSpec(memory_space=pltpu.VMEM)
    wide, gains = values[6], values[8]
    share = gains.shape[1] // (lax.axis_size("seq") * lax.axis_size("dp"))
    like = list(values[:6]) + [wide[0], wide[1], values[7]]
    return pl.pallas_call(
        finish_kernel,
        name="finish",
        out_shape=[jax.ShapeDtypeStruct(value.shape, value.dtype) for value in like]
        + [jax.ShapeDtypeStruct((4, share), F32)],
        in_specs=[vmem] * 9,
        out_specs=[hbm] * 9 + [vmem],
        scratch_shapes=[pltpu.SemaphoreType.DMA((9,))],
        compiler_params=pltpu.CompilerParams(vmem_limit_bytes=62 << 20),
    )(*values)


def xor_permute(value, axis, mask):
    return lax.ppermute(value, axis, [(i, i ^ mask) for i in range(lax.axis_size(axis))])


def quadrants(left):
    n, parts = lax.axis_size("seq"), lax.axis_size("dp")
    tokens, rows = left.shape
    shard = rows // (n * parts)
    split = left.reshape(tokens, n, parts, shard).transpose(2, 0, 1, 3)
    split = split.reshape(parts, tokens, n * shard)
    me = lax.axis_index("dp")
    return jnp.concatenate(
        [lax.dynamic_index_in_dim(split, me ^ m, 0, keepdims=True) for m in range(parts)]
    )


def other_core(left, right):
    core = lax.axis_index("seq") % 2
    half = right.shape[1] // 2
    mine = lax.dynamic_slice_in_dim(right, core * half, half, 1)
    theirs = lax.dynamic_slice_in_dim(right, (1 - core) * half, half, 1)
    left_in = xor_permute(left, "seq", 1)
    right_in = xor_permute(theirs, "seq", 1)
    return jnp.concatenate([left, left_in], axis=1), jnp.concatenate([mine, right_in], axis=0)


def scattered_sum(left, right, bits):
    n, parts = lax.axis_size("seq"), lax.axis_size("dp")
    cols = right.shape[1]
    left, right = other_core(quadrants(left), right)
    got = {}
    masks = list(range(parts))
    for bit in bits:
        outgoing = [m for m in masks if m >> bit & 1]
        masks = [m for m in masks if not m >> bit & 1]
        blocks = []
        for m in outgoing:
            block = dot_tn(left[m], right)
            for more in got.get(m, ()):
                block = block + more.astype(F32)
            blocks.append(block.astype(BF16))
        incoming = xor_permute(jnp.stack(blocks), "dp", 1 << bit)
        for k, m in enumerate(outgoing):
            got.setdefault(m ^ (1 << bit), []).append(incoming[k])
    block = dot_tn(left[0], right)
    for more in got.get(0, ()):
        block = block + more.astype(F32)
    shard = block.shape[0] // n
    block = block.astype(BF16).reshape(n, shard, cols // 2)
    block = lax.all_to_all(block, "seq", 0, 0)
    block = jnp.sum(block.reshape(n // 2, 2, shard, cols // 2).astype(F32), axis=0)
    return block.transpose(1, 0, 2).reshape(shard, cols)


def small_sum(value):
    value = value.reshape(value.shape[0], -1, value.shape[1])
    for axis in ("seq", "dp"):
        size = lax.axis_size(axis)
        me = lax.axis_index(axis)
        for bit in reversed(range(size.bit_length() - 1)):
            half = value.shape[2] // 2
            mine = (me >> bit) & 1
            kept = lax.dynamic_slice_in_dim(value, mine * half, half, 2)
            sent = lax.dynamic_slice_in_dim(value, (1 - mine) * half, half, 2)
            value = kept + xor_permute(sent, axis, 1 << bit)
    return value[:, 0]


def local(state, embedded, cotangent, w_adapt, w_qkv, w_out, w_gate, w_up, w_down, gains):
    seq_count, rows, width = state.shape
    n, parts = lax.axis_size("seq"), lax.axis_size("dp")
    tokens = seq_count * rows
    me = lax.axis_index("seq")
    bits = list(range(parts.bit_length() - 1))
    copies = max(1, n // HEADS)
    held = max(1, HEADS // n)
    owners = n // copies
    cos_np, sin_np = angle_tables(n * rows)
    cos_all, sin_all = jnp.asarray(cos_np), jnp.asarray(sin_np)
    cos = lax.dynamic_slice_in_dim(cos_all, me * rows, rows, 0)[:, None, :]
    sin = lax.dynamic_slice_in_dim(sin_all, me * rows, rows, 0)[:, None, :]
    gain_rows = gains.astype(F32)
    state, embedded = state.reshape(tokens, width), embedded.reshape(tokens, width)

    def to_heads(flat):
        return flat.reshape(tokens, HEADS, HEAD_DIM)

    def to_owner(parts_in):
        sent = jnp.stack(parts_in).reshape(len(parts_in), tokens, owners, held, HEAD_DIM)
        sent = sent.transpose(2, 3, 0, 1, 4)
        if copies > 1:
            sent = jnp.repeat(sent, copies, axis=0)
        return lax.all_to_all(sent, "seq", 0, 0)

    def from_owner(value):
        back = lax.all_to_all(value, "seq", 0, 0)[::copies]
        back = back.reshape(HEADS, -1, tokens, HEAD_DIM)
        return back.transpose(2, 1, 0, 3).reshape(tokens, -1)

    table = jnp.asarray(np.concatenate([cos_np, sin_np], axis=1))
    if n == HEADS and seq_count == 1 and parts == 4:
        resid, normed, attended, qkv, attended_t, logsum, left_n, left_j = front(
            state, embedded, w_adapt, w_qkv, gains, table
        )
        qkv, attended_t, logsum = qkv[:, None], attended_t[:, None], logsum[:, None]
    else:
        resid = dot(state, w_adapt[:width]) + dot(embedded, w_adapt[width:])
        normed = mean_norm(resid, gain_rows[0]).astype(BF16)
        packed = dot(normed, w_qkv)
        queries = rotate(to_heads(packed[:, :width]), cos, sin).astype(BF16)
        keys = rotate(to_heads(packed[:, width : 2 * width]), cos, sin).astype(BF16)
        values = to_heads(packed[:, 2 * width :]).astype(BF16)
        qkv = to_owner((queries, keys, values))
        attended, attended_t, logsum = attention(qkv)
        attended = from_owner(attended[:, :, None])
    shape = (seq_count, rows, width)
    if n == HEADS and parts == 4 and seq_count == 1:
        layer_out, middle_grad, gain_parts, packed_low, *kept = middle_block(
            attended,
            resid,
            cotangent.reshape(tokens, width),
            gains,
            w_out,
            w_gate,
            w_up,
            w_down,
            qkv[:, 0],
            attended_t[:, 0],
            logsum[:, 0],
            table,
        )
        grad_state, grad_embedded, grad_adapt, grad_qkv, grad_out, grad_wide, grad_down, gains_sum = tail(
            kept[:3] + [kept[3].reshape(4, width // 4, width // 2)],
            packed_low,
            left_n,
            left_j,
            w_qkv,
            w_adapt,
            resid,
            middle_grad,
            gains,
            gain_parts,
        )
        outs = finish(
            layer_out,
            grad_state,
            grad_embedded,
            grad_adapt,
            grad_qkv,
            grad_out,
            grad_wide,
            grad_down,
            gains_sum,
        )
        return tuple(value.reshape(shape) for value in outs[:3]) + tuple(outs[3:])
    branch = dot(attended, w_out)
    middle = resid + mean_norm(branch, gain_rows[1])
    normed_mid = mean_norm(middle, gain_rows[2]).astype(BF16)
    gate_pre = dot(normed_mid, w_gate)
    up_pre = dot(normed_mid, w_up)
    sigmoid_gate = jax.nn.sigmoid(gate_pre)
    silu_gate = gate_pre * sigmoid_gate
    hidden = (silu_gate * up_pre).astype(BF16)
    down_out = dot(hidden, w_down)
    layer_out = middle + mean_norm(down_out, gain_rows[3])
    out_grad = cotangent.astype(F32).reshape(tokens, width)
    down_grad, gain_grad3 = norm_back(down_out, gain_rows[3], out_grad)
    down_low = down_grad.astype(BF16)
    hidden_grad = dot_nt(down_low, w_down)
    gate_low = (
        hidden_grad * up_pre * sigmoid_gate * (1.0 + gate_pre * (1.0 - sigmoid_gate))
    ).astype(BF16)
    up_low = (hidden_grad * silu_gate).astype(BF16)
    mid_norm_grad = dot_nt(gate_low, w_gate) + dot_nt(up_low, w_up)
    middle_part, gain_grad2 = norm_back(middle, gain_rows[2], mid_norm_grad)
    middle_grad = out_grad + middle_part
    branch_grad, gain_grad1 = norm_back(branch, gain_rows[1], middle_grad)
    branch_low = branch_grad.astype(BF16)
    attended_grad = dot_nt(branch_low, w_out).astype(BF16)
    upstream = to_owner((to_heads(attended_grad),))[:, :, 0]
    packed_grad = attention_back(qkv, upstream, attended_t, logsum, cos_all, sin_all)
    packed_low = from_owner(packed_grad)
    normed_grad = dot_nt(packed_low, w_qkv)
    resid_part, gain_grad0 = norm_back(resid, gain_rows[0], normed_grad)
    resid_low = (middle_grad + resid_part).astype(BF16)
    grad_state = dot_nt(resid_low, w_adapt[:width])
    grad_embedded = dot_nt(resid_low, w_adapt[width:])
    flipped = bits[::-1]
    joined = jnp.concatenate([state, embedded], axis=-1)
    grad_down = scattered_sum(hidden, down_low, bits)
    grad_gate = scattered_sum(normed_mid, gate_low, flipped)
    grad_up = scattered_sum(normed_mid, up_low, bits)
    grad_out = scattered_sum(attended, branch_low, flipped)
    grad_qkv = scattered_sum(normed, packed_low, flipped)
    grad_adapt = scattered_sum(joined, resid_low, bits)
    grad_gains = jnp.stack([gain_grad0, gain_grad1, gain_grad2, gain_grad3])
    grad_gains = small_sum(grad_gains)
    return (
        layer_out.reshape(shape).astype(BF16),
        grad_state.reshape(shape),
        grad_embedded.reshape(shape),
        grad_adapt,
        grad_qkv,
        grad_out,
        grad_gate,
        grad_up,
        grad_down,
        grad_gains,
    )


def solution(mesh):
    tokens = P("dp", "seq", None)
    rows = P(("seq", "dp"), None)
    return jax.shard_map(
        local,
        mesh=mesh,
        in_specs=(tokens,) * 3 + (P(),) * 7,
        out_specs=(tokens,) * 3 + (rows,) * 6 + (P(None, ("seq", "dp")),),
        check_vma=False,
    )
```

```python
import functools
import math

import jax
import jax.numpy as jnp
import numpy as np
from jax import lax
from jax.experimental import pallas as pl
from jax.experimental.pallas import tpu as pltpu
from jax.sharding import PartitionSpec as P

HEADS = 8
HEAD_DIM = 128
norm_eps = 1e-06
rope_base = 50000.0
F32 = jnp.float32
BF16 = jnp.bfloat16
MESH = pl.DeviceIdType.MESH
NEG = -1e30
SCORE_SCALE = 1.0 / math.sqrt(HEAD_DIM)
LOG2E = 1.0 / math.log(2.0)


def mean_norm(values_in, gain_row):
    return (
        values_in
        * lax.rsqrt(jnp.mean(values_in * values_in, axis=-1, keepdims=True) + norm_eps)
        * gain_row
    )


def norm_back(values_in, gain_row, upstream):
    inverse = lax.rsqrt(jnp.mean(values_in * values_in, axis=-1, keepdims=True) + norm_eps)
    scaled = upstream * gain_row
    value_grad = inverse * scaled - values_in * (inverse * inverse * inverse) * jnp.mean(
        values_in * scaled, axis=-1, keepdims=True
    )
    gain_grad = jnp.sum(upstream * values_in * inverse, axis=0)
    return (value_grad, gain_grad)


def angle_tables(length):
    half_dim = HEAD_DIM // 2
    freqs = np.exp(
        np.arange(half_dim, dtype=np.float32) * np.float32(-2.0 * math.log(rope_base) / HEAD_DIM)
    ).astype(np.float32)
    angles = np.arange(length, dtype=np.float32)[:, None] * freqs[None, :]
    return np.cos(angles).astype(np.float32), np.sin(angles).astype(np.float32)


def rotate(heads_in, cos_table, sin_table):
    half_dim = heads_in.shape[-1] // 2
    lower_half = heads_in[..., :half_dim]
    upper_half = heads_in[..., half_dim:]
    return jnp.concatenate(
        [
            lower_half * cos_table - upper_half * sin_table,
            upper_half * cos_table + lower_half * sin_table,
        ],
        axis=-1,
    )


def dot(a, b):
    return lax.dot_general(a, b, (((1,), (0,)), ((), ())), preferred_element_type=F32)


def dot_tn(a, b):
    return lax.dot_general(a, b, (((0,), (0,)), ((), ())), preferred_element_type=F32)


def dot_nt(a, b):
    return lax.dot_general(a, b, (((1,), (1,)), ((), ())), preferred_element_type=F32)


def span(low, high, body, unrolled):
    if unrolled:
        for i in range(low, high):
            body(i)
    else:
        lax.fori_loop(low, high, lambda i, c: (body(i), c)[1], 0)


def causal_fill(block, fill):
    kv = lax.broadcasted_iota(jnp.int32, block.shape, 0)
    q = lax.broadcasted_iota(jnp.int32, block.shape, 1)
    return jnp.where(q >= kv, block, fill)


def attention_kernel(x_ref, o_ref, ot_ref, ls_ref, vt_ref, s_ref):
    n, hp, _, rows, _ = x_ref.shape
    unrolled = n <= 8
    factor = SCORE_SCALE * LOG2E
    for h in range(hp):
        for j in range(n):
            vt_ref[j] = x_ref[j, h, 2].astype(F32).T.astype(BF16)

        def query_block(i):
            q = x_ref[i, h, 0]
            diag = causal_fill(dot_nt(x_ref[i, h, 1], q), NEG)

            def first(j, peak):
                s = dot_nt(x_ref[j, h, 1], q)
                s_ref[j] = s
                return jnp.maximum(peak, jnp.max(s, axis=0, keepdims=True))

            peak = jnp.max(diag, axis=0, keepdims=True)
            if unrolled:
                for j in range(i):
                    peak = first(j, peak)
            else:
                peak = lax.fori_loop(0, i, first, peak)
            shift = peak * factor
            p = jnp.exp2(diag * factor - shift)
            total = jnp.sum(p, axis=0, keepdims=True)
            acc = dot(vt_ref[i], p.astype(BF16))

            def second(j, state):
                total, acc = state
                p = jnp.exp2(s_ref[j] * factor - shift)
                return (
                    total + jnp.sum(p, axis=0, keepdims=True),
                    acc + dot(vt_ref[j], p.astype(BF16)),
                )

            state = (total, acc)
            if unrolled:
                for j in range(i):
                    state = second(j, state)
            else:
                state = lax.fori_loop(0, i, second, state)
            total, acc = state
            acc = acc / total
            ot_ref[i, h] = acc
            o_ref[i, h] = acc.T.astype(BF16)
            ls_ref[i, h] = shift + jnp.log2(total)

        span(0, n, query_block, unrolled)


def attention(x):
    n, hp, _, rows, dim = x.shape
    pairs = n * (n + 1) // 2 * rows * rows * hp
    return pl.pallas_call(
        attention_kernel,
        name="attention",
        out_shape=(
            jax.ShapeDtypeStruct((n, hp, rows, dim), BF16),
            jax.ShapeDtypeStruct((n, hp, dim, rows), F32),
            jax.ShapeDtypeStruct((n, hp, 1, rows), F32),
        ),
        scratch_shapes=[
            pltpu.VMEM((n, dim, rows), BF16),
            pltpu.VMEM((n, rows, rows), F32),
        ],
        compiler_params=pltpu.CompilerParams(vmem_limit_bytes=40 << 20),
        cost_estimate=pl.CostEstimate(
            flops=pairs * dim * 8, bytes_accessed=x.size * 4, transcendentals=pairs
        ),
    )(x)


def attention_back_kernel(
    x_ref, g_ref, ot_ref, ls_ref, cos_ref, sin_ref, out_ref, kt_ref, dqt_ref, delta_ref
):
    n, hp, _, rows, _ = x_ref.shape
    unrolled = n <= 8
    factor = SCORE_SCALE * LOG2E
    for h in range(hp):
        for j in range(n):
            kt_ref[j] = x_ref[j, h, 1].astype(F32).T.astype(BF16)
            delta_ref[j] = jnp.sum(
                g_ref[j, h].astype(F32).T * ot_ref[j, h], axis=0, keepdims=True
            )

        def unrotated(value, i):
            turned = pl.ds(i * rows, rows)
            cos, sin = cos_ref[turned], sin_ref[turned]
            return rotate(value * SCORE_SCALE, cos, -sin).astype(BF16)

        def pair(i, j, diagonal):
            q, g = x_ref[i, h, 0], g_ref[i, h]
            p = jnp.exp2(dot_nt(x_ref[j, h, 1], q) * factor - ls_ref[i, h])
            if diagonal:
                p = causal_fill(p, 0.0)
            dv = dot(p.astype(BF16), g)
            ds = (p * (dot_nt(x_ref[j, h, 2], g) - delta_ref[i])).astype(BF16)
            dk = dot(ds, q)
            dqt = dot(kt_ref[j], ds)
            return dv, dk, dqt

        def key_block(j):
            dv, dk, dqt = pair(j, j, True)
            if unrolled:
                dqt_ref[j] = dqt if j == 0 else dqt_ref[j] + dqt
            else:
                dqt_ref[j] = jnp.where(j == 0, 0.0, dqt_ref[j]) + dqt

            def step(i, state):
                dv, dk = state
                v, k, t = pair(i, j, False)
                if unrolled:
                    dqt_ref[i] = t if j == 0 else dqt_ref[i] + t
                else:
                    dqt_ref[i] = jnp.where(j == 0, 0.0, dqt_ref[i]) + t
                return dv + v, dk + k

            state = (dv, dk)
            if unrolled:
                for i in range(j + 1, n):
                    state = step(i, state)
            else:
                state = lax.fori_loop(j + 1, n, step, state)
            dv, dk = state
            out_ref[j, h, 0] = unrotated(dqt_ref[j].T, j)
            out_ref[j, h, 1] = unrotated(dk, j)
            out_ref[j, h, 2] = dv.astype(BF16)

        span(0, n, key_block, unrolled)


def attention_back(x, g, ot, ls, cos, sin):
    n, hp, _, rows, dim = x.shape
    pairs = n * (n + 1) // 2 * rows * rows * hp
    return pl.pallas_call(
        attention_back_kernel,
        name="attention_back",
        out_shape=jax.ShapeDtypeStruct(x.shape, BF16),
        scratch_shapes=[
            pltpu.VMEM((n, dim, rows), BF16),
            pltpu.VMEM((n, dim, rows), F32),
            pltpu.VMEM((n, 1, rows), F32),
        ],
        compiler_params=pltpu.CompilerParams(vmem_limit_bytes=40 << 20),
        cost_estimate=pl.CostEstimate(
            flops=pairs * dim * 20, bytes_accessed=x.size * 6, transcendentals=pairs
        ),
    )(x, g, ot, ls, cos, sin)


def seq_device(index):
    return {"seq": index}


def greet(peers):
    barrier = pltpu.get_barrier_semaphore()
    for device in peers:
        pl.semaphore_signal(barrier, inc=1, device_id=device, device_id_type=MESH)


def greeted(count):
    pl.semaphore_wait(pltpu.get_barrier_semaphore(), count)


def remote(src, dst, send, recv, device):
    return pltpu.make_async_remote_copy(
        src_ref=src,
        dst_ref=dst,
        send_sem=send,
        recv_sem=recv,
        device_id=device,
        device_id_type=MESH,
    )


def front_kernel(
    state_ref,
    embedded_ref,
    wa_ref,
    wq_ref,
    gain_ref,
    table_ref,
    resid_out,
    normed_out,
    att_out,
    x_out,
    ot_out,
    ls_out,
    ltn_out,
    ltj_out,
    wa,
    wq,
    joined,
    resid,
    normed,
    sent,
    x,
    vt,
    scores,
    ot,
    o_sent,
    att,
    ltn,
    ltj,
    table,
    load_sem,
    store_sem,
    send_sem,
    recv_sem,
    o_send_sem,
    o_recv_sem,
    l_send_sem,
    l_recv_sem,
):
    n, rows, width = HEADS, state_ref.shape[0], state_ref.shape[1]
    me = lax.axis_index("seq")
    dp = lax.axis_index("dp")
    peers = [seq_device((me + k) % n) for k in range(1, n)]
    across = [{"dp": flipped(0, dp)}, {"dp": flipped(1, dp)}]
    near = seq_device(flipped(0, me))
    greet(peers + across)
    loads = [
        pltpu.make_async_copy(state_ref, joined.at[0], load_sem.at[0]),
        pltpu.make_async_copy(wa_ref.at[pl.ds(0, width)], wa.at[0], load_sem.at[1]),
        pltpu.make_async_copy(embedded_ref, joined.at[1], load_sem.at[2]),
        pltpu.make_async_copy(wa_ref.at[pl.ds(width, width)], wa.at[1], load_sem.at[3]),
        pltpu.make_async_copy(wq_ref, wq, load_sem.at[4]),
        pltpu.make_async_copy(
            table_ref.at[pl.ds(pl.multiple_of(me * rows, 8), rows)], table, load_sem.at[5]
        ),
    ]
    for copy in loads:
        copy.start()
    tile = 256
    for half in range(2):
        loads[2 * half].wait()
        loads[2 * half + 1].wait()

        for begin in range(0, width, tile):
            cols = pl.ds(begin, tile)
            block = dot(joined[half], wa[half, :, cols])
            resid[:, cols] = block if half == 0 else resid[:, cols] + block
    normed[...] = mean_norm(resid[...], gain_ref[0:1, :].astype(F32)).astype(BF16)
    stores = [
        pltpu.make_async_copy(resid, resid_out, store_sem.at[0]),
        pltpu.make_async_copy(normed, normed_out, store_sem.at[1]),
    ]
    for copy in stores:
        copy.start()
    loads[4].wait()
    lefts = []

    def share(source, out, slot, device):
        k = len(lefts)
        copy = remote(source, out.at[slot], l_send_sem.at[k], l_recv_sem.at[k], device)
        copy.start()
        lefts.append(copy)
    loads[5].wait()
    cos, sin = table[:, 0 : HEAD_DIM // 2], table[:, HEAD_DIM // 2 : HEAD_DIM]
    pairs = n // 2
    order = [2, 1, 3, 0] if pairs == 4 else list(range(pairs - 1, -1, -1))
    sends = []
    for k in order:
        chip = (me // 2 + k) % pairs
        for part in range(3):
            cols = pl.ds(pl.multiple_of(part * width + chip * 2 * HEAD_DIM, 2 * HEAD_DIM), 2 * HEAD_DIM)
            block = dot(normed[...], wq[:, cols])
            for core in range(2):
                head = block[:, core * HEAD_DIM : (core + 1) * HEAD_DIM]
                if part < 2:
                    head = rotate(head, cos, sin)
                sent[2 * chip + core, part] = head.astype(BF16)
        if k == order[0]:
            greeted(n + 1)
        for core in range(2):
            owner = 2 * chip + core
            if k == 0:
                continue
            copy = remote(sent.at[owner], x.at[me], send_sem.at[owner], recv_sem.at[me], seq_device(owner))
            copy.start()
            sends.append(copy)
    mate = me + 1 - 2 * (me % 2)
    copy = remote(sent.at[mate], x.at[me], send_sem.at[mate], recv_sem.at[me], seq_device(mate))
    copy.start()
    sends.append(copy)
    x[me] = sent[me]
    transposed_into(normed, ltn)
    for half in range(2):
        transposed_into(joined.at[half], ltj.at[pl.ds(half * width, width)])
    stores.append(pltpu.make_async_copy(ltn, ltn_out.at[0], store_sem.at[4]))
    stores.append(pltpu.make_async_copy(ltj, ltj_out.at[0], store_sem.at[5]))
    for copy in stores[2:]:
        copy.start()
    share(ltn, ltn_out, 2, across[0])
    share(ltn, ltn_out, 4, across[1])
    share(ltj, ltj_out, 2, across[1])
    share(ltn, ltn_out, 1, near)
    share(ltj, ltj_out, 1, near)
    factor = SCORE_SCALE * LOG2E
    for i in range(n):

        @pl.when(me != i)
        def arrive():
            remote(sent.at[0], x.at[i], send_sem.at[0], recv_sem.at[i], seq_device(i)).wait_recv()

        vt[i] = x[i, 2].astype(F32).T.astype(BF16)
        q = x[i, 0]
        diag = causal_fill(dot_nt(x[i, 1], q), NEG)
        peak = jnp.max(diag, axis=0, keepdims=True)
        for j in range(i):
            block = dot_nt(x[j, 1], q)
            scores[j] = block
            peak = jnp.maximum(peak, jnp.max(block, axis=0, keepdims=True))
        shift = peak * factor
        p = jnp.exp2(diag * factor - shift)
        total = jnp.sum(p, axis=0, keepdims=True)
        acc = dot(vt[i], p.astype(BF16))
        for j in range(i):
            p = jnp.exp2(scores[j] * factor - shift)
            total = total + jnp.sum(p, axis=0, keepdims=True)
            acc = acc + dot(vt[j], p.astype(BF16))
        acc = acc / total
        ot[i] = acc
        o_sent[i] = acc.T.astype(BF16)
        ls_out[i] = shift + jnp.log2(total)
        mine = pl.ds(pl.multiple_of(me * HEAD_DIM, HEAD_DIM), HEAD_DIM)

        @pl.when(me != i)
        def give():
            remote(o_sent.at[i], att.at[:, mine], o_send_sem.at[i], o_recv_sem.at[me], seq_device(i)).start()

        @pl.when(me == i)
        def keep():
            att[:, mine] = o_sent[i]

    stores.append(pltpu.make_async_copy(x, x_out, store_sem.at[2]))
    stores.append(pltpu.make_async_copy(ot, ot_out, store_sem.at[3]))
    for copy in stores[4:]:
        copy.start()
    for k, out, slot in ((0, ltn_out, 2), (1, ltn_out, 4), (2, ltj_out, 2)):
        lefts[k].wait_recv()
        share(out.at[slot], out, slot + 1, near)
    for copy in sends:
        copy.wait_send()
    for i in range(n):

        @pl.when(me != i)
        def finish():
            cols = pl.ds(i * HEAD_DIM, HEAD_DIM)
            copy = remote(o_sent.at[i], att.at[:, cols], o_send_sem.at[i], o_recv_sem.at[i], seq_device(i))
            copy.wait_send()
            copy.wait_recv()

    att_out[...] = att[...]
    for copy in stores:
        copy.wait()
    for k, copy in enumerate(lefts):
        copy.wait_send()
        if k > 2:
            copy.wait_recv()


def front(state, embedded, w_adapt, w_qkv, gains, table):
    n = HEADS
    rows, width = state.shape
    hbm = pl.BlockSpec(memory_space=pl.ANY)
    vmem = pl.BlockSpec(memory_space=pltpu.VMEM)
    return pl.pallas_call(
        front_kernel,
        name="front",
        out_shape=(
            jax.ShapeDtypeStruct((rows, width), F32),
            jax.ShapeDtypeStruct((rows, width), BF16),
            jax.ShapeDtypeStruct((rows, width), BF16),
            jax.ShapeDtypeStruct((n, 3, rows, HEAD_DIM), BF16),
            jax.ShapeDtypeStruct((n, HEAD_DIM, rows), F32),
            jax.ShapeDtypeStruct((n, 1, rows), F32),
            jax.ShapeDtypeStruct((6, width, rows), BF16),
            jax.ShapeDtypeStruct((4, 2 * width, rows), BF16),
        ),
        in_specs=[hbm, hbm, hbm, hbm, vmem, hbm],
        out_specs=(hbm, hbm, vmem, hbm, hbm, vmem, hbm, hbm),
        scratch_shapes=[
            pltpu.VMEM((2, width, width), BF16),
            pltpu.VMEM((width, 3 * width), BF16),
            pltpu.VMEM((2, rows, width), BF16),
            pltpu.VMEM((rows, width), F32),
            pltpu.VMEM((rows, width), BF16),
            pltpu.VMEM((n, 3, rows, HEAD_DIM), BF16),
            pltpu.VMEM((n, 3, rows, HEAD_DIM), BF16),
            pltpu.VMEM((n, HEAD_DIM, rows), BF16),
            pltpu.VMEM((n, rows, rows), F32),
            pltpu.VMEM((n, HEAD_DIM, rows), F32),
            pltpu.VMEM((n, rows, HEAD_DIM), BF16),
            pltpu.VMEM((rows, width), BF16),
            pltpu.VMEM((width, rows), BF16),
            pltpu.VMEM((2 * width, rows), BF16),
            pltpu.VMEM((rows, HEAD_DIM), F32),
            pltpu.SemaphoreType.DMA((6,)),
            pltpu.SemaphoreType.DMA((6,)),
            pltpu.SemaphoreType.DMA((n,)),
            pltpu.SemaphoreType.DMA((n,)),
            pltpu.SemaphoreType.DMA((n,)),
            pltpu.SemaphoreType.DMA((n,)),
            pltpu.SemaphoreType.DMA((8,)),
            pltpu.SemaphoreType.DMA((8,)),
        ],
        compiler_params=pltpu.CompilerParams(
            collective_id=1, has_side_effects=True, vmem_limit_bytes=62 << 20
        ),
    )(state, embedded, w_adapt, w_qkv, gains, table)


def flipped(bit, value):
    return value + (1 - 2 * ((value // (1 << bit)) % 2)) * (1 << bit)


def unit_slots(first, dp):
    slots = []
    for q in range(4):
        turned = [(dp + q) % 2, (dp // 2 + q // 2) % 2]
        slots.append(turned[first] * 2 + turned[1 - first])
    return slots


def transposed_into(source, target):
    tile = 256
    for begin in range(0, source.shape[1], tile):
        target[pl.ds(begin, tile), :] = source[:, pl.ds(begin, tile)].T


def add_into(target, more):
    rows = target.shape[0]
    chunk = 16
    while rows % (chunk * 2) == 0 and chunk < 64:
        chunk *= 2

    def step(t, c):
        at = pl.ds(pl.multiple_of(t * chunk, chunk), chunk)
        target[at, :] = (target[at, :].astype(F32) + more[at, :].astype(F32)).astype(BF16)
        return c

    lax.fori_loop(0, rows // chunk, step, 0)


CHUNKS = ((0, 512), (512, 512), (1024, 384))


def z_place(z):
    return (z % 2) * 2 + z // 2


def transposed_blocks(source, target):
    tile = 256
    parts, size = target.shape[1], target.shape[2]
    for begin in range(0, source.shape[1], tile):
        block = source[:, pl.ds(begin, tile)].T
        for k in range(begin // size, (begin + tile - 1) // size + 1):
            low, high = max(begin, size * k), min(begin + tile, size * (k + 1))
            target[k // parts, k % parts, pl.ds(low - size * k, high - low), :] = block[
                low - begin : high - begin
            ]


def middle_kernel(*refs):
    refs = list(refs)

    def take(count):
        taken, refs[:count] = refs[:count], []
        return taken

    (att_in, resid_in, cot_in, gain_rows, wo_in, wg_in, wu_in, wd_in) = take(8)
    (x_in, ot_in, ls_ref, table_in) = take(4)
    (layer_out, above_out, gains_out, packed_out) = take(4)
    (kept_d, kept_z, kept_g, kept_h, kept_o) = take(5)
    (wo, wg, wu, wd, att, cot, resid, branch, mid, down, above) = take(11)
    (normed, hidden, gate_by, up_by, down_low, wide_low, branch_low, dout) = take(8)
    (left_n, left_h, left_m, left_a, right_g, right_d, right_b) = take(7)
    (got_g, got_d, got_z) = take(3)
    (work, x, ot, table, g, kt, dqt, delta, dsent, packed) = take(10)
    (load_sem, store_sem, g_send, g_recv, d_send, d_recv, m_send, m_recv, s_send, s_recv) = take(10)
    n, (rows, width) = HEADS, resid.shape
    ff = wg.shape[1]
    half, part = ff // 2, width // 2
    me = lax.axis_index("seq")
    dp = lax.axis_index("dp")
    core = me % 2
    mate = flipped(0, me)
    bits = [dp % 2, dp // 2]
    near = seq_device(mate)
    across = [{"dp": flipped(0, dp)}, {"dp": flipped(1, dp)}]
    diagonal = [{"seq": mate, "dp": flipped(0, dp)}, {"seq": mate, "dp": flipped(1, dp)}]
    greet([seq_device((me + k) % n) for k in range(1, n)] + across + diagonal)
    loads = {}
    for key, src, dst in (
        ("att", att_in, att),
        ("wo", wo_in, wo),
        ("resid", resid_in, resid),
        ("wg", wg_in, wg),
        ("wu", wu_in, wu),
        ("cot", cot_in, cot),
        ("wd", wd_in, wd),
        ("x", x_in, x),
        ("ot", ot_in, ot),
        ("table", table_in, table),
    ):
        copy = pltpu.make_async_copy(src, dst, load_sem.at[len(loads)])
        copy.start()
        loads[key] = copy
    tile = 256
    gains = [gain_rows[k : k + 1, :].astype(F32) for k in range(4)]

    def tiles(total, body):
        for begin in range(0, total, tile):
            body(pl.ds(begin, tile))

    sends = []
    given = {}

    issued = []

    def give(key, src, dst, device):
        k = len(issued)
        copy = remote(src, dst, m_send.at[k], m_recv.at[k], device)
        copy.start()
        issued.append(key)
        sends.append(copy)
        given[key] = copy

    loads["att"].wait()
    loads["wo"].wait()

    def project(cols):
        branch[:, cols] = dot(att[...], wo[:, cols])

    tiles(width, project)
    loads["resid"].wait()
    mid[...] = resid[...] + mean_norm(branch[...], gains[1])
    normed[...] = mean_norm(mid[...], gains[2]).astype(BF16)
    transposed_into(normed, left_n.at[0])
    greeted(n + 3)
    give("n1", left_n.at[0], left_n.at[1], near)
    give("n2", left_n.at[0], left_n.at[2], across[0])
    loads["wg"].wait()
    loads["wu"].wait()

    def widen(cols):
        gate = dot(normed[...], wg[:, cols])
        up = dot(normed[...], wu[:, cols])
        bent = jax.nn.sigmoid(gate)
        silu = gate * bent
        hidden[:, cols] = (silu * up).astype(BF16)
        gate_by[:, cols] = (up * bent * (1.0 + gate * (1.0 - bent))).astype(BF16)
        up_by[:, cols] = silu.astype(BF16)

    tiles(ff, widen)
    loads["wd"].wait()

    transposed_blocks(hidden, left_h)
    give("h2", left_h.at[:, 1 - bits[1]], left_m.at[1], across[1])
    give("h1", left_h.at[:, bits[1]], left_m.at[0], near)

    def narrow(cols):
        down[:, cols] = dot(hidden[...], wd[:, cols])

    tiles(width, narrow)
    loads["cot"].wait()
    grad, gain3 = norm_back(down[...], gains[3], cot[...].astype(F32))
    down_low[...] = grad.astype(BF16)
    mine_d = pl.ds(pl.multiple_of(core * part, 128), part)
    theirs_d = pl.ds(pl.multiple_of((1 - core) * part, 128), part)
    give("d2", down_low.at[:, mine_d], right_d.at[1], across[1])
    give("d3", down_low.at[:, theirs_d], right_d.at[2], diagonal[1])
    give("d1", down_low.at[:, theirs_d], right_d.at[0], near)

    def widen_back(cols):
        block = dot_nt(down_low[...], wd[cols, :])
        wide_low[0, :, cols] = (block * gate_by[:, cols].astype(F32)).astype(BF16)
        wide_low[1, :, cols] = (block * up_by[:, cols].astype(F32)).astype(BF16)

    tiles(ff, widen_back)

    def chunk_of(c, which_core, which_bit):
        at, wide = CHUNKS[c]
        return wide_low.at[which_core, :, pl.ds(pl.multiple_of(which_bit * half + at, 128), wide)]

    def give_chunk(c):
        at, wide = CHUNKS[c]
        cols = pl.ds(at, wide)
        give(("g2", c), chunk_of(c, core, 1 - bits[0]), right_g.at[1, :, cols], across[0])
        give(("g3", c), chunk_of(c, 1 - core, 1 - bits[0]), right_g.at[2, :, cols], diagonal[0])
        give(("g1", c), chunk_of(c, 1 - core, bits[0]), right_g.at[0, :, cols], near)

    give_chunk(0)

    def narrow_back(cols):
        above[:, cols] = dot_nt(wide_low[0], wg[cols, :]) + dot_nt(wide_low[1], wu[cols, :])

    tiles(width, narrow_back)
    grad, gain2 = norm_back(mid[...], gains[2], above[...])
    resid[...] = cot[...].astype(F32) + grad
    grad, gain1 = norm_back(branch[...], gains[1], resid[...])
    branch_low[...] = grad.astype(BF16)

    def project_back(cols):
        dout[:, cols] = dot_nt(branch_low[...], wo[cols, :]).astype(BF16)

    tiles(width, project_back)
    my_cols = pl.ds(pl.multiple_of(me * HEAD_DIM, HEAD_DIM), HEAD_DIM)
    for k in (4, 5, 3, 2, 6, 7, 1):
        owner = (me + k) % n
        cols = pl.ds(pl.multiple_of(owner * HEAD_DIM, HEAD_DIM), HEAD_DIM)
        copy = remote(dout.at[:, cols], g.at[me], g_send.at[owner], g_recv.at[me], seq_device(owner))
        copy.start()
        sends.append(copy)
    g[me] = dout[:, my_cols]
    given["n2"].wait_recv()
    give("n3", left_n.at[2], left_n.at[3], near)
    transposed_into(att, left_a.at[0])
    give("a1", left_a.at[0], left_a.at[1], near)
    give("b1", branch_low.at[:, theirs_d], right_b, near)
    layer_out[...] = (mid[...] + mean_norm(down[...], gains[3])).astype(BF16)
    stores = []

    def store(src, dst):
        copy = pltpu.make_async_copy(src, dst, store_sem.at[len(stores)])
        copy.start()
        stores.append(copy)

    store(resid, above_out)
    gains_out[...] = jnp.zeros_like(gains_out)
    gains_out[1:2, :] = gain1[None, :]
    gains_out[2:3, :] = gain2[None, :]
    gains_out[3:4, :] = gain3[None, :]
    seconds = {}
    z_low = (me // 2) % 2

    def wide_sum(c):
        at, wide = CHUNKS[c]
        for key in ("n1", "n3"):
            if key in given:
                given.pop(key).wait_recv()
        for key in ("g1", "g2", "g3"):
            given[key, c].wait_recv()
        shard = width // 32
        spread = [(bits[1] + other) % 2 for other in range(2)]
        own = chunk_of(c, core, bits[0])
        for begin in range(0, wide, 256):
            step = min(256, wide - begin)
            cols = pl.ds(at + begin, step)
            block = dot(left_n[0], own[:, pl.ds(begin, step)])
            for k in range(1, 4):
                block += dot(left_n[k], right_g[k - 1, :, cols])
            work[0:width, 0:step] = block
            for z in range(4):
                for other in range(2):
                    pieces = [
                        work[pl.ds((8 * z + 4 * c2 + 2 * other + b) * shard, shard), 0:step]
                        for c2 in range(2)
                        for b in range(2)
                    ]
                    place = pl.multiple_of(spread[other] * part + z_place(z) * 4 * shard, 16)
                    wg[pl.ds(place, 4 * shard), cols] = jnp.concatenate(pieces, axis=0).astype(BF16)
        cols = pl.ds(at, wide)
        if c == len(CHUNKS) - 1:
            store(wg.at[:, cols], kept_h)
            return
        seconds[c] = remote(
            wg.at[pl.ds(part, part), cols], got_g.at[:, cols], s_send.at[c], s_recv.at[c], across[1]
        )
        seconds[c].start()
        sends.append(seconds[c])

    def down_sum():
        for key in ("h1", "h3", "d1", "d2", "d3"):
            given[key].wait_recv()
        tall = ff // 4
        shard = ff // 32
        spread = [(bits[0] + other) % 2 for other in range(2)]
        for begin in range(0, part, 256):
            cols = pl.ds(begin, 256)
            own = down_low.at[:, mine_d]
            block = dot(left_h[:, bits[1]].reshape(2 * tall, rows), own[:, cols])
            for k in range(3):
                block += dot(left_m[k].reshape(2 * tall, rows), right_d[k, :, cols])
            work[...] = block
            for z in range(4):
                for other in range(2):
                    pieces = [
                        work[pl.ds((4 * z + 2 * c2 + other) * shard, shard), :] for c2 in range(2)
                    ]
                    place = pl.multiple_of(spread[other] * tall + z_place(z) * 2 * shard, 16)
                    wd[pl.ds(place, 2 * shard), cols] = jnp.concatenate(pieces, axis=0).astype(BF16)
        cols = pl.ds(0, part)
        seconds["d"] = remote(
            wd.at[pl.ds(tall, tall), cols], got_d, s_send.at[3], s_recv.at[3], across[0]
        )
        seconds["d"].start()
        sends.append(seconds["d"])

    def out_sum():
        given["a1"].wait_recv()
        given["b1"].wait_recv()
        shard = width // 32
        slots = unit_slots(0, dp)
        for begin in range(0, part, 256):
            cols = pl.ds(begin, 256)
            block = dot(left_a[0], branch_low.at[:, mine_d][:, cols])
            work[0:width, :] = block + dot(left_a[1], right_b[:, cols])
            for z in range(4):
                for q in range(4):
                    pieces = [
                        work[pl.ds((8 * z + 4 * c2 + q) * shard, shard), :] for c2 in range(2)
                    ]
                    place = pl.multiple_of(slots[q] * (width // 4) + z_place(z) * 2 * shard, 16)
                    wu[pl.ds(place, 2 * shard), cols] = jnp.concatenate(pieces, axis=0).astype(BF16)
        store(wu.at[:, pl.ds(0, part)], kept_o)

    loads["x"].wait()
    factor = SCORE_SCALE * LOG2E
    half_dim = HEAD_DIM // 2
    pairs = [(i, j) for j in range(n) for i in range(j, n)]
    across_blocks = ff // rows

    def probs(i, j):
        k = pairs.index((i, j))
        at, cols = k // across_blocks * rows, k % across_blocks * rows
        return wu.at[pl.ds(at, rows), pl.ds(cols, rows)]

    give_chunk(1)
    for j in range(n):
        kt[j] = x[j, 1].astype(F32).T.astype(BF16)
        for i in range(j, n):
            p = jnp.exp2(dot_nt(x[j, 1], x[i, 0]) * factor - ls_ref[i])
            if i == j:
                p = causal_fill(p, 0.0)
            probs(i, j)[...] = p.astype(BF16)
    give_chunk(2)
    loads["ot"].wait()
    loads["table"].wait()
    arrived, summed = set(), set()

    def upstream(i):
        if i not in arrived:
            arrived.add(i)

            @pl.when(me != i)
            def arrive():
                remote(g.at[0], g.at[i], g_send.at[0], g_recv.at[i], seq_device(i)).wait_recv()

            delta[i] = jnp.sum(g[i].astype(F32).T * ot[i], axis=0, keepdims=True)
        return g[i]

    def give_head(j, first, count, sem):
        span = pl.ds(first, count)

        @pl.when(me != j)
        def over():
            remote(
                dsent.at[j, span], packed.at[span, :, my_cols], d_send.at[sem], d_recv.at[sem - j + me], seq_device(j)
            ).start()

        @pl.when(me == j)
        def keep():
            packed[span, :, my_cols] = dsent[j, span]

    def unrotated(value, j):
        here = pl.ds(j * rows, rows)
        cos, sin = table[here, 0:half_dim], -table[here, half_dim:HEAD_DIM]
        return rotate(value * SCORE_SCALE, cos, sin).astype(BF16)

    order = [n - 1, n - 2, 0]
    for k in range(1, n // 2 - 1):
        order += [n - 2 - k, k]
    order += [n // 2 - 1]
    for j in order:
        dk = dv = None
        for i in range(j, n):
            up = upstream(i)
            p = probs(i, j)[...]
            v = dot(p, up)
            ds = (p.astype(F32) * (dot_nt(x[j, 2], up) - delta[i])).astype(BF16)
            k = dot(ds, x[i, 0])
            t = dot(kt[j], ds)
            dqt[i] = dqt[i] + t if i in summed else t
            summed.add(i)
            dv, dk = (v, k) if i == j else (dv + v, dk + k)
        dsent[j, 1] = unrotated(dk, j)
        dsent[j, 2] = dv.astype(BF16)
        give_head(j, 1, 2, j)
        if j < n // 2:
            dsent[j, 0] = unrotated(dqt[j].T, j)
            give_head(j, 0, 1, n + j)
        if j == 0:
            wide_sum(0)
        if j == 1:
            given["h2"].wait_recv()
            give("h3", left_m.at[1], left_m.at[2], near)
    for j in range(n // 2, n):
        dsent[j, 0] = unrotated(dqt[j].T, j)
        give_head(j, 0, 1, n + j)

    down_sum()
    wide_sum(1)
    wide_sum(2)
    out_sum()

    def finish_wide(c):
        at, wide = CHUNKS[c]
        cols = pl.ds(at, wide)
        seconds[c].wait_recv()
        add_into(wg.at[pl.ds(0, part), cols], got_g.at[:, cols])
        if c > 0:
            store(wg.at[pl.ds(0, part), cols], kept_g)
            return
        third[0].start()
        sends.append(third[0])

    def z_rows(which):
        return wg.at[pl.ds(pl.multiple_of(which * (part // 2), 16), part // 2), pl.ds(0, CHUNKS[0][1])]

    def finish_z():
        third[0].wait_recv()
        add_into(z_rows(z_low), got_z)
        store(z_rows(z_low), kept_z)

    third = [
        remote(z_rows(1 - z_low), got_z, s_send.at[4], s_recv.at[4], seq_device(flipped(1, me)))
    ]
    finish_wide(0)
    finish_wide(1)
    seconds["d"].wait_recv()
    mine = wd.at[pl.ds(0, ff // 4), pl.ds(0, part)]
    add_into(mine, got_d)
    store(mine, kept_d)
    finish_z()
    for first, count in ((1, 2), (0, 1)):
        span = pl.ds(first, count)
        for j in range(n):

            @pl.when(me != j)
            def finish():
                cols = pl.ds(j * HEAD_DIM, HEAD_DIM)
                sem = j if first == 1 else n + j
                copy = remote(
                    dsent.at[j, span], packed.at[span, :, cols], d_send.at[sem], d_recv.at[sem], seq_device(j)
                )
                copy.wait_send()
                copy.wait_recv()

    store(packed, packed_out)
    for copy in sends:
        copy.wait_send()
    for copy in stores:
        copy.wait()


def middle_block(att, resid, cot, gain_rows, w_out, w_gate, w_up, w_down, x, ot, ls, table):
    n = HEADS
    rows, width = resid.shape
    ff = w_gate.shape[1]
    half, part = ff // 2, width // 2
    hbm = pl.BlockSpec(memory_space=pl.ANY)
    vmem = pl.BlockSpec(memory_space=pltpu.VMEM)
    dma = pltpu.SemaphoreType.DMA
    low = pltpu.VMEM((rows, width), BF16)
    wide = pltpu.VMEM((rows, ff), BF16)
    full = pltpu.VMEM((rows, width), F32)
    scratch = [pltpu.VMEM(w.shape, BF16) for w in (w_out, w_gate, w_up, w_down)]
    scratch += [low, low, full, full, full, full, full]
    scratch += [low, wide, wide, wide, low, pltpu.VMEM((2, rows, ff), BF16), low, low]
    scratch += [
        pltpu.VMEM((4, width, rows), BF16),
        pltpu.VMEM((8, 2, ff // 16, rows), BF16),
        pltpu.VMEM((3, 8, ff // 16, rows), BF16),
        pltpu.VMEM((2, width, rows), BF16),
        pltpu.VMEM((3, rows, half), BF16),
        pltpu.VMEM((3, rows, part), BF16),
        pltpu.VMEM((rows, part), BF16),
        pltpu.VMEM((part, CHUNKS[-1][0]), BF16),
        pltpu.VMEM((ff // 4, part), BF16),
        pltpu.VMEM((part // 2, CHUNKS[0][1]), BF16),
        pltpu.VMEM((half, 256), F32),
        pltpu.VMEM(x.shape, BF16),
        pltpu.VMEM(ot.shape, F32),
        pltpu.VMEM(table.shape, F32),
        pltpu.VMEM((n, rows, HEAD_DIM), BF16),
        pltpu.VMEM((n, HEAD_DIM, rows), BF16),
        pltpu.VMEM((n, HEAD_DIM, rows), F32),
        pltpu.VMEM((n, 1, rows), F32),
        pltpu.VMEM((n, 3, rows, HEAD_DIM), BF16),
        pltpu.VMEM((3, rows, width), BF16),
        dma((10,)),
        dma((7,)),
        dma((n,)),
        dma((n,)),
        dma((2 * n,)),
        dma((2 * n,)),
        dma((20,)),
        dma((20,)),
        dma((5,)),
        dma((5,)),
    ]
    return pl.pallas_call(
        middle_kernel,
        name="middle",
        out_shape=[
            jax.ShapeDtypeStruct((rows, width), BF16),
            jax.ShapeDtypeStruct((rows, width), F32),
            jax.ShapeDtypeStruct((8, width), F32),
            jax.ShapeDtypeStruct((3, rows, width), BF16),
            jax.ShapeDtypeStruct((ff // 4, part), BF16),
            jax.ShapeDtypeStruct((part // 2, CHUNKS[0][1]), BF16),
            jax.ShapeDtypeStruct((part, CHUNKS[1][1]), BF16),
            jax.ShapeDtypeStruct((width, CHUNKS[-1][1]), BF16),
            jax.ShapeDtypeStruct((width, part), BF16),
        ],
        in_specs=[hbm] * 3 + [vmem] + [hbm] * 6 + [vmem] + [hbm],
        out_specs=[vmem, hbm, vmem, hbm] + [hbm] * 5,
        scratch_shapes=scratch,
        compiler_params=pltpu.CompilerParams(
            collective_id=2, has_side_effects=True, vmem_limit_bytes=62 << 20
        ),
    )(att, resid, cot, gain_rows, w_out, w_gate, w_up, w_down, x, ot, ls, table)


BEGUN = ((1, 0, 512, None), (2, 0, 512, None), (0, 0, 256, None), (0, 256, 256, None), (3, 0, 384, 1))
FRESH = ((1, 0, 0), (1, 1024, 0), (1, 2048, 1), (0, 0, 1))
SCHEDULE = (
    ("S", 4), ("2", 0), ("F", 5), ("1", 3), ("P", 0), ("1", 1), ("D", 3), ("2", 3),
    ("E", 0), ("U", 9), ("O", 0), ("U", 7), ("C", 4), ("G", 0), ("E", 3), ("B", 5),
    ("1", 2), ("S", 5), ("D", 1), ("2", 1), ("W", 9), ("S", 9), ("1", 4), ("W", 7),
    ("S", 7), ("D", 2), ("G", 1), ("2", 2), ("C", 5), ("E", 1), ("1", 5), ("D", 4),
    ("G", 2), ("2", 4), ("U", 8), ("E", 2), ("C", 7), ("1", 7), ("D", 5), ("G", 3),
    ("U", 6), ("2", 5), ("C", 9), ("1", 9), ("E", 4), ("D", 7), ("G", 4), ("2", 7),
    ("W", 8), ("E", 5), ("S", 8), ("W", 6), ("S", 6), ("E", 7), ("D", 9), ("2", 9),
    ("C", 8), ("1", 8), ("C", 6), ("1", 6), ("E", 9), ("D", 8), ("2", 8), ("D", 6),
    ("2", 6), ("E", 8), ("E", 6),
)


def dealt_blocks(left, slots, right, spread, bit, out, work):
    total = left.shape[1]
    shard = total // 32
    block = dot(left[slots[0]], right[0])
    for k in range(1, 4):
        block += dot(left[slots[k]], right[k])
    work[0:total, :] = block
    for z in range(4):
        for other in range(2):
            pieces = []
            for core in range(2):
                for b in range(2):
                    q = (b << bit) | (other << (1 - bit))
                    pieces.append(work[pl.ds((8 * z + 4 * core + q) * shard, shard), :])
            out[spread[other], pl.ds(z_place(z) * 4 * shard, 4 * shard), :] = jnp.concatenate(
                pieces, axis=0
            ).astype(BF16)


def tail_kernel(*refs):
    refs = list(refs)

    def take(count):
        taken, refs[:count] = refs[:count], []
        return taken

    begun, fresh = len(BEGUN), len(FRESH)
    single = begun
    first_fresh = begun + 1
    count = first_fresh + fresh
    kept_in = take(5)
    packed_in, ltn_in, ltj_in, wq_in, wa_in = take(5)
    resid, above, gain_rows, gain_parts = take(4)
    grad_joined = take(2)
    outs = take(5)
    (gains_out,) = take(1)
    held = take(3)
    sums, arrived2 = [None] * 4 + take(count - 4), [None] * 4 + take(count - 4)
    parts, arrived3, arrived4, finals = take(count), take(count), take(count), take(count)
    (got_o, wq, wa, packed, ltn, ltj, dealt, low, work, back_sum, gain_buf, gain_got) = take(12)
    (load_sem, u_send, u_recv, s_send, s_recv, z1_send, z1_recv) = take(7)
    (z2_send, z2_recv, c_send, c_recv, gain_send, gain_recv) = take(6)
    rows, width = resid.shape
    me = lax.axis_index("seq")
    dp = lax.axis_index("dp")
    core = me % 2
    bits = [dp % 2, dp // 2]
    z_low, z_high = (me // 2) % 2, me // 4
    mate = flipped(0, me)
    near = seq_device(mate)
    across = [{"dp": flipped(0, dp)}, {"dp": flipped(1, dp)}]
    diagonal = [{"seq": mate, "dp": flipped(0, dp)}, {"seq": mate, "dp": flipped(1, dp)}]
    beside = [seq_device(flipped(1, me)), seq_device(flipped(2, me))]
    greet([near] + across + diagonal + beside)
    loads = {}

    def load(key, src, dst):
        loads[key] = pltpu.make_async_copy(src, dst, load_sem.at[len(loads)])
        loads[key].start()

    load("packed", packed_in, packed)
    load("wq", wq_in, wq)
    greeted(7)
    sends = []

    def send(src, dst, send_sem, recv_sem, device):
        copy = remote(src, dst, send_sem, recv_sem, device)
        copy.start()
        sends.append(copy)
        return copy

    first, dealing, second, third, fourth, finished, taken = [], {}, {}, {}, {}, {}, set()

    def ready(key):
        if key not in taken:
            taken.add(key)
            loads[key].wait()

    def z_rows(u, which):
        tall = finals[u].shape[0]
        return pl.ds(pl.multiple_of(which * 2 * tall, 16), 2 * tall)

    def one_z(u, which):
        tall = finals[u].shape[0]
        return pl.ds(pl.multiple_of(which * tall, 16), tall)

    def start_first(u):
        first.append(send(kept_in[4].at[pl.ds(2, 2)], got_o, s_send.at[count], s_recv.at[count], across[0]))

    def take_first(u):
        first[0].wait_recv()
        ready(single)
        for k in (1, 0):
            add_into(sums[single].at[k], got_o.at[k])

    def start_columns(u):
        k = u - first_fresh
        bit = FRESH[k][2]
        source = low if k == 3 else packed.at[k]
        if k < 3:
            ready("packed")

        def columns(other_core, other_bit):
            place = (core + (1 - 2 * core) * other_core) * 2
            place = place + bits[bit] + (1 - 2 * bits[bit]) * other_bit
            return pl.ds(pl.multiple_of(place * 256, 256), 256)

        dealing[u] = [
            send(
                source.at[:, columns(*there)],
                dealt.at[k, slot],
                u_send.at[3 * k + slot - 1],
                u_recv.at[3 * k + slot - 1],
                device,
            )
            for there, slot, device in (
                ((0, 1), 2, across[bit]),
                ((1, 1), 3, diagonal[bit]),
                ((1, 0), 1, near),
            )
        ]
        dealt[k, 0] = source[:, columns(0, 0)]

    def start_second(u):
        if u < begun:
            array, at, wide, bit = BEGUN[u]
            rows_in = kept_in[array].shape[0] // 2
            src = kept_in[array].at[pl.ds(rows_in, rows_in), pl.ds(at, wide)]
        else:
            bit = 1 if u == single else 1 - FRESH[u - first_fresh][2]
            src = sums[u].at[1]
        second[u] = send(src, arrived2[u], s_send.at[u], s_recv.at[u], across[bit])

    def multiply(u):
        k = u - first_fresh
        out, column, bit = FRESH[k]
        slots = (0, 1, 2, 3) if (bit == 0 or k == 3) else (0, 1, 4, 5)
        left = ltj if k == 3 else ltn
        ready("ltj" if k == 3 else "ltn")
        for copy in dealing[u]:
            copy.wait_recv()
        spread = [(bits[1 - bit] + other) % 2 for other in range(2)]
        dealt_blocks(left, slots, dealt.at[k], spread, bit, sums[u], work)

    def take_second(u):
        second[u].wait_recv()
        if u < begun:
            ready(u)
        add_into(sums[u].at[0], arrived2[u])

    def start_third(u):
        theirs = z_rows(u, 1 - z_low)
        if u < 4:
            array, at, wide, _ = BEGUN[u]
            src = kept_in[array].at[theirs, pl.ds(at, wide)]
        else:
            src = sums[u].at[0, theirs]
        third[u] = send(src, arrived3[u], z1_send.at[u], z1_recv.at[u], beside[0])

    def take_third(u):
        third[u].wait_recv()
        if u < 4:
            array, at, wide, _ = BEGUN[u]
            ready(array)
            mine = held[array][:, pl.ds(at, wide)]
        else:
            mine = sums[u][0, z_rows(u, z_low), :]
        parts[u][...] = (mine.astype(F32) + arrived3[u][...].astype(F32)).astype(BF16)

    def start_fourth(u):
        source = kept_in[1] if u == 0 else parts[u]
        fourth[u] = send(
            source.at[one_z(u, 1 - z_high)], arrived4[u], z2_send.at[u], z2_recv.at[u], beside[1]
        )

    def take_fourth(u):
        fourth[u].wait_recv()
        if u == 0:
            ready(1)
        source = held[1] if u == 0 else parts[u]
        finals[u][...] = source[one_z(u, z_high), :].astype(F32) + arrived4[u][...].astype(F32)
        if u in (0, 1, 4):
            at, wide = CHUNKS[min(u, 2)]
            bit = 0
            cols = pl.ds(pl.multiple_of(bits[0] * (outs[3].shape[2] // 2) + at, 128), wide)
            target = outs[3].at[core, :, cols]
        elif u <= single:
            out, at, wide = (2, 0, width // 2) if u == single else (4,) + BEGUN[u][1:3]
            bit = None
            target = outs[out].at[:, pl.ds(pl.multiple_of(core * (width // 2) + at, 128), wide)]
        else:
            out, column, bit = FRESH[u - first_fresh]
            cols = pl.ds(pl.multiple_of((core * 2 + bits[bit]) * 256 + column, 256), 256)
            target = outs[out].at[:, cols]
        if bit is None:
            owners = [(core, None), (1 - core, near)]
        else:
            here, there = bits[bit], 1 - bits[bit]
            owners = [
                (core * 2 + here, None),
                ((1 - core) * 2 + here, near),
                (core * 2 + there, across[bit]),
                ((1 - core) * 2 + there, diagonal[bit]),
            ]
        shard = finals[u].shape[0] // len(owners)
        finished[u] = []
        for k, (place, device) in enumerate(owners):
            at = pl.ds(pl.multiple_of(place * shard, 8), shard)
            if k == 0:
                target[...] = finals[u][at, :]
            else:
                sem = 3 * u + k - 1
                finished[u].append(
                    send(finals[u].at[at], target, c_send.at[sem], c_recv.at[sem], device)
                )

    gain_steps = {}
    gain_partners = [near] + across + beside

    def send_gain(k):
        gain_steps[k] = send(
            gain_buf.at[k], gain_got.at[k], gain_send.at[k], gain_recv.at[k], gain_partners[k]
        )

    def add_gain(k):
        gain_steps[k].wait_recv()
        total = gain_buf[k] + gain_got[k]
        if k == 4:
            gains_out[...] = total
        else:
            gain_buf[k + 1] = total
            send_gain(k + 1)

    tile = 256

    def dense_back(_):
        ready("packed")
        ready("wq")
        load(1, kept_in[1], held[1])
        load(2, kept_in[2].at[z_rows(1, z_low)], held[2])
        load(0, kept_in[0].at[z_rows(2, z_low)], held[0])
        load(single, kept_in[4].at[pl.ds(0, 2)], sums[single])
        load(4, kept_in[3].at[pl.ds(0, kept_in[3].shape[0] // 2)], sums[4].at[0])
        load("ltn", ltn_in, ltn)
        load("ltj", ltj_in, ltj)
        load("wa", wa_in, wa)
        for begin in range(0, width, tile):
            at = pl.ds(begin, tile)
            block = dot_nt(packed[0], wq[at, pl.ds(0, width)])
            block += dot_nt(packed[1], wq[at, pl.ds(width, width)])
            block += dot_nt(packed[2], wq[at, pl.ds(2 * width, width)])
            back_sum[:, at] = block
        part, gain0 = norm_back(resid[...], gain_rows[0:1, :].astype(F32), back_sum[...])
        low[...] = (above[...] + part).astype(BF16)
        gain_buf[0] = gain_parts[...]
        gain_buf[0, 0:1, :] = gain0[None, :]
        send_gain(0)

    def dense_out(_):
        ready("wa")
        for k in range(2):
            for begin in range(0, width, tile):
                from_row = pl.ds(k * width + begin, tile)
                grad_joined[k][:, pl.ds(begin, tile)] = dot_nt(low[...], wa[from_row, :])

    actions = {
        "F": start_first,
        "B": take_first,
        "U": start_columns,
        "S": start_second,
        "1": start_third,
        "2": start_fourth,
        "W": multiply,
        "C": take_second,
        "D": take_third,
        "E": take_fourth,
        "G": add_gain,
        "P": dense_back,
        "O": dense_out,
    }
    for action, u in SCHEDULE:
        actions[action](u)
    for u in range(count):
        for copy in finished[u]:
            copy.wait_recv()
    for copy in sends:
        copy.wait_send()


def tail(kept, packed, left_n, left_j, w_qkv, w_adapt, resid, above, gain_rows, gain_parts):
    rows, width = resid.shape
    hbm = pl.BlockSpec(memory_space=pl.ANY)
    vmem = pl.BlockSpec(memory_space=pltpu.VMEM)
    dma = pltpu.SemaphoreType.DMA
    fresh = len(FRESH)
    down, gate, gate_next, last, out = kept
    left_over = (4, 2, 4, 8)
    every = [(kept[array].shape[0] // left_over[array], wide) for array, _, wide, _ in BEGUN]
    every += [(out.shape[1] // 4, out.shape[2])]
    every += [(width // 8, 256)] * 3 + [(width // 4, 256)]
    count = len(every)
    slots = [1] + [2] * (1 + fresh)
    shapes = [
        (2 * width // 32, width),
        (width // 32, 3 * width),
        (width // 32, width),
        (2, width // 32, 2 * (gate.shape[1] + gate_next.shape[1] + last.shape[1])),
        (down.shape[0] // 8, width),
    ]
    scratch = [
        pltpu.VMEM(shape, BF16)
        for shape in (
            (down.shape[0] // 2, down.shape[1]),
            gate.shape,
            (gate_next.shape[0] // 2, gate_next.shape[1]),
        )
    ]
    scratch += [pltpu.VMEM((k, 4 * tall, wide), BF16) for k, (tall, wide) in zip(slots, every[4:])]
    scratch += [pltpu.VMEM((4 * tall, wide), BF16) for tall, wide in every[4:]]
    scratch += [pltpu.VMEM((2 * tall, wide), BF16) for tall, wide in every]
    scratch += [pltpu.VMEM((2 * tall, wide), BF16) for tall, wide in every]
    scratch += [pltpu.VMEM((tall, wide), BF16) for tall, wide in every]
    scratch += [pltpu.VMEM((tall, wide), F32) for tall, wide in every]
    scratch += [
        pltpu.VMEM((2,) + out.shape[1:], BF16),
        pltpu.VMEM(w_qkv.shape, BF16),
        pltpu.VMEM(w_adapt.shape, BF16),
        pltpu.VMEM(packed.shape, BF16),
        pltpu.VMEM(left_n.shape, BF16),
        pltpu.VMEM(left_j.shape, BF16),
        pltpu.VMEM((4, 4, rows, 256), BF16),
        pltpu.VMEM((rows, width), BF16),
        pltpu.VMEM((2 * width, 256), F32),
        pltpu.VMEM((rows, width), F32),
        pltpu.VMEM((5, 8, width), F32),
        pltpu.VMEM((5, 8, width), F32),
    ]
    scratch += [dma((12,)), dma((3 * fresh,)), dma((3 * fresh,))]
    scratch += [dma((count + 1,)) for _ in range(2)]
    scratch += [dma((count,)) for _ in range(4)]
    scratch += [dma((3 * count,)) for _ in range(2)]
    scratch += [dma((5,)) for _ in range(2)]
    return pl.pallas_call(
        tail_kernel,
        name="tail",
        out_shape=[jax.ShapeDtypeStruct((rows, width), F32)] * 2
        + [jax.ShapeDtypeStruct(shape, F32) for shape in shapes]
        + [jax.ShapeDtypeStruct((8, width), F32)],
        in_specs=[hbm] * 10 + [vmem] * 4,
        out_specs=[vmem] * 8,
        scratch_shapes=scratch,
        compiler_params=pltpu.CompilerParams(
            collective_id=3, has_side_effects=True, vmem_limit_bytes=62 << 20
        ),
    )(*kept, packed, left_n, left_j, w_qkv, w_adapt, resid, above, gain_rows, gain_parts)


def finish_kernel(*refs):
    sources, gain_ref, targets, gain_out, sem = refs[:8], refs[8], refs[9:18], refs[18], refs[19]
    wide = sources[6]
    pairs = list(zip(sources[:6], targets[:6]))
    pairs += [(wide.at[0], targets[6]), (wide.at[1], targets[7]), (sources[7], targets[8])]
    copies = [
        pltpu.make_async_copy(src, dst, sem.at[k]) for k, (src, dst) in enumerate(pairs)
    ]
    for copy in copies:
        copy.start()
    share = gain_out.shape[1]
    at = (lax.axis_index("seq") * lax.axis_size("dp") + lax.axis_index("dp")) * share
    block = gain_ref[:, pl.ds(pl.multiple_of(at // 128 * 128, 128), 128)]
    here = lax.broadcasted_iota(jnp.int32, (128, share), 0) - at % 128
    picked = here == lax.broadcasted_iota(jnp.int32, (128, share), 1)
    gain_out[...] = lax.dot_general(
        block,
        picked.astype(F32),
        (((1,), (0,)), ((), ())),
        precision=lax.Precision.HIGHEST,
        preferred_element_type=F32,
    )[:4]
    for copy in copies:
        copy.wait()


def finish(*values):
    hbm = pl.BlockSpec(memory_space=pl.ANY)
    vmem = pl.BlockSpec(memory_space=pltpu.VMEM)
    wide, gains = values[6], values[8]
    share = gains.shape[1] // (lax.axis_size("seq") * lax.axis_size("dp"))
    like = list(values[:6]) + [wide[0], wide[1], values[7]]
    return pl.pallas_call(
        finish_kernel,
        name="finish",
        out_shape=[jax.ShapeDtypeStruct(value.shape, value.dtype) for value in like]
        + [jax.ShapeDtypeStruct((4, share), F32)],
        in_specs=[vmem] * 9,
        out_specs=[hbm] * 9 + [vmem],
        scratch_shapes=[pltpu.SemaphoreType.DMA((9,))],
        compiler_params=pltpu.CompilerParams(vmem_limit_bytes=62 << 20),
    )(*values)


def xor_permute(value, axis, mask):
    return lax.ppermute(value, axis, [(i, i ^ mask) for i in range(lax.axis_size(axis))])


def quadrants(left):
    n, parts = lax.axis_size("seq"), lax.axis_size("dp")
    tokens, rows = left.shape
    shard = rows // (n * parts)
    split = left.reshape(tokens, n, parts, shard).transpose(2, 0, 1, 3)
    split = split.reshape(parts, tokens, n * shard)
    me = lax.axis_index("dp")
    return jnp.concatenate(
        [lax.dynamic_index_in_dim(split, me ^ m, 0, keepdims=True) for m in range(parts)]
    )


def other_core(left, right):
    core = lax.axis_index("seq") % 2
    half = right.shape[1] // 2
    mine = lax.dynamic_slice_in_dim(right, core * half, half, 1)
    theirs = lax.dynamic_slice_in_dim(right, (1 - core) * half, half, 1)
    left_in = xor_permute(left, "seq", 1)
    right_in = xor_permute(theirs, "seq", 1)
    return jnp.concatenate([left, left_in], axis=1), jnp.concatenate([mine, right_in], axis=0)


def scattered_sum(left, right, bits):
    n, parts = lax.axis_size("seq"), lax.axis_size("dp")
    cols = right.shape[1]
    left, right = other_core(quadrants(left), right)
    got = {}
    masks = list(range(parts))
    for bit in bits:
        outgoing = [m for m in masks if m >> bit & 1]
        masks = [m for m in masks if not m >> bit & 1]
        blocks = []
        for m in outgoing:
            block = dot_tn(left[m], right)
            for more in got.get(m, ()):
                block = block + more.astype(F32)
            blocks.append(block.astype(BF16))
        incoming = xor_permute(jnp.stack(blocks), "dp", 1 << bit)
        for k, m in enumerate(outgoing):
            got.setdefault(m ^ (1 << bit), []).append(incoming[k])
    block = dot_tn(left[0], right)
    for more in got.get(0, ()):
        block = block + more.astype(F32)
    shard = block.shape[0] // n
    block = block.astype(BF16).reshape(n, shard, cols // 2)
    block = lax.all_to_all(block, "seq", 0, 0)
    block = jnp.sum(block.reshape(n // 2, 2, shard, cols // 2).astype(F32), axis=0)
    return block.transpose(1, 0, 2).reshape(shard, cols)


def small_sum(value):
    value = value.reshape(value.shape[0], -1, value.shape[1])
    for axis in ("seq", "dp"):
        size = lax.axis_size(axis)
        me = lax.axis_index(axis)
        for bit in reversed(range(size.bit_length() - 1)):
            half = value.shape[2] // 2
            mine = (me >> bit) & 1
            kept = lax.dynamic_slice_in_dim(value, mine * half, half, 2)
            sent = lax.dynamic_slice_in_dim(value, (1 - mine) * half, half, 2)
            value = kept + xor_permute(sent, axis, 1 << bit)
    return value[:, 0]


def local(state, embedded, cotangent, w_adapt, w_qkv, w_out, w_gate, w_up, w_down, gains):
    seq_count, rows, width = state.shape
    n, parts = lax.axis_size("seq"), lax.axis_size("dp")
    tokens = seq_count * rows
    me = lax.axis_index("seq")
    bits = list(range(parts.bit_length() - 1))
    copies = max(1, n // HEADS)
    held = max(1, HEADS // n)
    owners = n // copies
    cos_np, sin_np = angle_tables(n * rows)
    cos_all, sin_all = jnp.asarray(cos_np), jnp.asarray(sin_np)
    cos = lax.dynamic_slice_in_dim(cos_all, me * rows, rows, 0)[:, None, :]
    sin = lax.dynamic_slice_in_dim(sin_all, me * rows, rows, 0)[:, None, :]
    gain_rows = gains.astype(F32)
    state, embedded = state.reshape(tokens, width), embedded.reshape(tokens, width)

    def to_heads(flat):
        return flat.reshape(tokens, HEADS, HEAD_DIM)

    def to_owner(parts_in):
        sent = jnp.stack(parts_in).reshape(len(parts_in), tokens, owners, held, HEAD_DIM)
        sent = sent.transpose(2, 3, 0, 1, 4)
        if copies > 1:
            sent = jnp.repeat(sent, copies, axis=0)
        return lax.all_to_all(sent, "seq", 0, 0)

    def from_owner(value):
        back = lax.all_to_all(value, "seq", 0, 0)[::copies]
        back = back.reshape(HEADS, -1, tokens, HEAD_DIM)
        return back.transpose(2, 1, 0, 3).reshape(tokens, -1)

    table = jnp.asarray(np.concatenate([cos_np, sin_np], axis=1))
    if n == HEADS and seq_count == 1 and parts == 4:
        resid, normed, attended, qkv, attended_t, logsum, left_n, left_j = front(
            state, embedded, w_adapt, w_qkv, gains, table
        )
        qkv, attended_t, logsum = qkv[:, None], attended_t[:, None], logsum[:, None]
    else:
        resid = dot(state, w_adapt[:width]) + dot(embedded, w_adapt[width:])
        normed = mean_norm(resid, gain_rows[0]).astype(BF16)
        packed = dot(normed, w_qkv)
        queries = rotate(to_heads(packed[:, :width]), cos, sin).astype(BF16)
        keys = rotate(to_heads(packed[:, width : 2 * width]), cos, sin).astype(BF16)
        values = to_heads(packed[:, 2 * width :]).astype(BF16)
        qkv = to_owner((queries, keys, values))
        attended, attended_t, logsum = attention(qkv)
        attended = from_owner(attended[:, :, None])
    shape = (seq_count, rows, width)
    if n == HEADS and parts == 4 and seq_count == 1:
        layer_out, middle_grad, gain_parts, packed_low, *kept = middle_block(
            attended,
            resid,
            cotangent.reshape(tokens, width),
            gains,
            w_out,
            w_gate,
            w_up,
            w_down,
            qkv[:, 0],
            attended_t[:, 0],
            logsum[:, 0],
            table,
        )
        grad_state, grad_embedded, grad_adapt, grad_qkv, grad_out, grad_wide, grad_down, gains_sum = tail(
            kept[:4] + [kept[4].reshape(4, width // 4, width // 2)],
            packed_low,
            left_n,
            left_j,
            w_qkv,
            w_adapt,
            resid,
            middle_grad,
            gains,
            gain_parts,
        )
        outs = finish(
            layer_out,
            grad_state,
            grad_embedded,
            grad_adapt,
            grad_qkv,
            grad_out,
            grad_wide,
            grad_down,
            gains_sum,
        )
        return tuple(value.reshape(shape) for value in outs[:3]) + tuple(outs[3:])
    branch = dot(attended, w_out)
    middle = resid + mean_norm(branch, gain_rows[1])
    normed_mid = mean_norm(middle, gain_rows[2]).astype(BF16)
    gate_pre = dot(normed_mid, w_gate)
    up_pre = dot(normed_mid, w_up)
    sigmoid_gate = jax.nn.sigmoid(gate_pre)
    silu_gate = gate_pre * sigmoid_gate
    hidden = (silu_gate * up_pre).astype(BF16)
    down_out = dot(hidden, w_down)
    layer_out = middle + mean_norm(down_out, gain_rows[3])
    out_grad = cotangent.astype(F32).reshape(tokens, width)
    down_grad, gain_grad3 = norm_back(down_out, gain_rows[3], out_grad)
    down_low = down_grad.astype(BF16)
    hidden_grad = dot_nt(down_low, w_down)
    gate_low = (
        hidden_grad * up_pre * sigmoid_gate * (1.0 + gate_pre * (1.0 - sigmoid_gate))
    ).astype(BF16)
    up_low = (hidden_grad * silu_gate).astype(BF16)
    mid_norm_grad = dot_nt(gate_low, w_gate) + dot_nt(up_low, w_up)
    middle_part, gain_grad2 = norm_back(middle, gain_rows[2], mid_norm_grad)
    middle_grad = out_grad + middle_part
    branch_grad, gain_grad1 = norm_back(branch, gain_rows[1], middle_grad)
    branch_low = branch_grad.astype(BF16)
    attended_grad = dot_nt(branch_low, w_out).astype(BF16)
    upstream = to_owner((to_heads(attended_grad),))[:, :, 0]
    packed_grad = attention_back(qkv, upstream, attended_t, logsum, cos_all, sin_all)
    packed_low = from_owner(packed_grad)
    normed_grad = dot_nt(packed_low, w_qkv)
    resid_part, gain_grad0 = norm_back(resid, gain_rows[0], normed_grad)
    resid_low = (middle_grad + resid_part).astype(BF16)
    grad_state = dot_nt(resid_low, w_adapt[:width])
    grad_embedded = dot_nt(resid_low, w_adapt[width:])
    flipped = bits[::-1]
    joined = jnp.concatenate([state, embedded], axis=-1)
    grad_down = scattered_sum(hidden, down_low, bits)
    grad_gate = scattered_sum(normed_mid, gate_low, flipped)
    grad_up = scattered_sum(normed_mid, up_low, bits)
    grad_out = scattered_sum(attended, branch_low, flipped)
    grad_qkv = scattered_sum(normed, packed_low, flipped)
    grad_adapt = scattered_sum(joined, resid_low, bits)
    grad_gains = jnp.stack([gain_grad0, gain_grad1, gain_grad2, gain_grad3])
    grad_gains = small_sum(grad_gains)
    return (
        layer_out.reshape(shape).astype(BF16),
        grad_state.reshape(shape),
        grad_embedded.reshape(shape),
        grad_adapt,
        grad_qkv,
        grad_out,
        grad_gate,
        grad_up,
        grad_down,
        grad_gains,
    )


def solution(mesh):
    tokens = P("dp", "seq", None)
    rows = P(("seq", "dp"), None)
    return jax.shard_map(
        local,
        mesh=mesh,
        in_specs=(tokens,) * 3 + (P(),) * 7,
        out_specs=(tokens,) * 3 + (rows,) * 6 + (P(None, ("seq", "dp")),),
        check_vma=False,
    )
```

```python
import functools
import math

import jax
import jax.numpy as jnp
import numpy as np
from jax import lax
from jax.experimental import pallas as pl
from jax.experimental.pallas import tpu as pltpu
from jax.sharding import PartitionSpec as P

HEADS = 8
HEAD_DIM = 128
norm_eps = 1e-06
rope_base = 50000.0
F32 = jnp.float32
BF16 = jnp.bfloat16
MESH = pl.DeviceIdType.MESH
NEG = -1e30
SCORE_SCALE = 1.0 / math.sqrt(HEAD_DIM)
LOG2E = 1.0 / math.log(2.0)


def mean_norm(values_in, gain_row):
    return (
        values_in
        * lax.rsqrt(jnp.mean(values_in * values_in, axis=-1, keepdims=True) + norm_eps)
        * gain_row
    )


def norm_back(values_in, gain_row, upstream):
    inverse = lax.rsqrt(jnp.mean(values_in * values_in, axis=-1, keepdims=True) + norm_eps)
    scaled = upstream * gain_row
    value_grad = inverse * scaled - values_in * (inverse * inverse * inverse) * jnp.mean(
        values_in * scaled, axis=-1, keepdims=True
    )
    gain_grad = jnp.sum(upstream * values_in * inverse, axis=0)
    return (value_grad, gain_grad)


def gain_sum(values_in, upstream):
    inverse = lax.rsqrt(jnp.mean(values_in * values_in, axis=-1, keepdims=True) + norm_eps)
    return jnp.sum(upstream * values_in * inverse, axis=0, keepdims=True)


def angle_tables(length):
    half_dim = HEAD_DIM // 2
    freqs = np.exp(
        np.arange(half_dim, dtype=np.float32) * np.float32(-2.0 * math.log(rope_base) / HEAD_DIM)
    ).astype(np.float32)
    angles = np.arange(length, dtype=np.float32)[:, None] * freqs[None, :]
    return np.cos(angles).astype(np.float32), np.sin(angles).astype(np.float32)


def rotate(heads_in, cos_table, sin_table):
    half_dim = heads_in.shape[-1] // 2
    lower_half = heads_in[..., :half_dim]
    upper_half = heads_in[..., half_dim:]
    return jnp.concatenate(
        [
            lower_half * cos_table - upper_half * sin_table,
            upper_half * cos_table + lower_half * sin_table,
        ],
        axis=-1,
    )


def dot(a, b):
    return lax.dot_general(a, b, (((1,), (0,)), ((), ())), preferred_element_type=F32)


def dot_tn(a, b):
    return lax.dot_general(a, b, (((0,), (0,)), ((), ())), preferred_element_type=F32)


def dot_nt(a, b):
    return lax.dot_general(a, b, (((1,), (1,)), ((), ())), preferred_element_type=F32)


def span(low, high, body, unrolled):
    if unrolled:
        for i in range(low, high):
            body(i)
    else:
        lax.fori_loop(low, high, lambda i, c: (body(i), c)[1], 0)


def causal_fill(block, fill):
    kv = lax.broadcasted_iota(jnp.int32, block.shape, 0)
    q = lax.broadcasted_iota(jnp.int32, block.shape, 1)
    return jnp.where(q >= kv, block, fill)


def attention_kernel(x_ref, o_ref, ot_ref, ls_ref, vt_ref, s_ref):
    n, hp, _, rows, _ = x_ref.shape
    unrolled = n <= 8
    factor = SCORE_SCALE * LOG2E
    for h in range(hp):
        for j in range(n):
            vt_ref[j] = x_ref[j, h, 2].astype(F32).T.astype(BF16)

        def query_block(i):
            q = x_ref[i, h, 0]
            diag = causal_fill(dot_nt(x_ref[i, h, 1], q), NEG)

            def first(j, peak):
                s = dot_nt(x_ref[j, h, 1], q)
                s_ref[j] = s
                return jnp.maximum(peak, jnp.max(s, axis=0, keepdims=True))

            peak = jnp.max(diag, axis=0, keepdims=True)
            if unrolled:
                for j in range(i):
                    peak = first(j, peak)
            else:
                peak = lax.fori_loop(0, i, first, peak)
            shift = peak * factor
            p = jnp.exp2(diag * factor - shift)
            total = jnp.sum(p, axis=0, keepdims=True)
            acc = dot(vt_ref[i], p.astype(BF16))

            def second(j, state):
                total, acc = state
                p = jnp.exp2(s_ref[j] * factor - shift)
                return (
                    total + jnp.sum(p, axis=0, keepdims=True),
                    acc + dot(vt_ref[j], p.astype(BF16)),
                )

            state = (total, acc)
            if unrolled:
                for j in range(i):
                    state = second(j, state)
            else:
                state = lax.fori_loop(0, i, second, state)
            total, acc = state
            acc = acc / total
            ot_ref[i, h] = acc
            o_ref[i, h] = acc.T.astype(BF16)
            ls_ref[i, h] = shift + jnp.log2(total)

        span(0, n, query_block, unrolled)


def attention(x):
    n, hp, _, rows, dim = x.shape
    pairs = n * (n + 1) // 2 * rows * rows * hp
    return pl.pallas_call(
        attention_kernel,
        name="attention",
        out_shape=(
            jax.ShapeDtypeStruct((n, hp, rows, dim), BF16),
            jax.ShapeDtypeStruct((n, hp, dim, rows), F32),
            jax.ShapeDtypeStruct((n, hp, 1, rows), F32),
        ),
        scratch_shapes=[
            pltpu.VMEM((n, dim, rows), BF16),
            pltpu.VMEM((n, rows, rows), F32),
        ],
        compiler_params=pltpu.CompilerParams(vmem_limit_bytes=40 << 20),
        cost_estimate=pl.CostEstimate(
            flops=pairs * dim * 8, bytes_accessed=x.size * 4, transcendentals=pairs
        ),
    )(x)


def attention_back_kernel(
    x_ref, g_ref, ot_ref, ls_ref, cos_ref, sin_ref, out_ref, kt_ref, dqt_ref, delta_ref
):
    n, hp, _, rows, _ = x_ref.shape
    unrolled = n <= 8
    factor = SCORE_SCALE * LOG2E
    for h in range(hp):
        for j in range(n):
            kt_ref[j] = x_ref[j, h, 1].astype(F32).T.astype(BF16)
            delta_ref[j] = jnp.sum(
                g_ref[j, h].astype(F32).T * ot_ref[j, h], axis=0, keepdims=True
            )

        def unrotated(value, i):
            turned = pl.ds(i * rows, rows)
            cos, sin = cos_ref[turned], sin_ref[turned]
            return rotate(value * SCORE_SCALE, cos, -sin).astype(BF16)

        def pair(i, j, diagonal):
            q, g = x_ref[i, h, 0], g_ref[i, h]
            p = jnp.exp2(dot_nt(x_ref[j, h, 1], q) * factor - ls_ref[i, h])
            if diagonal:
                p = causal_fill(p, 0.0)
            dv = dot(p.astype(BF16), g)
            ds = (p * (dot_nt(x_ref[j, h, 2], g) - delta_ref[i])).astype(BF16)
            dk = dot(ds, q)
            dqt = dot(kt_ref[j], ds)
            return dv, dk, dqt

        def key_block(j):
            dv, dk, dqt = pair(j, j, True)
            if unrolled:
                dqt_ref[j] = dqt if j == 0 else dqt_ref[j] + dqt
            else:
                dqt_ref[j] = jnp.where(j == 0, 0.0, dqt_ref[j]) + dqt

            def step(i, state):
                dv, dk = state
                v, k, t = pair(i, j, False)
                if unrolled:
                    dqt_ref[i] = t if j == 0 else dqt_ref[i] + t
                else:
                    dqt_ref[i] = jnp.where(j == 0, 0.0, dqt_ref[i]) + t
                return dv + v, dk + k

            state = (dv, dk)
            if unrolled:
                for i in range(j + 1, n):
                    state = step(i, state)
            else:
                state = lax.fori_loop(j + 1, n, step, state)
            dv, dk = state
            out_ref[j, h, 0] = unrotated(dqt_ref[j].T, j)
            out_ref[j, h, 1] = unrotated(dk, j)
            out_ref[j, h, 2] = dv.astype(BF16)

        span(0, n, key_block, unrolled)


def attention_back(x, g, ot, ls, cos, sin):
    n, hp, _, rows, dim = x.shape
    pairs = n * (n + 1) // 2 * rows * rows * hp
    return pl.pallas_call(
        attention_back_kernel,
        name="attention_back",
        out_shape=jax.ShapeDtypeStruct(x.shape, BF16),
        scratch_shapes=[
            pltpu.VMEM((n, dim, rows), BF16),
            pltpu.VMEM((n, dim, rows), F32),
            pltpu.VMEM((n, 1, rows), F32),
        ],
        compiler_params=pltpu.CompilerParams(vmem_limit_bytes=40 << 20),
        cost_estimate=pl.CostEstimate(
            flops=pairs * dim * 20, bytes_accessed=x.size * 6, transcendentals=pairs
        ),
    )(x, g, ot, ls, cos, sin)


def seq_device(index):
    return {"seq": index}


def greet(peers):
    barrier = pltpu.get_barrier_semaphore()
    for device in peers:
        pl.semaphore_signal(barrier, inc=1, device_id=device, device_id_type=MESH)


def greeted(count):
    pl.semaphore_wait(pltpu.get_barrier_semaphore(), count)


def remote(src, dst, send, recv, device):
    return pltpu.make_async_remote_copy(
        src_ref=src,
        dst_ref=dst,
        send_sem=send,
        recv_sem=recv,
        device_id=device,
        device_id_type=MESH,
    )


def front_kernel(
    state_ref,
    embedded_ref,
    wa_ref,
    wq_ref,
    gain_ref,
    table_ref,
    resid_out,
    normed_out,
    att_out,
    x_out,
    ot_out,
    ls_out,
    ltn_out,
    ltj_out,
    wa,
    wq,
    joined,
    resid,
    normed,
    sent,
    x,
    vt,
    scores,
    ot,
    o_sent,
    att,
    ltn,
    ltj,
    table,
    load_sem,
    store_sem,
    send_sem,
    recv_sem,
    o_send_sem,
    o_recv_sem,
    l_send_sem,
    l_recv_sem,
):
    n, rows, width = HEADS, state_ref.shape[0], state_ref.shape[1]
    me = lax.axis_index("seq")
    dp = lax.axis_index("dp")
    peers = [seq_device((me + k) % n) for k in range(1, n)]
    across = [{"dp": flipped(0, dp)}, {"dp": flipped(1, dp)}]
    near = seq_device(flipped(0, me))
    greet(peers + across)
    loads = [
        pltpu.make_async_copy(state_ref, joined.at[0], load_sem.at[0]),
        pltpu.make_async_copy(wa_ref.at[pl.ds(0, width)], wa.at[0], load_sem.at[1]),
        pltpu.make_async_copy(embedded_ref, joined.at[1], load_sem.at[2]),
        pltpu.make_async_copy(wa_ref.at[pl.ds(width, width)], wa.at[1], load_sem.at[3]),
        pltpu.make_async_copy(wq_ref, wq, load_sem.at[4]),
        pltpu.make_async_copy(
            table_ref.at[pl.ds(pl.multiple_of(me * rows, 8), rows)], table, load_sem.at[5]
        ),
    ]
    for copy in loads:
        copy.start()
    tile = 256
    for half in range(2):
        loads[2 * half].wait()
        loads[2 * half + 1].wait()

        for begin in range(0, width, tile):
            cols = pl.ds(begin, tile)
            block = dot(joined[half], wa[half, :, cols])
            resid[:, cols] = block if half == 0 else resid[:, cols] + block
    normed[...] = mean_norm(resid[...], gain_ref[0:1, :].astype(F32)).astype(BF16)
    stores = [
        pltpu.make_async_copy(resid, resid_out, store_sem.at[0]),
        pltpu.make_async_copy(normed, normed_out, store_sem.at[1]),
    ]
    for copy in stores:
        copy.start()
    loads[4].wait()
    lefts = []

    def share(source, out, slot, device):
        k = len(lefts)
        copy = remote(source, out.at[slot], l_send_sem.at[k], l_recv_sem.at[k], device)
        copy.start()
        lefts.append(copy)
    loads[5].wait()
    cos, sin = table[:, 0 : HEAD_DIM // 2], table[:, HEAD_DIM // 2 : HEAD_DIM]
    pairs = n // 2
    order = [2, 1, 3, 0] if pairs == 4 else list(range(pairs - 1, -1, -1))
    sends = []
    for k in order:
        chip = (me // 2 + k) % pairs
        for part in range(3):
            cols = pl.ds(pl.multiple_of(part * width + chip * 2 * HEAD_DIM, 2 * HEAD_DIM), 2 * HEAD_DIM)
            block = dot(normed[...], wq[:, cols])
            for core in range(2):
                head = block[:, core * HEAD_DIM : (core + 1) * HEAD_DIM]
                if part < 2:
                    head = rotate(head, cos, sin)
                sent[2 * chip + core, part] = head.astype(BF16)
        if k == order[0]:
            greeted(n + 1)
        for core in range(2):
            owner = 2 * chip + core
            if k == 0:
                continue
            copy = remote(sent.at[owner], x.at[me], send_sem.at[owner], recv_sem.at[me], seq_device(owner))
            copy.start()
            sends.append(copy)
    mate = me + 1 - 2 * (me % 2)
    copy = remote(sent.at[mate], x.at[me], send_sem.at[mate], recv_sem.at[me], seq_device(mate))
    copy.start()
    sends.append(copy)
    x[me] = sent[me]
    transposed_into(normed, ltn)
    for half in range(2):
        transposed_into(joined.at[half], ltj.at[pl.ds(half * width, width)])
    stores.append(pltpu.make_async_copy(ltn, ltn_out.at[0], store_sem.at[4]))
    stores.append(pltpu.make_async_copy(ltj, ltj_out.at[0], store_sem.at[5]))
    for copy in stores[2:]:
        copy.start()
    share(ltn, ltn_out, 2, across[0])
    share(ltn, ltn_out, 4, across[1])
    share(ltj, ltj_out, 2, across[1])
    share(ltn, ltn_out, 1, near)
    share(ltj, ltj_out, 1, near)
    factor = SCORE_SCALE * LOG2E
    for i in range(n):

        @pl.when(me != i)
        def arrive():
            remote(sent.at[0], x.at[i], send_sem.at[0], recv_sem.at[i], seq_device(i)).wait_recv()

        vt[i] = x[i, 2].astype(F32).T.astype(BF16)
        q = x[i, 0]
        diag = causal_fill(dot_nt(x[i, 1], q), NEG)
        peak = jnp.max(diag, axis=0, keepdims=True)
        for j in range(i):
            block = dot_nt(x[j, 1], q)
            scores[j] = block
            peak = jnp.maximum(peak, jnp.max(block, axis=0, keepdims=True))
        shift = peak * factor
        p = jnp.exp2(diag * factor - shift)
        total = jnp.sum(p, axis=0, keepdims=True)
        acc = dot(vt[i], p.astype(BF16))
        for j in range(i):
            p = jnp.exp2(scores[j] * factor - shift)
            total = total + jnp.sum(p, axis=0, keepdims=True)
            acc = acc + dot(vt[j], p.astype(BF16))
        acc = acc / total
        ot[i] = acc
        o_sent[i] = acc.T.astype(BF16)
        ls_out[i] = shift + jnp.log2(total)
        mine = pl.ds(pl.multiple_of(me * HEAD_DIM, HEAD_DIM), HEAD_DIM)

        @pl.when(me != i)
        def give():
            remote(o_sent.at[i], att.at[:, mine], o_send_sem.at[i], o_recv_sem.at[me], seq_device(i)).start()

        @pl.when(me == i)
        def keep():
            att[:, mine] = o_sent[i]

    stores.append(pltpu.make_async_copy(x, x_out, store_sem.at[2]))
    stores.append(pltpu.make_async_copy(ot, ot_out, store_sem.at[3]))
    for copy in stores[4:]:
        copy.start()
    for k, out, slot in ((0, ltn_out, 2), (1, ltn_out, 4), (2, ltj_out, 2)):
        lefts[k].wait_recv()
        share(out.at[slot], out, slot + 1, near)
    for copy in sends:
        copy.wait_send()
    for i in range(n):

        @pl.when(me != i)
        def finish():
            cols = pl.ds(i * HEAD_DIM, HEAD_DIM)
            copy = remote(o_sent.at[i], att.at[:, cols], o_send_sem.at[i], o_recv_sem.at[i], seq_device(i))
            copy.wait_send()
            copy.wait_recv()

    att_out[...] = att[...]
    for copy in stores:
        copy.wait()
    for k, copy in enumerate(lefts):
        copy.wait_send()
        if k > 2:
            copy.wait_recv()


def front(state, embedded, w_adapt, w_qkv, gains, table):
    n = HEADS
    rows, width = state.shape
    hbm = pl.BlockSpec(memory_space=pl.ANY)
    vmem = pl.BlockSpec(memory_space=pltpu.VMEM)
    return pl.pallas_call(
        front_kernel,
        name="front",
        out_shape=(
            jax.ShapeDtypeStruct((rows, width), F32),
            jax.ShapeDtypeStruct((rows, width), BF16),
            jax.ShapeDtypeStruct((rows, width), BF16),
            jax.ShapeDtypeStruct((n, 3, rows, HEAD_DIM), BF16),
            jax.ShapeDtypeStruct((n, HEAD_DIM, rows), F32),
            jax.ShapeDtypeStruct((n, 1, rows), F32),
            jax.ShapeDtypeStruct((6, width, rows), BF16),
            jax.ShapeDtypeStruct((4, 2 * width, rows), BF16),
        ),
        in_specs=[hbm, hbm, hbm, hbm, vmem, hbm],
        out_specs=(hbm, hbm, vmem, hbm, hbm, vmem, hbm, hbm),
        scratch_shapes=[
            pltpu.VMEM((2, width, width), BF16),
            pltpu.VMEM((width, 3 * width), BF16),
            pltpu.VMEM((2, rows, width), BF16),
            pltpu.VMEM((rows, width), F32),
            pltpu.VMEM((rows, width), BF16),
            pltpu.VMEM((n, 3, rows, HEAD_DIM), BF16),
            pltpu.VMEM((n, 3, rows, HEAD_DIM), BF16),
            pltpu.VMEM((n, HEAD_DIM, rows), BF16),
            pltpu.VMEM((n, rows, rows), F32),
            pltpu.VMEM((n, HEAD_DIM, rows), F32),
            pltpu.VMEM((n, rows, HEAD_DIM), BF16),
            pltpu.VMEM((rows, width), BF16),
            pltpu.VMEM((width, rows), BF16),
            pltpu.VMEM((2 * width, rows), BF16),
            pltpu.VMEM((rows, HEAD_DIM), F32),
            pltpu.SemaphoreType.DMA((6,)),
            pltpu.SemaphoreType.DMA((6,)),
            pltpu.SemaphoreType.DMA((n,)),
            pltpu.SemaphoreType.DMA((n,)),
            pltpu.SemaphoreType.DMA((n,)),
            pltpu.SemaphoreType.DMA((n,)),
            pltpu.SemaphoreType.DMA((8,)),
            pltpu.SemaphoreType.DMA((8,)),
        ],
        compiler_params=pltpu.CompilerParams(
            collective_id=1, has_side_effects=True, vmem_limit_bytes=62 << 20
        ),
    )(state, embedded, w_adapt, w_qkv, gains, table)


def flipped(bit, value):
    return value + (1 - 2 * ((value // (1 << bit)) % 2)) * (1 << bit)


def unit_slots(first, dp):
    slots = []
    for q in range(4):
        turned = [(dp + q) % 2, (dp // 2 + q // 2) % 2]
        slots.append(turned[first] * 2 + turned[1 - first])
    return slots


def transposed_into(source, target):
    tile = 256
    for begin in range(0, source.shape[1], tile):
        target[pl.ds(begin, tile), :] = source[:, pl.ds(begin, tile)].T


def add_into(target, more):
    rows = target.shape[0]
    chunk = 16
    while rows % (chunk * 2) == 0 and chunk < 64:
        chunk *= 2

    def step(t, c):
        at = pl.ds(pl.multiple_of(t * chunk, chunk), chunk)
        target[at, :] = (target[at, :].astype(F32) + more[at, :].astype(F32)).astype(BF16)
        return c

    lax.fori_loop(0, rows // chunk, step, 0)


CHUNKS = ((0, 512), (512, 512), (1024, 384))


def z_place(z):
    return (z % 2) * 2 + z // 2


def transposed_blocks(source, target, first, last):
    tile = 256
    parts, size = target.shape[1], target.shape[2]
    for begin in range(first * tile, min(last * tile, source.shape[1]), tile):
        block = source[:, pl.ds(begin, tile)].T
        for k in range(begin // size, (begin + tile - 1) // size + 1):
            low, high = max(begin, size * k), min(begin + tile, size * (k + 1))
            target[k // parts, k % parts, pl.ds(low - size * k, high - low), :] = block[
                low - begin : high - begin
            ]


def middle_kernel(*refs):
    refs = list(refs)

    def take(count):
        taken, refs[:count] = refs[:count], []
        return taken

    (att_in, resid_in, cot_in, gain_rows, wo_in, wg_in, wu_in, wd_in) = take(8)
    (x_in, ot_in, ls_ref, table_in) = take(4)
    (layer_out, above_out, gains_out, packed_out) = take(4)
    (kept_d, kept_z, kept_g, kept_h, kept_o) = take(5)
    (wo, wg, wu, wd, att, cot, resid, branch, mid, down, above) = take(11)
    (normed, hidden, gate_by, up_by, down_low, wide_low, branch_low, dout) = take(8)
    (left_n, left_h, left_m, left_a, right_g, right_d, right_b) = take(7)
    (got_g, got_d, got_z) = take(3)
    (work, x, ot, table, g, kt, dqt, delta, dsent, packed) = take(10)
    (load_sem, store_sem, g_send, g_recv, d_send, d_recv, m_send, m_recv, s_send, s_recv) = take(10)
    n, (rows, width) = HEADS, resid.shape
    ff = wg.shape[1]
    half, part = ff // 2, width // 2
    me = lax.axis_index("seq")
    dp = lax.axis_index("dp")
    core = me % 2
    mate = flipped(0, me)
    bits = [dp % 2, dp // 2]
    near = seq_device(mate)
    across = [{"dp": flipped(0, dp)}, {"dp": flipped(1, dp)}]
    diagonal = [{"seq": mate, "dp": flipped(0, dp)}, {"seq": mate, "dp": flipped(1, dp)}]
    greet([seq_device((me + k) % n) for k in range(1, n)] + across + diagonal)
    loads = {}
    for key, src, dst in (
        ("att", att_in, att),
        ("wo", wo_in, wo),
        ("resid", resid_in, resid),
        ("wg", wg_in, wg),
        ("wu", wu_in, wu),
        ("cot", cot_in, cot),
        ("wd", wd_in, wd),
        ("x", x_in, x),
        ("ot", ot_in, ot),
        ("table", table_in, table),
    ):
        copy = pltpu.make_async_copy(src, dst, load_sem.at[len(loads)])
        copy.start()
        loads[key] = copy
    tile = 256
    gains = [gain_rows[k : k + 1, :].astype(F32) for k in range(4)]

    def tiles(total, body):
        for begin in range(0, total, tile):
            body(pl.ds(begin, tile))

    sends = []
    given = {}

    issued = []

    def give(key, src, dst, device):
        k = len(issued)
        copy = remote(src, dst, m_send.at[k], m_recv.at[k], device)
        copy.start()
        issued.append(key)
        sends.append(copy)
        given[key] = copy

    loads["att"].wait()
    loads["wo"].wait()

    def project(cols):
        branch[:, cols] = dot(att[...], wo[:, cols])

    tiles(width, project)
    loads["resid"].wait()
    mid[...] = resid[...] + mean_norm(branch[...], gains[1])
    normed[...] = mean_norm(mid[...], gains[2]).astype(BF16)
    transposed_into(normed, left_n.at[0])
    greeted(n + 3)
    give("n1", left_n.at[0], left_n.at[1], near)
    give("n2", left_n.at[0], left_n.at[2], across[0])
    loads["wg"].wait()
    loads["wu"].wait()

    def widen(cols):
        gate = dot(normed[...], wg[:, cols])
        up = dot(normed[...], wu[:, cols])
        bent = jax.nn.sigmoid(gate)
        silu = gate * bent
        hidden[:, cols] = (silu * up).astype(BF16)
        gate_by[:, cols] = (up * bent * (1.0 + gate * (1.0 - bent))).astype(BF16)
        up_by[:, cols] = silu.astype(BF16)

    tiles(ff, widen)
    loads["wd"].wait()

    steps = width // tile
    share = -(-ff // tile // steps)
    for k in range(steps):
        cols = pl.ds(k * tile, tile)
        down[:, cols] = dot(hidden[...], wd[:, cols])
        transposed_blocks(hidden, left_h, k * share, (k + 1) * share)
    give("h2", left_h.at[:, 1 - bits[1]], left_m.at[1], across[1])
    give("h1", left_h.at[:, bits[1]], left_m.at[0], near)
    loads["cot"].wait()
    grad, _ = norm_back(down[...], gains[3], cot[...].astype(F32))
    down_low[...] = grad.astype(BF16)
    mine_d = pl.ds(pl.multiple_of(core * part, 128), part)
    theirs_d = pl.ds(pl.multiple_of((1 - core) * part, 128), part)
    give("d2", down_low.at[:, mine_d], right_d.at[1], across[1])
    give("d3", down_low.at[:, theirs_d], right_d.at[2], diagonal[1])
    give("d1", down_low.at[:, theirs_d], right_d.at[0], near)

    def widen_back(cols):
        block = dot_nt(down_low[...], wd[cols, :])
        wide_low[0, :, cols] = (block * gate_by[:, cols].astype(F32)).astype(BF16)
        wide_low[1, :, cols] = (block * up_by[:, cols].astype(F32)).astype(BF16)

    tiles(ff, widen_back)

    def chunk_of(c, which_core, which_bit):
        at, wide = CHUNKS[c]
        return wide_low.at[which_core, :, pl.ds(pl.multiple_of(which_bit * half + at, 128), wide)]

    def give_chunk(c):
        at, wide = CHUNKS[c]
        cols = pl.ds(at, wide)
        give(("g2", c), chunk_of(c, core, 1 - bits[0]), right_g.at[1, :, cols], across[0])
        give(("g3", c), chunk_of(c, 1 - core, 1 - bits[0]), right_g.at[2, :, cols], diagonal[0])
        give(("g1", c), chunk_of(c, 1 - core, bits[0]), right_g.at[0, :, cols], near)

    give_chunk(0)

    def narrow_back(cols):
        above[:, cols] = dot_nt(wide_low[0], wg[cols, :]) + dot_nt(wide_low[1], wu[cols, :])

    tiles(width, narrow_back)
    grad, _ = norm_back(mid[...], gains[2], above[...])
    resid[...] = cot[...].astype(F32) + grad
    grad, _ = norm_back(branch[...], gains[1], resid[...])
    branch_low[...] = grad.astype(BF16)

    def project_back(cols):
        dout[:, cols] = dot_nt(branch_low[...], wo[cols, :]).astype(BF16)

    tiles(width, project_back)
    my_cols = pl.ds(pl.multiple_of(me * HEAD_DIM, HEAD_DIM), HEAD_DIM)
    for k in (4, 5, 3, 2, 6, 7, 1):
        owner = (me + k) % n
        cols = pl.ds(pl.multiple_of(owner * HEAD_DIM, HEAD_DIM), HEAD_DIM)
        copy = remote(dout.at[:, cols], g.at[me], g_send.at[owner], g_recv.at[me], seq_device(owner))
        copy.start()
        sends.append(copy)
    g[me] = dout[:, my_cols]
    given["n2"].wait_recv()
    give("n3", left_n.at[2], left_n.at[3], near)
    transposed_into(att, left_a.at[0])
    give("a1", left_a.at[0], left_a.at[1], near)
    give("b1", branch_low.at[:, theirs_d], right_b, near)
    layer_out[...] = (mid[...] + mean_norm(down[...], gains[3])).astype(BF16)
    stores = []

    def store(src, dst):
        copy = pltpu.make_async_copy(src, dst, store_sem.at[len(stores)])
        copy.start()
        stores.append(copy)

    store(resid, above_out)
    gains_out[...] = jnp.zeros_like(gains_out)
    gains_out[1:2, :] = gain_sum(branch[...], resid[...])
    gains_out[2:3, :] = gain_sum(mid[...], above[...])
    gains_out[3:4, :] = gain_sum(down[...], cot[...].astype(F32))
    seconds = {}
    z_low = (me // 2) % 2

    def wide_sum(c):
        at, wide = CHUNKS[c]
        for key in ("n1", "n3"):
            if key in given:
                given.pop(key).wait_recv()
        for key in ("g1", "g2", "g3"):
            given[key, c].wait_recv()
        shard = width // 32
        spread = [(bits[1] + other) % 2 for other in range(2)]
        own = chunk_of(c, core, bits[0])
        for begin in range(0, wide, 256):
            step = min(256, wide - begin)
            cols = pl.ds(at + begin, step)
            block = dot(left_n[0], own[:, pl.ds(begin, step)])
            for k in range(1, 4):
                block += dot(left_n[k], right_g[k - 1, :, cols])
            work[0:width, 0:step] = block
            for z in range(4):
                for other in range(2):
                    pieces = [
                        work[pl.ds((8 * z + 4 * c2 + 2 * other + b) * shard, shard), 0:step]
                        for c2 in range(2)
                        for b in range(2)
                    ]
                    place = pl.multiple_of(spread[other] * part + z_place(z) * 4 * shard, 16)
                    wg[pl.ds(place, 4 * shard), cols] = jnp.concatenate(pieces, axis=0).astype(BF16)
        cols = pl.ds(at, wide)
        if c == len(CHUNKS) - 1:
            store(wg.at[:, cols], kept_h)
            return
        seconds[c] = remote(
            wg.at[pl.ds(part, part), cols], got_g.at[:, cols], s_send.at[c], s_recv.at[c], across[1]
        )
        seconds[c].start()
        sends.append(seconds[c])

    def down_sum():
        for key in ("h1", "h3", "d1", "d2", "d3"):
            given[key].wait_recv()
        tall = ff // 4
        shard = ff // 32
        spread = [(bits[0] + other) % 2 for other in range(2)]
        for begin in range(0, part, 256):
            cols = pl.ds(begin, 256)
            own = down_low.at[:, mine_d]
            block = dot(left_h[:, bits[1]].reshape(2 * tall, rows), own[:, cols])
            for k in range(3):
                block += dot(left_m[k].reshape(2 * tall, rows), right_d[k, :, cols])
            work[...] = block
            for z in range(4):
                for other in range(2):
                    pieces = [
                        work[pl.ds((4 * z + 2 * c2 + other) * shard, shard), :] for c2 in range(2)
                    ]
                    place = pl.multiple_of(spread[other] * tall + z_place(z) * 2 * shard, 16)
                    wd[pl.ds(place, 2 * shard), cols] = jnp.concatenate(pieces, axis=0).astype(BF16)
        cols = pl.ds(0, part)
        seconds["d"] = remote(
            wd.at[pl.ds(tall, tall), cols], got_d, s_send.at[3], s_recv.at[3], across[0]
        )
        seconds["d"].start()
        sends.append(seconds["d"])

    def out_sum():
        given["a1"].wait_recv()
        given["b1"].wait_recv()
        shard = width // 32
        slots = unit_slots(0, dp)
        for begin in range(0, part, 256):
            cols = pl.ds(begin, 256)
            block = dot(left_a[0], branch_low.at[:, mine_d][:, cols])
            work[0:width, :] = block + dot(left_a[1], right_b[:, cols])
            for z in range(4):
                for q in range(4):
                    pieces = [
                        work[pl.ds((8 * z + 4 * c2 + q) * shard, shard), :] for c2 in range(2)
                    ]
                    place = pl.multiple_of(slots[q] * (width // 4) + z_place(z) * 2 * shard, 16)
                    wu[pl.ds(place, 2 * shard), cols] = jnp.concatenate(pieces, axis=0).astype(BF16)
        store(wu.at[:, pl.ds(0, part)], kept_o)

    loads["x"].wait()
    factor = SCORE_SCALE * LOG2E
    half_dim = HEAD_DIM // 2
    pairs = [(i, j) for j in range(n) for i in range(j, n)]
    across_blocks = ff // rows

    def probs(i, j):
        k = pairs.index((i, j))
        at, cols = k // across_blocks * rows, k % across_blocks * rows
        return wu.at[pl.ds(at, rows), pl.ds(cols, rows)]

    give_chunk(1)
    for j in range(n):
        kt[j] = x[j, 1].astype(F32).T.astype(BF16)
        for i in range(j, n):
            p = jnp.exp2(dot_nt(x[j, 1], x[i, 0]) * factor - ls_ref[i])
            if i == j:
                p = causal_fill(p, 0.0)
            probs(i, j)[...] = p.astype(BF16)
    give_chunk(2)
    loads["ot"].wait()
    loads["table"].wait()
    arrived, summed = set(), set()

    def upstream(i):
        if i not in arrived:
            arrived.add(i)

            @pl.when(me != i)
            def arrive():
                remote(g.at[0], g.at[i], g_send.at[0], g_recv.at[i], seq_device(i)).wait_recv()

            delta[i] = jnp.sum(g[i].astype(F32).T * ot[i], axis=0, keepdims=True)
        return g[i]

    def give_head(j, first, count, sem):
        span = pl.ds(first, count)

        @pl.when(me != j)
        def over():
            remote(
                dsent.at[j, span], packed.at[span, :, my_cols], d_send.at[sem], d_recv.at[sem - j + me], seq_device(j)
            ).start()

        @pl.when(me == j)
        def keep():
            packed[span, :, my_cols] = dsent[j, span]

    def unrotated(value, j):
        here = pl.ds(j * rows, rows)
        cos, sin = table[here, 0:half_dim], -table[here, half_dim:HEAD_DIM]
        return rotate(value * SCORE_SCALE, cos, sin).astype(BF16)

    order = [n - 1, n - 2, 0]
    for k in range(1, n // 2 - 1):
        order += [n - 2 - k, k]
    order += [n // 2 - 1]
    for j in order:
        dk = dv = None
        for i in range(j, n):
            up = upstream(i)
            p = probs(i, j)[...]
            v = dot(p, up)
            ds = (p.astype(F32) * (dot_nt(x[j, 2], up) - delta[i])).astype(BF16)
            k = dot(ds, x[i, 0])
            t = dot(kt[j], ds)
            dqt[i] = dqt[i] + t if i in summed else t
            summed.add(i)
            dv, dk = (v, k) if i == j else (dv + v, dk + k)
        dsent[j, 1] = unrotated(dk, j)
        dsent[j, 2] = dv.astype(BF16)
        give_head(j, 1, 2, j)
        if j < n // 2:
            dsent[j, 0] = unrotated(dqt[j].T, j)
            give_head(j, 0, 1, n + j)
        if j == 0:
            wide_sum(0)
        if j == 1:
            given["h2"].wait_recv()
            give("h3", left_m.at[1], left_m.at[2], near)
    for j in range(n // 2, n):
        dsent[j, 0] = unrotated(dqt[j].T, j)
        give_head(j, 0, 1, n + j)

    down_sum()
    wide_sum(1)
    wide_sum(2)
    out_sum()

    def finish_wide(c):
        at, wide = CHUNKS[c]
        cols = pl.ds(at, wide)
        seconds[c].wait_recv()
        add_into(wg.at[pl.ds(0, part), cols], got_g.at[:, cols])
        if c > 0:
            store(wg.at[pl.ds(0, part), cols], kept_g)
            return
        third[0].start()
        sends.append(third[0])

    def z_rows(which):
        return wg.at[pl.ds(pl.multiple_of(which * (part // 2), 16), part // 2), pl.ds(0, CHUNKS[0][1])]

    def finish_z():
        third[0].wait_recv()
        add_into(z_rows(z_low), got_z)
        store(z_rows(z_low), kept_z)

    third = [
        remote(z_rows(1 - z_low), got_z, s_send.at[4], s_recv.at[4], seq_device(flipped(1, me)))
    ]
    finish_wide(0)
    finish_wide(1)
    seconds["d"].wait_recv()
    mine = wd.at[pl.ds(0, ff // 4), pl.ds(0, part)]
    add_into(mine, got_d)
    store(mine, kept_d)
    finish_z()
    for first, count in ((1, 2), (0, 1)):
        span = pl.ds(first, count)
        for j in range(n):

            @pl.when(me != j)
            def finish():
                cols = pl.ds(j * HEAD_DIM, HEAD_DIM)
                sem = j if first == 1 else n + j
                copy = remote(
                    dsent.at[j, span], packed.at[span, :, cols], d_send.at[sem], d_recv.at[sem], seq_device(j)
                )
                copy.wait_send()
                copy.wait_recv()

    store(packed, packed_out)
    for copy in sends:
        copy.wait_send()
    for copy in stores:
        copy.wait()


def middle_block(att, resid, cot, gain_rows, w_out, w_gate, w_up, w_down, x, ot, ls, table):
    n = HEADS
    rows, width = resid.shape
    ff = w_gate.shape[1]
    half, part = ff // 2, width // 2
    hbm = pl.BlockSpec(memory_space=pl.ANY)
    vmem = pl.BlockSpec(memory_space=pltpu.VMEM)
    dma = pltpu.SemaphoreType.DMA
    low = pltpu.VMEM((rows, width), BF16)
    wide = pltpu.VMEM((rows, ff), BF16)
    full = pltpu.VMEM((rows, width), F32)
    scratch = [pltpu.VMEM(w.shape, BF16) for w in (w_out, w_gate, w_up, w_down)]
    scratch += [low, low, full, full, full, full, full]
    scratch += [low, wide, wide, wide, low, pltpu.VMEM((2, rows, ff), BF16), low, low]
    scratch += [
        pltpu.VMEM((4, width, rows), BF16),
        pltpu.VMEM((8, 2, ff // 16, rows), BF16),
        pltpu.VMEM((3, 8, ff // 16, rows), BF16),
        pltpu.VMEM((2, width, rows), BF16),
        pltpu.VMEM((3, rows, half), BF16),
        pltpu.VMEM((3, rows, part), BF16),
        pltpu.VMEM((rows, part), BF16),
        pltpu.VMEM((part, CHUNKS[-1][0]), BF16),
        pltpu.VMEM((ff // 4, part), BF16),
        pltpu.VMEM((part // 2, CHUNKS[0][1]), BF16),
        pltpu.VMEM((half, 256), F32),
        pltpu.VMEM(x.shape, BF16),
        pltpu.VMEM(ot.shape, F32),
        pltpu.VMEM(table.shape, F32),
        pltpu.VMEM((n, rows, HEAD_DIM), BF16),
        pltpu.VMEM((n, HEAD_DIM, rows), BF16),
        pltpu.VMEM((n, HEAD_DIM, rows), F32),
        pltpu.VMEM((n, 1, rows), F32),
        pltpu.VMEM((n, 3, rows, HEAD_DIM), BF16),
        pltpu.VMEM((3, rows, width), BF16),
        dma((10,)),
        dma((7,)),
        dma((n,)),
        dma((n,)),
        dma((2 * n,)),
        dma((2 * n,)),
        dma((20,)),
        dma((20,)),
        dma((5,)),
        dma((5,)),
    ]
    return pl.pallas_call(
        middle_kernel,
        name="middle",
        out_shape=[
            jax.ShapeDtypeStruct((rows, width), BF16),
            jax.ShapeDtypeStruct((rows, width), F32),
            jax.ShapeDtypeStruct((8, width), F32),
            jax.ShapeDtypeStruct((3, rows, width), BF16),
            jax.ShapeDtypeStruct((ff // 4, part), BF16),
            jax.ShapeDtypeStruct((part // 2, CHUNKS[0][1]), BF16),
            jax.ShapeDtypeStruct((part, CHUNKS[1][1]), BF16),
            jax.ShapeDtypeStruct((width, CHUNKS[-1][1]), BF16),
            jax.ShapeDtypeStruct((width, part), BF16),
        ],
        in_specs=[hbm] * 3 + [vmem] + [hbm] * 6 + [vmem] + [hbm],
        out_specs=[vmem, hbm, vmem, hbm] + [hbm] * 5,
        scratch_shapes=scratch,
        compiler_params=pltpu.CompilerParams(
            collective_id=2, has_side_effects=True, vmem_limit_bytes=62 << 20
        ),
    )(att, resid, cot, gain_rows, w_out, w_gate, w_up, w_down, x, ot, ls, table)


BEGUN = ((1, 0, 512, None), (2, 0, 512, None), (0, 0, 256, None), (0, 256, 256, None), (3, 0, 384, 1))
FRESH = ((1, 0, 0), (1, 1024, 0), (1, 2048, 1), (0, 0, 1))
SCHEDULE = (
    ("S", 4), ("2", 0), ("F", 5), ("1", 3), ("P", 0), ("1", 1), ("D", 3), ("2", 3),
    ("E", 0), ("U", 9), ("O", 0), ("U", 7), ("C", 4), ("G", 0), ("E", 3), ("B", 5),
    ("1", 2), ("S", 5), ("D", 1), ("2", 1), ("W", 9), ("S", 9), ("1", 4), ("W", 7),
    ("S", 7), ("D", 2), ("G", 1), ("2", 2), ("C", 5), ("E", 1), ("1", 5), ("D", 4),
    ("G", 2), ("2", 4), ("U", 8), ("E", 2), ("C", 7), ("1", 7), ("D", 5), ("G", 3),
    ("U", 6), ("2", 5), ("C", 9), ("1", 9), ("E", 4), ("D", 7), ("G", 4), ("2", 7),
    ("W", 8), ("E", 5), ("S", 8), ("W", 6), ("S", 6), ("E", 7), ("D", 9), ("2", 9),
    ("C", 8), ("1", 8), ("C", 6), ("1", 6), ("E", 9), ("D", 8), ("2", 8), ("D", 6),
    ("2", 6), ("E", 8), ("E", 6),
)


def dealt_blocks(left, slots, right, spread, bit, out, work):
    total = left.shape[1]
    shard = total // 32
    block = dot(left[slots[0]], right[0])
    for k in range(1, 4):
        block += dot(left[slots[k]], right[k])
    work[0:total, :] = block
    for z in range(4):
        for other in range(2):
            pieces = []
            for core in range(2):
                for b in range(2):
                    q = (b << bit) | (other << (1 - bit))
                    pieces.append(work[pl.ds((8 * z + 4 * core + q) * shard, shard), :])
            out[spread[other], pl.ds(z_place(z) * 4 * shard, 4 * shard), :] = jnp.concatenate(
                pieces, axis=0
            ).astype(BF16)


def tail_kernel(*refs):
    refs = list(refs)

    def take(count):
        taken, refs[:count] = refs[:count], []
        return taken

    begun, fresh = len(BEGUN), len(FRESH)
    single = begun
    first_fresh = begun + 1
    count = first_fresh + fresh
    kept_in = take(5)
    packed_in, ltn_in, ltj_in, wq_in, wa_in = take(5)
    resid_in, above_in, gain_rows, gain_parts = take(4)
    grad_joined = take(2)
    outs = take(5)
    (gains_out,) = take(1)
    held = take(3)
    sums, arrived2 = [None] * 4 + take(count - 4), [None] * 4 + take(count - 4)
    parts, arrived3, arrived4, finals = take(count), take(count), take(count), take(count)
    (got_o, wq, wa, packed, ltn, ltj, dealt, low, work, back_sum, gain_buf, gain_got) = take(12)
    (resid, above, joined_0, joined_1) = take(4)
    joined = (joined_0, joined_1)
    (load_sem, u_send, u_recv, s_send, s_recv, z1_send, z1_recv) = take(7)
    (z2_send, z2_recv, c_send, c_recv, gain_send, gain_recv, store_sem) = take(7)
    rows, width = resid.shape
    me = lax.axis_index("seq")
    dp = lax.axis_index("dp")
    core = me % 2
    bits = [dp % 2, dp // 2]
    z_low, z_high = (me // 2) % 2, me // 4
    mate = flipped(0, me)
    near = seq_device(mate)
    across = [{"dp": flipped(0, dp)}, {"dp": flipped(1, dp)}]
    diagonal = [{"seq": mate, "dp": flipped(0, dp)}, {"seq": mate, "dp": flipped(1, dp)}]
    beside = [seq_device(flipped(1, me)), seq_device(flipped(2, me))]
    greet([near] + across + diagonal + beside)
    loads = {}

    def load(key, src, dst):
        loads[key] = pltpu.make_async_copy(src, dst, load_sem.at[len(loads)])
        loads[key].start()

    load("packed", packed_in, packed)
    load("wq", wq_in, wq)
    load("resid", resid_in, resid)
    load("above", above_in, above)
    greeted(7)
    sends = []

    def send(src, dst, send_sem, recv_sem, device):
        copy = remote(src, dst, send_sem, recv_sem, device)
        copy.start()
        sends.append(copy)
        return copy

    first, dealing, second, third, fourth, finished, taken = [], {}, {}, {}, {}, {}, set()

    def ready(key):
        if key not in taken:
            taken.add(key)
            loads[key].wait()

    def z_rows(u, which):
        tall = finals[u].shape[0]
        return pl.ds(pl.multiple_of(which * 2 * tall, 16), 2 * tall)

    def one_z(u, which):
        tall = finals[u].shape[0]
        return pl.ds(pl.multiple_of(which * tall, 16), tall)

    def start_first(u):
        first.append(send(kept_in[4].at[pl.ds(2, 2)], got_o, s_send.at[count], s_recv.at[count], across[0]))

    def take_first(u):
        first[0].wait_recv()
        ready(single)
        for k in (1, 0):
            add_into(sums[single].at[k], got_o.at[k])

    def start_columns(u):
        k = u - first_fresh
        bit = FRESH[k][2]
        source = low if k == 3 else packed.at[k]
        if k < 3:
            ready("packed")

        def columns(other_core, other_bit):
            place = (core + (1 - 2 * core) * other_core) * 2
            place = place + bits[bit] + (1 - 2 * bits[bit]) * other_bit
            return pl.ds(pl.multiple_of(place * 256, 256), 256)

        dealing[u] = [
            send(
                source.at[:, columns(*there)],
                dealt.at[k, slot],
                u_send.at[3 * k + slot - 1],
                u_recv.at[3 * k + slot - 1],
                device,
            )
            for there, slot, device in (
                ((0, 1), 2, across[bit]),
                ((1, 1), 3, diagonal[bit]),
                ((1, 0), 1, near),
            )
        ]
        dealt[k, 0] = source[:, columns(0, 0)]

    def start_second(u):
        if u < begun:
            array, at, wide, bit = BEGUN[u]
            rows_in = kept_in[array].shape[0] // 2
            src = kept_in[array].at[pl.ds(rows_in, rows_in), pl.ds(at, wide)]
        else:
            bit = 1 if u == single else 1 - FRESH[u - first_fresh][2]
            src = sums[u].at[1]
        second[u] = send(src, arrived2[u], s_send.at[u], s_recv.at[u], across[bit])

    def multiply(u):
        k = u - first_fresh
        out, column, bit = FRESH[k]
        slots = (0, 1, 2, 3) if (bit == 0 or k == 3) else (0, 1, 4, 5)
        left = ltj if k == 3 else ltn
        ready("ltj" if k == 3 else "ltn")
        for copy in dealing[u]:
            copy.wait_recv()
        spread = [(bits[1 - bit] + other) % 2 for other in range(2)]
        dealt_blocks(left, slots, dealt.at[k], spread, bit, sums[u], work)

    def take_second(u):
        second[u].wait_recv()
        if u < begun:
            ready(u)
        add_into(sums[u].at[0], arrived2[u])

    def start_third(u):
        theirs = z_rows(u, 1 - z_low)
        if u < 4:
            array, at, wide, _ = BEGUN[u]
            src = kept_in[array].at[theirs, pl.ds(at, wide)]
        else:
            src = sums[u].at[0, theirs]
        third[u] = send(src, arrived3[u], z1_send.at[u], z1_recv.at[u], beside[0])

    def take_third(u):
        third[u].wait_recv()
        if u < 4:
            array, at, wide, _ = BEGUN[u]
            ready(array)
            mine = held[array][:, pl.ds(at, wide)]
        else:
            mine = sums[u][0, z_rows(u, z_low), :]
        parts[u][...] = (mine.astype(F32) + arrived3[u][...].astype(F32)).astype(BF16)

    def start_fourth(u):
        source = kept_in[1] if u == 0 else parts[u]
        fourth[u] = send(
            source.at[one_z(u, 1 - z_high)], arrived4[u], z2_send.at[u], z2_recv.at[u], beside[1]
        )

    def take_fourth(u):
        fourth[u].wait_recv()
        if u == 0:
            ready(1)
        source = held[1] if u == 0 else parts[u]
        finals[u][...] = source[one_z(u, z_high), :].astype(F32) + arrived4[u][...].astype(F32)
        if u in (0, 1, 4):
            at, wide = CHUNKS[min(u, 2)]
            bit = 0
            cols = pl.ds(pl.multiple_of(bits[0] * (outs[3].shape[2] // 2) + at, 128), wide)
            target = outs[3].at[core, :, cols]
        elif u <= single:
            out, at, wide = (2, 0, width // 2) if u == single else (4,) + BEGUN[u][1:3]
            bit = None
            target = outs[out].at[:, pl.ds(pl.multiple_of(core * (width // 2) + at, 128), wide)]
        else:
            out, column, bit = FRESH[u - first_fresh]
            cols = pl.ds(pl.multiple_of((core * 2 + bits[bit]) * 256 + column, 256), 256)
            target = outs[out].at[:, cols]
        if bit is None:
            owners = [(core, None), (1 - core, near)]
        else:
            here, there = bits[bit], 1 - bits[bit]
            owners = [
                (core * 2 + here, None),
                ((1 - core) * 2 + here, near),
                (core * 2 + there, across[bit]),
                ((1 - core) * 2 + there, diagonal[bit]),
            ]
        shard = finals[u].shape[0] // len(owners)
        finished[u] = []
        for k, (place, device) in enumerate(owners):
            at = pl.ds(pl.multiple_of(place * shard, 8), shard)
            if k == 0:
                target[...] = finals[u][at, :]
            else:
                sem = 3 * u + k - 1
                finished[u].append(
                    send(finals[u].at[at], target, c_send.at[sem], c_recv.at[sem], device)
                )

    gain_steps = {}
    gain_partners = [near] + across + beside

    def send_gain(k):
        gain_steps[k] = send(
            gain_buf.at[k], gain_got.at[k], gain_send.at[k], gain_recv.at[k], gain_partners[k]
        )

    def add_gain(k):
        gain_steps[k].wait_recv()
        total = gain_buf[k] + gain_got[k]
        if k == 4:
            gains_out[...] = total
        else:
            gain_buf[k + 1] = total
            send_gain(k + 1)

    tile = 256
    stores = []

    def dense_back(_):
        ready("packed")
        ready("wq")
        load(1, kept_in[1], held[1])
        load(2, kept_in[2].at[z_rows(1, z_low)], held[2])
        load(0, kept_in[0].at[z_rows(2, z_low)], held[0])
        load(single, kept_in[4].at[pl.ds(0, 2)], sums[single])
        load(4, kept_in[3].at[pl.ds(0, kept_in[3].shape[0] // 2)], sums[4].at[0])
        load("ltn", ltn_in, ltn)
        load("ltj", ltj_in, ltj)
        load("wa", wa_in, wa)
        for begin in range(0, width, tile):
            at = pl.ds(begin, tile)
            block = dot_nt(packed[0], wq[at, pl.ds(0, width)])
            block += dot_nt(packed[1], wq[at, pl.ds(width, width)])
            block += dot_nt(packed[2], wq[at, pl.ds(2 * width, width)])
            back_sum[:, at] = block
        ready("resid")
        ready("above")
        part, gain0 = norm_back(resid[...], gain_rows[0:1, :].astype(F32), back_sum[...])
        low[...] = (above[...] + part).astype(BF16)
        gain_buf[0] = gain_parts[...]
        gain_buf[0, 0:1, :] = gain0[None, :]
        send_gain(0)

    def dense_out(_):
        ready("wa")
        for k in range(2):
            for begin in range(0, width, tile):
                from_row = pl.ds(k * width + begin, tile)
                joined[k][:, pl.ds(begin, tile)] = dot_nt(low[...], wa[from_row, :])
            stores.append(pltpu.make_async_copy(joined[k], grad_joined[k], store_sem.at[k]))
            stores[k].start()

    actions = {
        "F": start_first,
        "B": take_first,
        "U": start_columns,
        "S": start_second,
        "1": start_third,
        "2": start_fourth,
        "W": multiply,
        "C": take_second,
        "D": take_third,
        "E": take_fourth,
        "G": add_gain,
        "P": dense_back,
        "O": dense_out,
    }
    for action, u in SCHEDULE:
        actions[action](u)
    for u in range(count):
        for copy in finished[u]:
            copy.wait_recv()
    for copy in sends:
        copy.wait_send()
    for copy in stores:
        copy.wait()


def tail(kept, packed, left_n, left_j, w_qkv, w_adapt, resid, above, gain_rows, gain_parts):
    rows, width = resid.shape
    hbm = pl.BlockSpec(memory_space=pl.ANY)
    vmem = pl.BlockSpec(memory_space=pltpu.VMEM)
    dma = pltpu.SemaphoreType.DMA
    fresh = len(FRESH)
    down, gate, gate_next, last, out = kept
    left_over = (4, 2, 4, 8)
    every = [(kept[array].shape[0] // left_over[array], wide) for array, _, wide, _ in BEGUN]
    every += [(out.shape[1] // 4, out.shape[2])]
    every += [(width // 8, 256)] * 3 + [(width // 4, 256)]
    count = len(every)
    slots = [1] + [2] * (1 + fresh)
    shapes = [
        (2 * width // 32, width),
        (width // 32, 3 * width),
        (width // 32, width),
        (2, width // 32, 2 * (gate.shape[1] + gate_next.shape[1] + last.shape[1])),
        (down.shape[0] // 8, width),
    ]
    scratch = [
        pltpu.VMEM(shape, BF16)
        for shape in (
            (down.shape[0] // 2, down.shape[1]),
            gate.shape,
            (gate_next.shape[0] // 2, gate_next.shape[1]),
        )
    ]
    scratch += [pltpu.VMEM((k, 4 * tall, wide), BF16) for k, (tall, wide) in zip(slots, every[4:])]
    scratch += [pltpu.VMEM((4 * tall, wide), BF16) for tall, wide in every[4:]]
    scratch += [pltpu.VMEM((2 * tall, wide), BF16) for tall, wide in every]
    scratch += [pltpu.VMEM((2 * tall, wide), BF16) for tall, wide in every]
    scratch += [pltpu.VMEM((tall, wide), BF16) for tall, wide in every]
    scratch += [pltpu.VMEM((tall, wide), F32) for tall, wide in every]
    scratch += [
        pltpu.VMEM((2,) + out.shape[1:], BF16),
        pltpu.VMEM(w_qkv.shape, BF16),
        pltpu.VMEM(w_adapt.shape, BF16),
        pltpu.VMEM(packed.shape, BF16),
        pltpu.VMEM(left_n.shape, BF16),
        pltpu.VMEM(left_j.shape, BF16),
        pltpu.VMEM((4, 4, rows, 256), BF16),
        pltpu.VMEM((rows, width), BF16),
        pltpu.VMEM((2 * width, 256), F32),
        pltpu.VMEM((rows, width), F32),
        pltpu.VMEM((5, 8, width), F32),
        pltpu.VMEM((5, 8, width), F32),
    ]
    scratch += [pltpu.VMEM((rows, width), F32) for _ in range(4)]
    scratch += [dma((14,)), dma((3 * fresh,)), dma((3 * fresh,))]
    scratch += [dma((count + 1,)) for _ in range(2)]
    scratch += [dma((count,)) for _ in range(4)]
    scratch += [dma((3 * count,)) for _ in range(2)]
    scratch += [dma((5,)) for _ in range(2)] + [dma((2,))]
    return pl.pallas_call(
        tail_kernel,
        name="tail",
        out_shape=[jax.ShapeDtypeStruct((rows, width), F32)] * 2
        + [jax.ShapeDtypeStruct(shape, F32) for shape in shapes]
        + [jax.ShapeDtypeStruct((8, width), F32)],
        in_specs=[hbm] * 12 + [vmem] * 2,
        out_specs=[hbm] * 2 + [vmem] * 6,
        scratch_shapes=scratch,
        compiler_params=pltpu.CompilerParams(
            collective_id=3, has_side_effects=True, vmem_limit_bytes=62 << 20
        ),
    )(*kept, packed, left_n, left_j, w_qkv, w_adapt, resid, above, gain_rows, gain_parts)


def finish_kernel(*refs):
    sources, gain_ref, targets, gain_out, sem = refs[:8], refs[8], refs[9:18], refs[18], refs[19]
    wide = sources[6]
    pairs = list(zip(sources[:6], targets[:6]))
    pairs += [(wide.at[0], targets[6]), (wide.at[1], targets[7]), (sources[7], targets[8])]
    copies = [
        pltpu.make_async_copy(src, dst, sem.at[k]) for k, (src, dst) in enumerate(pairs)
    ]
    for copy in copies:
        copy.start()
    share = gain_out.shape[1]
    at = (lax.axis_index("seq") * lax.axis_size("dp") + lax.axis_index("dp")) * share
    block = gain_ref[:, pl.ds(pl.multiple_of(at // 128 * 128, 128), 128)]
    here = lax.broadcasted_iota(jnp.int32, (128, share), 0) - at % 128
    picked = here == lax.broadcasted_iota(jnp.int32, (128, share), 1)
    gain_out[...] = lax.dot_general(
        block,
        picked.astype(F32),
        (((1,), (0,)), ((), ())),
        precision=lax.Precision.HIGHEST,
        preferred_element_type=F32,
    )[:4]
    for copy in copies:
        copy.wait()


def finish(*values):
    hbm = pl.BlockSpec(memory_space=pl.ANY)
    vmem = pl.BlockSpec(memory_space=pltpu.VMEM)
    wide, gains = values[6], values[8]
    share = gains.shape[1] // (lax.axis_size("seq") * lax.axis_size("dp"))
    like = list(values[:6]) + [wide[0], wide[1], values[7]]
    return pl.pallas_call(
        finish_kernel,
        name="finish",
        out_shape=[jax.ShapeDtypeStruct(value.shape, value.dtype) for value in like]
        + [jax.ShapeDtypeStruct((4, share), F32)],
        in_specs=[vmem] * 9,
        out_specs=[hbm] * 9 + [vmem],
        scratch_shapes=[pltpu.SemaphoreType.DMA((9,))],
        compiler_params=pltpu.CompilerParams(vmem_limit_bytes=62 << 20),
    )(*values)


def xor_permute(value, axis, mask):
    return lax.ppermute(value, axis, [(i, i ^ mask) for i in range(lax.axis_size(axis))])


def quadrants(left):
    n, parts = lax.axis_size("seq"), lax.axis_size("dp")
    tokens, rows = left.shape
    shard = rows // (n * parts)
    split = left.reshape(tokens, n, parts, shard).transpose(2, 0, 1, 3)
    split = split.reshape(parts, tokens, n * shard)
    me = lax.axis_index("dp")
    return jnp.concatenate(
        [lax.dynamic_index_in_dim(split, me ^ m, 0, keepdims=True) for m in range(parts)]
    )


def other_core(left, right):
    core = lax.axis_index("seq") % 2
    half = right.shape[1] // 2
    mine = lax.dynamic_slice_in_dim(right, core * half, half, 1)
    theirs = lax.dynamic_slice_in_dim(right, (1 - core) * half, half, 1)
    left_in = xor_permute(left, "seq", 1)
    right_in = xor_permute(theirs, "seq", 1)
    return jnp.concatenate([left, left_in], axis=1), jnp.concatenate([mine, right_in], axis=0)


def scattered_sum(left, right, bits):
    n, parts = lax.axis_size("seq"), lax.axis_size("dp")
    cols = right.shape[1]
    left, right = other_core(quadrants(left), right)
    got = {}
    masks = list(range(parts))
    for bit in bits:
        outgoing = [m for m in masks if m >> bit & 1]
        masks = [m for m in masks if not m >> bit & 1]
        blocks = []
        for m in outgoing:
            block = dot_tn(left[m], right)
            for more in got.get(m, ()):
                block = block + more.astype(F32)
            blocks.append(block.astype(BF16))
        incoming = xor_permute(jnp.stack(blocks), "dp", 1 << bit)
        for k, m in enumerate(outgoing):
            got.setdefault(m ^ (1 << bit), []).append(incoming[k])
    block = dot_tn(left[0], right)
    for more in got.get(0, ()):
        block = block + more.astype(F32)
    shard = block.shape[0] // n
    block = block.astype(BF16).reshape(n, shard, cols // 2)
    block = lax.all_to_all(block, "seq", 0, 0)
    block = jnp.sum(block.reshape(n // 2, 2, shard, cols // 2).astype(F32), axis=0)
    return block.transpose(1, 0, 2).reshape(shard, cols)


def small_sum(value):
    value = value.reshape(value.shape[0], -1, value.shape[1])
    for axis in ("seq", "dp"):
        size = lax.axis_size(axis)
        me = lax.axis_index(axis)
        for bit in reversed(range(size.bit_length() - 1)):
            half = value.shape[2] // 2
            mine = (me >> bit) & 1
            kept = lax.dynamic_slice_in_dim(value, mine * half, half, 2)
            sent = lax.dynamic_slice_in_dim(value, (1 - mine) * half, half, 2)
            value = kept + xor_permute(sent, axis, 1 << bit)
    return value[:, 0]


def local(state, embedded, cotangent, w_adapt, w_qkv, w_out, w_gate, w_up, w_down, gains):
    seq_count, rows, width = state.shape
    n, parts = lax.axis_size("seq"), lax.axis_size("dp")
    tokens = seq_count * rows
    me = lax.axis_index("seq")
    bits = list(range(parts.bit_length() - 1))
    copies = max(1, n // HEADS)
    held = max(1, HEADS // n)
    owners = n // copies
    cos_np, sin_np = angle_tables(n * rows)
    cos_all, sin_all = jnp.asarray(cos_np), jnp.asarray(sin_np)
    cos = lax.dynamic_slice_in_dim(cos_all, me * rows, rows, 0)[:, None, :]
    sin = lax.dynamic_slice_in_dim(sin_all, me * rows, rows, 0)[:, None, :]
    gain_rows = gains.astype(F32)
    state, embedded = state.reshape(tokens, width), embedded.reshape(tokens, width)

    def to_heads(flat):
        return flat.reshape(tokens, HEADS, HEAD_DIM)

    def to_owner(parts_in):
        sent = jnp.stack(parts_in).reshape(len(parts_in), tokens, owners, held, HEAD_DIM)
        sent = sent.transpose(2, 3, 0, 1, 4)
        if copies > 1:
            sent = jnp.repeat(sent, copies, axis=0)
        return lax.all_to_all(sent, "seq", 0, 0)

    def from_owner(value):
        back = lax.all_to_all(value, "seq", 0, 0)[::copies]
        back = back.reshape(HEADS, -1, tokens, HEAD_DIM)
        return back.transpose(2, 1, 0, 3).reshape(tokens, -1)

    table = jnp.asarray(np.concatenate([cos_np, sin_np], axis=1))
    if n == HEADS and seq_count == 1 and parts == 4:
        resid, normed, attended, qkv, attended_t, logsum, left_n, left_j = front(
            state, embedded, w_adapt, w_qkv, gains, table
        )
        qkv, attended_t, logsum = qkv[:, None], attended_t[:, None], logsum[:, None]
    else:
        resid = dot(state, w_adapt[:width]) + dot(embedded, w_adapt[width:])
        normed = mean_norm(resid, gain_rows[0]).astype(BF16)
        packed = dot(normed, w_qkv)
        queries = rotate(to_heads(packed[:, :width]), cos, sin).astype(BF16)
        keys = rotate(to_heads(packed[:, width : 2 * width]), cos, sin).astype(BF16)
        values = to_heads(packed[:, 2 * width :]).astype(BF16)
        qkv = to_owner((queries, keys, values))
        attended, attended_t, logsum = attention(qkv)
        attended = from_owner(attended[:, :, None])
    shape = (seq_count, rows, width)
    if n == HEADS and parts == 4 and seq_count == 1:
        layer_out, middle_grad, gain_parts, packed_low, *kept = middle_block(
            attended,
            resid,
            cotangent.reshape(tokens, width),
            gains,
            w_out,
            w_gate,
            w_up,
            w_down,
            qkv[:, 0],
            attended_t[:, 0],
            logsum[:, 0],
            table,
        )
        grad_state, grad_embedded, grad_adapt, grad_qkv, grad_out, grad_wide, grad_down, gains_sum = tail(
            kept[:4] + [kept[4].reshape(4, width // 4, width // 2)],
            packed_low,
            left_n,
            left_j,
            w_qkv,
            w_adapt,
            resid,
            middle_grad,
            gains,
            gain_parts,
        )
        outs = finish(
            layer_out,
            grad_state,
            grad_embedded,
            grad_adapt,
            grad_qkv,
            grad_out,
            grad_wide,
            grad_down,
            gains_sum,
        )
        return tuple(value.reshape(shape) for value in outs[:3]) + tuple(outs[3:])
    branch = dot(attended, w_out)
    middle = resid + mean_norm(branch, gain_rows[1])
    normed_mid = mean_norm(middle, gain_rows[2]).astype(BF16)
    gate_pre = dot(normed_mid, w_gate)
    up_pre = dot(normed_mid, w_up)
    sigmoid_gate = jax.nn.sigmoid(gate_pre)
    silu_gate = gate_pre * sigmoid_gate
    hidden = (silu_gate * up_pre).astype(BF16)
    down_out = dot(hidden, w_down)
    layer_out = middle + mean_norm(down_out, gain_rows[3])
    out_grad = cotangent.astype(F32).reshape(tokens, width)
    down_grad, gain_grad3 = norm_back(down_out, gain_rows[3], out_grad)
    down_low = down_grad.astype(BF16)
    hidden_grad = dot_nt(down_low, w_down)
    gate_low = (
        hidden_grad * up_pre * sigmoid_gate * (1.0 + gate_pre * (1.0 - sigmoid_gate))
    ).astype(BF16)
    up_low = (hidden_grad * silu_gate).astype(BF16)
    mid_norm_grad = dot_nt(gate_low, w_gate) + dot_nt(up_low, w_up)
    middle_part, gain_grad2 = norm_back(middle, gain_rows[2], mid_norm_grad)
    middle_grad = out_grad + middle_part
    branch_grad, gain_grad1 = norm_back(branch, gain_rows[1], middle_grad)
    branch_low = branch_grad.astype(BF16)
    attended_grad = dot_nt(branch_low, w_out).astype(BF16)
    upstream = to_owner((to_heads(attended_grad),))[:, :, 0]
    packed_grad = attention_back(qkv, upstream, attended_t, logsum, cos_all, sin_all)
    packed_low = from_owner(packed_grad)
    normed_grad = dot_nt(packed_low, w_qkv)
    resid_part, gain_grad0 = norm_back(resid, gain_rows[0], normed_grad)
    resid_low = (middle_grad + resid_part).astype(BF16)
    grad_state = dot_nt(resid_low, w_adapt[:width])
    grad_embedded = dot_nt(resid_low, w_adapt[width:])
    flipped = bits[::-1]
    joined = jnp.concatenate([state, embedded], axis=-1)
    grad_down = scattered_sum(hidden, down_low, bits)
    grad_gate = scattered_sum(normed_mid, gate_low, flipped)
    grad_up = scattered_sum(normed_mid, up_low, bits)
    grad_out = scattered_sum(attended, branch_low, flipped)
    grad_qkv = scattered_sum(normed, packed_low, flipped)
    grad_adapt = scattered_sum(joined, resid_low, bits)
    grad_gains = jnp.stack([gain_grad0, gain_grad1, gain_grad2, gain_grad3])
    grad_gains = small_sum(grad_gains)
    return (
        layer_out.reshape(shape).astype(BF16),
        grad_state.reshape(shape),
        grad_embedded.reshape(shape),
        grad_adapt,
        grad_qkv,
        grad_out,
        grad_gate,
        grad_up,
        grad_down,
        grad_gains,
    )


def solution(mesh):
    tokens = P("dp", "seq", None)
    rows = P(("seq", "dp"), None)
    return jax.shard_map(
        local,
        mesh=mesh,
        in_specs=(tokens,) * 3 + (P(),) * 7,
        out_specs=(tokens,) * 3 + (rows,) * 6 + (P(None, ("seq", "dp")),),
        check_vma=False,
    )
```

```python
import functools
import math

import jax
import jax.numpy as jnp
import numpy as np
from jax import lax
from jax.experimental import pallas as pl
from jax.experimental.pallas import tpu as pltpu
from jax.sharding import PartitionSpec as P

HEADS = 8
HEAD_DIM = 128
norm_eps = 1e-06
rope_base = 50000.0
F32 = jnp.float32
BF16 = jnp.bfloat16
MESH = pl.DeviceIdType.MESH
NEG = -1e30
SCORE_SCALE = 1.0 / math.sqrt(HEAD_DIM)
LOG2E = 1.0 / math.log(2.0)


def mean_norm(values_in, gain_row):
    return (
        values_in
        * lax.rsqrt(jnp.mean(values_in * values_in, axis=-1, keepdims=True) + norm_eps)
        * gain_row
    )


def norm_back(values_in, gain_row, upstream):
    inverse = lax.rsqrt(jnp.mean(values_in * values_in, axis=-1, keepdims=True) + norm_eps)
    scaled = upstream * gain_row
    value_grad = inverse * scaled - values_in * (inverse * inverse * inverse) * jnp.mean(
        values_in * scaled, axis=-1, keepdims=True
    )
    gain_grad = jnp.sum(upstream * values_in * inverse, axis=0)
    return (value_grad, gain_grad)


def gain_sum(values_in, upstream):
    inverse = lax.rsqrt(jnp.mean(values_in * values_in, axis=-1, keepdims=True) + norm_eps)
    return jnp.sum(upstream * values_in * inverse, axis=0, keepdims=True)


def angle_tables(length):
    half_dim = HEAD_DIM // 2
    freqs = np.exp(
        np.arange(half_dim, dtype=np.float32) * np.float32(-2.0 * math.log(rope_base) / HEAD_DIM)
    ).astype(np.float32)
    angles = np.arange(length, dtype=np.float32)[:, None] * freqs[None, :]
    return np.cos(angles).astype(np.float32), np.sin(angles).astype(np.float32)


def rotate(heads_in, cos_table, sin_table):
    half_dim = heads_in.shape[-1] // 2
    lower_half = heads_in[..., :half_dim]
    upper_half = heads_in[..., half_dim:]
    return jnp.concatenate(
        [
            lower_half * cos_table - upper_half * sin_table,
            upper_half * cos_table + lower_half * sin_table,
        ],
        axis=-1,
    )


def dot(a, b):
    return lax.dot_general(a, b, (((1,), (0,)), ((), ())), preferred_element_type=F32)


def dot_tn(a, b):
    return lax.dot_general(a, b, (((0,), (0,)), ((), ())), preferred_element_type=F32)


def dot_nt(a, b):
    return lax.dot_general(a, b, (((1,), (1,)), ((), ())), preferred_element_type=F32)


def span(low, high, body, unrolled):
    if unrolled:
        for i in range(low, high):
            body(i)
    else:
        lax.fori_loop(low, high, lambda i, c: (body(i), c)[1], 0)


def causal_fill(block, fill):
    kv = lax.broadcasted_iota(jnp.int32, block.shape, 0)
    q = lax.broadcasted_iota(jnp.int32, block.shape, 1)
    return jnp.where(q >= kv, block, fill)


def attention_kernel(x_ref, o_ref, ot_ref, ls_ref, vt_ref, s_ref):
    n, hp, _, rows, _ = x_ref.shape
    unrolled = n <= 8
    factor = SCORE_SCALE * LOG2E
    for h in range(hp):
        for j in range(n):
            vt_ref[j] = x_ref[j, h, 2].astype(F32).T.astype(BF16)

        def query_block(i):
            q = x_ref[i, h, 0]
            diag = causal_fill(dot_nt(x_ref[i, h, 1], q), NEG)

            def first(j, peak):
                s = dot_nt(x_ref[j, h, 1], q)
                s_ref[j] = s
                return jnp.maximum(peak, jnp.max(s, axis=0, keepdims=True))

            peak = jnp.max(diag, axis=0, keepdims=True)
            if unrolled:
                for j in range(i):
                    peak = first(j, peak)
            else:
                peak = lax.fori_loop(0, i, first, peak)
            shift = peak * factor
            p = jnp.exp2(diag * factor - shift)
            total = jnp.sum(p, axis=0, keepdims=True)
            acc = dot(vt_ref[i], p.astype(BF16))

            def second(j, state):
                total, acc = state
                p = jnp.exp2(s_ref[j] * factor - shift)
                return (
                    total + jnp.sum(p, axis=0, keepdims=True),
                    acc + dot(vt_ref[j], p.astype(BF16)),
                )

            state = (total, acc)
            if unrolled:
                for j in range(i):
                    state = second(j, state)
            else:
                state = lax.fori_loop(0, i, second, state)
            total, acc = state
            acc = acc / total
            ot_ref[i, h] = acc
            o_ref[i, h] = acc.T.astype(BF16)
            ls_ref[i, h] = shift + jnp.log2(total)

        span(0, n, query_block, unrolled)


def attention(x):
    n, hp, _, rows, dim = x.shape
    pairs = n * (n + 1) // 2 * rows * rows * hp
    return pl.pallas_call(
        attention_kernel,
        name="attention",
        out_shape=(
            jax.ShapeDtypeStruct((n, hp, rows, dim), BF16),
            jax.ShapeDtypeStruct((n, hp, dim, rows), F32),
            jax.ShapeDtypeStruct((n, hp, 1, rows), F32),
        ),
        scratch_shapes=[
            pltpu.VMEM((n, dim, rows), BF16),
            pltpu.VMEM((n, rows, rows), F32),
        ],
        compiler_params=pltpu.CompilerParams(vmem_limit_bytes=40 << 20),
        cost_estimate=pl.CostEstimate(
            flops=pairs * dim * 8, bytes_accessed=x.size * 4, transcendentals=pairs
        ),
    )(x)


def attention_back_kernel(
    x_ref, g_ref, ot_ref, ls_ref, cos_ref, sin_ref, out_ref, kt_ref, dqt_ref, delta_ref
):
    n, hp, _, rows, _ = x_ref.shape
    unrolled = n <= 8
    factor = SCORE_SCALE * LOG2E
    for h in range(hp):
        for j in range(n):
            kt_ref[j] = x_ref[j, h, 1].astype(F32).T.astype(BF16)
            delta_ref[j] = jnp.sum(
                g_ref[j, h].astype(F32).T * ot_ref[j, h], axis=0, keepdims=True
            )

        def unrotated(value, i):
            turned = pl.ds(i * rows, rows)
            cos, sin = cos_ref[turned], sin_ref[turned]
            return rotate(value * SCORE_SCALE, cos, -sin).astype(BF16)

        def pair(i, j, diagonal):
            q, g = x_ref[i, h, 0], g_ref[i, h]
            p = jnp.exp2(dot_nt(x_ref[j, h, 1], q) * factor - ls_ref[i, h])
            if diagonal:
                p = causal_fill(p, 0.0)
            dv = dot(p.astype(BF16), g)
            ds = (p * (dot_nt(x_ref[j, h, 2], g) - delta_ref[i])).astype(BF16)
            dk = dot(ds, q)
            dqt = dot(kt_ref[j], ds)
            return dv, dk, dqt

        def key_block(j):
            dv, dk, dqt = pair(j, j, True)
            if unrolled:
                dqt_ref[j] = dqt if j == 0 else dqt_ref[j] + dqt
            else:
                dqt_ref[j] = jnp.where(j == 0, 0.0, dqt_ref[j]) + dqt

            def step(i, state):
                dv, dk = state
                v, k, t = pair(i, j, False)
                if unrolled:
                    dqt_ref[i] = t if j == 0 else dqt_ref[i] + t
                else:
                    dqt_ref[i] = jnp.where(j == 0, 0.0, dqt_ref[i]) + t
                return dv + v, dk + k

            state = (dv, dk)
            if unrolled:
                for i in range(j + 1, n):
                    state = step(i, state)
            else:
                state = lax.fori_loop(j + 1, n, step, state)
            dv, dk = state
            out_ref[j, h, 0] = unrotated(dqt_ref[j].T, j)
            out_ref[j, h, 1] = unrotated(dk, j)
            out_ref[j, h, 2] = dv.astype(BF16)

        span(0, n, key_block, unrolled)


def attention_back(x, g, ot, ls, cos, sin):
    n, hp, _, rows, dim = x.shape
    pairs = n * (n + 1) // 2 * rows * rows * hp
    return pl.pallas_call(
        attention_back_kernel,
        name="attention_back",
        out_shape=jax.ShapeDtypeStruct(x.shape, BF16),
        scratch_shapes=[
            pltpu.VMEM((n, dim, rows), BF16),
            pltpu.VMEM((n, dim, rows), F32),
            pltpu.VMEM((n, 1, rows), F32),
        ],
        compiler_params=pltpu.CompilerParams(vmem_limit_bytes=40 << 20),
        cost_estimate=pl.CostEstimate(
            flops=pairs * dim * 20, bytes_accessed=x.size * 6, transcendentals=pairs
        ),
    )(x, g, ot, ls, cos, sin)


def seq_device(index):
    return {"seq": index}


def greet(peers):
    barrier = pltpu.get_barrier_semaphore()
    for device in peers:
        pl.semaphore_signal(barrier, inc=1, device_id=device, device_id_type=MESH)


def greeted(count):
    pl.semaphore_wait(pltpu.get_barrier_semaphore(), count)


def remote(src, dst, send, recv, device):
    return pltpu.make_async_remote_copy(
        src_ref=src,
        dst_ref=dst,
        send_sem=send,
        recv_sem=recv,
        device_id=device,
        device_id_type=MESH,
    )


def front_kernel(
    state_ref,
    embedded_ref,
    wa_ref,
    wq_ref,
    gain_ref,
    table_ref,
    resid_out,
    normed_out,
    att_out,
    x_out,
    ot_out,
    ls_out,
    ltn_out,
    ltj_out,
    wa,
    wq,
    joined,
    resid,
    normed,
    sent,
    x,
    vt,
    scores,
    ot,
    o_sent,
    att,
    ltn,
    ltj,
    table,
    load_sem,
    store_sem,
    send_sem,
    recv_sem,
    o_send_sem,
    o_recv_sem,
    l_send_sem,
    l_recv_sem,
):
    n, rows, width = HEADS, state_ref.shape[0], state_ref.shape[1]
    me = lax.axis_index("seq")
    dp = lax.axis_index("dp")
    peers = [seq_device((me + k) % n) for k in range(1, n)]
    across = [{"dp": flipped(0, dp)}, {"dp": flipped(1, dp)}]
    near = seq_device(flipped(0, me))
    greet(peers + across)
    loads = [
        pltpu.make_async_copy(state_ref, joined.at[0], load_sem.at[0]),
        pltpu.make_async_copy(wa_ref.at[pl.ds(0, width)], wa.at[0], load_sem.at[1]),
        pltpu.make_async_copy(embedded_ref, joined.at[1], load_sem.at[2]),
        pltpu.make_async_copy(wa_ref.at[pl.ds(width, width)], wa.at[1], load_sem.at[3]),
        pltpu.make_async_copy(wq_ref, wq, load_sem.at[4]),
        pltpu.make_async_copy(
            table_ref.at[pl.ds(pl.multiple_of(me * rows, 8), rows)], table, load_sem.at[5]
        ),
    ]
    for copy in loads:
        copy.start()
    tile = 256
    for half in range(2):
        loads[2 * half].wait()
        loads[2 * half + 1].wait()

        for begin in range(0, width, tile):
            cols = pl.ds(begin, tile)
            block = dot(joined[half], wa[half, :, cols])
            resid[:, cols] = block if half == 0 else resid[:, cols] + block
    normed[...] = mean_norm(resid[...], gain_ref[0:1, :].astype(F32)).astype(BF16)
    stores = [
        pltpu.make_async_copy(resid, resid_out, store_sem.at[0]),
        pltpu.make_async_copy(normed, normed_out, store_sem.at[1]),
    ]
    for copy in stores:
        copy.start()
    loads[4].wait()
    lefts = []

    def share(source, out, slot, device):
        k = len(lefts)
        copy = remote(source, out.at[slot], l_send_sem.at[k], l_recv_sem.at[k], device)
        copy.start()
        lefts.append(copy)
    loads[5].wait()
    cos, sin = table[:, 0 : HEAD_DIM // 2], table[:, HEAD_DIM // 2 : HEAD_DIM]
    pairs = n // 2
    order = [2, 1, 3, 0] if pairs == 4 else list(range(pairs - 1, -1, -1))
    sends = []
    for k in order:
        chip = (me // 2 + k) % pairs
        for part in range(3):
            cols = pl.ds(pl.multiple_of(part * width + chip * 2 * HEAD_DIM, 2 * HEAD_DIM), 2 * HEAD_DIM)
            block = dot(normed[...], wq[:, cols])
            for core in range(2):
                head = block[:, core * HEAD_DIM : (core + 1) * HEAD_DIM]
                if part < 2:
                    head = rotate(head, cos, sin)
                sent[2 * chip + core, part] = head.astype(BF16)
        if k == order[0]:
            greeted(n + 1)
        for core in range(2):
            owner = 2 * chip + core
            if k == 0:
                continue
            copy = remote(sent.at[owner], x.at[me], send_sem.at[owner], recv_sem.at[me], seq_device(owner))
            copy.start()
            sends.append(copy)
    mate = me + 1 - 2 * (me % 2)
    copy = remote(sent.at[mate], x.at[me], send_sem.at[mate], recv_sem.at[me], seq_device(mate))
    copy.start()
    sends.append(copy)
    x[me] = sent[me]
    transposed_into(normed, ltn)
    for half in range(2):
        transposed_into(joined.at[half], ltj.at[pl.ds(half * width, width)])
    stores.append(pltpu.make_async_copy(ltn, ltn_out.at[0], store_sem.at[4]))
    stores.append(pltpu.make_async_copy(ltj, ltj_out.at[0], store_sem.at[5]))
    for copy in stores[2:]:
        copy.start()
    share(ltn, ltn_out, 2, across[0])
    share(ltn, ltn_out, 4, across[1])
    share(ltj, ltj_out, 2, across[1])
    share(ltn, ltn_out, 1, near)
    share(ltj, ltj_out, 1, near)
    factor = SCORE_SCALE * LOG2E
    for i in range(n):

        @pl.when(me != i)
        def arrive():
            remote(sent.at[0], x.at[i], send_sem.at[0], recv_sem.at[i], seq_device(i)).wait_recv()

        vt[i] = x[i, 2].astype(F32).T.astype(BF16)
        q = x[i, 0]
        diag = causal_fill(dot_nt(x[i, 1], q), NEG)
        peak = jnp.max(diag, axis=0, keepdims=True)
        for j in range(i):
            block = dot_nt(x[j, 1], q)
            scores[j] = block
            peak = jnp.maximum(peak, jnp.max(block, axis=0, keepdims=True))
        shift = peak * factor
        p = jnp.exp2(diag * factor - shift)
        total = jnp.sum(p, axis=0, keepdims=True)
        acc = dot(vt[i], p.astype(BF16))
        for j in range(i):
            p = jnp.exp2(scores[j] * factor - shift)
            total = total + jnp.sum(p, axis=0, keepdims=True)
            acc = acc + dot(vt[j], p.astype(BF16))
        acc = acc / total
        ot[i] = acc
        o_sent[i] = acc.T.astype(BF16)
        ls_out[i] = shift + jnp.log2(total)
        mine = pl.ds(pl.multiple_of(me * HEAD_DIM, HEAD_DIM), HEAD_DIM)

        @pl.when(me != i)
        def give():
            remote(o_sent.at[i], att.at[:, mine], o_send_sem.at[i], o_recv_sem.at[me], seq_device(i)).start()

        @pl.when(me == i)
        def keep():
            att[:, mine] = o_sent[i]

    stores.append(pltpu.make_async_copy(x, x_out, store_sem.at[2]))
    stores.append(pltpu.make_async_copy(ot, ot_out, store_sem.at[3]))
    for copy in stores[4:]:
        copy.start()
    for k, out, slot in ((0, ltn_out, 2), (1, ltn_out, 4), (2, ltj_out, 2)):
        lefts[k].wait_recv()
        share(out.at[slot], out, slot + 1, near)
    for copy in sends:
        copy.wait_send()
    for i in range(n):

        @pl.when(me != i)
        def finish():
            cols = pl.ds(i * HEAD_DIM, HEAD_DIM)
            copy = remote(o_sent.at[i], att.at[:, cols], o_send_sem.at[i], o_recv_sem.at[i], seq_device(i))
            copy.wait_send()
            copy.wait_recv()

    att_out[...] = att[...]
    for copy in stores:
        copy.wait()
    for k, copy in enumerate(lefts):
        copy.wait_send()
        if k > 2:
            copy.wait_recv()


def front(state, embedded, w_adapt, w_qkv, gains, table):
    n = HEADS
    rows, width = state.shape
    hbm = pl.BlockSpec(memory_space=pl.ANY)
    vmem = pl.BlockSpec(memory_space=pltpu.VMEM)
    return pl.pallas_call(
        front_kernel,
        name="front",
        out_shape=(
            jax.ShapeDtypeStruct((rows, width), F32),
            jax.ShapeDtypeStruct((rows, width), BF16),
            jax.ShapeDtypeStruct((rows, width), BF16),
            jax.ShapeDtypeStruct((n, 3, rows, HEAD_DIM), BF16),
            jax.ShapeDtypeStruct((n, HEAD_DIM, rows), F32),
            jax.ShapeDtypeStruct((n, 1, rows), F32),
            jax.ShapeDtypeStruct((6, width, rows), BF16),
            jax.ShapeDtypeStruct((4, 2 * width, rows), BF16),
        ),
        in_specs=[hbm, hbm, hbm, hbm, vmem, hbm],
        out_specs=(hbm, hbm, vmem, hbm, hbm, vmem, hbm, hbm),
        scratch_shapes=[
            pltpu.VMEM((2, width, width), BF16),
            pltpu.VMEM((width, 3 * width), BF16),
            pltpu.VMEM((2, rows, width), BF16),
            pltpu.VMEM((rows, width), F32),
            pltpu.VMEM((rows, width), BF16),
            pltpu.VMEM((n, 3, rows, HEAD_DIM), BF16),
            pltpu.VMEM((n, 3, rows, HEAD_DIM), BF16),
            pltpu.VMEM((n, HEAD_DIM, rows), BF16),
            pltpu.VMEM((n, rows, rows), F32),
            pltpu.VMEM((n, HEAD_DIM, rows), F32),
            pltpu.VMEM((n, rows, HEAD_DIM), BF16),
            pltpu.VMEM((rows, width), BF16),
            pltpu.VMEM((width, rows), BF16),
            pltpu.VMEM((2 * width, rows), BF16),
            pltpu.VMEM((rows, HEAD_DIM), F32),
            pltpu.SemaphoreType.DMA((6,)),
            pltpu.SemaphoreType.DMA((6,)),
            pltpu.SemaphoreType.DMA((n,)),
            pltpu.SemaphoreType.DMA((n,)),
            pltpu.SemaphoreType.DMA((n,)),
            pltpu.SemaphoreType.DMA((n,)),
            pltpu.SemaphoreType.DMA((8,)),
            pltpu.SemaphoreType.DMA((8,)),
        ],
        compiler_params=pltpu.CompilerParams(
            collective_id=1, has_side_effects=True, vmem_limit_bytes=62 << 20
        ),
    )(state, embedded, w_adapt, w_qkv, gains, table)


def flipped(bit, value):
    return value + (1 - 2 * ((value // (1 << bit)) % 2)) * (1 << bit)


def unit_slots(first, dp):
    slots = []
    for q in range(4):
        turned = [(dp + q) % 2, (dp // 2 + q // 2) % 2]
        slots.append(turned[first] * 2 + turned[1 - first])
    return slots


def transposed_into(source, target):
    tile = 256
    for begin in range(0, source.shape[1], tile):
        target[pl.ds(begin, tile), :] = source[:, pl.ds(begin, tile)].T


def add_into(target, more):
    rows = target.shape[0]
    chunk = 16
    while rows % (chunk * 2) == 0 and chunk < 64:
        chunk *= 2

    def step(t, c):
        at = pl.ds(pl.multiple_of(t * chunk, chunk), chunk)
        target[at, :] = (target[at, :].astype(F32) + more[at, :].astype(F32)).astype(BF16)
        return c

    lax.fori_loop(0, rows // chunk, step, 0)


CHUNKS = ((0, 512), (512, 512), (1024, 384))


def z_place(z):
    return (z % 2) * 2 + z // 2


def transposed_blocks(source, target, first, last):
    tile = 256
    parts, size = target.shape[1], target.shape[2]
    for begin in range(first * tile, min(last * tile, source.shape[1]), tile):
        block = source[:, pl.ds(begin, tile)].T
        for k in range(begin // size, (begin + tile - 1) // size + 1):
            low, high = max(begin, size * k), min(begin + tile, size * (k + 1))
            target[k // parts, k % parts, pl.ds(low - size * k, high - low), :] = block[
                low - begin : high - begin
            ]


def middle_kernel(*refs):
    refs = list(refs)

    def take(count):
        taken, refs[:count] = refs[:count], []
        return taken

    (att_in, resid_in, cot_in, gain_rows, wo_in, wg_in, wu_in, wd_in) = take(8)
    (x_in, ot_in, ls_ref, table_in) = take(4)
    (layer_out, above_out, gains_out, packed_out) = take(4)
    (kept_d, kept_z, kept_g, kept_h, kept_o) = take(5)
    (wo, wg, wu, wd, att, cot, resid, branch, mid, down, above) = take(11)
    (normed, hidden, gate_by, up_by, down_low, wide_low, branch_low, dout) = take(8)
    (left_n, left_h, left_m, left_a, right_g, right_d, right_b) = take(7)
    (got_g, got_d, got_z) = take(3)
    (work, x, ot, table, g, kt, dqt, delta, dsent, packed) = take(10)
    (load_sem, store_sem, g_send, g_recv, d_send, d_recv, m_send, m_recv, s_send, s_recv) = take(10)
    n, (rows, width) = HEADS, resid.shape
    ff = wg.shape[1]
    half, part = ff // 2, width // 2
    me = lax.axis_index("seq")
    dp = lax.axis_index("dp")
    core = me % 2
    mate = flipped(0, me)
    bits = [dp % 2, dp // 2]
    near = seq_device(mate)
    across = [{"dp": flipped(0, dp)}, {"dp": flipped(1, dp)}]
    diagonal = [{"seq": mate, "dp": flipped(0, dp)}, {"seq": mate, "dp": flipped(1, dp)}]
    greet([seq_device((me + k) % n) for k in range(1, n)] + across + diagonal)
    loads = {}
    for key, src, dst in (
        ("att", att_in, att),
        ("wo", wo_in, wo),
        ("resid", resid_in, resid),
        ("wg", wg_in, wg),
        ("wu", wu_in, wu),
        ("cot", cot_in, cot),
        ("wd", wd_in, wd),
        ("x", x_in, x),
        ("ot", ot_in, ot),
        ("table", table_in, table),
    ):
        copy = pltpu.make_async_copy(src, dst, load_sem.at[len(loads)])
        copy.start()
        loads[key] = copy
    tile = 256
    gains = [gain_rows[k : k + 1, :].astype(F32) for k in range(4)]

    def tiles(total, body):
        for begin in range(0, total, tile):
            body(pl.ds(begin, tile))

    sends = []
    given = {}

    issued = []

    def give(key, src, dst, device):
        k = len(issued)
        copy = remote(src, dst, m_send.at[k], m_recv.at[k], device)
        copy.start()
        issued.append(key)
        sends.append(copy)
        given[key] = copy

    loads["att"].wait()
    loads["wo"].wait()

    def project(cols):
        branch[:, cols] = dot(att[...], wo[:, cols])

    tiles(width, project)
    loads["resid"].wait()
    mid[...] = resid[...] + mean_norm(branch[...], gains[1])
    normed[...] = mean_norm(mid[...], gains[2]).astype(BF16)
    transposed_into(normed, left_n.at[0])
    greeted(n + 3)
    give("n1", left_n.at[0], left_n.at[1], near)
    give("n2", left_n.at[0], left_n.at[2], across[0])
    loads["wg"].wait()
    loads["wu"].wait()

    def widen(cols):
        gate = dot(normed[...], wg[:, cols])
        up = dot(normed[...], wu[:, cols])
        bent = jax.nn.sigmoid(gate)
        silu = gate * bent
        hidden[:, cols] = (silu * up).astype(BF16)
        gate_by[:, cols] = (up * bent * (1.0 + gate * (1.0 - bent))).astype(BF16)
        up_by[:, cols] = silu.astype(BF16)

    tiles(ff, widen)
    loads["wd"].wait()

    steps = width // tile
    share = -(-ff // tile // steps)
    for k in range(steps):
        cols = pl.ds(k * tile, tile)
        down[:, cols] = dot(hidden[...], wd[:, cols])
        transposed_blocks(hidden, left_h, k * share, (k + 1) * share)
    give("h2", left_h.at[:, 1 - bits[1]], left_m.at[1], across[1])
    give("h1", left_h.at[:, bits[1]], left_m.at[0], near)
    loads["cot"].wait()
    grad, _ = norm_back(down[...], gains[3], cot[...].astype(F32))
    down_low[...] = grad.astype(BF16)
    mine_d = pl.ds(pl.multiple_of(core * part, 128), part)
    theirs_d = pl.ds(pl.multiple_of((1 - core) * part, 128), part)
    give("d2", down_low.at[:, mine_d], right_d.at[1], across[1])
    give("d3", down_low.at[:, theirs_d], right_d.at[2], diagonal[1])
    give("d1", down_low.at[:, theirs_d], right_d.at[0], near)

    def widen_back(cols):
        block = dot_nt(down_low[...], wd[cols, :])
        wide_low[0, :, cols] = (block * gate_by[:, cols].astype(F32)).astype(BF16)
        wide_low[1, :, cols] = (block * up_by[:, cols].astype(F32)).astype(BF16)

    tiles(ff, widen_back)

    def chunk_of(c, which_core, which_bit):
        at, wide = CHUNKS[c]
        return wide_low.at[which_core, :, pl.ds(pl.multiple_of(which_bit * half + at, 128), wide)]

    def give_chunk(c):
        at, wide = CHUNKS[c]
        cols = pl.ds(at, wide)
        give(("g2", c), chunk_of(c, core, 1 - bits[0]), right_g.at[1, :, cols], across[0])
        give(("g3", c), chunk_of(c, 1 - core, 1 - bits[0]), right_g.at[2, :, cols], diagonal[0])
        give(("g1", c), chunk_of(c, 1 - core, bits[0]), right_g.at[0, :, cols], near)

    give_chunk(0)

    def narrow_back(cols):
        above[:, cols] = dot_nt(wide_low[0], wg[cols, :]) + dot_nt(wide_low[1], wu[cols, :])

    tiles(width, narrow_back)
    grad, _ = norm_back(mid[...], gains[2], above[...])
    resid[...] = cot[...].astype(F32) + grad
    grad, _ = norm_back(branch[...], gains[1], resid[...])
    branch_low[...] = grad.astype(BF16)

    def project_back(cols):
        dout[:, cols] = dot_nt(branch_low[...], wo[cols, :]).astype(BF16)

    tiles(width, project_back)
    my_cols = pl.ds(pl.multiple_of(me * HEAD_DIM, HEAD_DIM), HEAD_DIM)
    for k in (4, 5, 3, 2, 6, 7, 1):
        owner = (me + k) % n
        cols = pl.ds(pl.multiple_of(owner * HEAD_DIM, HEAD_DIM), HEAD_DIM)
        copy = remote(dout.at[:, cols], g.at[me], g_send.at[owner], g_recv.at[me], seq_device(owner))
        copy.start()
        sends.append(copy)
    g[me] = dout[:, my_cols]
    given["n2"].wait_recv()
    give("n3", left_n.at[2], left_n.at[3], near)
    transposed_into(att, left_a.at[0])
    give("a1", left_a.at[0], left_a.at[1], near)
    give("b1", branch_low.at[:, theirs_d], right_b, near)
    layer_out[...] = (mid[...] + mean_norm(down[...], gains[3])).astype(BF16)
    stores = []

    def store(src, dst):
        copy = pltpu.make_async_copy(src, dst, store_sem.at[len(stores)])
        copy.start()
        stores.append(copy)

    store(resid, above_out)
    gains_out[...] = jnp.zeros_like(gains_out)
    gains_out[1:2, :] = gain_sum(branch[...], resid[...])
    gains_out[2:3, :] = gain_sum(mid[...], above[...])
    gains_out[3:4, :] = gain_sum(down[...], cot[...].astype(F32))
    seconds = {}
    z_low = (me // 2) % 2

    def wide_sum(c):
        at, wide = CHUNKS[c]
        for key in ("n1", "n3"):
            if key in given:
                given.pop(key).wait_recv()
        for key in ("g1", "g2", "g3"):
            given[key, c].wait_recv()
        shard = width // 32
        spread = [(bits[1] + other) % 2 for other in range(2)]
        own = chunk_of(c, core, bits[0])
        for begin in range(0, wide, 256):
            step = min(256, wide - begin)
            cols = pl.ds(at + begin, step)
            block = dot(left_n[0], own[:, pl.ds(begin, step)])
            for k in range(1, 4):
                block += dot(left_n[k], right_g[k - 1, :, cols])
            work[0:width, 0:step] = block
            for z in range(4):
                for other in range(2):
                    pieces = [
                        work[pl.ds((8 * z + 4 * c2 + 2 * other + b) * shard, shard), 0:step]
                        for c2 in range(2)
                        for b in range(2)
                    ]
                    place = pl.multiple_of(spread[other] * part + z_place(z) * 4 * shard, 16)
                    wg[pl.ds(place, 4 * shard), cols] = jnp.concatenate(pieces, axis=0).astype(BF16)
        cols = pl.ds(at, wide)
        if c == len(CHUNKS) - 1:
            store(wg.at[:, cols], kept_h)
            return
        seconds[c] = remote(
            wg.at[pl.ds(part, part), cols], got_g.at[:, cols], s_send.at[c], s_recv.at[c], across[1]
        )
        seconds[c].start()
        sends.append(seconds[c])

    def down_sum():
        for key in ("h1", "h3", "d1", "d2", "d3"):
            given[key].wait_recv()
        tall = ff // 4
        shard = ff // 32
        spread = [(bits[0] + other) % 2 for other in range(2)]
        for begin in range(0, part, 256):
            cols = pl.ds(begin, 256)
            own = down_low.at[:, mine_d]
            block = dot(left_h[:, bits[1]].reshape(2 * tall, rows), own[:, cols])
            for k in range(3):
                block += dot(left_m[k].reshape(2 * tall, rows), right_d[k, :, cols])
            work[...] = block
            for z in range(4):
                for other in range(2):
                    pieces = [
                        work[pl.ds((4 * z + 2 * c2 + other) * shard, shard), :] for c2 in range(2)
                    ]
                    place = pl.multiple_of(spread[other] * tall + z_place(z) * 2 * shard, 16)
                    wd[pl.ds(place, 2 * shard), cols] = jnp.concatenate(pieces, axis=0).astype(BF16)
            k = begin // 256
            seconds["d", k] = remote(
                wd.at[pl.ds(tall, tall), cols],
                got_d.at[:, cols],
                s_send.at[2 + k],
                s_recv.at[2 + k],
                across[0],
            )
            seconds["d", k].start()
            sends.append(seconds["d", k])

    def out_sum():
        given["a1"].wait_recv()
        given["b1"].wait_recv()
        shard = width // 32
        slots = unit_slots(0, dp)
        for begin in range(0, part, 256):
            cols = pl.ds(begin, 256)
            block = dot(left_a[0], branch_low.at[:, mine_d][:, cols])
            work[0:width, :] = block + dot(left_a[1], right_b[:, cols])
            for z in range(4):
                for q in range(4):
                    pieces = [
                        work[pl.ds((8 * z + 4 * c2 + q) * shard, shard), :] for c2 in range(2)
                    ]
                    place = pl.multiple_of(slots[q] * (width // 4) + z_place(z) * 2 * shard, 16)
                    wu[pl.ds(place, 2 * shard), cols] = jnp.concatenate(pieces, axis=0).astype(BF16)
        store(wu.at[:, pl.ds(0, part)], kept_o)

    loads["x"].wait()
    factor = SCORE_SCALE * LOG2E
    half_dim = HEAD_DIM // 2
    pairs = [(i, j) for j in range(n) for i in range(j, n)]
    across_blocks = ff // rows

    def probs(i, j):
        k = pairs.index((i, j))
        at, cols = k // across_blocks * rows, k % across_blocks * rows
        return wu.at[pl.ds(at, rows), pl.ds(cols, rows)]

    give_chunk(1)
    for j in range(n):
        kt[j] = x[j, 1].astype(F32).T.astype(BF16)
        for i in range(j, n):
            p = jnp.exp2(dot_nt(x[j, 1], x[i, 0]) * factor - ls_ref[i])
            if i == j:
                p = causal_fill(p, 0.0)
            probs(i, j)[...] = p.astype(BF16)
    give_chunk(2)
    loads["ot"].wait()
    loads["table"].wait()
    arrived, summed = set(), set()

    def upstream(i):
        if i not in arrived:
            arrived.add(i)

            @pl.when(me != i)
            def arrive():
                remote(g.at[0], g.at[i], g_send.at[0], g_recv.at[i], seq_device(i)).wait_recv()

            delta[i] = jnp.sum(g[i].astype(F32).T * ot[i], axis=0, keepdims=True)
        return g[i]

    def give_head(j, first, count, sem):
        span = pl.ds(first, count)

        @pl.when(me != j)
        def over():
            remote(
                dsent.at[j, span], packed.at[span, :, my_cols], d_send.at[sem], d_recv.at[sem - j + me], seq_device(j)
            ).start()

        @pl.when(me == j)
        def keep():
            packed[span, :, my_cols] = dsent[j, span]

    def unrotated(value, j):
        here = pl.ds(j * rows, rows)
        cos, sin = table[here, 0:half_dim], -table[here, half_dim:HEAD_DIM]
        return rotate(value * SCORE_SCALE, cos, sin).astype(BF16)

    order = [n - 1, n - 2, 0]
    for k in range(1, n // 2 - 1):
        order += [n - 2 - k, k]
    order += [n // 2 - 1]
    for j in order:
        dk = dv = None
        for i in range(j, n):
            up = upstream(i)
            p = probs(i, j)[...]
            v = dot(p, up)
            ds = (p.astype(F32) * (dot_nt(x[j, 2], up) - delta[i])).astype(BF16)
            k = dot(ds, x[i, 0])
            t = dot(kt[j], ds)
            dqt[i] = dqt[i] + t if i in summed else t
            summed.add(i)
            dv, dk = (v, k) if i == j else (dv + v, dk + k)
        dsent[j, 1] = unrotated(dk, j)
        dsent[j, 2] = dv.astype(BF16)
        give_head(j, 1, 2, j)
        if j < n // 2:
            dsent[j, 0] = unrotated(dqt[j].T, j)
            give_head(j, 0, 1, n + j)
        if j == 0:
            wide_sum(0)
        if j == 2:
            given["h2"].wait_recv()
            give("h3", left_m.at[1], left_m.at[2], near)
    for j in range(n // 2, n):
        dsent[j, 0] = unrotated(dqt[j].T, j)
        give_head(j, 0, 1, n + j)

    down_sum()
    wide_sum(1)
    wide_sum(2)
    out_sum()

    def finish_wide(c):
        at, wide = CHUNKS[c]
        cols = pl.ds(at, wide)
        seconds[c].wait_recv()
        add_into(wg.at[pl.ds(0, part), cols], got_g.at[:, cols])
        if c > 0:
            store(wg.at[pl.ds(0, part), cols], kept_g)
            return
        third[0].start()
        sends.append(third[0])

    def z_rows(which):
        return wg.at[pl.ds(pl.multiple_of(which * (part // 2), 16), part // 2), pl.ds(0, CHUNKS[0][1])]

    def finish_z():
        third[0].wait_recv()
        add_into(z_rows(z_low), got_z)
        store(z_rows(z_low), kept_z)

    third = [
        remote(z_rows(1 - z_low), got_z, s_send.at[4], s_recv.at[4], seq_device(flipped(1, me)))
    ]
    finish_wide(0)
    finish_wide(1)
    for k in range(part // 256):
        cols = pl.ds(256 * k, 256)
        seconds["d", k].wait_recv()
        mine = wd.at[pl.ds(0, ff // 4), cols]
        add_into(mine, got_d.at[:, cols])
        store(mine, kept_d.at[:, cols])
    finish_z()
    for first, count in ((1, 2), (0, 1)):
        span = pl.ds(first, count)
        for j in range(n):

            @pl.when(me != j)
            def finish():
                cols = pl.ds(j * HEAD_DIM, HEAD_DIM)
                sem = j if first == 1 else n + j
                copy = remote(
                    dsent.at[j, span], packed.at[span, :, cols], d_send.at[sem], d_recv.at[sem], seq_device(j)
                )
                copy.wait_send()
                copy.wait_recv()

    store(packed, packed_out)
    for copy in sends:
        copy.wait_send()
    for copy in stores:
        copy.wait()


def middle_block(att, resid, cot, gain_rows, w_out, w_gate, w_up, w_down, x, ot, ls, table):
    n = HEADS
    rows, width = resid.shape
    ff = w_gate.shape[1]
    half, part = ff // 2, width // 2
    hbm = pl.BlockSpec(memory_space=pl.ANY)
    vmem = pl.BlockSpec(memory_space=pltpu.VMEM)
    dma = pltpu.SemaphoreType.DMA
    low = pltpu.VMEM((rows, width), BF16)
    wide = pltpu.VMEM((rows, ff), BF16)
    full = pltpu.VMEM((rows, width), F32)
    scratch = [pltpu.VMEM(w.shape, BF16) for w in (w_out, w_gate, w_up, w_down)]
    scratch += [low, low, full, full, full, full, full]
    scratch += [low, wide, wide, wide, low, pltpu.VMEM((2, rows, ff), BF16), low, low]
    scratch += [
        pltpu.VMEM((4, width, rows), BF16),
        pltpu.VMEM((8, 2, ff // 16, rows), BF16),
        pltpu.VMEM((3, 8, ff // 16, rows), BF16),
        pltpu.VMEM((2, width, rows), BF16),
        pltpu.VMEM((3, rows, half), BF16),
        pltpu.VMEM((3, rows, part), BF16),
        pltpu.VMEM((rows, part), BF16),
        pltpu.VMEM((part, CHUNKS[-1][0]), BF16),
        pltpu.VMEM((ff // 4, part), BF16),
        pltpu.VMEM((part // 2, CHUNKS[0][1]), BF16),
        pltpu.VMEM((half, 256), F32),
        pltpu.VMEM(x.shape, BF16),
        pltpu.VMEM(ot.shape, F32),
        pltpu.VMEM(table.shape, F32),
        pltpu.VMEM((n, rows, HEAD_DIM), BF16),
        pltpu.VMEM((n, HEAD_DIM, rows), BF16),
        pltpu.VMEM((n, HEAD_DIM, rows), F32),
        pltpu.VMEM((n, 1, rows), F32),
        pltpu.VMEM((n, 3, rows, HEAD_DIM), BF16),
        pltpu.VMEM((3, rows, width), BF16),
        dma((10,)),
        dma((8,)),
        dma((n,)),
        dma((n,)),
        dma((2 * n,)),
        dma((2 * n,)),
        dma((20,)),
        dma((20,)),
        dma((5,)),
        dma((5,)),
    ]
    return pl.pallas_call(
        middle_kernel,
        name="middle",
        out_shape=[
            jax.ShapeDtypeStruct((rows, width), BF16),
            jax.ShapeDtypeStruct((rows, width), F32),
            jax.ShapeDtypeStruct((8, width), F32),
            jax.ShapeDtypeStruct((3, rows, width), BF16),
            jax.ShapeDtypeStruct((ff // 4, part), BF16),
            jax.ShapeDtypeStruct((part // 2, CHUNKS[0][1]), BF16),
            jax.ShapeDtypeStruct((part, CHUNKS[1][1]), BF16),
            jax.ShapeDtypeStruct((width, CHUNKS[-1][1]), BF16),
            jax.ShapeDtypeStruct((width, part), BF16),
        ],
        in_specs=[hbm] * 3 + [vmem] + [hbm] * 6 + [vmem] + [hbm],
        out_specs=[vmem, hbm, vmem, hbm] + [hbm] * 5,
        scratch_shapes=scratch,
        compiler_params=pltpu.CompilerParams(
            collective_id=2, has_side_effects=True, vmem_limit_bytes=62 << 20
        ),
    )(att, resid, cot, gain_rows, w_out, w_gate, w_up, w_down, x, ot, ls, table)


BEGUN = ((1, 0, 512, None), (2, 0, 512, None), (0, 0, 256, None), (0, 256, 256, None), (3, 0, 384, 1))
FRESH = ((1, 0, 0), (1, 1024, 0), (1, 2048, 1), (0, 0, 1))
SCHEDULE = (
    ("S", 4), ("2", 0), ("F", 5), ("1", 3), ("P", 0), ("1", 1), ("D", 3), ("2", 3),
    ("E", 0), ("U", 9), ("O", 0), ("U", 7), ("C", 4), ("G", 0), ("E", 3), ("B", 5),
    ("1", 2), ("S", 5), ("D", 1), ("2", 1), ("W", 9), ("S", 9), ("1", 4), ("W", 7),
    ("S", 7), ("D", 2), ("G", 1), ("2", 2), ("C", 5), ("E", 1), ("1", 5), ("D", 4),
    ("G", 2), ("2", 4), ("U", 8), ("E", 2), ("C", 7), ("1", 7), ("D", 5), ("G", 3),
    ("U", 6), ("2", 5), ("C", 9), ("1", 9), ("E", 4), ("D", 7), ("G", 4), ("2", 7),
    ("W", 8), ("E", 5), ("S", 8), ("W", 6), ("S", 6), ("E", 7), ("D", 9), ("2", 9),
    ("C", 8), ("1", 8), ("C", 6), ("1", 6), ("E", 9), ("D", 8), ("2", 8), ("D", 6),
    ("2", 6), ("E", 8), ("E", 6),
)


def dealt_blocks(left, slots, right, spread, bit, out, work):
    total = left.shape[1]
    shard = total // 32
    block = dot(left[slots[0]], right[0])
    for k in range(1, 4):
        block += dot(left[slots[k]], right[k])
    work[0:total, :] = block
    for z in range(4):
        for other in range(2):
            pieces = []
            for core in range(2):
                for b in range(2):
                    q = (b << bit) | (other << (1 - bit))
                    pieces.append(work[pl.ds((8 * z + 4 * core + q) * shard, shard), :])
            out[spread[other], pl.ds(z_place(z) * 4 * shard, 4 * shard), :] = jnp.concatenate(
                pieces, axis=0
            ).astype(BF16)


def tail_kernel(*refs):
    refs = list(refs)

    def take(count):
        taken, refs[:count] = refs[:count], []
        return taken

    begun, fresh = len(BEGUN), len(FRESH)
    single = begun
    first_fresh = begun + 1
    count = first_fresh + fresh
    kept_in = take(5)
    packed_in, ltn_in, ltj_in, wq_in, wa_in = take(5)
    resid_in, above_in, gain_rows, gain_parts = take(4)
    grad_joined = take(2)
    outs = take(5)
    (gains_out,) = take(1)
    held = take(3)
    sums, arrived2 = [None] * 4 + take(count - 4), [None] * 4 + take(count - 4)
    parts, arrived3, arrived4, finals = take(count), take(count), take(count), take(count)
    (got_o, wq, wa, packed, ltn, ltj, dealt, low, work, back_sum, gain_buf, gain_got) = take(12)
    (resid, above, joined_0, joined_1) = take(4)
    joined = (joined_0, joined_1)
    (load_sem, u_send, u_recv, s_send, s_recv, z1_send, z1_recv) = take(7)
    (z2_send, z2_recv, c_send, c_recv, gain_send, gain_recv, store_sem) = take(7)
    rows, width = resid.shape
    me = lax.axis_index("seq")
    dp = lax.axis_index("dp")
    core = me % 2
    bits = [dp % 2, dp // 2]
    z_low, z_high = (me // 2) % 2, me // 4
    mate = flipped(0, me)
    near = seq_device(mate)
    across = [{"dp": flipped(0, dp)}, {"dp": flipped(1, dp)}]
    diagonal = [{"seq": mate, "dp": flipped(0, dp)}, {"seq": mate, "dp": flipped(1, dp)}]
    beside = [seq_device(flipped(1, me)), seq_device(flipped(2, me))]
    greet([near] + across + diagonal + beside)
    loads = {}

    def load(key, src, dst):
        loads[key] = pltpu.make_async_copy(src, dst, load_sem.at[len(loads)])
        loads[key].start()

    load("packed", packed_in, packed)
    load("wq", wq_in, wq)
    load("resid", resid_in, resid)
    load("above", above_in, above)
    greeted(7)
    sends = []

    def send(src, dst, send_sem, recv_sem, device):
        copy = remote(src, dst, send_sem, recv_sem, device)
        copy.start()
        sends.append(copy)
        return copy

    first, dealing, second, third, fourth, finished, taken = [], {}, {}, {}, {}, {}, set()

    def ready(key):
        if key not in taken:
            taken.add(key)
            loads[key].wait()

    def z_rows(u, which):
        tall = finals[u].shape[0]
        return pl.ds(pl.multiple_of(which * 2 * tall, 16), 2 * tall)

    def one_z(u, which):
        tall = finals[u].shape[0]
        return pl.ds(pl.multiple_of(which * tall, 16), tall)

    def start_first(u):
        first.append(send(kept_in[4].at[pl.ds(2, 2)], got_o, s_send.at[count], s_recv.at[count], across[0]))

    def take_first(u):
        first[0].wait_recv()
        ready(single)
        for k in (1, 0):
            add_into(sums[single].at[k], got_o.at[k])

    def start_columns(u):
        k = u - first_fresh
        bit = FRESH[k][2]
        source = low if k == 3 else packed.at[k]
        if k < 3:
            ready("packed")

        def columns(other_core, other_bit):
            place = (core + (1 - 2 * core) * other_core) * 2
            place = place + bits[bit] + (1 - 2 * bits[bit]) * other_bit
            return pl.ds(pl.multiple_of(place * 256, 256), 256)

        dealing[u] = [
            send(
                source.at[:, columns(*there)],
                dealt.at[k, slot],
                u_send.at[3 * k + slot - 1],
                u_recv.at[3 * k + slot - 1],
                device,
            )
            for there, slot, device in (
                ((0, 1), 2, across[bit]),
                ((1, 1), 3, diagonal[bit]),
                ((1, 0), 1, near),
            )
        ]
        dealt[k, 0] = source[:, columns(0, 0)]

    def start_second(u):
        if u < begun:
            array, at, wide, bit = BEGUN[u]
            rows_in = kept_in[array].shape[0] // 2
            src = kept_in[array].at[pl.ds(rows_in, rows_in), pl.ds(at, wide)]
        else:
            bit = 1 if u == single else 1 - FRESH[u - first_fresh][2]
            src = sums[u].at[1]
        second[u] = send(src, arrived2[u], s_send.at[u], s_recv.at[u], across[bit])

    def multiply(u):
        k = u - first_fresh
        out, column, bit = FRESH[k]
        slots = (0, 1, 2, 3) if (bit == 0 or k == 3) else (0, 1, 4, 5)
        left = ltj if k == 3 else ltn
        ready("ltj" if k == 3 else "ltn")
        for copy in dealing[u]:
            copy.wait_recv()
        spread = [(bits[1 - bit] + other) % 2 for other in range(2)]
        dealt_blocks(left, slots, dealt.at[k], spread, bit, sums[u], work)

    def take_second(u):
        second[u].wait_recv()
        if u < begun:
            ready(u)
        add_into(sums[u].at[0], arrived2[u])

    def start_third(u):
        theirs = z_rows(u, 1 - z_low)
        if u < 4:
            array, at, wide, _ = BEGUN[u]
            src = kept_in[array].at[theirs, pl.ds(at, wide)]
        else:
            src = sums[u].at[0, theirs]
        third[u] = send(src, arrived3[u], z1_send.at[u], z1_recv.at[u], beside[0])

    def take_third(u):
        third[u].wait_recv()
        if u < 4:
            array, at, wide, _ = BEGUN[u]
            ready(array)
            mine = held[array][:, pl.ds(at, wide)]
        else:
            mine = sums[u][0, z_rows(u, z_low), :]
        parts[u][...] = (mine.astype(F32) + arrived3[u][...].astype(F32)).astype(BF16)

    def start_fourth(u):
        source = kept_in[1] if u == 0 else parts[u]
        fourth[u] = send(
            source.at[one_z(u, 1 - z_high)], arrived4[u], z2_send.at[u], z2_recv.at[u], beside[1]
        )

    def take_fourth(u):
        fourth[u].wait_recv()
        if u == 0:
            ready(1)
        source = held[1] if u == 0 else parts[u]
        finals[u][...] = source[one_z(u, z_high), :].astype(F32) + arrived4[u][...].astype(F32)
        if u in (0, 1, 4):
            at, wide = CHUNKS[min(u, 2)]
            bit = 0
            cols = pl.ds(pl.multiple_of(bits[0] * (outs[3].shape[2] // 2) + at, 128), wide)
            target = outs[3].at[core, :, cols]
        elif u <= single:
            out, at, wide = (2, 0, width // 2) if u == single else (4,) + BEGUN[u][1:3]
            bit = None
            target = outs[out].at[:, pl.ds(pl.multiple_of(core * (width // 2) + at, 128), wide)]
        else:
            out, column, bit = FRESH[u - first_fresh]
            cols = pl.ds(pl.multiple_of((core * 2 + bits[bit]) * 256 + column, 256), 256)
            target = outs[out].at[:, cols]
        if bit is None:
            owners = [(core, None), (1 - core, near)]
        else:
            here, there = bits[bit], 1 - bits[bit]
            owners = [
                (core * 2 + here, None),
                ((1 - core) * 2 + here, near),
                (core * 2 + there, across[bit]),
                ((1 - core) * 2 + there, diagonal[bit]),
            ]
        shard = finals[u].shape[0] // len(owners)
        finished[u] = []
        for k, (place, device) in enumerate(owners):
            at = pl.ds(pl.multiple_of(place * shard, 8), shard)
            if k == 0:
                target[...] = finals[u][at, :]
            else:
                sem = 3 * u + k - 1
                finished[u].append(
                    send(finals[u].at[at], target, c_send.at[sem], c_recv.at[sem], device)
                )

    gain_steps = {}
    gain_partners = [near] + across + beside

    def send_gain(k):
        gain_steps[k] = send(
            gain_buf.at[k], gain_got.at[k], gain_send.at[k], gain_recv.at[k], gain_partners[k]
        )

    def add_gain(k):
        gain_steps[k].wait_recv()
        total = gain_buf[k] + gain_got[k]
        if k == 4:
            gains_out[...] = total
        else:
            gain_buf[k + 1] = total
            send_gain(k + 1)

    tile = 256
    stores = []

    def dense_back(_):
        ready("packed")
        ready("wq")
        load(1, kept_in[1], held[1])
        load(2, kept_in[2].at[z_rows(1, z_low)], held[2])
        load(0, kept_in[0].at[z_rows(2, z_low)], held[0])
        load(single, kept_in[4].at[pl.ds(0, 2)], sums[single])
        load(4, kept_in[3].at[pl.ds(0, kept_in[3].shape[0] // 2)], sums[4].at[0])
        load("ltn", ltn_in, ltn)
        load("ltj", ltj_in, ltj)
        load("wa", wa_in, wa)
        for begin in range(0, width, tile):
            at = pl.ds(begin, tile)
            block = dot_nt(packed[0], wq[at, pl.ds(0, width)])
            block += dot_nt(packed[1], wq[at, pl.ds(width, width)])
            block += dot_nt(packed[2], wq[at, pl.ds(2 * width, width)])
            back_sum[:, at] = block
        ready("resid")
        ready("above")
        part, gain0 = norm_back(resid[...], gain_rows[0:1, :].astype(F32), back_sum[...])
        low[...] = (above[...] + part).astype(BF16)
        gain_buf[0] = gain_parts[...]
        gain_buf[0, 0:1, :] = gain0[None, :]
        send_gain(0)

    def dense_out(_):
        ready("wa")
        for k in range(2):
            for begin in range(0, width, tile):
                from_row = pl.ds(k * width + begin, tile)
                joined[k][:, pl.ds(begin, tile)] = dot_nt(low[...], wa[from_row, :])
            stores.append(pltpu.make_async_copy(joined[k], grad_joined[k], store_sem.at[k]))
            stores[k].start()

    actions = {
        "F": start_first,
        "B": take_first,
        "U": start_columns,
        "S": start_second,
        "1": start_third,
        "2": start_fourth,
        "W": multiply,
        "C": take_second,
        "D": take_third,
        "E": take_fourth,
        "G": add_gain,
        "P": dense_back,
        "O": dense_out,
    }
    for action, u in SCHEDULE:
        actions[action](u)
    for u in range(count):
        for copy in finished[u]:
            copy.wait_recv()
    for copy in sends:
        copy.wait_send()
    for copy in stores:
        copy.wait()


def tail(kept, packed, left_n, left_j, w_qkv, w_adapt, resid, above, gain_rows, gain_parts):
    rows, width = resid.shape
    hbm = pl.BlockSpec(memory_space=pl.ANY)
    vmem = pl.BlockSpec(memory_space=pltpu.VMEM)
    dma = pltpu.SemaphoreType.DMA
    fresh = len(FRESH)
    down, gate, gate_next, last, out = kept
    left_over = (4, 2, 4, 8)
    every = [(kept[array].shape[0] // left_over[array], wide) for array, _, wide, _ in BEGUN]
    every += [(out.shape[1] // 4, out.shape[2])]
    every += [(width // 8, 256)] * 3 + [(width // 4, 256)]
    count = len(every)
    slots = [1] + [2] * (1 + fresh)
    shapes = [
        (2 * width // 32, width),
        (width // 32, 3 * width),
        (width // 32, width),
        (2, width // 32, 2 * (gate.shape[1] + gate_next.shape[1] + last.shape[1])),
        (down.shape[0] // 8, width),
    ]
    scratch = [
        pltpu.VMEM(shape, BF16)
        for shape in (
            (down.shape[0] // 2, down.shape[1]),
            gate.shape,
            (gate_next.shape[0] // 2, gate_next.shape[1]),
        )
    ]
    scratch += [pltpu.VMEM((k, 4 * tall, wide), BF16) for k, (tall, wide) in zip(slots, every[4:])]
    scratch += [pltpu.VMEM((4 * tall, wide), BF16) for tall, wide in every[4:]]
    scratch += [pltpu.VMEM((2 * tall, wide), BF16) for tall, wide in every]
    scratch += [pltpu.VMEM((2 * tall, wide), BF16) for tall, wide in every]
    scratch += [pltpu.VMEM((tall, wide), BF16) for tall, wide in every]
    scratch += [pltpu.VMEM((tall, wide), F32) for tall, wide in every]
    scratch += [
        pltpu.VMEM((2,) + out.shape[1:], BF16),
        pltpu.VMEM(w_qkv.shape, BF16),
        pltpu.VMEM(w_adapt.shape, BF16),
        pltpu.VMEM(packed.shape, BF16),
        pltpu.VMEM(left_n.shape, BF16),
        pltpu.VMEM(left_j.shape, BF16),
        pltpu.VMEM((4, 4, rows, 256), BF16),
        pltpu.VMEM((rows, width), BF16),
        pltpu.VMEM((2 * width, 256), F32),
        pltpu.VMEM((rows, width), F32),
        pltpu.VMEM((5, 8, width), F32),
        pltpu.VMEM((5, 8, width), F32),
    ]
    scratch += [pltpu.VMEM((rows, width), F32) for _ in range(4)]
    scratch += [dma((14,)), dma((3 * fresh,)), dma((3 * fresh,))]
    scratch += [dma((count + 1,)) for _ in range(2)]
    scratch += [dma((count,)) for _ in range(4)]
    scratch += [dma((3 * count,)) for _ in range(2)]
    scratch += [dma((5,)) for _ in range(2)] + [dma((2,))]
    return pl.pallas_call(
        tail_kernel,
        name="tail",
        out_shape=[jax.ShapeDtypeStruct((rows, width), F32)] * 2
        + [jax.ShapeDtypeStruct(shape, F32) for shape in shapes]
        + [jax.ShapeDtypeStruct((8, width), F32)],
        in_specs=[hbm] * 12 + [vmem] * 2,
        out_specs=[hbm] * 2 + [vmem] * 6,
        scratch_shapes=scratch,
        compiler_params=pltpu.CompilerParams(
            collective_id=3, has_side_effects=True, vmem_limit_bytes=62 << 20
        ),
    )(*kept, packed, left_n, left_j, w_qkv, w_adapt, resid, above, gain_rows, gain_parts)


def finish_kernel(*refs):
    sources, gain_ref, targets, gain_out, sem = refs[:8], refs[8], refs[9:18], refs[18], refs[19]
    wide = sources[6]
    pairs = list(zip(sources[:6], targets[:6]))
    pairs += [(wide.at[0], targets[6]), (wide.at[1], targets[7]), (sources[7], targets[8])]
    copies = [
        pltpu.make_async_copy(src, dst, sem.at[k]) for k, (src, dst) in enumerate(pairs)
    ]
    for copy in copies:
        copy.start()
    share = gain_out.shape[1]
    at = (lax.axis_index("seq") * lax.axis_size("dp") + lax.axis_index("dp")) * share
    block = gain_ref[:, pl.ds(pl.multiple_of(at // 128 * 128, 128), 128)]
    here = lax.broadcasted_iota(jnp.int32, (128, share), 0) - at % 128
    picked = here == lax.broadcasted_iota(jnp.int32, (128, share), 1)
    gain_out[...] = lax.dot_general(
        block,
        picked.astype(F32),
        (((1,), (0,)), ((), ())),
        precision=lax.Precision.HIGHEST,
        preferred_element_type=F32,
    )[:4]
    for copy in copies:
        copy.wait()


def finish(*values):
    hbm = pl.BlockSpec(memory_space=pl.ANY)
    vmem = pl.BlockSpec(memory_space=pltpu.VMEM)
    wide, gains = values[6], values[8]
    share = gains.shape[1] // (lax.axis_size("seq") * lax.axis_size("dp"))
    like = list(values[:6]) + [wide[0], wide[1], values[7]]
    return pl.pallas_call(
        finish_kernel,
        name="finish",
        out_shape=[jax.ShapeDtypeStruct(value.shape, value.dtype) for value in like]
        + [jax.ShapeDtypeStruct((4, share), F32)],
        in_specs=[vmem] * 9,
        out_specs=[hbm] * 9 + [vmem],
        scratch_shapes=[pltpu.SemaphoreType.DMA((9,))],
        compiler_params=pltpu.CompilerParams(vmem_limit_bytes=62 << 20),
    )(*values)


def xor_permute(value, axis, mask):
    return lax.ppermute(value, axis, [(i, i ^ mask) for i in range(lax.axis_size(axis))])


def quadrants(left):
    n, parts = lax.axis_size("seq"), lax.axis_size("dp")
    tokens, rows = left.shape
    shard = rows // (n * parts)
    split = left.reshape(tokens, n, parts, shard).transpose(2, 0, 1, 3)
    split = split.reshape(parts, tokens, n * shard)
    me = lax.axis_index("dp")
    return jnp.concatenate(
        [lax.dynamic_index_in_dim(split, me ^ m, 0, keepdims=True) for m in range(parts)]
    )


def other_core(left, right):
    core = lax.axis_index("seq") % 2
    half = right.shape[1] // 2
    mine = lax.dynamic_slice_in_dim(right, core * half, half, 1)
    theirs = lax.dynamic_slice_in_dim(right, (1 - core) * half, half, 1)
    left_in = xor_permute(left, "seq", 1)
    right_in = xor_permute(theirs, "seq", 1)
    return jnp.concatenate([left, left_in], axis=1), jnp.concatenate([mine, right_in], axis=0)


def scattered_sum(left, right, bits):
    n, parts = lax.axis_size("seq"), lax.axis_size("dp")
    cols = right.shape[1]
    left, right = other_core(quadrants(left), right)
    got = {}
    masks = list(range(parts))
    for bit in bits:
        outgoing = [m for m in masks if m >> bit & 1]
        masks = [m for m in masks if not m >> bit & 1]
        blocks = []
        for m in outgoing:
            block = dot_tn(left[m], right)
            for more in got.get(m, ()):
                block = block + more.astype(F32)
            blocks.append(block.astype(BF16))
        incoming = xor_permute(jnp.stack(blocks), "dp", 1 << bit)
        for k, m in enumerate(outgoing):
            got.setdefault(m ^ (1 << bit), []).append(incoming[k])
    block = dot_tn(left[0], right)
    for more in got.get(0, ()):
        block = block + more.astype(F32)
    shard = block.shape[0] // n
    block = block.astype(BF16).reshape(n, shard, cols // 2)
    block = lax.all_to_all(block, "seq", 0, 0)
    block = jnp.sum(block.reshape(n // 2, 2, shard, cols // 2).astype(F32), axis=0)
    return block.transpose(1, 0, 2).reshape(shard, cols)


def small_sum(value):
    value = value.reshape(value.shape[0], -1, value.shape[1])
    for axis in ("seq", "dp"):
        size = lax.axis_size(axis)
        me = lax.axis_index(axis)
        for bit in reversed(range(size.bit_length() - 1)):
            half = value.shape[2] // 2
            mine = (me >> bit) & 1
            kept = lax.dynamic_slice_in_dim(value, mine * half, half, 2)
            sent = lax.dynamic_slice_in_dim(value, (1 - mine) * half, half, 2)
            value = kept + xor_permute(sent, axis, 1 << bit)
    return value[:, 0]


def local(state, embedded, cotangent, w_adapt, w_qkv, w_out, w_gate, w_up, w_down, gains):
    seq_count, rows, width = state.shape
    n, parts = lax.axis_size("seq"), lax.axis_size("dp")
    tokens = seq_count * rows
    me = lax.axis_index("seq")
    bits = list(range(parts.bit_length() - 1))
    copies = max(1, n // HEADS)
    held = max(1, HEADS // n)
    owners = n // copies
    cos_np, sin_np = angle_tables(n * rows)
    cos_all, sin_all = jnp.asarray(cos_np), jnp.asarray(sin_np)
    cos = lax.dynamic_slice_in_dim(cos_all, me * rows, rows, 0)[:, None, :]
    sin = lax.dynamic_slice_in_dim(sin_all, me * rows, rows, 0)[:, None, :]
    gain_rows = gains.astype(F32)
    state, embedded = state.reshape(tokens, width), embedded.reshape(tokens, width)

    def to_heads(flat):
        return flat.reshape(tokens, HEADS, HEAD_DIM)

    def to_owner(parts_in):
        sent = jnp.stack(parts_in).reshape(len(parts_in), tokens, owners, held, HEAD_DIM)
        sent = sent.transpose(2, 3, 0, 1, 4)
        if copies > 1:
            sent = jnp.repeat(sent, copies, axis=0)
        return lax.all_to_all(sent, "seq", 0, 0)

    def from_owner(value):
        back = lax.all_to_all(value, "seq", 0, 0)[::copies]
        back = back.reshape(HEADS, -1, tokens, HEAD_DIM)
        return back.transpose(2, 1, 0, 3).reshape(tokens, -1)

    table = jnp.asarray(np.concatenate([cos_np, sin_np], axis=1))
    if n == HEADS and seq_count == 1 and parts == 4:
        resid, normed, attended, qkv, attended_t, logsum, left_n, left_j = front(
            state, embedded, w_adapt, w_qkv, gains, table
        )
        qkv, attended_t, logsum = qkv[:, None], attended_t[:, None], logsum[:, None]
    else:
        resid = dot(state, w_adapt[:width]) + dot(embedded, w_adapt[width:])
        normed = mean_norm(resid, gain_rows[0]).astype(BF16)
        packed = dot(normed, w_qkv)
        queries = rotate(to_heads(packed[:, :width]), cos, sin).astype(BF16)
        keys = rotate(to_heads(packed[:, width : 2 * width]), cos, sin).astype(BF16)
        values = to_heads(packed[:, 2 * width :]).astype(BF16)
        qkv = to_owner((queries, keys, values))
        attended, attended_t, logsum = attention(qkv)
        attended = from_owner(attended[:, :, None])
    shape = (seq_count, rows, width)
    if n == HEADS and parts == 4 and seq_count == 1:
        layer_out, middle_grad, gain_parts, packed_low, *kept = middle_block(
            attended,
            resid,
            cotangent.reshape(tokens, width),
            gains,
            w_out,
            w_gate,
            w_up,
            w_down,
            qkv[:, 0],
            attended_t[:, 0],
            logsum[:, 0],
            table,
        )
        grad_state, grad_embedded, grad_adapt, grad_qkv, grad_out, grad_wide, grad_down, gains_sum = tail(
            kept[:4] + [kept[4].reshape(4, width // 4, width // 2)],
            packed_low,
            left_n,
            left_j,
            w_qkv,
            w_adapt,
            resid,
            middle_grad,
            gains,
            gain_parts,
        )
        outs = finish(
            layer_out,
            grad_state,
            grad_embedded,
            grad_adapt,
            grad_qkv,
            grad_out,
            grad_wide,
            grad_down,
            gains_sum,
        )
        return tuple(value.reshape(shape) for value in outs[:3]) + tuple(outs[3:])
    branch = dot(attended, w_out)
    middle = resid + mean_norm(branch, gain_rows[1])
    normed_mid = mean_norm(middle, gain_rows[2]).astype(BF16)
    gate_pre = dot(normed_mid, w_gate)
    up_pre = dot(normed_mid, w_up)
    sigmoid_gate = jax.nn.sigmoid(gate_pre)
    silu_gate = gate_pre * sigmoid_gate
    hidden = (silu_gate * up_pre).astype(BF16)
    down_out = dot(hidden, w_down)
    layer_out = middle + mean_norm(down_out, gain_rows[3])
    out_grad = cotangent.astype(F32).reshape(tokens, width)
    down_grad, gain_grad3 = norm_back(down_out, gain_rows[3], out_grad)
    down_low = down_grad.astype(BF16)
    hidden_grad = dot_nt(down_low, w_down)
    gate_low = (
        hidden_grad * up_pre * sigmoid_gate * (1.0 + gate_pre * (1.0 - sigmoid_gate))
    ).astype(BF16)
    up_low = (hidden_grad * silu_gate).astype(BF16)
    mid_norm_grad = dot_nt(gate_low, w_gate) + dot_nt(up_low, w_up)
    middle_part, gain_grad2 = norm_back(middle, gain_rows[2], mid_norm_grad)
    middle_grad = out_grad + middle_part
    branch_grad, gain_grad1 = norm_back(branch, gain_rows[1], middle_grad)
    branch_low = branch_grad.astype(BF16)
    attended_grad = dot_nt(branch_low, w_out).astype(BF16)
    upstream = to_owner((to_heads(attended_grad),))[:, :, 0]
    packed_grad = attention_back(qkv, upstream, attended_t, logsum, cos_all, sin_all)
    packed_low = from_owner(packed_grad)
    normed_grad = dot_nt(packed_low, w_qkv)
    resid_part, gain_grad0 = norm_back(resid, gain_rows[0], normed_grad)
    resid_low = (middle_grad + resid_part).astype(BF16)
    grad_state = dot_nt(resid_low, w_adapt[:width])
    grad_embedded = dot_nt(resid_low, w_adapt[width:])
    flipped = bits[::-1]
    joined = jnp.concatenate([state, embedded], axis=-1)
    grad_down = scattered_sum(hidden, down_low, bits)
    grad_gate = scattered_sum(normed_mid, gate_low, flipped)
    grad_up = scattered_sum(normed_mid, up_low, bits)
    grad_out = scattered_sum(attended, branch_low, flipped)
    grad_qkv = scattered_sum(normed, packed_low, flipped)
    grad_adapt = scattered_sum(joined, resid_low, bits)
    grad_gains = jnp.stack([gain_grad0, gain_grad1, gain_grad2, gain_grad3])
    grad_gains = small_sum(grad_gains)
    return (
        layer_out.reshape(shape).astype(BF16),
        grad_state.reshape(shape),
        grad_embedded.reshape(shape),
        grad_adapt,
        grad_qkv,
        grad_out,
        grad_gate,
        grad_up,
        grad_down,
        grad_gains,
    )


def solution(mesh):
    tokens = P("dp", "seq", None)
    rows = P(("seq", "dp"), None)
    return jax.shard_map(
        local,
        mesh=mesh,
        in_specs=(tokens,) * 3 + (P(),) * 7,
        out_specs=(tokens,) * 3 + (rows,) * 6 + (P(None, ("seq", "dp")),),
        check_vma=False,
    )
```

```python
import functools
import math

import jax
import jax.numpy as jnp
import numpy as np
from jax import lax
from jax.experimental import pallas as pl
from jax.experimental.pallas import tpu as pltpu
from jax.sharding import PartitionSpec as P

HEADS = 8
HEAD_DIM = 128
norm_eps = 1e-06
rope_base = 50000.0
F32 = jnp.float32
BF16 = jnp.bfloat16
MESH = pl.DeviceIdType.MESH
NEG = -1e30
SCORE_SCALE = 1.0 / math.sqrt(HEAD_DIM)
LOG2E = 1.0 / math.log(2.0)


def mean_norm(values_in, gain_row):
    return (
        values_in
        * lax.rsqrt(jnp.mean(values_in * values_in, axis=-1, keepdims=True) + norm_eps)
        * gain_row
    )


def norm_back(values_in, gain_row, upstream):
    inverse = lax.rsqrt(jnp.mean(values_in * values_in, axis=-1, keepdims=True) + norm_eps)
    scaled = upstream * gain_row
    value_grad = inverse * scaled - values_in * (inverse * inverse * inverse) * jnp.mean(
        values_in * scaled, axis=-1, keepdims=True
    )
    gain_grad = jnp.sum(upstream * values_in * inverse, axis=0)
    return (value_grad, gain_grad)


def gain_sum(values_in, upstream):
    inverse = lax.rsqrt(jnp.mean(values_in * values_in, axis=-1, keepdims=True) + norm_eps)
    return jnp.sum(upstream * values_in * inverse, axis=0, keepdims=True)


def angle_tables(length):
    half_dim = HEAD_DIM // 2
    freqs = np.exp(
        np.arange(half_dim, dtype=np.float32) * np.float32(-2.0 * math.log(rope_base) / HEAD_DIM)
    ).astype(np.float32)
    angles = np.arange(length, dtype=np.float32)[:, None] * freqs[None, :]
    return np.cos(angles).astype(np.float32), np.sin(angles).astype(np.float32)


def rotate(heads_in, cos_table, sin_table):
    half_dim = heads_in.shape[-1] // 2
    lower_half = heads_in[..., :half_dim]
    upper_half = heads_in[..., half_dim:]
    return jnp.concatenate(
        [
            lower_half * cos_table - upper_half * sin_table,
            upper_half * cos_table + lower_half * sin_table,
        ],
        axis=-1,
    )


def dot(a, b):
    return lax.dot_general(a, b, (((1,), (0,)), ((), ())), preferred_element_type=F32)


def dot_tn(a, b):
    return lax.dot_general(a, b, (((0,), (0,)), ((), ())), preferred_element_type=F32)


def dot_nt(a, b):
    return lax.dot_general(a, b, (((1,), (1,)), ((), ())), preferred_element_type=F32)


def span(low, high, body, unrolled):
    if unrolled:
        for i in range(low, high):
            body(i)
    else:
        lax.fori_loop(low, high, lambda i, c: (body(i), c)[1], 0)


def causal_fill(block, fill):
    kv = lax.broadcasted_iota(jnp.int32, block.shape, 0)
    q = lax.broadcasted_iota(jnp.int32, block.shape, 1)
    return jnp.where(q >= kv, block, fill)


def attention_kernel(x_ref, o_ref, ot_ref, ls_ref, vt_ref, s_ref):
    n, hp, _, rows, _ = x_ref.shape
    unrolled = n <= 8
    factor = SCORE_SCALE * LOG2E
    for h in range(hp):
        for j in range(n):
            vt_ref[j] = x_ref[j, h, 2].astype(F32).T.astype(BF16)

        def query_block(i):
            q = x_ref[i, h, 0]
            diag = causal_fill(dot_nt(x_ref[i, h, 1], q), NEG)

            def first(j, peak):
                s = dot_nt(x_ref[j, h, 1], q)
                s_ref[j] = s
                return jnp.maximum(peak, jnp.max(s, axis=0, keepdims=True))

            peak = jnp.max(diag, axis=0, keepdims=True)
            if unrolled:
                for j in range(i):
                    peak = first(j, peak)
            else:
                peak = lax.fori_loop(0, i, first, peak)
            shift = peak * factor
            p = jnp.exp2(diag * factor - shift)
            total = jnp.sum(p, axis=0, keepdims=True)
            acc = dot(vt_ref[i], p.astype(BF16))

            def second(j, state):
                total, acc = state
                p = jnp.exp2(s_ref[j] * factor - shift)
                return (
                    total + jnp.sum(p, axis=0, keepdims=True),
                    acc + dot(vt_ref[j], p.astype(BF16)),
                )

            state = (total, acc)
            if unrolled:
                for j in range(i):
                    state = second(j, state)
            else:
                state = lax.fori_loop(0, i, second, state)
            total, acc = state
            acc = acc / total
            ot_ref[i, h] = acc
            o_ref[i, h] = acc.T.astype(BF16)
            ls_ref[i, h] = shift + jnp.log2(total)

        span(0, n, query_block, unrolled)


def attention(x):
    n, hp, _, rows, dim = x.shape
    pairs = n * (n + 1) // 2 * rows * rows * hp
    return pl.pallas_call(
        attention_kernel,
        name="attention",
        out_shape=(
            jax.ShapeDtypeStruct((n, hp, rows, dim), BF16),
            jax.ShapeDtypeStruct((n, hp, dim, rows), F32),
            jax.ShapeDtypeStruct((n, hp, 1, rows), F32),
        ),
        scratch_shapes=[
            pltpu.VMEM((n, dim, rows), BF16),
            pltpu.VMEM((n, rows, rows), F32),
        ],
        compiler_params=pltpu.CompilerParams(vmem_limit_bytes=40 << 20),
        cost_estimate=pl.CostEstimate(
            flops=pairs * dim * 8, bytes_accessed=x.size * 4, transcendentals=pairs
        ),
    )(x)


def attention_back_kernel(
    x_ref, g_ref, ot_ref, ls_ref, cos_ref, sin_ref, out_ref, kt_ref, dqt_ref, delta_ref
):
    n, hp, _, rows, _ = x_ref.shape
    unrolled = n <= 8
    factor = SCORE_SCALE * LOG2E
    for h in range(hp):
        for j in range(n):
            kt_ref[j] = x_ref[j, h, 1].astype(F32).T.astype(BF16)
            delta_ref[j] = jnp.sum(
                g_ref[j, h].astype(F32).T * ot_ref[j, h], axis=0, keepdims=True
            )

        def unrotated(value, i):
            turned = pl.ds(i * rows, rows)
            cos, sin = cos_ref[turned], sin_ref[turned]
            return rotate(value * SCORE_SCALE, cos, -sin).astype(BF16)

        def pair(i, j, diagonal):
            q, g = x_ref[i, h, 0], g_ref[i, h]
            p = jnp.exp2(dot_nt(x_ref[j, h, 1], q) * factor - ls_ref[i, h])
            if diagonal:
                p = causal_fill(p, 0.0)
            dv = dot(p.astype(BF16), g)
            ds = (p * (dot_nt(x_ref[j, h, 2], g) - delta_ref[i])).astype(BF16)
            dk = dot(ds, q)
            dqt = dot(kt_ref[j], ds)
            return dv, dk, dqt

        def key_block(j):
            dv, dk, dqt = pair(j, j, True)
            if unrolled:
                dqt_ref[j] = dqt if j == 0 else dqt_ref[j] + dqt
            else:
                dqt_ref[j] = jnp.where(j == 0, 0.0, dqt_ref[j]) + dqt

            def step(i, state):
                dv, dk = state
                v, k, t = pair(i, j, False)
                if unrolled:
                    dqt_ref[i] = t if j == 0 else dqt_ref[i] + t
                else:
                    dqt_ref[i] = jnp.where(j == 0, 0.0, dqt_ref[i]) + t
                return dv + v, dk + k

            state = (dv, dk)
            if unrolled:
                for i in range(j + 1, n):
                    state = step(i, state)
            else:
                state = lax.fori_loop(j + 1, n, step, state)
            dv, dk = state
            out_ref[j, h, 0] = unrotated(dqt_ref[j].T, j)
            out_ref[j, h, 1] = unrotated(dk, j)
            out_ref[j, h, 2] = dv.astype(BF16)

        span(0, n, key_block, unrolled)


def attention_back(x, g, ot, ls, cos, sin):
    n, hp, _, rows, dim = x.shape
    pairs = n * (n + 1) // 2 * rows * rows * hp
    return pl.pallas_call(
        attention_back_kernel,
        name="attention_back",
        out_shape=jax.ShapeDtypeStruct(x.shape, BF16),
        scratch_shapes=[
            pltpu.VMEM((n, dim, rows), BF16),
            pltpu.VMEM((n, dim, rows), F32),
            pltpu.VMEM((n, 1, rows), F32),
        ],
        compiler_params=pltpu.CompilerParams(vmem_limit_bytes=40 << 20),
        cost_estimate=pl.CostEstimate(
            flops=pairs * dim * 20, bytes_accessed=x.size * 6, transcendentals=pairs
        ),
    )(x, g, ot, ls, cos, sin)


def seq_device(index):
    return {"seq": index}


def greet(peers):
    barrier = pltpu.get_barrier_semaphore()
    for device in peers:
        pl.semaphore_signal(barrier, inc=1, device_id=device, device_id_type=MESH)


def greeted(count):
    pl.semaphore_wait(pltpu.get_barrier_semaphore(), count)


def remote(src, dst, send, recv, device):
    return pltpu.make_async_remote_copy(
        src_ref=src,
        dst_ref=dst,
        send_sem=send,
        recv_sem=recv,
        device_id=device,
        device_id_type=MESH,
    )


def front_kernel(
    state_ref,
    embedded_ref,
    wa_ref,
    wq_ref,
    gain_ref,
    table_ref,
    resid_out,
    normed_out,
    att_out,
    x_out,
    ot_out,
    ls_out,
    ltn_out,
    ltj_out,
    wa,
    wq,
    joined,
    resid,
    normed,
    sent,
    x,
    vt,
    scores,
    ot,
    o_sent,
    att,
    ltn,
    ltj,
    table,
    load_sem,
    store_sem,
    send_sem,
    recv_sem,
    o_send_sem,
    o_recv_sem,
    l_send_sem,
    l_recv_sem,
):
    n, rows, width = HEADS, state_ref.shape[0], state_ref.shape[1]
    me = lax.axis_index("seq")
    dp = lax.axis_index("dp")
    peers = [seq_device((me + k) % n) for k in range(1, n)]
    across = [{"dp": flipped(0, dp)}, {"dp": flipped(1, dp)}]
    near = seq_device(flipped(0, me))
    greet(peers + across)
    loads = [
        pltpu.make_async_copy(state_ref, joined.at[0], load_sem.at[0]),
        pltpu.make_async_copy(wa_ref.at[pl.ds(0, width)], wa.at[0], load_sem.at[1]),
        pltpu.make_async_copy(embedded_ref, joined.at[1], load_sem.at[2]),
        pltpu.make_async_copy(wa_ref.at[pl.ds(width, width)], wa.at[1], load_sem.at[3]),
        pltpu.make_async_copy(wq_ref, wq, load_sem.at[4]),
        pltpu.make_async_copy(
            table_ref.at[pl.ds(pl.multiple_of(me * rows, 8), rows)], table, load_sem.at[5]
        ),
    ]
    for copy in loads:
        copy.start()
    tile = 256
    for half in range(2):
        loads[2 * half].wait()
        loads[2 * half + 1].wait()

        for begin in range(0, width, tile):
            cols = pl.ds(begin, tile)
            block = dot(joined[half], wa[half, :, cols])
            resid[:, cols] = block if half == 0 else resid[:, cols] + block
    normed[...] = mean_norm(resid[...], gain_ref[0:1, :].astype(F32)).astype(BF16)
    stores = [
        pltpu.make_async_copy(resid, resid_out, store_sem.at[0]),
        pltpu.make_async_copy(normed, normed_out, store_sem.at[1]),
    ]
    for copy in stores:
        copy.start()
    loads[4].wait()
    lefts = []

    def share(source, out, slot, device):
        k = len(lefts)
        copy = remote(source, out.at[slot], l_send_sem.at[k], l_recv_sem.at[k], device)
        copy.start()
        lefts.append(copy)
    loads[5].wait()
    cos, sin = table[:, 0 : HEAD_DIM // 2], table[:, HEAD_DIM // 2 : HEAD_DIM]
    pairs = n // 2
    order = [2, 1, 3, 0] if pairs == 4 else list(range(pairs - 1, -1, -1))
    sends = []
    for k in order:
        chip = (me // 2 + k) % pairs
        for part in range(3):
            cols = pl.ds(pl.multiple_of(part * width + chip * 2 * HEAD_DIM, 2 * HEAD_DIM), 2 * HEAD_DIM)
            block = dot(normed[...], wq[:, cols])
            for core in range(2):
                head = block[:, core * HEAD_DIM : (core + 1) * HEAD_DIM]
                if part < 2:
                    head = rotate(head, cos, sin)
                sent[2 * chip + core, part] = head.astype(BF16)
        if k == order[0]:
            greeted(n + 1)
        for core in range(2):
            owner = 2 * chip + core
            if k == 0:
                continue
            copy = remote(sent.at[owner], x.at[me], send_sem.at[owner], recv_sem.at[me], seq_device(owner))
            copy.start()
            sends.append(copy)
    mate = me + 1 - 2 * (me % 2)
    copy = remote(sent.at[mate], x.at[me], send_sem.at[mate], recv_sem.at[me], seq_device(mate))
    copy.start()
    sends.append(copy)
    x[me] = sent[me]
    transposed_into(normed, ltn)
    for half in range(2):
        transposed_into(joined.at[half], ltj.at[pl.ds(half * width, width)])
    stores.append(pltpu.make_async_copy(ltn, ltn_out.at[0], store_sem.at[4]))
    stores.append(pltpu.make_async_copy(ltj, ltj_out.at[0], store_sem.at[5]))
    for copy in stores[2:]:
        copy.start()
    share(ltn, ltn_out, 2, across[0])
    share(ltn, ltn_out, 4, across[1])
    share(ltj, ltj_out, 2, across[1])
    share(ltn, ltn_out, 1, near)
    share(ltj, ltj_out, 1, near)
    factor = SCORE_SCALE * LOG2E
    for i in range(n):

        @pl.when(me != i)
        def arrive():
            remote(sent.at[0], x.at[i], send_sem.at[0], recv_sem.at[i], seq_device(i)).wait_recv()

        vt[i] = x[i, 2].astype(F32).T.astype(BF16)
        q = x[i, 0]
        diag = causal_fill(dot_nt(x[i, 1], q), NEG)
        peak = jnp.max(diag, axis=0, keepdims=True)
        for j in range(i):
            block = dot_nt(x[j, 1], q)
            scores[j] = block
            peak = jnp.maximum(peak, jnp.max(block, axis=0, keepdims=True))
        shift = peak * factor
        p = jnp.exp2(diag * factor - shift)
        total = jnp.sum(p, axis=0, keepdims=True)
        acc = dot(vt[i], p.astype(BF16))
        for j in range(i):
            p = jnp.exp2(scores[j] * factor - shift)
            total = total + jnp.sum(p, axis=0, keepdims=True)
            acc = acc + dot(vt[j], p.astype(BF16))
        acc = acc / total
        ot[i] = acc
        o_sent[i] = acc.T.astype(BF16)
        ls_out[i] = shift + jnp.log2(total)
        mine = pl.ds(pl.multiple_of(me * HEAD_DIM, HEAD_DIM), HEAD_DIM)

        @pl.when(me != i)
        def give():
            remote(o_sent.at[i], att.at[:, mine], o_send_sem.at[i], o_recv_sem.at[me], seq_device(i)).start()

        @pl.when(me == i)
        def keep():
            att[:, mine] = o_sent[i]

    stores.append(pltpu.make_async_copy(x, x_out, store_sem.at[2]))
    stores.append(pltpu.make_async_copy(ot, ot_out, store_sem.at[3]))
    for copy in stores[4:]:
        copy.start()
    for k, out, slot in ((0, ltn_out, 2), (1, ltn_out, 4), (2, ltj_out, 2)):
        lefts[k].wait_recv()
        share(out.at[slot], out, slot + 1, near)
    for copy in sends:
        copy.wait_send()
    for i in range(n):

        @pl.when(me != i)
        def finish():
            cols = pl.ds(i * HEAD_DIM, HEAD_DIM)
            copy = remote(o_sent.at[i], att.at[:, cols], o_send_sem.at[i], o_recv_sem.at[i], seq_device(i))
            copy.wait_send()
            copy.wait_recv()

    att_out[...] = att[...]
    for copy in stores:
        copy.wait()
    for k, copy in enumerate(lefts):
        copy.wait_send()
        if k > 2:
            copy.wait_recv()


def front(state, embedded, w_adapt, w_qkv, gains, table):
    n = HEADS
    rows, width = state.shape
    hbm = pl.BlockSpec(memory_space=pl.ANY)
    vmem = pl.BlockSpec(memory_space=pltpu.VMEM)
    return pl.pallas_call(
        front_kernel,
        name="front",
        out_shape=(
            jax.ShapeDtypeStruct((rows, width), F32),
            jax.ShapeDtypeStruct((rows, width), BF16),
            jax.ShapeDtypeStruct((rows, width), BF16),
            jax.ShapeDtypeStruct((n, 3, rows, HEAD_DIM), BF16),
            jax.ShapeDtypeStruct((n, HEAD_DIM, rows), F32),
            jax.ShapeDtypeStruct((n, 1, rows), F32),
            jax.ShapeDtypeStruct((6, width, rows), BF16),
            jax.ShapeDtypeStruct((4, 2 * width, rows), BF16),
        ),
        in_specs=[hbm, hbm, hbm, hbm, vmem, hbm],
        out_specs=(hbm, hbm, vmem, hbm, hbm, vmem, hbm, hbm),
        scratch_shapes=[
            pltpu.VMEM((2, width, width), BF16),
            pltpu.VMEM((width, 3 * width), BF16),
            pltpu.VMEM((2, rows, width), BF16),
            pltpu.VMEM((rows, width), F32),
            pltpu.VMEM((rows, width), BF16),
            pltpu.VMEM((n, 3, rows, HEAD_DIM), BF16),
            pltpu.VMEM((n, 3, rows, HEAD_DIM), BF16),
            pltpu.VMEM((n, HEAD_DIM, rows), BF16),
            pltpu.VMEM((n, rows, rows), F32),
            pltpu.VMEM((n, HEAD_DIM, rows), F32),
            pltpu.VMEM((n, rows, HEAD_DIM), BF16),
            pltpu.VMEM((rows, width), BF16),
            pltpu.VMEM((width, rows), BF16),
            pltpu.VMEM((2 * width, rows), BF16),
            pltpu.VMEM((rows, HEAD_DIM), F32),
            pltpu.SemaphoreType.DMA((6,)),
            pltpu.SemaphoreType.DMA((6,)),
            pltpu.SemaphoreType.DMA((n,)),
            pltpu.SemaphoreType.DMA((n,)),
            pltpu.SemaphoreType.DMA((n,)),
            pltpu.SemaphoreType.DMA((n,)),
            pltpu.SemaphoreType.DMA((8,)),
            pltpu.SemaphoreType.DMA((8,)),
        ],
        compiler_params=pltpu.CompilerParams(
            collective_id=1, has_side_effects=True, vmem_limit_bytes=62 << 20
        ),
    )(state, embedded, w_adapt, w_qkv, gains, table)


def flipped(bit, value):
    return value + (1 - 2 * ((value // (1 << bit)) % 2)) * (1 << bit)


def unit_slots(first, dp):
    slots = []
    for q in range(4):
        turned = [(dp + q) % 2, (dp // 2 + q // 2) % 2]
        slots.append(turned[first] * 2 + turned[1 - first])
    return slots


def transposed_into(source, target):
    tile = 256
    for begin in range(0, source.shape[1], tile):
        target[pl.ds(begin, tile), :] = source[:, pl.ds(begin, tile)].T


def add_into(target, more):
    rows = target.shape[0]
    chunk = 16
    while rows % (chunk * 2) == 0 and chunk < 64:
        chunk *= 2

    def step(t, c):
        at = pl.ds(pl.multiple_of(t * chunk, chunk), chunk)
        target[at, :] = (target[at, :].astype(F32) + more[at, :].astype(F32)).astype(BF16)
        return c

    lax.fori_loop(0, rows // chunk, step, 0)


CHUNKS = ((0, 512), (512, 512), (1024, 384))


def z_place(z):
    return (z % 2) * 2 + z // 2


def transposed_blocks(source, target, first, last):
    tile = 256
    parts, size = target.shape[1], target.shape[2]
    for begin in range(first * tile, min(last * tile, source.shape[1]), tile):
        block = source[:, pl.ds(begin, tile)].T
        for k in range(begin // size, (begin + tile - 1) // size + 1):
            low, high = max(begin, size * k), min(begin + tile, size * (k + 1))
            target[k // parts, k % parts, pl.ds(low - size * k, high - low), :] = block[
                low - begin : high - begin
            ]


def middle_kernel(*refs):
    refs = list(refs)

    def take(count):
        taken, refs[:count] = refs[:count], []
        return taken

    (att_in, resid_in, cot_in, gain_rows, wo_in, wg_in, wu_in, wd_in) = take(8)
    (x_in, ot_in, ls_ref, table_in) = take(4)
    (layer_out, above_out, gains_out, packed_out) = take(4)
    (kept_d, kept_z, kept_g, kept_h, kept_o) = take(5)
    (wo, wg, wu, wd, att, cot, resid, branch, mid, down, above) = take(11)
    (normed, hidden, gate_by, up_by, down_low, wide_low, branch_low, dout) = take(8)
    (left_n, left_h, left_m, left_a, right_g, right_d, right_b) = take(7)
    (got_g, got_d, got_z) = take(3)
    (work, x, ot, table, g, kt, dqt, delta, dsent, packed) = take(10)
    (load_sem, store_sem, g_send, g_recv, d_send, d_recv, m_send, m_recv, s_send, s_recv) = take(10)
    n, (rows, width) = HEADS, resid.shape
    ff = wg.shape[1]
    half, part = ff // 2, width // 2
    me = lax.axis_index("seq")
    dp = lax.axis_index("dp")
    core = me % 2
    mate = flipped(0, me)
    bits = [dp % 2, dp // 2]
    near = seq_device(mate)
    across = [{"dp": flipped(0, dp)}, {"dp": flipped(1, dp)}]
    diagonal = [{"seq": mate, "dp": flipped(0, dp)}, {"seq": mate, "dp": flipped(1, dp)}]
    greet([seq_device((me + k) % n) for k in range(1, n)] + across + diagonal)
    loads = {}
    for key, src, dst in (
        ("att", att_in, att),
        ("wo", wo_in, wo),
        ("resid", resid_in, resid),
        ("wg", wg_in, wg),
        ("wu", wu_in, wu),
        ("cot", cot_in, cot),
        ("wd", wd_in, wd),
        ("x", x_in, x),
        ("ot", ot_in, ot),
        ("table", table_in, table),
    ):
        copy = pltpu.make_async_copy(src, dst, load_sem.at[len(loads)])
        copy.start()
        loads[key] = copy
    tile = 256
    gains = [gain_rows[k : k + 1, :].astype(F32) for k in range(4)]

    def tiles(total, body):
        for begin in range(0, total, tile):
            body(pl.ds(begin, tile))

    sends = []
    given = {}

    issued = []

    def give(key, src, dst, device):
        k = len(issued)
        copy = remote(src, dst, m_send.at[k], m_recv.at[k], device)
        copy.start()
        issued.append(key)
        sends.append(copy)
        given[key] = copy

    loads["att"].wait()
    loads["wo"].wait()

    def project(cols):
        branch[:, cols] = dot(att[...], wo[:, cols])

    tiles(width, project)
    loads["resid"].wait()
    mid[...] = resid[...] + mean_norm(branch[...], gains[1])
    normed[...] = mean_norm(mid[...], gains[2]).astype(BF16)
    transposed_into(normed, left_n.at[0])
    greeted(n + 3)
    give("n1", left_n.at[0], left_n.at[1], near)
    give("n2", left_n.at[0], left_n.at[2], across[0])
    loads["wg"].wait()
    loads["wu"].wait()

    def widen(cols):
        gate = dot(normed[...], wg[:, cols])
        up = dot(normed[...], wu[:, cols])
        bent = jax.nn.sigmoid(gate)
        silu = gate * bent
        hidden[:, cols] = (silu * up).astype(BF16)
        gate_by[:, cols] = (up * bent * (1.0 + gate * (1.0 - bent))).astype(BF16)
        up_by[:, cols] = silu.astype(BF16)

    tiles(ff, widen)
    loads["wd"].wait()

    steps = width // tile
    share = -(-ff // tile // steps)
    for k in range(steps):
        cols = pl.ds(k * tile, tile)
        down[:, cols] = dot(hidden[...], wd[:, cols])
        transposed_blocks(hidden, left_h, k * share, (k + 1) * share)
    give("h2", left_h.at[:, 1 - bits[1]], left_m.at[1], across[1])
    give("h1", left_h.at[:, bits[1]], left_m.at[0], near)
    loads["cot"].wait()
    grad, _ = norm_back(down[...], gains[3], cot[...].astype(F32))
    down_low[...] = grad.astype(BF16)
    mine_d = pl.ds(pl.multiple_of(core * part, 128), part)
    theirs_d = pl.ds(pl.multiple_of((1 - core) * part, 128), part)
    give("d2", down_low.at[:, mine_d], right_d.at[1], across[1])
    give("d3", down_low.at[:, theirs_d], right_d.at[2], diagonal[1])
    give("d1", down_low.at[:, theirs_d], right_d.at[0], near)

    def widen_back(cols):
        block = dot_nt(down_low[...], wd[cols, :])
        wide_low[0, :, cols] = (block * gate_by[:, cols].astype(F32)).astype(BF16)
        wide_low[1, :, cols] = (block * up_by[:, cols].astype(F32)).astype(BF16)

    tiles(ff, widen_back)

    def chunk_of(c, which_core, which_bit):
        at, wide = CHUNKS[c]
        return wide_low.at[which_core, :, pl.ds(pl.multiple_of(which_bit * half + at, 128), wide)]

    def give_chunk(c):
        at, wide = CHUNKS[c]
        cols = pl.ds(at, wide)
        give(("g2", c), chunk_of(c, core, 1 - bits[0]), right_g.at[1, :, cols], across[0])
        give(("g3", c), chunk_of(c, 1 - core, 1 - bits[0]), right_g.at[2, :, cols], diagonal[0])
        give(("g1", c), chunk_of(c, 1 - core, bits[0]), right_g.at[0, :, cols], near)

    give_chunk(0)

    def narrow_back(cols):
        above[:, cols] = dot_nt(wide_low[0], wg[cols, :]) + dot_nt(wide_low[1], wu[cols, :])

    tiles(width, narrow_back)
    grad, _ = norm_back(mid[...], gains[2], above[...])
    resid[...] = cot[...].astype(F32) + grad
    grad, _ = norm_back(branch[...], gains[1], resid[...])
    branch_low[...] = grad.astype(BF16)

    def project_back(cols):
        dout[:, cols] = dot_nt(branch_low[...], wo[cols, :]).astype(BF16)

    tiles(width, project_back)
    my_cols = pl.ds(pl.multiple_of(me * HEAD_DIM, HEAD_DIM), HEAD_DIM)
    for k in (4, 5, 3, 2, 6, 7, 1):
        owner = (me + k) % n
        cols = pl.ds(pl.multiple_of(owner * HEAD_DIM, HEAD_DIM), HEAD_DIM)
        copy = remote(dout.at[:, cols], g.at[me], g_send.at[owner], g_recv.at[me], seq_device(owner))
        copy.start()
        sends.append(copy)
    g[me] = dout[:, my_cols]
    given["n2"].wait_recv()
    give("n3", left_n.at[2], left_n.at[3], near)
    transposed_into(att, left_a.at[0])
    give("a1", left_a.at[0], left_a.at[1], near)
    give("b1", branch_low.at[:, theirs_d], right_b, near)
    layer_out[...] = (mid[...] + mean_norm(down[...], gains[3])).astype(BF16)
    stores = []

    def store(src, dst):
        copy = pltpu.make_async_copy(src, dst, store_sem.at[len(stores)])
        copy.start()
        stores.append(copy)

    store(resid, above_out)
    gains_out[...] = jnp.zeros_like(gains_out)
    gains_out[1:2, :] = gain_sum(branch[...], resid[...])
    gains_out[2:3, :] = gain_sum(mid[...], above[...])
    gains_out[3:4, :] = gain_sum(down[...], cot[...].astype(F32))
    seconds = {}
    z_low = (me // 2) % 2

    def wide_sum(c):
        at, wide = CHUNKS[c]
        for key in ("n1", "n3"):
            if key in given:
                given.pop(key).wait_recv()
        for key in ("g1", "g2", "g3"):
            given[key, c].wait_recv()
        shard = width // 32
        spread = [(bits[1] + other) % 2 for other in range(2)]
        own = chunk_of(c, core, bits[0])
        for begin in range(0, wide, 256):
            step = min(256, wide - begin)
            cols = pl.ds(at + begin, step)
            block = dot(left_n[0], own[:, pl.ds(begin, step)])
            for k in range(1, 4):
                block += dot(left_n[k], right_g[k - 1, :, cols])
            work[0:width, 0:step] = block
            for z in range(4):
                for other in range(2):
                    pieces = [
                        work[pl.ds((8 * z + 4 * c2 + 2 * other + b) * shard, shard), 0:step]
                        for c2 in range(2)
                        for b in range(2)
                    ]
                    place = pl.multiple_of(spread[other] * part + z_place(z) * 4 * shard, 16)
                    wg[pl.ds(place, 4 * shard), cols] = jnp.concatenate(pieces, axis=0).astype(BF16)
        cols = pl.ds(at, wide)
        if c == len(CHUNKS) - 1:
            store(wg.at[:, cols], kept_h)
            return
        seconds[c] = remote(
            wg.at[pl.ds(part, part), cols], got_g.at[:, cols], s_send.at[c], s_recv.at[c], across[1]
        )
        seconds[c].start()
        sends.append(seconds[c])

    def down_sum():
        for key in ("h1", "h3", "d1", "d2", "d3"):
            given[key].wait_recv()
        tall = ff // 4
        shard = ff // 32
        spread = [(bits[0] + other) % 2 for other in range(2)]
        for begin in range(0, part, 256):
            cols = pl.ds(begin, 256)
            own = down_low.at[:, mine_d]
            block = dot(left_h[:, bits[1]].reshape(2 * tall, rows), own[:, cols])
            for k in range(3):
                block += dot(left_m[k].reshape(2 * tall, rows), right_d[k, :, cols])
            work[...] = block
            for z in range(4):
                for other in range(2):
                    pieces = [
                        work[pl.ds((4 * z + 2 * c2 + other) * shard, shard), :] for c2 in range(2)
                    ]
                    place = pl.multiple_of(spread[other] * tall + z_place(z) * 2 * shard, 16)
                    wd[pl.ds(place, 2 * shard), cols] = jnp.concatenate(pieces, axis=0).astype(BF16)
            k = begin // 256
            seconds["d", k] = remote(
                wd.at[pl.ds(tall, tall), cols],
                got_d.at[:, cols],
                s_send.at[2 + k],
                s_recv.at[2 + k],
                across[0],
            )
            seconds["d", k].start()
            sends.append(seconds["d", k])

    def out_sum():
        given["a1"].wait_recv()
        given["b1"].wait_recv()
        shard = width // 32
        slots = unit_slots(0, dp)
        for begin in range(0, part, 256):
            cols = pl.ds(begin, 256)
            block = dot(left_a[0], branch_low.at[:, mine_d][:, cols])
            work[0:width, :] = block + dot(left_a[1], right_b[:, cols])
            for z in range(4):
                for q in range(4):
                    pieces = [
                        work[pl.ds((8 * z + 4 * c2 + q) * shard, shard), :] for c2 in range(2)
                    ]
                    place = pl.multiple_of(slots[q] * (width // 4) + z_place(z) * 2 * shard, 16)
                    wu[pl.ds(place, 2 * shard), cols] = jnp.concatenate(pieces, axis=0).astype(BF16)
        store(wu.at[:, pl.ds(0, part)], kept_o)

    loads["x"].wait()
    factor = SCORE_SCALE * LOG2E
    half_dim = HEAD_DIM // 2
    pairs = [(i, j) for j in range(n) for i in range(j, n)]
    across_blocks = ff // rows

    def probs(i, j):
        k = pairs.index((i, j))
        at, cols = k // across_blocks * rows, k % across_blocks * rows
        return wu.at[pl.ds(at, rows), pl.ds(cols, rows)]

    give_chunk(1)
    for j in range(n):
        kt[j] = x[j, 1].astype(F32).T.astype(BF16)
        for i in range(j, n):
            p = jnp.exp2(dot_nt(x[j, 1], x[i, 0]) * factor - ls_ref[i])
            if i == j:
                p = causal_fill(p, 0.0)
            probs(i, j)[...] = p.astype(BF16)
    give_chunk(2)
    loads["ot"].wait()
    loads["table"].wait()
    arrived, summed = set(), set()

    def upstream(i):
        if i not in arrived:
            arrived.add(i)

            @pl.when(me != i)
            def arrive():
                remote(g.at[0], g.at[i], g_send.at[0], g_recv.at[i], seq_device(i)).wait_recv()

            delta[i] = jnp.sum(g[i].astype(F32).T * ot[i], axis=0, keepdims=True)
        return g[i]

    def give_head(j, first, count, sem):
        span = pl.ds(first, count)

        @pl.when(me != j)
        def over():
            remote(
                dsent.at[j, span], packed.at[span, :, my_cols], d_send.at[sem], d_recv.at[sem - j + me], seq_device(j)
            ).start()

        @pl.when(me == j)
        def keep():
            packed[span, :, my_cols] = dsent[j, span]

    def unrotated(value, j):
        here = pl.ds(j * rows, rows)
        cos, sin = table[here, 0:half_dim], -table[here, half_dim:HEAD_DIM]
        return rotate(value * SCORE_SCALE, cos, sin).astype(BF16)

    order = [n - 1, n - 2, 0]
    for k in range(1, n // 2 - 1):
        order += [n - 2 - k, k]
    order += [n // 2 - 1]
    for j in order:
        dk = dv = None
        for i in range(j, n):
            up = upstream(i)
            p = probs(i, j)[...]
            v = dot(p, up)
            ds = (p.astype(F32) * (dot_nt(x[j, 2], up) - delta[i])).astype(BF16)
            k = dot(ds, x[i, 0])
            t = dot(kt[j], ds)
            dqt[i] = dqt[i] + t if i in summed else t
            summed.add(i)
            dv, dk = (v, k) if i == j else (dv + v, dk + k)
        dsent[j, 1] = unrotated(dk, j)
        dsent[j, 2] = dv.astype(BF16)
        give_head(j, 1, 2, j)
        if j < n // 2:
            dsent[j, 0] = unrotated(dqt[j].T, j)
            give_head(j, 0, 1, n + j)
        if j == 0:
            wide_sum(0)
        if j == 2:
            given["h2"].wait_recv()
            give("h3", left_m.at[1], left_m.at[2], near)
    for j in range(n // 2, n):
        dsent[j, 0] = unrotated(dqt[j].T, j)
        give_head(j, 0, 1, n + j)

    down_sum()
    wide_sum(1)
    wide_sum(2)
    out_sum()

    def finish_wide(c):
        at, wide = CHUNKS[c]
        cols = pl.ds(at, wide)
        seconds[c].wait_recv()
        add_into(wg.at[pl.ds(0, part), cols], got_g.at[:, cols])
        if c > 0:
            store(wg.at[pl.ds(0, part), cols], kept_g)
            return
        third[0].start()
        sends.append(third[0])

    def z_rows(which):
        return wg.at[pl.ds(pl.multiple_of(which * (part // 2), 16), part // 2), pl.ds(0, CHUNKS[0][1])]

    def finish_z():
        third[0].wait_recv()
        add_into(z_rows(z_low), got_z)
        store(z_rows(z_low), kept_z)

    third = [
        remote(z_rows(1 - z_low), got_z, s_send.at[4], s_recv.at[4], seq_device(flipped(1, me)))
    ]
    finish_wide(0)
    finish_wide(1)
    for k in range(part // 256):
        cols = pl.ds(256 * k, 256)
        seconds["d", k].wait_recv()
        mine = wd.at[pl.ds(0, ff // 4), cols]
        add_into(mine, got_d.at[:, cols])
        store(mine, kept_d.at[:, cols])
    finish_z()
    for first, count in ((1, 2), (0, 1)):
        span = pl.ds(first, count)
        for j in range(n):

            @pl.when(me != j)
            def finish():
                cols = pl.ds(j * HEAD_DIM, HEAD_DIM)
                sem = j if first == 1 else n + j
                copy = remote(
                    dsent.at[j, span], packed.at[span, :, cols], d_send.at[sem], d_recv.at[sem], seq_device(j)
                )
                copy.wait_send()
                copy.wait_recv()

    store(packed, packed_out)
    for copy in sends:
        copy.wait_send()
    for copy in stores:
        copy.wait()


def middle_block(att, resid, cot, gain_rows, w_out, w_gate, w_up, w_down, x, ot, ls, table):
    n = HEADS
    rows, width = resid.shape
    ff = w_gate.shape[1]
    half, part = ff // 2, width // 2
    hbm = pl.BlockSpec(memory_space=pl.ANY)
    vmem = pl.BlockSpec(memory_space=pltpu.VMEM)
    dma = pltpu.SemaphoreType.DMA
    low = pltpu.VMEM((rows, width), BF16)
    wide = pltpu.VMEM((rows, ff), BF16)
    full = pltpu.VMEM((rows, width), F32)
    scratch = [pltpu.VMEM(w.shape, BF16) for w in (w_out, w_gate, w_up, w_down)]
    scratch += [low, low, full, full, full, full, full]
    scratch += [low, wide, wide, wide, low, pltpu.VMEM((2, rows, ff), BF16), low, low]
    scratch += [
        pltpu.VMEM((4, width, rows), BF16),
        pltpu.VMEM((8, 2, ff // 16, rows), BF16),
        pltpu.VMEM((3, 8, ff // 16, rows), BF16),
        pltpu.VMEM((2, width, rows), BF16),
        pltpu.VMEM((3, rows, half), BF16),
        pltpu.VMEM((3, rows, part), BF16),
        pltpu.VMEM((rows, part), BF16),
        pltpu.VMEM((part, CHUNKS[-1][0]), BF16),
        pltpu.VMEM((ff // 4, part), BF16),
        pltpu.VMEM((part // 2, CHUNKS[0][1]), BF16),
        pltpu.VMEM((half, 256), F32),
        pltpu.VMEM(x.shape, BF16),
        pltpu.VMEM(ot.shape, F32),
        pltpu.VMEM(table.shape, F32),
        pltpu.VMEM((n, rows, HEAD_DIM), BF16),
        pltpu.VMEM((n, HEAD_DIM, rows), BF16),
        pltpu.VMEM((n, HEAD_DIM, rows), F32),
        pltpu.VMEM((n, 1, rows), F32),
        pltpu.VMEM((n, 3, rows, HEAD_DIM), BF16),
        pltpu.VMEM((3, rows, width), BF16),
        dma((10,)),
        dma((8,)),
        dma((n,)),
        dma((n,)),
        dma((2 * n,)),
        dma((2 * n,)),
        dma((20,)),
        dma((20,)),
        dma((5,)),
        dma((5,)),
    ]
    return pl.pallas_call(
        middle_kernel,
        name="middle",
        out_shape=[
            jax.ShapeDtypeStruct((rows, width), BF16),
            jax.ShapeDtypeStruct((rows, width), F32),
            jax.ShapeDtypeStruct((8, width), F32),
            jax.ShapeDtypeStruct((3, rows, width), BF16),
            jax.ShapeDtypeStruct((ff // 4, part), BF16),
            jax.ShapeDtypeStruct((part // 2, CHUNKS[0][1]), BF16),
            jax.ShapeDtypeStruct((part, CHUNKS[1][1]), BF16),
            jax.ShapeDtypeStruct((width, CHUNKS[-1][1]), BF16),
            jax.ShapeDtypeStruct((width, part), BF16),
        ],
        in_specs=[hbm] * 3 + [vmem] + [hbm] * 6 + [vmem] + [hbm],
        out_specs=[vmem, hbm, vmem, hbm] + [hbm] * 5,
        scratch_shapes=scratch,
        compiler_params=pltpu.CompilerParams(
            collective_id=2, has_side_effects=True, vmem_limit_bytes=62 << 20
        ),
    )(att, resid, cot, gain_rows, w_out, w_gate, w_up, w_down, x, ot, ls, table)


BEGUN = ((1, 0, 512, None), (2, 0, 512, None), (0, 0, 256, None), (0, 256, 256, None), (3, 0, 384, 1))
FRESH = ((1, 0, 0), (1, 1024, 0), (1, 2048, 1), (0, 0, 1))
SCHEDULE = (
    ("S", 4), ("2", 0), ("F", 5), ("1", 3), ("P", 0), ("1", 1), ("D", 3), ("2", 3),
    ("E", 0), ("U", 9), ("O", 0), ("U", 7), ("C", 4), ("G", 0), ("E", 3), ("B", 5),
    ("1", 2), ("S", 5), ("D", 1), ("2", 1), ("W", 9), ("S", 9), ("1", 4), ("W", 7),
    ("S", 7), ("D", 2), ("G", 1), ("2", 2), ("C", 5), ("E", 1), ("1", 5), ("D", 4),
    ("G", 2), ("2", 4), ("U", 8), ("E", 2), ("C", 7), ("1", 7), ("D", 5), ("G", 3),
    ("U", 6), ("2", 5), ("C", 9), ("1", 9), ("E", 4), ("D", 7), ("G", 4), ("2", 7),
    ("W", 8), ("E", 5), ("S", 8), ("W", 6), ("S", 6), ("E", 7), ("D", 9), ("2", 9),
    ("C", 8), ("1", 8), ("C", 6), ("1", 6), ("E", 9), ("D", 8), ("2", 8), ("D", 6),
    ("2", 6), ("E", 8), ("E", 6),
)


def dealt_blocks(left, slots, right, spread, bit, out, work):
    total = left.shape[1]
    shard = total // 32
    block = dot(left[slots[0]], right[0])
    for k in range(1, 4):
        block += dot(left[slots[k]], right[k])
    work[0:total, :] = block
    for z in range(4):
        for other in range(2):
            pieces = []
            for core in range(2):
                for b in range(2):
                    q = (b << bit) | (other << (1 - bit))
                    pieces.append(work[pl.ds((8 * z + 4 * core + q) * shard, shard), :])
            out[spread[other], pl.ds(z_place(z) * 4 * shard, 4 * shard), :] = jnp.concatenate(
                pieces, axis=0
            ).astype(BF16)


def tail_kernel(*refs):
    refs = list(refs)

    def take(count):
        taken, refs[:count] = refs[:count], []
        return taken

    begun, fresh = len(BEGUN), len(FRESH)
    single = begun
    first_fresh = begun + 1
    count = first_fresh + fresh
    kept_in = take(5)
    packed_in, ltn_in, ltj_in, wq_in, wa_in = take(5)
    resid_in, above_in, gain_rows, gain_parts = take(4)
    grad_joined = take(2)
    outs = take(5)
    (gains_out,) = take(1)
    held = take(3)
    sums, arrived2 = [None] * 4 + take(count - 4), [None] * 4 + take(count - 4)
    parts, arrived3, arrived4, finals = take(count), take(count), take(count), take(count)
    (got_o, wq, wa, packed, ltn, ltj, dealt, low, work, back_sum, gain_buf, gain_got) = take(12)
    (resid, above, joined_0, joined_1) = take(4)
    joined = (joined_0, joined_1)
    (load_sem, u_send, u_recv, s_send, s_recv, z1_send, z1_recv) = take(7)
    (z2_send, z2_recv, c_send, c_recv, gain_send, gain_recv, store_sem) = take(7)
    rows, width = resid.shape
    me = lax.axis_index("seq")
    dp = lax.axis_index("dp")
    core = me % 2
    bits = [dp % 2, dp // 2]
    z_low, z_high = (me // 2) % 2, me // 4
    mate = flipped(0, me)
    near = seq_device(mate)
    across = [{"dp": flipped(0, dp)}, {"dp": flipped(1, dp)}]
    diagonal = [{"seq": mate, "dp": flipped(0, dp)}, {"seq": mate, "dp": flipped(1, dp)}]
    beside = [seq_device(flipped(1, me)), seq_device(flipped(2, me))]
    greet([near] + across + diagonal + beside)
    loads = {}

    def load(key, src, dst):
        loads[key] = pltpu.make_async_copy(src, dst, load_sem.at[len(loads)])
        loads[key].start()

    load("packed", packed_in, packed)
    load("wq", wq_in, wq)
    load("resid", resid_in, resid)
    load("above", above_in, above)
    greeted(7)
    sends = []

    def send(src, dst, send_sem, recv_sem, device):
        copy = remote(src, dst, send_sem, recv_sem, device)
        copy.start()
        sends.append(copy)
        return copy

    first, dealing, second, third, fourth, finished, taken = [], {}, {}, {}, {}, {}, set()

    def ready(key):
        if key not in taken:
            taken.add(key)
            loads[key].wait()

    def z_rows(u, which):
        tall = finals[u].shape[0]
        return pl.ds(pl.multiple_of(which * 2 * tall, 16), 2 * tall)

    def one_z(u, which):
        tall = finals[u].shape[0]
        return pl.ds(pl.multiple_of(which * tall, 16), tall)

    def start_first(u):
        first.append(send(kept_in[4].at[pl.ds(2, 2)], got_o, s_send.at[count], s_recv.at[count], across[0]))

    def take_first(u):
        first[0].wait_recv()
        ready(single)
        for k in (1, 0):
            add_into(sums[single].at[k], got_o.at[k])

    def start_columns(u):
        k = u - first_fresh
        bit = FRESH[k][2]
        source = low if k == 3 else packed.at[k]
        if k < 3:
            ready("packed")

        def columns(other_core, other_bit):
            place = (core + (1 - 2 * core) * other_core) * 2
            place = place + bits[bit] + (1 - 2 * bits[bit]) * other_bit
            return pl.ds(pl.multiple_of(place * 256, 256), 256)

        dealing[u] = [
            send(
                source.at[:, columns(*there)],
                dealt.at[k, slot],
                u_send.at[3 * k + slot - 1],
                u_recv.at[3 * k + slot - 1],
                device,
            )
            for there, slot, device in (
                ((0, 1), 2, across[bit]),
                ((1, 1), 3, diagonal[bit]),
                ((1, 0), 1, near),
            )
        ]
        dealt[k, 0] = source[:, columns(0, 0)]

    def start_second(u):
        if u < begun:
            array, at, wide, bit = BEGUN[u]
            rows_in = kept_in[array].shape[0] // 2
            src = kept_in[array].at[pl.ds(rows_in, rows_in), pl.ds(at, wide)]
        else:
            bit = 1 if u == single else 1 - FRESH[u - first_fresh][2]
            src = sums[u].at[1]
        second[u] = send(src, arrived2[u], s_send.at[u], s_recv.at[u], across[bit])

    def multiply(u):
        k = u - first_fresh
        out, column, bit = FRESH[k]
        slots = (0, 1, 2, 3) if (bit == 0 or k == 3) else (0, 1, 4, 5)
        left = ltj if k == 3 else ltn
        ready("ltj" if k == 3 else "ltn")
        for copy in dealing[u]:
            copy.wait_recv()
        spread = [(bits[1 - bit] + other) % 2 for other in range(2)]
        dealt_blocks(left, slots, dealt.at[k], spread, bit, sums[u], work)

    def take_second(u):
        second[u].wait_recv()
        if u < begun:
            ready(u)
        add_into(sums[u].at[0], arrived2[u])

    def start_third(u):
        theirs = z_rows(u, 1 - z_low)
        if u < 4:
            array, at, wide, _ = BEGUN[u]
            src = kept_in[array].at[theirs, pl.ds(at, wide)]
        else:
            src = sums[u].at[0, theirs]
        third[u] = send(src, arrived3[u], z1_send.at[u], z1_recv.at[u], beside[0])

    def take_third(u):
        third[u].wait_recv()
        if u < 4:
            array, at, wide, _ = BEGUN[u]
            ready(array)
            mine = held[array][:, pl.ds(at, wide)]
        else:
            mine = sums[u][0, z_rows(u, z_low), :]
        parts[u][...] = (mine.astype(F32) + arrived3[u][...].astype(F32)).astype(BF16)

    def start_fourth(u):
        source = kept_in[1] if u == 0 else parts[u]
        fourth[u] = send(
            source.at[one_z(u, 1 - z_high)], arrived4[u], z2_send.at[u], z2_recv.at[u], beside[1]
        )

    def take_fourth(u):
        fourth[u].wait_recv()
        if u == 0:
            ready(1)
        source = held[1] if u == 0 else parts[u]
        finals[u][...] = source[one_z(u, z_high), :].astype(F32) + arrived4[u][...].astype(F32)
        if u in (0, 1, 4):
            at, wide = CHUNKS[min(u, 2)]
            bit = 0
            cols = pl.ds(pl.multiple_of(bits[0] * (outs[3].shape[2] // 2) + at, 128), wide)
            target = outs[3].at[core, :, cols]
        elif u <= single:
            out, at, wide = (2, 0, width // 2) if u == single else (4,) + BEGUN[u][1:3]
            bit = None
            target = outs[out].at[:, pl.ds(pl.multiple_of(core * (width // 2) + at, 128), wide)]
        else:
            out, column, bit = FRESH[u - first_fresh]
            cols = pl.ds(pl.multiple_of((core * 2 + bits[bit]) * 256 + column, 256), 256)
            target = outs[out].at[:, cols]
        if bit is None:
            owners = [(core, None), (1 - core, near)]
        else:
            here, there = bits[bit], 1 - bits[bit]
            owners = [
                (core * 2 + here, None),
                ((1 - core) * 2 + here, near),
                (core * 2 + there, across[bit]),
                ((1 - core) * 2 + there, diagonal[bit]),
            ]
        shard = finals[u].shape[0] // len(owners)
        finished[u] = []
        for k, (place, device) in enumerate(owners):
            at = pl.ds(pl.multiple_of(place * shard, 8), shard)
            if k == 0:
                target[...] = finals[u][at, :]
            else:
                sem = 3 * u + k - 1
                finished[u].append(
                    send(finals[u].at[at], target, c_send.at[sem], c_recv.at[sem], device)
                )

    gain_steps = {}
    gain_partners = [near] + across + beside

    def send_gain(k):
        gain_steps[k] = send(
            gain_buf.at[k], gain_got.at[k], gain_send.at[k], gain_recv.at[k], gain_partners[k]
        )

    def add_gain(k):
        gain_steps[k].wait_recv()
        total = gain_buf[k] + gain_got[k]
        if k == 4:
            gains_out[...] = total
        else:
            gain_buf[k + 1] = total
            send_gain(k + 1)

    tile = 256
    stores = []

    def dense_back(_):
        ready("packed")
        ready("wq")
        load(1, kept_in[1], held[1])
        load(2, kept_in[2].at[z_rows(1, z_low)], held[2])
        load(0, kept_in[0].at[z_rows(2, z_low)], held[0])
        load(single, kept_in[4].at[pl.ds(0, 2)], sums[single])
        load(4, kept_in[3].at[pl.ds(0, kept_in[3].shape[0] // 2)], sums[4].at[0])
        load("ltn", ltn_in, ltn)
        load("ltj", ltj_in, ltj)
        load("wa", wa_in, wa)
        for begin in range(0, width, tile):
            at = pl.ds(begin, tile)
            block = dot_nt(packed[0], wq[at, pl.ds(0, width)])
            block += dot_nt(packed[1], wq[at, pl.ds(width, width)])
            block += dot_nt(packed[2], wq[at, pl.ds(2 * width, width)])
            back_sum[:, at] = block
        ready("resid")
        ready("above")
        part, gain0 = norm_back(resid[...], gain_rows[0:1, :].astype(F32), back_sum[...])
        low[...] = (above[...] + part).astype(BF16)
        gain_buf[0] = gain_parts[...]
        gain_buf[0, 0:1, :] = gain0[None, :]
        send_gain(0)

    def dense_out(_):
        ready("wa")
        for k in range(2):
            for begin in range(0, width, tile):
                from_row = pl.ds(k * width + begin, tile)
                joined[k][:, pl.ds(begin, tile)] = dot_nt(low[...], wa[from_row, :])
            stores.append(pltpu.make_async_copy(joined[k], grad_joined[k], store_sem.at[k]))
            stores[k].start()

    actions = {
        "F": start_first,
        "B": take_first,
        "U": start_columns,
        "S": start_second,
        "1": start_third,
        "2": start_fourth,
        "W": multiply,
        "C": take_second,
        "D": take_third,
        "E": take_fourth,
        "G": add_gain,
        "P": dense_back,
        "O": dense_out,
    }
    for action, u in SCHEDULE:
        actions[action](u)
    for u in range(count):
        for copy in finished[u]:
            copy.wait_recv()
    for copy in sends:
        copy.wait_send()
    for copy in stores:
        copy.wait()


def tail(kept, packed, left_n, left_j, w_qkv, w_adapt, resid, above, gain_rows, gain_parts):
    rows, width = resid.shape
    hbm = pl.BlockSpec(memory_space=pl.ANY)
    vmem = pl.BlockSpec(memory_space=pltpu.VMEM)
    dma = pltpu.SemaphoreType.DMA
    fresh = len(FRESH)
    down, gate, gate_next, last, out = kept
    left_over = (4, 2, 4, 8)
    every = [(kept[array].shape[0] // left_over[array], wide) for array, _, wide, _ in BEGUN]
    every += [(out.shape[1] // 4, out.shape[2])]
    every += [(width // 8, 256)] * 3 + [(width // 4, 256)]
    count = len(every)
    slots = [1] + [2] * (1 + fresh)
    shapes = [
        (2 * width // 32, width),
        (width // 32, 3 * width),
        (width // 32, width),
        (2, width // 32, 2 * (gate.shape[1] + gate_next.shape[1] + last.shape[1])),
        (down.shape[0] // 8, width),
    ]
    scratch = [
        pltpu.VMEM(shape, BF16)
        for shape in (
            (down.shape[0] // 2, down.shape[1]),
            gate.shape,
            (gate_next.shape[0] // 2, gate_next.shape[1]),
        )
    ]
    scratch += [pltpu.VMEM((k, 4 * tall, wide), BF16) for k, (tall, wide) in zip(slots, every[4:])]
    scratch += [pltpu.VMEM((4 * tall, wide), BF16) for tall, wide in every[4:]]
    scratch += [pltpu.VMEM((2 * tall, wide), BF16) for tall, wide in every]
    scratch += [pltpu.VMEM((2 * tall, wide), BF16) for tall, wide in every]
    scratch += [pltpu.VMEM((tall, wide), BF16) for tall, wide in every]
    scratch += [pltpu.VMEM((tall, wide), F32) for tall, wide in every]
    scratch += [
        pltpu.VMEM((2,) + out.shape[1:], BF16),
        pltpu.VMEM(w_qkv.shape, BF16),
        pltpu.VMEM(w_adapt.shape, BF16),
        pltpu.VMEM(packed.shape, BF16),
        pltpu.VMEM(left_n.shape, BF16),
        pltpu.VMEM(left_j.shape, BF16),
        pltpu.VMEM((4, 4, rows, 256), BF16),
        pltpu.VMEM((rows, width), BF16),
        pltpu.VMEM((2 * width, 256), F32),
        pltpu.VMEM((rows, width), F32),
        pltpu.VMEM((5, 8, width), F32),
        pltpu.VMEM((5, 8, width), F32),
    ]
    scratch += [pltpu.VMEM((rows, width), F32) for _ in range(4)]
    scratch += [dma((14,)), dma((3 * fresh,)), dma((3 * fresh,))]
    scratch += [dma((count + 1,)) for _ in range(2)]
    scratch += [dma((count,)) for _ in range(4)]
    scratch += [dma((3 * count,)) for _ in range(2)]
    scratch += [dma((5,)) for _ in range(2)] + [dma((2,))]
    return pl.pallas_call(
        tail_kernel,
        name="tail",
        out_shape=[jax.ShapeDtypeStruct((rows, width), F32)] * 2
        + [jax.ShapeDtypeStruct(shape, F32) for shape in shapes]
        + [jax.ShapeDtypeStruct((8, width), F32)],
        in_specs=[hbm] * 12 + [vmem] * 2,
        out_specs=[hbm] * 2 + [vmem] * 6,
        scratch_shapes=scratch,
        compiler_params=pltpu.CompilerParams(
            collective_id=3, has_side_effects=True, vmem_limit_bytes=62 << 20
        ),
    )(*kept, packed, left_n, left_j, w_qkv, w_adapt, resid, above, gain_rows, gain_parts)


def finish_kernel(*refs):
    sources, gain_ref, targets, gain_out = refs[:8], refs[8], refs[9:18], refs[18]
    for source, target in zip(sources[:6], targets[:6]):
        target[...] = source[...]
    targets[6][...] = sources[6][0]
    targets[7][...] = sources[6][1]
    targets[8][...] = sources[7][...]

    @pl.when(pl.program_id(0) == 0)
    def pick_gains():
        share = gain_out.shape[1]
        at = (lax.axis_index("seq") * lax.axis_size("dp") + lax.axis_index("dp")) * share
        block = gain_ref[:, pl.ds(pl.multiple_of(at // 128 * 128, 128), 128)]
        here = lax.broadcasted_iota(jnp.int32, (128, share), 0) - at % 128
        picked = here == lax.broadcasted_iota(jnp.int32, (128, share), 1)
        gain_out[...] = lax.dot_general(
            block,
            picked.astype(F32),
            (((1,), (0,)), ((), ())),
            precision=lax.Precision.HIGHEST,
            preferred_element_type=F32,
        )[:4]


def finish(*values):
    steps = 2
    wide, gains = values[6], values[8]
    share = gains.shape[1] // (lax.axis_size("seq") * lax.axis_size("dp"))
    like = list(values[:6]) + [wide[0], wide[1], values[7]]

    def columns(shape):
        lead = len(shape) - 1
        return pl.BlockSpec(shape[:-1] + (shape[-1] // steps,), lambda i: (0,) * lead + (i,))

    return pl.pallas_call(
        finish_kernel,
        name="finish",
        grid=(steps,),
        out_shape=[jax.ShapeDtypeStruct(value.shape, value.dtype) for value in like]
        + [jax.ShapeDtypeStruct((4, share), F32)],
        in_specs=[columns(value.shape) for value in values[:8]]
        + [pl.BlockSpec(gains.shape, lambda i: (0, 0))],
        out_specs=[columns(value.shape) for value in like]
        + [pl.BlockSpec((4, share), lambda i: (0, 0))],
        compiler_params=pltpu.CompilerParams(vmem_limit_bytes=62 << 20),
    )(*values)


def xor_permute(value, axis, mask):
    return lax.ppermute(value, axis, [(i, i ^ mask) for i in range(lax.axis_size(axis))])


def quadrants(left):
    n, parts = lax.axis_size("seq"), lax.axis_size("dp")
    tokens, rows = left.shape
    shard = rows // (n * parts)
    split = left.reshape(tokens, n, parts, shard).transpose(2, 0, 1, 3)
    split = split.reshape(parts, tokens, n * shard)
    me = lax.axis_index("dp")
    return jnp.concatenate(
        [lax.dynamic_index_in_dim(split, me ^ m, 0, keepdims=True) for m in range(parts)]
    )


def other_core(left, right):
    core = lax.axis_index("seq") % 2
    half = right.shape[1] // 2
    mine = lax.dynamic_slice_in_dim(right, core * half, half, 1)
    theirs = lax.dynamic_slice_in_dim(right, (1 - core) * half, half, 1)
    left_in = xor_permute(left, "seq", 1)
    right_in = xor_permute(theirs, "seq", 1)
    return jnp.concatenate([left, left_in], axis=1), jnp.concatenate([mine, right_in], axis=0)


def scattered_sum(left, right, bits):
    n, parts = lax.axis_size("seq"), lax.axis_size("dp")
    cols = right.shape[1]
    left, right = other_core(quadrants(left), right)
    got = {}
    masks = list(range(parts))
    for bit in bits:
        outgoing = [m for m in masks if m >> bit & 1]
        masks = [m for m in masks if not m >> bit & 1]
        blocks = []
        for m in outgoing:
            block = dot_tn(left[m], right)
            for more in got.get(m, ()):
                block = block + more.astype(F32)
            blocks.append(block.astype(BF16))
        incoming = xor_permute(jnp.stack(blocks), "dp", 1 << bit)
        for k, m in enumerate(outgoing):
            got.setdefault(m ^ (1 << bit), []).append(incoming[k])
    block = dot_tn(left[0], right)
    for more in got.get(0, ()):
        block = block + more.astype(F32)
    shard = block.shape[0] // n
    block = block.astype(BF16).reshape(n, shard, cols // 2)
    block = lax.all_to_all(block, "seq", 0, 0)
    block = jnp.sum(block.reshape(n // 2, 2, shard, cols // 2).astype(F32), axis=0)
    return block.transpose(1, 0, 2).reshape(shard, cols)


def small_sum(value):
    value = value.reshape(value.shape[0], -1, value.shape[1])
    for axis in ("seq", "dp"):
        size = lax.axis_size(axis)
        me = lax.axis_index(axis)
        for bit in reversed(range(size.bit_length() - 1)):
            half = value.shape[2] // 2
            mine = (me >> bit) & 1
            kept = lax.dynamic_slice_in_dim(value, mine * half, half, 2)
            sent = lax.dynamic_slice_in_dim(value, (1 - mine) * half, half, 2)
            value = kept + xor_permute(sent, axis, 1 << bit)
    return value[:, 0]


def local(state, embedded, cotangent, w_adapt, w_qkv, w_out, w_gate, w_up, w_down, gains):
    seq_count, rows, width = state.shape
    n, parts = lax.axis_size("seq"), lax.axis_size("dp")
    tokens = seq_count * rows
    me = lax.axis_index("seq")
    bits = list(range(parts.bit_length() - 1))
    copies = max(1, n // HEADS)
    held = max(1, HEADS // n)
    owners = n // copies
    cos_np, sin_np = angle_tables(n * rows)
    cos_all, sin_all = jnp.asarray(cos_np), jnp.asarray(sin_np)
    cos = lax.dynamic_slice_in_dim(cos_all, me * rows, rows, 0)[:, None, :]
    sin = lax.dynamic_slice_in_dim(sin_all, me * rows, rows, 0)[:, None, :]
    gain_rows = gains.astype(F32)
    state, embedded = state.reshape(tokens, width), embedded.reshape(tokens, width)

    def to_heads(flat):
        return flat.reshape(tokens, HEADS, HEAD_DIM)

    def to_owner(parts_in):
        sent = jnp.stack(parts_in).reshape(len(parts_in), tokens, owners, held, HEAD_DIM)
        sent = sent.transpose(2, 3, 0, 1, 4)
        if copies > 1:
            sent = jnp.repeat(sent, copies, axis=0)
        return lax.all_to_all(sent, "seq", 0, 0)

    def from_owner(value):
        back = lax.all_to_all(value, "seq", 0, 0)[::copies]
        back = back.reshape(HEADS, -1, tokens, HEAD_DIM)
        return back.transpose(2, 1, 0, 3).reshape(tokens, -1)

    table = jnp.asarray(np.concatenate([cos_np, sin_np], axis=1))
    if n == HEADS and seq_count == 1 and parts == 4:
        resid, normed, attended, qkv, attended_t, logsum, left_n, left_j = front(
            state, embedded, w_adapt, w_qkv, gains, table
        )
        qkv, attended_t, logsum = qkv[:, None], attended_t[:, None], logsum[:, None]
    else:
        resid = dot(state, w_adapt[:width]) + dot(embedded, w_adapt[width:])
        normed = mean_norm(resid, gain_rows[0]).astype(BF16)
        packed = dot(normed, w_qkv)
        queries = rotate(to_heads(packed[:, :width]), cos, sin).astype(BF16)
        keys = rotate(to_heads(packed[:, width : 2 * width]), cos, sin).astype(BF16)
        values = to_heads(packed[:, 2 * width :]).astype(BF16)
        qkv = to_owner((queries, keys, values))
        attended, attended_t, logsum = attention(qkv)
        attended = from_owner(attended[:, :, None])
    shape = (seq_count, rows, width)
    if n == HEADS and parts == 4 and seq_count == 1:
        layer_out, middle_grad, gain_parts, packed_low, *kept = middle_block(
            attended,
            resid,
            cotangent.reshape(tokens, width),
            gains,
            w_out,
            w_gate,
            w_up,
            w_down,
            qkv[:, 0],
            attended_t[:, 0],
            logsum[:, 0],
            table,
        )
        grad_state, grad_embedded, grad_adapt, grad_qkv, grad_out, grad_wide, grad_down, gains_sum = tail(
            kept[:4] + [kept[4].reshape(4, width // 4, width // 2)],
            packed_low,
            left_n,
            left_j,
            w_qkv,
            w_adapt,
            resid,
            middle_grad,
            gains,
            gain_parts,
        )
        outs = finish(
            layer_out,
            grad_state,
            grad_embedded,
            grad_adapt,
            grad_qkv,
            grad_out,
            grad_wide,
            grad_down,
            gains_sum,
        )
        return tuple(value.reshape(shape) for value in outs[:3]) + tuple(outs[3:])
    branch = dot(attended, w_out)
    middle = resid + mean_norm(branch, gain_rows[1])
    normed_mid = mean_norm(middle, gain_rows[2]).astype(BF16)
    gate_pre = dot(normed_mid, w_gate)
    up_pre = dot(normed_mid, w_up)
    sigmoid_gate = jax.nn.sigmoid(gate_pre)
    silu_gate = gate_pre * sigmoid_gate
    hidden = (silu_gate * up_pre).astype(BF16)
    down_out = dot(hidden, w_down)
    layer_out = middle + mean_norm(down_out, gain_rows[3])
    out_grad = cotangent.astype(F32).reshape(tokens, width)
    down_grad, gain_grad3 = norm_back(down_out, gain_rows[3], out_grad)
    down_low = down_grad.astype(BF16)
    hidden_grad = dot_nt(down_low, w_down)
    gate_low = (
        hidden_grad * up_pre * sigmoid_gate * (1.0 + gate_pre * (1.0 - sigmoid_gate))
    ).astype(BF16)
    up_low = (hidden_grad * silu_gate).astype(BF16)
    mid_norm_grad = dot_nt(gate_low, w_gate) + dot_nt(up_low, w_up)
    middle_part, gain_grad2 = norm_back(middle, gain_rows[2], mid_norm_grad)
    middle_grad = out_grad + middle_part
    branch_grad, gain_grad1 = norm_back(branch, gain_rows[1], middle_grad)
    branch_low = branch_grad.astype(BF16)
    attended_grad = dot_nt(branch_low, w_out).astype(BF16)
    upstream = to_owner((to_heads(attended_grad),))[:, :, 0]
    packed_grad = attention_back(qkv, upstream, attended_t, logsum, cos_all, sin_all)
    packed_low = from_owner(packed_grad)
    normed_grad = dot_nt(packed_low, w_qkv)
    resid_part, gain_grad0 = norm_back(resid, gain_rows[0], normed_grad)
    resid_low = (middle_grad + resid_part).astype(BF16)
    grad_state = dot_nt(resid_low, w_adapt[:width])
    grad_embedded = dot_nt(resid_low, w_adapt[width:])
    flipped = bits[::-1]
    joined = jnp.concatenate([state, embedded], axis=-1)
    grad_down = scattered_sum(hidden, down_low, bits)
    grad_gate = scattered_sum(normed_mid, gate_low, flipped)
    grad_up = scattered_sum(normed_mid, up_low, bits)
    grad_out = scattered_sum(attended, branch_low, flipped)
    grad_qkv = scattered_sum(normed, packed_low, flipped)
    grad_adapt = scattered_sum(joined, resid_low, bits)
    grad_gains = jnp.stack([gain_grad0, gain_grad1, gain_grad2, gain_grad3])
    grad_gains = small_sum(grad_gains)
    return (
        layer_out.reshape(shape).astype(BF16),
        grad_state.reshape(shape),
        grad_embedded.reshape(shape),
        grad_adapt,
        grad_qkv,
        grad_out,
        grad_gate,
        grad_up,
        grad_down,
        grad_gains,
    )


def solution(mesh):
    tokens = P("dp", "seq", None)
    rows = P(("seq", "dp"), None)
    return jax.shard_map(
        local,
        mesh=mesh,
        in_specs=(tokens,) * 3 + (P(),) * 7,
        out_specs=(tokens,) * 3 + (rows,) * 6 + (P(None, ("seq", "dp")),),
        check_vma=False,
    )
```

```python
import functools
import math

import jax
import jax.numpy as jnp
import numpy as np
from jax import lax
from jax.experimental import pallas as pl
from jax.experimental.pallas import tpu as pltpu
from jax.sharding import PartitionSpec as P

HEADS = 8
HEAD_DIM = 128
norm_eps = 1e-06
rope_base = 50000.0
F32 = jnp.float32
BF16 = jnp.bfloat16
MESH = pl.DeviceIdType.MESH
NEG = -1e30
SCORE_SCALE = 1.0 / math.sqrt(HEAD_DIM)
LOG2E = 1.0 / math.log(2.0)


def mean_norm(values_in, gain_row):
    return (
        values_in
        * lax.rsqrt(jnp.mean(values_in * values_in, axis=-1, keepdims=True) + norm_eps)
        * gain_row
    )


def norm_back(values_in, gain_row, upstream):
    inverse = lax.rsqrt(jnp.mean(values_in * values_in, axis=-1, keepdims=True) + norm_eps)
    scaled = upstream * gain_row
    value_grad = inverse * scaled - values_in * (inverse * inverse * inverse) * jnp.mean(
        values_in * scaled, axis=-1, keepdims=True
    )
    gain_grad = jnp.sum(upstream * values_in * inverse, axis=0)
    return (value_grad, gain_grad)


def gain_sum(values_in, upstream):
    inverse = lax.rsqrt(jnp.mean(values_in * values_in, axis=-1, keepdims=True) + norm_eps)
    return jnp.sum(upstream * values_in * inverse, axis=0, keepdims=True)


def angle_tables(length):
    half_dim = HEAD_DIM // 2
    freqs = np.exp(
        np.arange(half_dim, dtype=np.float32) * np.float32(-2.0 * math.log(rope_base) / HEAD_DIM)
    ).astype(np.float32)
    angles = np.arange(length, dtype=np.float32)[:, None] * freqs[None, :]
    return np.cos(angles).astype(np.float32), np.sin(angles).astype(np.float32)


def rotate(heads_in, cos_table, sin_table):
    half_dim = heads_in.shape[-1] // 2
    lower_half = heads_in[..., :half_dim]
    upper_half = heads_in[..., half_dim:]
    return jnp.concatenate(
        [
            lower_half * cos_table - upper_half * sin_table,
            upper_half * cos_table + lower_half * sin_table,
        ],
        axis=-1,
    )


def dot(a, b):
    return lax.dot_general(a, b, (((1,), (0,)), ((), ())), preferred_element_type=F32)


def dot_tn(a, b):
    return lax.dot_general(a, b, (((0,), (0,)), ((), ())), preferred_element_type=F32)


def dot_nt(a, b):
    return lax.dot_general(a, b, (((1,), (1,)), ((), ())), preferred_element_type=F32)


def span(low, high, body, unrolled):
    if unrolled:
        for i in range(low, high):
            body(i)
    else:
        lax.fori_loop(low, high, lambda i, c: (body(i), c)[1], 0)


def causal_fill(block, fill):
    kv = lax.broadcasted_iota(jnp.int32, block.shape, 0)
    q = lax.broadcasted_iota(jnp.int32, block.shape, 1)
    return jnp.where(q >= kv, block, fill)


def attention_kernel(x_ref, o_ref, ot_ref, ls_ref, vt_ref, s_ref):
    n, hp, _, rows, _ = x_ref.shape
    unrolled = n <= 8
    factor = SCORE_SCALE * LOG2E
    for h in range(hp):
        for j in range(n):
            vt_ref[j] = x_ref[j, h, 2].astype(F32).T.astype(BF16)

        def query_block(i):
            q = x_ref[i, h, 0]
            diag = causal_fill(dot_nt(x_ref[i, h, 1], q), NEG)

            def first(j, peak):
                s = dot_nt(x_ref[j, h, 1], q)
                s_ref[j] = s
                return jnp.maximum(peak, jnp.max(s, axis=0, keepdims=True))

            peak = jnp.max(diag, axis=0, keepdims=True)
            if unrolled:
                for j in range(i):
                    peak = first(j, peak)
            else:
                peak = lax.fori_loop(0, i, first, peak)
            shift = peak * factor
            p = jnp.exp2(diag * factor - shift)
            total = jnp.sum(p, axis=0, keepdims=True)
            acc = dot(vt_ref[i], p.astype(BF16))

            def second(j, state):
                total, acc = state
                p = jnp.exp2(s_ref[j] * factor - shift)
                return (
                    total + jnp.sum(p, axis=0, keepdims=True),
                    acc + dot(vt_ref[j], p.astype(BF16)),
                )

            state = (total, acc)
            if unrolled:
                for j in range(i):
                    state = second(j, state)
            else:
                state = lax.fori_loop(0, i, second, state)
            total, acc = state
            acc = acc / total
            ot_ref[i, h] = acc
            o_ref[i, h] = acc.T.astype(BF16)
            ls_ref[i, h] = shift + jnp.log2(total)

        span(0, n, query_block, unrolled)


def attention(x):
    n, hp, _, rows, dim = x.shape
    pairs = n * (n + 1) // 2 * rows * rows * hp
    return pl.pallas_call(
        attention_kernel,
        name="attention",
        out_shape=(
            jax.ShapeDtypeStruct((n, hp, rows, dim), BF16),
            jax.ShapeDtypeStruct((n, hp, dim, rows), F32),
            jax.ShapeDtypeStruct((n, hp, 1, rows), F32),
        ),
        scratch_shapes=[
            pltpu.VMEM((n, dim, rows), BF16),
            pltpu.VMEM((n, rows, rows), F32),
        ],
        compiler_params=pltpu.CompilerParams(vmem_limit_bytes=40 << 20),
        cost_estimate=pl.CostEstimate(
            flops=pairs * dim * 8, bytes_accessed=x.size * 4, transcendentals=pairs
        ),
    )(x)


def attention_back_kernel(
    x_ref, g_ref, ot_ref, ls_ref, cos_ref, sin_ref, out_ref, kt_ref, dqt_ref, delta_ref
):
    n, hp, _, rows, _ = x_ref.shape
    unrolled = n <= 8
    factor = SCORE_SCALE * LOG2E
    for h in range(hp):
        for j in range(n):
            kt_ref[j] = x_ref[j, h, 1].astype(F32).T.astype(BF16)
            delta_ref[j] = jnp.sum(
                g_ref[j, h].astype(F32).T * ot_ref[j, h], axis=0, keepdims=True
            )

        def unrotated(value, i):
            turned = pl.ds(i * rows, rows)
            cos, sin = cos_ref[turned], sin_ref[turned]
            return rotate(value * SCORE_SCALE, cos, -sin).astype(BF16)

        def pair(i, j, diagonal):
            q, g = x_ref[i, h, 0], g_ref[i, h]
            p = jnp.exp2(dot_nt(x_ref[j, h, 1], q) * factor - ls_ref[i, h])
            if diagonal:
                p = causal_fill(p, 0.0)
            dv = dot(p.astype(BF16), g)
            ds = (p * (dot_nt(x_ref[j, h, 2], g) - delta_ref[i])).astype(BF16)
            dk = dot(ds, q)
            dqt = dot(kt_ref[j], ds)
            return dv, dk, dqt

        def key_block(j):
            dv, dk, dqt = pair(j, j, True)
            if unrolled:
                dqt_ref[j] = dqt if j == 0 else dqt_ref[j] + dqt
            else:
                dqt_ref[j] = jnp.where(j == 0, 0.0, dqt_ref[j]) + dqt

            def step(i, state):
                dv, dk = state
                v, k, t = pair(i, j, False)
                if unrolled:
                    dqt_ref[i] = t if j == 0 else dqt_ref[i] + t
                else:
                    dqt_ref[i] = jnp.where(j == 0, 0.0, dqt_ref[i]) + t
                return dv + v, dk + k

            state = (dv, dk)
            if unrolled:
                for i in range(j + 1, n):
                    state = step(i, state)
            else:
                state = lax.fori_loop(j + 1, n, step, state)
            dv, dk = state
            out_ref[j, h, 0] = unrotated(dqt_ref[j].T, j)
            out_ref[j, h, 1] = unrotated(dk, j)
            out_ref[j, h, 2] = dv.astype(BF16)

        span(0, n, key_block, unrolled)


def attention_back(x, g, ot, ls, cos, sin):
    n, hp, _, rows, dim = x.shape
    pairs = n * (n + 1) // 2 * rows * rows * hp
    return pl.pallas_call(
        attention_back_kernel,
        name="attention_back",
        out_shape=jax.ShapeDtypeStruct(x.shape, BF16),
        scratch_shapes=[
            pltpu.VMEM((n, dim, rows), BF16),
            pltpu.VMEM((n, dim, rows), F32),
            pltpu.VMEM((n, 1, rows), F32),
        ],
        compiler_params=pltpu.CompilerParams(vmem_limit_bytes=40 << 20),
        cost_estimate=pl.CostEstimate(
            flops=pairs * dim * 20, bytes_accessed=x.size * 6, transcendentals=pairs
        ),
    )(x, g, ot, ls, cos, sin)


def seq_device(index):
    return {"seq": index}


def greet(peers):
    barrier = pltpu.get_barrier_semaphore()
    for device in peers:
        pl.semaphore_signal(barrier, inc=1, device_id=device, device_id_type=MESH)


def greeted(count):
    pl.semaphore_wait(pltpu.get_barrier_semaphore(), count)


def remote(src, dst, send, recv, device):
    return pltpu.make_async_remote_copy(
        src_ref=src,
        dst_ref=dst,
        send_sem=send,
        recv_sem=recv,
        device_id=device,
        device_id_type=MESH,
    )


def front_kernel(
    state_ref,
    embedded_ref,
    wa_ref,
    wq_ref,
    gain_ref,
    table_ref,
    resid_out,
    normed_out,
    att_out,
    x_out,
    ot_out,
    ls_out,
    ltn_out,
    ltj_out,
    wa,
    wq,
    joined,
    resid,
    normed,
    sent,
    x,
    vt,
    scores,
    ot,
    o_sent,
    att,
    ltn,
    ltj,
    table,
    load_sem,
    store_sem,
    send_sem,
    recv_sem,
    o_send_sem,
    o_recv_sem,
    l_send_sem,
    l_recv_sem,
):
    n, rows, width = HEADS, state_ref.shape[0], state_ref.shape[1]
    me = lax.axis_index("seq")
    dp = lax.axis_index("dp")
    peers = [seq_device((me + k) % n) for k in range(1, n)]
    across = [{"dp": flipped(0, dp)}, {"dp": flipped(1, dp)}]
    near = seq_device(flipped(0, me))
    greet(peers + across)
    loads = [
        pltpu.make_async_copy(state_ref, joined.at[0], load_sem.at[0]),
        pltpu.make_async_copy(wa_ref.at[pl.ds(0, width)], wa.at[0], load_sem.at[1]),
        pltpu.make_async_copy(embedded_ref, joined.at[1], load_sem.at[2]),
        pltpu.make_async_copy(wa_ref.at[pl.ds(width, width)], wa.at[1], load_sem.at[3]),
        pltpu.make_async_copy(wq_ref, wq, load_sem.at[4]),
        pltpu.make_async_copy(
            table_ref.at[pl.ds(pl.multiple_of(me * rows, 8), rows)], table, load_sem.at[5]
        ),
    ]
    for copy in loads:
        copy.start()
    tile = 256
    for half in range(2):
        loads[2 * half].wait()
        loads[2 * half + 1].wait()

        for begin in range(0, width, tile):
            cols = pl.ds(begin, tile)
            block = dot(joined[half], wa[half, :, cols])
            resid[:, cols] = block if half == 0 else resid[:, cols] + block
    normed[...] = mean_norm(resid[...], gain_ref[0:1, :].astype(F32)).astype(BF16)
    stores = [
        pltpu.make_async_copy(resid, resid_out, store_sem.at[0]),
        pltpu.make_async_copy(normed, normed_out, store_sem.at[1]),
    ]
    for copy in stores:
        copy.start()
    loads[4].wait()
    lefts = []

    def share(source, out, slot, device):
        k = len(lefts)
        copy = remote(source, out.at[slot], l_send_sem.at[k], l_recv_sem.at[k], device)
        copy.start()
        lefts.append(copy)
    loads[5].wait()
    cos, sin = table[:, 0 : HEAD_DIM // 2], table[:, HEAD_DIM // 2 : HEAD_DIM]
    pairs = n // 2
    order = [2, 1, 3, 0] if pairs == 4 else list(range(pairs - 1, -1, -1))
    sends = []
    for k in order:
        chip = (me // 2 + k) % pairs
        for part in range(3):
            cols = pl.ds(pl.multiple_of(part * width + chip * 2 * HEAD_DIM, 2 * HEAD_DIM), 2 * HEAD_DIM)
            block = dot(normed[...], wq[:, cols])
            for core in range(2):
                head = block[:, core * HEAD_DIM : (core + 1) * HEAD_DIM]
                if part < 2:
                    head = rotate(head, cos, sin)
                sent[2 * chip + core, part] = head.astype(BF16)
        if k == order[0]:
            greeted(n + 1)
        for core in range(2):
            owner = 2 * chip + core
            if k == 0:
                continue
            copy = remote(sent.at[owner], x.at[me], send_sem.at[owner], recv_sem.at[me], seq_device(owner))
            copy.start()
            sends.append(copy)
    mate = me + 1 - 2 * (me % 2)
    copy = remote(sent.at[mate], x.at[me], send_sem.at[mate], recv_sem.at[me], seq_device(mate))
    copy.start()
    sends.append(copy)
    x[me] = sent[me]
    transposed_into(normed, ltn)
    for half in range(2):
        transposed_into(joined.at[half], ltj.at[pl.ds(half * width, width)])
    stores.append(pltpu.make_async_copy(ltn, ltn_out.at[0], store_sem.at[4]))
    stores.append(pltpu.make_async_copy(ltj, ltj_out.at[0], store_sem.at[5]))
    for copy in stores[2:]:
        copy.start()
    share(ltn, ltn_out, 2, across[0])
    share(ltn, ltn_out, 4, across[1])
    share(ltj, ltj_out, 2, across[1])
    share(ltn, ltn_out, 1, near)
    share(ltj, ltj_out, 1, near)
    factor = SCORE_SCALE * LOG2E
    for i in range(n):

        @pl.when(me != i)
        def arrive():
            remote(sent.at[0], x.at[i], send_sem.at[0], recv_sem.at[i], seq_device(i)).wait_recv()

        vt[i] = x[i, 2].astype(F32).T.astype(BF16)
        q = x[i, 0]
        diag = causal_fill(dot_nt(x[i, 1], q), NEG)
        peak = jnp.max(diag, axis=0, keepdims=True)
        for j in range(i):
            block = dot_nt(x[j, 1], q)
            scores[j] = block
            peak = jnp.maximum(peak, jnp.max(block, axis=0, keepdims=True))
        shift = peak * factor
        p = jnp.exp2(diag * factor - shift)
        total = jnp.sum(p, axis=0, keepdims=True)
        acc = dot(vt[i], p.astype(BF16))
        for j in range(i):
            p = jnp.exp2(scores[j] * factor - shift)
            total = total + jnp.sum(p, axis=0, keepdims=True)
            acc = acc + dot(vt[j], p.astype(BF16))
        acc = acc / total
        ot[i] = acc
        o_sent[i] = acc.T.astype(BF16)
        ls_out[i] = shift + jnp.log2(total)
        mine = pl.ds(pl.multiple_of(me * HEAD_DIM, HEAD_DIM), HEAD_DIM)

        @pl.when(me != i)
        def give():
            remote(o_sent.at[i], att.at[:, mine], o_send_sem.at[i], o_recv_sem.at[me], seq_device(i)).start()

        @pl.when(me == i)
        def keep():
            att[:, mine] = o_sent[i]

    stores.append(pltpu.make_async_copy(x, x_out, store_sem.at[2]))
    stores.append(pltpu.make_async_copy(ot, ot_out, store_sem.at[3]))
    for copy in stores[4:]:
        copy.start()
    for k, out, slot in ((0, ltn_out, 2), (1, ltn_out, 4), (2, ltj_out, 2)):
        lefts[k].wait_recv()
        share(out.at[slot], out, slot + 1, near)
    for copy in sends:
        copy.wait_send()
    for i in range(n):

        @pl.when(me != i)
        def finish():
            cols = pl.ds(i * HEAD_DIM, HEAD_DIM)
            copy = remote(o_sent.at[i], att.at[:, cols], o_send_sem.at[i], o_recv_sem.at[i], seq_device(i))
            copy.wait_send()
            copy.wait_recv()

    att_out[...] = att[...]
    for copy in stores:
        copy.wait()
    for k, copy in enumerate(lefts):
        copy.wait_send()
        if k > 2:
            copy.wait_recv()


def front(state, embedded, w_adapt, w_qkv, gains, table):
    n = HEADS
    rows, width = state.shape
    hbm = pl.BlockSpec(memory_space=pl.ANY)
    vmem = pl.BlockSpec(memory_space=pltpu.VMEM)
    return pl.pallas_call(
        front_kernel,
        name="front",
        out_shape=(
            jax.ShapeDtypeStruct((rows, width), F32),
            jax.ShapeDtypeStruct((rows, width), BF16),
            jax.ShapeDtypeStruct((rows, width), BF16),
            jax.ShapeDtypeStruct((n, 3, rows, HEAD_DIM), BF16),
            jax.ShapeDtypeStruct((n, HEAD_DIM, rows), F32),
            jax.ShapeDtypeStruct((n, 1, rows), F32),
            jax.ShapeDtypeStruct((6, width, rows), BF16),
            jax.ShapeDtypeStruct((4, 2 * width, rows), BF16),
        ),
        in_specs=[hbm, hbm, hbm, hbm, vmem, hbm],
        out_specs=(hbm, hbm, vmem, hbm, hbm, vmem, hbm, hbm),
        scratch_shapes=[
            pltpu.VMEM((2, width, width), BF16),
            pltpu.VMEM((width, 3 * width), BF16),
            pltpu.VMEM((2, rows, width), BF16),
            pltpu.VMEM((rows, width), F32),
            pltpu.VMEM((rows, width), BF16),
            pltpu.VMEM((n, 3, rows, HEAD_DIM), BF16),
            pltpu.VMEM((n, 3, rows, HEAD_DIM), BF16),
            pltpu.VMEM((n, HEAD_DIM, rows), BF16),
            pltpu.VMEM((n, rows, rows), F32),
            pltpu.VMEM((n, HEAD_DIM, rows), F32),
            pltpu.VMEM((n, rows, HEAD_DIM), BF16),
            pltpu.VMEM((rows, width), BF16),
            pltpu.VMEM((width, rows), BF16),
            pltpu.VMEM((2 * width, rows), BF16),
            pltpu.VMEM((rows, HEAD_DIM), F32),
            pltpu.SemaphoreType.DMA((6,)),
            pltpu.SemaphoreType.DMA((6,)),
            pltpu.SemaphoreType.DMA((n,)),
            pltpu.SemaphoreType.DMA((n,)),
            pltpu.SemaphoreType.DMA((n,)),
            pltpu.SemaphoreType.DMA((n,)),
            pltpu.SemaphoreType.DMA((8,)),
            pltpu.SemaphoreType.DMA((8,)),
        ],
        compiler_params=pltpu.CompilerParams(
            collective_id=1, has_side_effects=True, vmem_limit_bytes=62 << 20
        ),
    )(state, embedded, w_adapt, w_qkv, gains, table)


def flipped(bit, value):
    return value + (1 - 2 * ((value // (1 << bit)) % 2)) * (1 << bit)


def unit_slots(first, dp):
    slots = []
    for q in range(4):
        turned = [(dp + q) % 2, (dp // 2 + q // 2) % 2]
        slots.append(turned[first] * 2 + turned[1 - first])
    return slots


def transposed_into(source, target):
    tile = 256
    for begin in range(0, source.shape[1], tile):
        target[pl.ds(begin, tile), :] = source[:, pl.ds(begin, tile)].T


def add_into(target, more):
    rows = target.shape[0]
    chunk = 16
    while rows % (chunk * 2) == 0 and chunk < 64:
        chunk *= 2

    def step(t, c):
        at = pl.ds(pl.multiple_of(t * chunk, chunk), chunk)
        target[at, :] = (target[at, :].astype(F32) + more[at, :].astype(F32)).astype(BF16)
        return c

    lax.fori_loop(0, rows // chunk, step, 0)


CHUNKS = ((0, 512), (512, 512), (1024, 384))


def z_place(z):
    return (z % 2) * 2 + z // 2


def transposed_blocks(source, target, first, last):
    tile = 256
    parts, size = target.shape[1], target.shape[2]
    for begin in range(first * tile, min(last * tile, source.shape[1]), tile):
        block = source[:, pl.ds(begin, tile)].T
        for k in range(begin // size, (begin + tile - 1) // size + 1):
            low, high = max(begin, size * k), min(begin + tile, size * (k + 1))
            target[k // parts, k % parts, pl.ds(low - size * k, high - low), :] = block[
                low - begin : high - begin
            ]


def middle_kernel(*refs):
    refs = list(refs)

    def take(count):
        taken, refs[:count] = refs[:count], []
        return taken

    (att_in, resid_in, cot_in, gain_rows, wo_in, wg_in, wu_in, wd_in) = take(8)
    (x_in, ot_in, ls_ref, table_in) = take(4)
    (layer_out, above_out, gains_out, packed_out) = take(4)
    (kept_d, kept_z, kept_g, kept_h, kept_o) = take(5)
    (wo, wg, wu, wd, att, cot, resid, branch, mid, down, above) = take(11)
    (normed, hidden, gate_by, up_by, down_low, wide_low, branch_low, dout) = take(8)
    (left_n, left_h, left_m, left_a, right_g, right_d, right_b) = take(7)
    (got_g, got_d, got_z) = take(3)
    (work, x, ot, table, g, kt, dqt, delta, dsent, packed) = take(10)
    (load_sem, store_sem, g_send, g_recv, d_send, d_recv, m_send, m_recv, s_send, s_recv) = take(10)
    n, (rows, width) = HEADS, resid.shape
    ff = wg.shape[1]
    half, part = ff // 2, width // 2
    me = lax.axis_index("seq")
    dp = lax.axis_index("dp")
    core = me % 2
    mate = flipped(0, me)
    bits = [dp % 2, dp // 2]
    near = seq_device(mate)
    across = [{"dp": flipped(0, dp)}, {"dp": flipped(1, dp)}]
    diagonal = [{"seq": mate, "dp": flipped(0, dp)}, {"seq": mate, "dp": flipped(1, dp)}]
    greet([seq_device((me + k) % n) for k in range(1, n)] + across + diagonal)
    loads = {}
    for key, src, dst in (
        ("att", att_in, att),
        ("wo", wo_in, wo),
        ("resid", resid_in, resid),
        ("wg", wg_in, wg),
        ("wu", wu_in, wu),
        ("cot", cot_in, cot),
        ("wd", wd_in, wd),
        ("x", x_in, x),
        ("ot", ot_in, ot),
        ("table", table_in, table),
    ):
        copy = pltpu.make_async_copy(src, dst, load_sem.at[len(loads)])
        copy.start()
        loads[key] = copy
    tile = 256
    gains = [gain_rows[k : k + 1, :].astype(F32) for k in range(4)]

    def tiles(total, body):
        for begin in range(0, total, tile):
            body(pl.ds(begin, tile))

    sends = []
    given = {}

    issued = []

    def give(key, src, dst, device):
        k = len(issued)
        copy = remote(src, dst, m_send.at[k], m_recv.at[k], device)
        copy.start()
        issued.append(key)
        sends.append(copy)
        given[key] = copy

    loads["att"].wait()
    loads["wo"].wait()

    def project(cols):
        branch[:, cols] = dot(att[...], wo[:, cols])

    tiles(width, project)
    loads["resid"].wait()
    mid[...] = resid[...] + mean_norm(branch[...], gains[1])
    normed[...] = mean_norm(mid[...], gains[2]).astype(BF16)
    transposed_into(normed, left_n.at[0])
    greeted(n + 3)
    give("n1", left_n.at[0], left_n.at[1], near)
    give("n2", left_n.at[0], left_n.at[2], across[0])
    loads["wg"].wait()
    loads["wu"].wait()

    def widen(cols):
        gate = dot(normed[...], wg[:, cols])
        up = dot(normed[...], wu[:, cols])
        bent = jax.nn.sigmoid(gate)
        silu = gate * bent
        hidden[:, cols] = (silu * up).astype(BF16)
        gate_by[:, cols] = (up * bent * (1.0 + gate * (1.0 - bent))).astype(BF16)
        up_by[:, cols] = silu.astype(BF16)

    tiles(ff, widen)
    loads["wd"].wait()

    steps = width // tile
    share = -(-ff // tile // steps)
    for k in range(steps):
        cols = pl.ds(k * tile, tile)
        down[:, cols] = dot(hidden[...], wd[:, cols])
        transposed_blocks(hidden, left_h, k * share, (k + 1) * share)
    give("h2", left_h.at[:, 1 - bits[1]], left_m.at[1], across[1])
    give("h1", left_h.at[:, bits[1]], left_m.at[0], near)
    loads["cot"].wait()
    grad, _ = norm_back(down[...], gains[3], cot[...].astype(F32))
    down_low[...] = grad.astype(BF16)
    mine_d = pl.ds(pl.multiple_of(core * part, 128), part)
    theirs_d = pl.ds(pl.multiple_of((1 - core) * part, 128), part)
    give("d2", down_low.at[:, mine_d], right_d.at[1], across[1])
    give("d3", down_low.at[:, theirs_d], right_d.at[2], diagonal[1])
    give("d1", down_low.at[:, theirs_d], right_d.at[0], near)

    def widen_back(cols):
        block = dot_nt(down_low[...], wd[cols, :])
        wide_low[0, :, cols] = (block * gate_by[:, cols].astype(F32)).astype(BF16)
        wide_low[1, :, cols] = (block * up_by[:, cols].astype(F32)).astype(BF16)

    tiles(ff, widen_back)

    def chunk_of(c, which_core, which_bit):
        at, wide = CHUNKS[c]
        return wide_low.at[which_core, :, pl.ds(pl.multiple_of(which_bit * half + at, 128), wide)]

    def give_chunk(c):
        at, wide = CHUNKS[c]
        cols = pl.ds(at, wide)
        give(("g2", c), chunk_of(c, core, 1 - bits[0]), right_g.at[1, :, cols], across[0])
        give(("g3", c), chunk_of(c, 1 - core, 1 - bits[0]), right_g.at[2, :, cols], diagonal[0])
        give(("g1", c), chunk_of(c, 1 - core, bits[0]), right_g.at[0, :, cols], near)

    give_chunk(0)

    def narrow_back(cols):
        above[:, cols] = dot_nt(wide_low[0], wg[cols, :]) + dot_nt(wide_low[1], wu[cols, :])

    tiles(width, narrow_back)
    grad, _ = norm_back(mid[...], gains[2], above[...])
    resid[...] = cot[...].astype(F32) + grad
    grad, _ = norm_back(branch[...], gains[1], resid[...])
    branch_low[...] = grad.astype(BF16)

    def project_back(cols):
        dout[:, cols] = dot_nt(branch_low[...], wo[cols, :]).astype(BF16)

    tiles(width, project_back)
    my_cols = pl.ds(pl.multiple_of(me * HEAD_DIM, HEAD_DIM), HEAD_DIM)
    for k in (4, 5, 3, 2, 6, 7, 1):
        owner = (me + k) % n
        cols = pl.ds(pl.multiple_of(owner * HEAD_DIM, HEAD_DIM), HEAD_DIM)
        copy = remote(dout.at[:, cols], g.at[me], g_send.at[owner], g_recv.at[me], seq_device(owner))
        copy.start()
        sends.append(copy)
    g[me] = dout[:, my_cols]
    given["n2"].wait_recv()
    give("n3", left_n.at[2], left_n.at[3], near)
    transposed_into(att, left_a.at[0])
    give("a1", left_a.at[0], left_a.at[1], near)
    give("b1", branch_low.at[:, theirs_d], right_b, near)
    layer_out[...] = (mid[...] + mean_norm(down[...], gains[3])).astype(BF16)
    stores = []

    def store(src, dst):
        copy = pltpu.make_async_copy(src, dst, store_sem.at[len(stores)])
        copy.start()
        stores.append(copy)

    store(resid, above_out)
    gains_out[...] = jnp.zeros_like(gains_out)
    gains_out[1:2, :] = gain_sum(branch[...], resid[...])
    gains_out[2:3, :] = gain_sum(mid[...], above[...])
    gains_out[3:4, :] = gain_sum(down[...], cot[...].astype(F32))
    seconds = {}
    z_low = (me // 2) % 2

    def wide_sum(c):
        at, wide = CHUNKS[c]
        for key in ("n1", "n3"):
            if key in given:
                given.pop(key).wait_recv()
        for key in ("g1", "g2", "g3"):
            given[key, c].wait_recv()
        shard = width // 32
        spread = [(bits[1] + other) % 2 for other in range(2)]
        own = chunk_of(c, core, bits[0])
        for begin in range(0, wide, 256):
            step = min(256, wide - begin)
            cols = pl.ds(at + begin, step)
            block = dot(left_n[0], own[:, pl.ds(begin, step)])
            for k in range(1, 4):
                block += dot(left_n[k], right_g[k - 1, :, cols])
            work[0:width, 0:step] = block
            for z in range(4):
                for other in range(2):
                    pieces = [
                        work[pl.ds((8 * z + 4 * c2 + 2 * other + b) * shard, shard), 0:step]
                        for c2 in range(2)
                        for b in range(2)
                    ]
                    place = pl.multiple_of(spread[other] * part + z_place(z) * 4 * shard, 16)
                    wg[pl.ds(place, 4 * shard), cols] = jnp.concatenate(pieces, axis=0).astype(BF16)
        cols = pl.ds(at, wide)
        if c == len(CHUNKS) - 1:
            store(wg.at[:, cols], kept_h)
            return
        seconds[c] = remote(
            wg.at[pl.ds(part, part), cols], got_g.at[:, cols], s_send.at[c], s_recv.at[c], across[1]
        )
        seconds[c].start()
        sends.append(seconds[c])

    def down_sum():
        for key in ("h1", "h3", "d1", "d2", "d3"):
            given[key].wait_recv()
        tall = ff // 4
        shard = ff // 32
        spread = [(bits[0] + other) % 2 for other in range(2)]
        for begin in range(0, part, 256):
            cols = pl.ds(begin, 256)
            own = down_low.at[:, mine_d]
            block = dot(left_h[:, bits[1]].reshape(2 * tall, rows), own[:, cols])
            for k in range(3):
                block += dot(left_m[k].reshape(2 * tall, rows), right_d[k, :, cols])
            work[...] = block
            for z in range(4):
                for other in range(2):
                    pieces = [
                        work[pl.ds((4 * z + 2 * c2 + other) * shard, shard), :] for c2 in range(2)
                    ]
                    place = pl.multiple_of(spread[other] * tall + z_place(z) * 2 * shard, 16)
                    wd[pl.ds(place, 2 * shard), cols] = jnp.concatenate(pieces, axis=0).astype(BF16)
            k = begin // 256
            seconds["d", k] = remote(
                wd.at[pl.ds(tall, tall), cols],
                got_d.at[:, cols],
                s_send.at[2 + k],
                s_recv.at[2 + k],
                across[0],
            )
            seconds["d", k].start()
            sends.append(seconds["d", k])

    def out_sum():
        given["a1"].wait_recv()
        given["b1"].wait_recv()
        shard = width // 32
        slots = unit_slots(0, dp)
        for begin in range(0, part, 256):
            cols = pl.ds(begin, 256)
            block = dot(left_a[0], branch_low.at[:, mine_d][:, cols])
            work[0:width, :] = block + dot(left_a[1], right_b[:, cols])
            for z in range(4):
                for q in range(4):
                    pieces = [
                        work[pl.ds((8 * z + 4 * c2 + q) * shard, shard), :] for c2 in range(2)
                    ]
                    place = pl.multiple_of(slots[q] * (width // 4) + z_place(z) * 2 * shard, 16)
                    wu[pl.ds(place, 2 * shard), cols] = jnp.concatenate(pieces, axis=0).astype(BF16)
        store(wu.at[:, pl.ds(0, part)], kept_o)

    loads["x"].wait()
    factor = SCORE_SCALE * LOG2E
    half_dim = HEAD_DIM // 2
    pairs = [(i, j) for j in range(n) for i in range(j, n)]
    across_blocks = ff // rows

    def probs(i, j):
        k = pairs.index((i, j))
        at, cols = k // across_blocks * rows, k % across_blocks * rows
        return wu.at[pl.ds(at, rows), pl.ds(cols, rows)]

    give_chunk(1)
    for j in range(n):
        kt[j] = x[j, 1].astype(F32).T.astype(BF16)
        for i in range(j, n):
            p = jnp.exp2(dot_nt(x[j, 1], x[i, 0]) * factor - ls_ref[i])
            if i == j:
                p = causal_fill(p, 0.0)
            probs(i, j)[...] = p.astype(BF16)
    give_chunk(2)
    loads["ot"].wait()
    loads["table"].wait()
    arrived, summed = set(), set()

    def upstream(i):
        if i not in arrived:
            arrived.add(i)

            @pl.when(me != i)
            def arrive():
                remote(g.at[0], g.at[i], g_send.at[0], g_recv.at[i], seq_device(i)).wait_recv()

            delta[i] = jnp.sum(g[i].astype(F32).T * ot[i], axis=0, keepdims=True)
        return g[i]

    def give_head(j, first, count, sem):
        span = pl.ds(first, count)

        @pl.when(me != j)
        def over():
            remote(
                dsent.at[j, span], packed.at[span, :, my_cols], d_send.at[sem], d_recv.at[sem - j + me], seq_device(j)
            ).start()

        @pl.when(me == j)
        def keep():
            packed[span, :, my_cols] = dsent[j, span]

    def unrotated(value, j):
        here = pl.ds(j * rows, rows)
        cos, sin = table[here, 0:half_dim], -table[here, half_dim:HEAD_DIM]
        return rotate(value * SCORE_SCALE, cos, sin).astype(BF16)

    order = [n - 1, n - 2, 0]
    for k in range(1, n // 2 - 1):
        order += [n - 2 - k, k]
    order += [n // 2 - 1]
    for j in order:
        dk = dv = None
        for i in range(j, n):
            up = upstream(i)
            p = probs(i, j)[...]
            v = dot(p, up)
            ds = (p.astype(F32) * (dot_nt(x[j, 2], up) - delta[i])).astype(BF16)
            k = dot(ds, x[i, 0])
            t = dot(kt[j], ds)
            dqt[i] = dqt[i] + t if i in summed else t
            summed.add(i)
            dv, dk = (v, k) if i == j else (dv + v, dk + k)
        dsent[j, 1] = unrotated(dk, j)
        dsent[j, 2] = dv.astype(BF16)
        give_head(j, 1, 2, j)
        if j < n // 2:
            dsent[j, 0] = unrotated(dqt[j].T, j)
            give_head(j, 0, 1, n + j)
        if j == 0:
            wide_sum(0)
        if j == 2:
            given["h2"].wait_recv()
            give("h3", left_m.at[1], left_m.at[2], near)
    for j in range(n // 2, n):
        dsent[j, 0] = unrotated(dqt[j].T, j)
        give_head(j, 0, 1, n + j)

    down_sum()
    wide_sum(1)
    wide_sum(2)
    out_sum()

    def finish_wide(c):
        at, wide = CHUNKS[c]
        cols = pl.ds(at, wide)
        seconds[c].wait_recv()
        add_into(wg.at[pl.ds(0, part), cols], got_g.at[:, cols])
        if c > 0:
            store(wg.at[pl.ds(0, part), cols], kept_g)
            return
        third[0].start()
        sends.append(third[0])

    def z_rows(which):
        return wg.at[pl.ds(pl.multiple_of(which * (part // 2), 16), part // 2), pl.ds(0, CHUNKS[0][1])]

    def finish_z():
        third[0].wait_recv()
        add_into(z_rows(z_low), got_z)
        store(z_rows(z_low), kept_z)

    third = [
        remote(z_rows(1 - z_low), got_z, s_send.at[4], s_recv.at[4], seq_device(flipped(1, me)))
    ]
    finish_wide(0)
    finish_wide(1)
    for k in range(part // 256):
        cols = pl.ds(256 * k, 256)
        seconds["d", k].wait_recv()
        mine = wd.at[pl.ds(0, ff // 4), cols]
        add_into(mine, got_d.at[:, cols])
        store(mine, kept_d.at[:, cols])
    finish_z()
    for first, count in ((1, 2), (0, 1)):
        span = pl.ds(first, count)
        for j in range(n):

            @pl.when(me != j)
            def finish():
                cols = pl.ds(j * HEAD_DIM, HEAD_DIM)
                sem = j if first == 1 else n + j
                copy = remote(
                    dsent.at[j, span], packed.at[span, :, cols], d_send.at[sem], d_recv.at[sem], seq_device(j)
                )
                copy.wait_send()
                copy.wait_recv()

    store(packed, packed_out)
    for copy in sends:
        copy.wait_send()
    for copy in stores:
        copy.wait()


def middle_block(att, resid, cot, gain_rows, w_out, w_gate, w_up, w_down, x, ot, ls, table):
    n = HEADS
    rows, width = resid.shape
    ff = w_gate.shape[1]
    half, part = ff // 2, width // 2
    hbm = pl.BlockSpec(memory_space=pl.ANY)
    vmem = pl.BlockSpec(memory_space=pltpu.VMEM)
    dma = pltpu.SemaphoreType.DMA
    low = pltpu.VMEM((rows, width), BF16)
    wide = pltpu.VMEM((rows, ff), BF16)
    full = pltpu.VMEM((rows, width), F32)
    scratch = [pltpu.VMEM(w.shape, BF16) for w in (w_out, w_gate, w_up, w_down)]
    scratch += [low, low, full, full, full, full, full]
    scratch += [low, wide, wide, wide, low, pltpu.VMEM((2, rows, ff), BF16), low, low]
    scratch += [
        pltpu.VMEM((4, width, rows), BF16),
        pltpu.VMEM((8, 2, ff // 16, rows), BF16),
        pltpu.VMEM((3, 8, ff // 16, rows), BF16),
        pltpu.VMEM((2, width, rows), BF16),
        pltpu.VMEM((3, rows, half), BF16),
        pltpu.VMEM((3, rows, part), BF16),
        pltpu.VMEM((rows, part), BF16),
        pltpu.VMEM((part, CHUNKS[-1][0]), BF16),
        pltpu.VMEM((ff // 4, part), BF16),
        pltpu.VMEM((part // 2, CHUNKS[0][1]), BF16),
        pltpu.VMEM((half, 256), F32),
        pltpu.VMEM(x.shape, BF16),
        pltpu.VMEM(ot.shape, F32),
        pltpu.VMEM(table.shape, F32),
        pltpu.VMEM((n, rows, HEAD_DIM), BF16),
        pltpu.VMEM((n, HEAD_DIM, rows), BF16),
        pltpu.VMEM((n, HEAD_DIM, rows), F32),
        pltpu.VMEM((n, 1, rows), F32),
        pltpu.VMEM((n, 3, rows, HEAD_DIM), BF16),
        pltpu.VMEM((3, rows, width), BF16),
        dma((10,)),
        dma((8,)),
        dma((n,)),
        dma((n,)),
        dma((2 * n,)),
        dma((2 * n,)),
        dma((20,)),
        dma((20,)),
        dma((5,)),
        dma((5,)),
    ]
    return pl.pallas_call(
        middle_kernel,
        name="middle",
        out_shape=[
            jax.ShapeDtypeStruct((rows, width), BF16),
            jax.ShapeDtypeStruct((rows, width), F32),
            jax.ShapeDtypeStruct((8, width), F32),
            jax.ShapeDtypeStruct((3, rows, width), BF16),
            jax.ShapeDtypeStruct((ff // 4, part), BF16),
            jax.ShapeDtypeStruct((part // 2, CHUNKS[0][1]), BF16),
            jax.ShapeDtypeStruct((part, CHUNKS[1][1]), BF16),
            jax.ShapeDtypeStruct((width, CHUNKS[-1][1]), BF16),
            jax.ShapeDtypeStruct((width, part), BF16),
        ],
        in_specs=[hbm] * 3 + [vmem] + [hbm] * 6 + [vmem] + [hbm],
        out_specs=[vmem, hbm, vmem, hbm] + [hbm] * 5,
        scratch_shapes=scratch,
        compiler_params=pltpu.CompilerParams(
            collective_id=2, has_side_effects=True, vmem_limit_bytes=62 << 20
        ),
    )(att, resid, cot, gain_rows, w_out, w_gate, w_up, w_down, x, ot, ls, table)


BEGUN = ((1, 0, 512, None), (2, 0, 512, None), (0, 0, 256, None), (0, 256, 256, None), (3, 0, 384, 1))
FRESH = ((1, 0, 0), (1, 1024, 0), (1, 2048, 1), (0, 0, 1))
SCHEDULE = (
    ("S", 4), ("2", 0), ("F", 5), ("1", 3), ("P", 0), ("1", 1), ("D", 3), ("2", 3),
    ("E", 0), ("U", 9), ("O", 0), ("U", 7), ("C", 4), ("G", 0), ("E", 3), ("B", 5),
    ("1", 2), ("S", 5), ("D", 1), ("2", 1), ("W", 9), ("S", 9), ("1", 4), ("W", 7),
    ("S", 7), ("D", 2), ("G", 1), ("2", 2), ("C", 5), ("E", 1), ("1", 5), ("D", 4),
    ("G", 2), ("2", 4), ("U", 8), ("E", 2), ("C", 7), ("1", 7), ("D", 5), ("G", 3),
    ("U", 6), ("2", 5), ("C", 9), ("1", 9), ("E", 4), ("D", 7), ("G", 4), ("2", 7),
    ("W", 8), ("E", 5), ("S", 8), ("W", 6), ("S", 6), ("E", 7), ("D", 9), ("2", 9),
    ("C", 8), ("1", 8), ("C", 6), ("1", 6), ("E", 9), ("D", 8), ("2", 8), ("D", 6),
    ("2", 6), ("E", 8), ("E", 6),
)


def dealt_blocks(left, slots, right, spread, bit, out, work):
    total = left.shape[1]
    shard = total // 32
    block = dot(left[slots[0]], right[0])
    for k in range(1, 4):
        block += dot(left[slots[k]], right[k])
    work[0:total, :] = block
    for z in range(4):
        for other in range(2):
            pieces = []
            for core in range(2):
                for b in range(2):
                    q = (b << bit) | (other << (1 - bit))
                    pieces.append(work[pl.ds((8 * z + 4 * core + q) * shard, shard), :])
            out[spread[other], pl.ds(z_place(z) * 4 * shard, 4 * shard), :] = jnp.concatenate(
                pieces, axis=0
            ).astype(BF16)


def tail_kernel(*refs):
    refs = list(refs)

    def take(count):
        taken, refs[:count] = refs[:count], []
        return taken

    begun, fresh = len(BEGUN), len(FRESH)
    single = begun
    first_fresh = begun + 1
    count = first_fresh + fresh
    kept_in = take(5)
    packed_in, ltn_in, ltj_in, wq_in, wa_in = take(5)
    resid_in, above_in, gain_rows, gain_parts = take(4)
    grad_joined = take(2)
    outs_to = take(5)
    (gains_out,) = take(1)
    held = take(3)
    sums, arrived2 = [None] * 4 + take(count - 4), [None] * 4 + take(count - 4)
    parts, arrived3, arrived4, finals = take(count), take(count), take(count), take(count)
    (got_o, wq, wa, packed, ltn, ltj, dealt, low, work, back_sum, gain_buf, gain_got) = take(12)
    (resid, above, joined_0, joined_1) = take(4)
    outs = take(5)
    joined = (joined_0, joined_1)
    (load_sem, u_send, u_recv, s_send, s_recv, z1_send, z1_recv) = take(7)
    (z2_send, z2_recv, c_send, c_recv, gain_send, gain_recv, store_sem) = take(7)
    rows, width = resid.shape
    me = lax.axis_index("seq")
    dp = lax.axis_index("dp")
    core = me % 2
    bits = [dp % 2, dp // 2]
    z_low, z_high = (me // 2) % 2, me // 4
    mate = flipped(0, me)
    near = seq_device(mate)
    across = [{"dp": flipped(0, dp)}, {"dp": flipped(1, dp)}]
    diagonal = [{"seq": mate, "dp": flipped(0, dp)}, {"seq": mate, "dp": flipped(1, dp)}]
    beside = [seq_device(flipped(1, me)), seq_device(flipped(2, me))]
    greet([near] + across + diagonal + beside)
    loads = {}

    def load(key, src, dst):
        loads[key] = pltpu.make_async_copy(src, dst, load_sem.at[len(loads)])
        loads[key].start()

    load("packed", packed_in, packed)
    load("wq", wq_in, wq)
    load("resid", resid_in, resid)
    load("above", above_in, above)
    greeted(7)
    sends = []

    def send(src, dst, send_sem, recv_sem, device):
        copy = remote(src, dst, send_sem, recv_sem, device)
        copy.start()
        sends.append(copy)
        return copy

    first, dealing, second, third, fourth, finished, taken = [], {}, {}, {}, {}, {}, set()

    def ready(key):
        if key not in taken:
            taken.add(key)
            loads[key].wait()

    def z_rows(u, which):
        tall = finals[u].shape[0]
        return pl.ds(pl.multiple_of(which * 2 * tall, 16), 2 * tall)

    def one_z(u, which):
        tall = finals[u].shape[0]
        return pl.ds(pl.multiple_of(which * tall, 16), tall)

    def start_first(u):
        first.append(send(kept_in[4].at[pl.ds(2, 2)], got_o, s_send.at[count], s_recv.at[count], across[0]))

    def take_first(u):
        first[0].wait_recv()
        ready(single)
        for k in (1, 0):
            add_into(sums[single].at[k], got_o.at[k])

    def start_columns(u):
        k = u - first_fresh
        bit = FRESH[k][2]
        source = low if k == 3 else packed.at[k]
        if k < 3:
            ready("packed")

        def columns(other_core, other_bit):
            place = (core + (1 - 2 * core) * other_core) * 2
            place = place + bits[bit] + (1 - 2 * bits[bit]) * other_bit
            return pl.ds(pl.multiple_of(place * 256, 256), 256)

        dealing[u] = [
            send(
                source.at[:, columns(*there)],
                dealt.at[k, slot],
                u_send.at[3 * k + slot - 1],
                u_recv.at[3 * k + slot - 1],
                device,
            )
            for there, slot, device in (
                ((0, 1), 2, across[bit]),
                ((1, 1), 3, diagonal[bit]),
                ((1, 0), 1, near),
            )
        ]
        dealt[k, 0] = source[:, columns(0, 0)]

    def start_second(u):
        if u < begun:
            array, at, wide, bit = BEGUN[u]
            rows_in = kept_in[array].shape[0] // 2
            src = kept_in[array].at[pl.ds(rows_in, rows_in), pl.ds(at, wide)]
        else:
            bit = 1 if u == single else 1 - FRESH[u - first_fresh][2]
            src = sums[u].at[1]
        second[u] = send(src, arrived2[u], s_send.at[u], s_recv.at[u], across[bit])

    def multiply(u):
        k = u - first_fresh
        out, column, bit = FRESH[k]
        slots = (0, 1, 2, 3) if (bit == 0 or k == 3) else (0, 1, 4, 5)
        left = ltj if k == 3 else ltn
        ready("ltj" if k == 3 else "ltn")
        for copy in dealing[u]:
            copy.wait_recv()
        spread = [(bits[1 - bit] + other) % 2 for other in range(2)]
        dealt_blocks(left, slots, dealt.at[k], spread, bit, sums[u], work)

    def take_second(u):
        second[u].wait_recv()
        if u < begun:
            ready(u)
        add_into(sums[u].at[0], arrived2[u])

    def start_third(u):
        theirs = z_rows(u, 1 - z_low)
        if u < 4:
            array, at, wide, _ = BEGUN[u]
            src = kept_in[array].at[theirs, pl.ds(at, wide)]
        else:
            src = sums[u].at[0, theirs]
        third[u] = send(src, arrived3[u], z1_send.at[u], z1_recv.at[u], beside[0])

    def take_third(u):
        third[u].wait_recv()
        if u < 4:
            array, at, wide, _ = BEGUN[u]
            ready(array)
            mine = held[array][:, pl.ds(at, wide)]
        else:
            mine = sums[u][0, z_rows(u, z_low), :]
        parts[u][...] = (mine.astype(F32) + arrived3[u][...].astype(F32)).astype(BF16)

    def start_fourth(u):
        source = kept_in[1] if u == 0 else parts[u]
        fourth[u] = send(
            source.at[one_z(u, 1 - z_high)], arrived4[u], z2_send.at[u], z2_recv.at[u], beside[1]
        )

    def take_fourth(u):
        fourth[u].wait_recv()
        if u == 0:
            ready(1)
        source = held[1] if u == 0 else parts[u]
        finals[u][...] = source[one_z(u, z_high), :].astype(F32) + arrived4[u][...].astype(F32)
        if u in (0, 1, 4):
            at, wide = CHUNKS[min(u, 2)]
            bit = 0
            cols = pl.ds(pl.multiple_of(bits[0] * (outs[3].shape[2] // 2) + at, 128), wide)
            target = outs[3].at[core, :, cols]
        elif u <= single:
            out, at, wide = (2, 0, width // 2) if u == single else (4,) + BEGUN[u][1:3]
            bit = None
            target = outs[out].at[:, pl.ds(pl.multiple_of(core * (width // 2) + at, 128), wide)]
        else:
            out, column, bit = FRESH[u - first_fresh]
            cols = pl.ds(pl.multiple_of((core * 2 + bits[bit]) * 256 + column, 256), 256)
            target = outs[out].at[:, cols]
        if bit is None:
            owners = [(core, None), (1 - core, near)]
        else:
            here, there = bits[bit], 1 - bits[bit]
            owners = [
                (core * 2 + here, None),
                ((1 - core) * 2 + here, near),
                (core * 2 + there, across[bit]),
                ((1 - core) * 2 + there, diagonal[bit]),
            ]
        shard = finals[u].shape[0] // len(owners)
        finished[u] = []
        for k, (place, device) in enumerate(owners):
            at = pl.ds(pl.multiple_of(place * shard, 8), shard)
            if k == 0:
                target[...] = finals[u][at, :]
            else:
                sem = 3 * u + k - 1
                finished[u].append(
                    send(finals[u].at[at], target, c_send.at[sem], c_recv.at[sem], device)
                )

    gain_steps = {}
    gain_partners = [near] + across + beside

    def send_gain(k):
        gain_steps[k] = send(
            gain_buf.at[k], gain_got.at[k], gain_send.at[k], gain_recv.at[k], gain_partners[k]
        )

    def add_gain(k):
        gain_steps[k].wait_recv()
        total = gain_buf[k] + gain_got[k]
        if k == 4:
            gains_out[...] = total
        else:
            gain_buf[k + 1] = total
            send_gain(k + 1)

    tile = 256
    stores = []

    def dense_back(_):
        ready("packed")
        ready("wq")
        load(1, kept_in[1], held[1])
        load(2, kept_in[2].at[z_rows(1, z_low)], held[2])
        load(0, kept_in[0].at[z_rows(2, z_low)], held[0])
        load(single, kept_in[4].at[pl.ds(0, 2)], sums[single])
        load(4, kept_in[3].at[pl.ds(0, kept_in[3].shape[0] // 2)], sums[4].at[0])
        load("ltn", ltn_in, ltn)
        load("ltj", ltj_in, ltj)
        load("wa", wa_in, wa)
        for begin in range(0, width, tile):
            at = pl.ds(begin, tile)
            block = dot_nt(packed[0], wq[at, pl.ds(0, width)])
            block += dot_nt(packed[1], wq[at, pl.ds(width, width)])
            block += dot_nt(packed[2], wq[at, pl.ds(2 * width, width)])
            back_sum[:, at] = block
        ready("resid")
        ready("above")
        part, gain0 = norm_back(resid[...], gain_rows[0:1, :].astype(F32), back_sum[...])
        low[...] = (above[...] + part).astype(BF16)
        gain_buf[0] = gain_parts[...]
        gain_buf[0, 0:1, :] = gain0[None, :]
        send_gain(0)

    def dense_out(_):
        ready("wa")
        for k in range(2):
            for begin in range(0, width, tile):
                from_row = pl.ds(k * width + begin, tile)
                joined[k][:, pl.ds(begin, tile)] = dot_nt(low[...], wa[from_row, :])
            stores.append(pltpu.make_async_copy(joined[k], grad_joined[k], store_sem.at[k]))
            stores[k].start()

    actions = {
        "F": start_first,
        "B": take_first,
        "U": start_columns,
        "S": start_second,
        "1": start_third,
        "2": start_fourth,
        "W": multiply,
        "C": take_second,
        "D": take_third,
        "E": take_fourth,
        "G": add_gain,
        "P": dense_back,
        "O": dense_out,
    }
    for action, u in SCHEDULE:
        actions[action](u)
    for out, units in ((3, (0, 1, 4)), (4, (2, 3)), (2, (5,)), (1, (6, 7, 8)), (0, (9,))):
        for u in units:
            for copy in finished[u]:
                copy.wait_recv()
        stores.append(pltpu.make_async_copy(outs[out], outs_to[out], store_sem.at[2 + out]))
        stores[-1].start()
    for copy in sends:
        copy.wait_send()
    for copy in stores:
        copy.wait()


def tail(kept, packed, left_n, left_j, w_qkv, w_adapt, resid, above, gain_rows, gain_parts):
    rows, width = resid.shape
    hbm = pl.BlockSpec(memory_space=pl.ANY)
    vmem = pl.BlockSpec(memory_space=pltpu.VMEM)
    dma = pltpu.SemaphoreType.DMA
    fresh = len(FRESH)
    down, gate, gate_next, last, out = kept
    left_over = (4, 2, 4, 8)
    every = [(kept[array].shape[0] // left_over[array], wide) for array, _, wide, _ in BEGUN]
    every += [(out.shape[1] // 4, out.shape[2])]
    every += [(width // 8, 256)] * 3 + [(width // 4, 256)]
    count = len(every)
    slots = [1] + [2] * (1 + fresh)
    shapes = [
        (2 * width // 32, width),
        (width // 32, 3 * width),
        (width // 32, width),
        (2, width // 32, 2 * (gate.shape[1] + gate_next.shape[1] + last.shape[1])),
        (down.shape[0] // 8, width),
    ]
    scratch = [
        pltpu.VMEM(shape, BF16)
        for shape in (
            (down.shape[0] // 2, down.shape[1]),
            gate.shape,
            (gate_next.shape[0] // 2, gate_next.shape[1]),
        )
    ]
    scratch += [pltpu.VMEM((k, 4 * tall, wide), BF16) for k, (tall, wide) in zip(slots, every[4:])]
    scratch += [pltpu.VMEM((4 * tall, wide), BF16) for tall, wide in every[4:]]
    scratch += [pltpu.VMEM((2 * tall, wide), BF16) for tall, wide in every]
    scratch += [pltpu.VMEM((2 * tall, wide), BF16) for tall, wide in every]
    scratch += [pltpu.VMEM((tall, wide), BF16) for tall, wide in every]
    scratch += [pltpu.VMEM((tall, wide), F32) for tall, wide in every]
    scratch += [
        pltpu.VMEM((2,) + out.shape[1:], BF16),
        pltpu.VMEM(w_qkv.shape, BF16),
        pltpu.VMEM(w_adapt.shape, BF16),
        pltpu.VMEM(packed.shape, BF16),
        pltpu.VMEM(left_n.shape, BF16),
        pltpu.VMEM(left_j.shape, BF16),
        pltpu.VMEM((4, 4, rows, 256), BF16),
        pltpu.VMEM((rows, width), BF16),
        pltpu.VMEM((2 * width, 256), F32),
        pltpu.VMEM((rows, width), F32),
        pltpu.VMEM((5, 8, width), F32),
        pltpu.VMEM((5, 8, width), F32),
    ]
    scratch += [pltpu.VMEM((rows, width), F32) for _ in range(4)]
    scratch += [pltpu.VMEM(shape, F32) for shape in shapes]
    scratch += [dma((14,)), dma((3 * fresh,)), dma((3 * fresh,))]
    scratch += [dma((count + 1,)) for _ in range(2)]
    scratch += [dma((count,)) for _ in range(4)]
    scratch += [dma((3 * count,)) for _ in range(2)]
    scratch += [dma((5,)) for _ in range(2)] + [dma((7,))]
    return pl.pallas_call(
        tail_kernel,
        name="tail",
        out_shape=[jax.ShapeDtypeStruct((rows, width), F32)] * 2
        + [jax.ShapeDtypeStruct(shape, F32) for shape in shapes]
        + [jax.ShapeDtypeStruct((8, width), F32)],
        in_specs=[hbm] * 12 + [vmem] * 2,
        out_specs=[hbm] * 7 + [vmem],
        scratch_shapes=scratch,
        compiler_params=pltpu.CompilerParams(
            collective_id=3, has_side_effects=True, vmem_limit_bytes=62 << 20
        ),
    )(*kept, packed, left_n, left_j, w_qkv, w_adapt, resid, above, gain_rows, gain_parts)


def finish_kernel(*refs):
    sources, gain_ref, targets, gain_out = refs[:8], refs[8], refs[9:18], refs[18]
    for source, target in zip(sources[:6], targets[:6]):
        target[...] = source[...]
    targets[6][...] = sources[6][0]
    targets[7][...] = sources[6][1]
    targets[8][...] = sources[7][...]

    @pl.when(pl.program_id(0) == 0)
    def pick_gains():
        share = gain_out.shape[1]
        at = (lax.axis_index("seq") * lax.axis_size("dp") + lax.axis_index("dp")) * share
        block = gain_ref[:, pl.ds(pl.multiple_of(at // 128 * 128, 128), 128)]
        here = lax.broadcasted_iota(jnp.int32, (128, share), 0) - at % 128
        picked = here == lax.broadcasted_iota(jnp.int32, (128, share), 1)
        gain_out[...] = lax.dot_general(
            block,
            picked.astype(F32),
            (((1,), (0,)), ((), ())),
            precision=lax.Precision.HIGHEST,
            preferred_element_type=F32,
        )[:4]


def finish(*values):
    steps = 2
    wide, gains = values[6], values[8]
    share = gains.shape[1] // (lax.axis_size("seq") * lax.axis_size("dp"))
    like = list(values[:6]) + [wide[0], wide[1], values[7]]

    def columns(shape):
        lead = len(shape) - 1
        return pl.BlockSpec(shape[:-1] + (shape[-1] // steps,), lambda i: (0,) * lead + (i,))

    return pl.pallas_call(
        finish_kernel,
        name="finish",
        grid=(steps,),
        out_shape=[jax.ShapeDtypeStruct(value.shape, value.dtype) for value in like]
        + [jax.ShapeDtypeStruct((4, share), F32)],
        in_specs=[columns(value.shape) for value in values[:8]]
        + [pl.BlockSpec(gains.shape, lambda i: (0, 0))],
        out_specs=[columns(value.shape) for value in like]
        + [pl.BlockSpec((4, share), lambda i: (0, 0))],
        compiler_params=pltpu.CompilerParams(vmem_limit_bytes=62 << 20),
    )(*values)


def xor_permute(value, axis, mask):
    return lax.ppermute(value, axis, [(i, i ^ mask) for i in range(lax.axis_size(axis))])


def quadrants(left):
    n, parts = lax.axis_size("seq"), lax.axis_size("dp")
    tokens, rows = left.shape
    shard = rows // (n * parts)
    split = left.reshape(tokens, n, parts, shard).transpose(2, 0, 1, 3)
    split = split.reshape(parts, tokens, n * shard)
    me = lax.axis_index("dp")
    return jnp.concatenate(
        [lax.dynamic_index_in_dim(split, me ^ m, 0, keepdims=True) for m in range(parts)]
    )


def other_core(left, right):
    core = lax.axis_index("seq") % 2
    half = right.shape[1] // 2
    mine = lax.dynamic_slice_in_dim(right, core * half, half, 1)
    theirs = lax.dynamic_slice_in_dim(right, (1 - core) * half, half, 1)
    left_in = xor_permute(left, "seq", 1)
    right_in = xor_permute(theirs, "seq", 1)
    return jnp.concatenate([left, left_in], axis=1), jnp.concatenate([mine, right_in], axis=0)


def scattered_sum(left, right, bits):
    n, parts = lax.axis_size("seq"), lax.axis_size("dp")
    cols = right.shape[1]
    left, right = other_core(quadrants(left), right)
    got = {}
    masks = list(range(parts))
    for bit in bits:
        outgoing = [m for m in masks if m >> bit & 1]
        masks = [m for m in masks if not m >> bit & 1]
        blocks = []
        for m in outgoing:
            block = dot_tn(left[m], right)
            for more in got.get(m, ()):
                block = block + more.astype(F32)
            blocks.append(block.astype(BF16))
        incoming = xor_permute(jnp.stack(blocks), "dp", 1 << bit)
        for k, m in enumerate(outgoing):
            got.setdefault(m ^ (1 << bit), []).append(incoming[k])
    block = dot_tn(left[0], right)
    for more in got.get(0, ()):
        block = block + more.astype(F32)
    shard = block.shape[0] // n
    block = block.astype(BF16).reshape(n, shard, cols // 2)
    block = lax.all_to_all(block, "seq", 0, 0)
    block = jnp.sum(block.reshape(n // 2, 2, shard, cols // 2).astype(F32), axis=0)
    return block.transpose(1, 0, 2).reshape(shard, cols)


def small_sum(value):
    value = value.reshape(value.shape[0], -1, value.shape[1])
    for axis in ("seq", "dp"):
        size = lax.axis_size(axis)
        me = lax.axis_index(axis)
        for bit in reversed(range(size.bit_length() - 1)):
            half = value.shape[2] // 2
            mine = (me >> bit) & 1
            kept = lax.dynamic_slice_in_dim(value, mine * half, half, 2)
            sent = lax.dynamic_slice_in_dim(value, (1 - mine) * half, half, 2)
            value = kept + xor_permute(sent, axis, 1 << bit)
    return value[:, 0]


def local(state, embedded, cotangent, w_adapt, w_qkv, w_out, w_gate, w_up, w_down, gains):
    seq_count, rows, width = state.shape
    n, parts = lax.axis_size("seq"), lax.axis_size("dp")
    tokens = seq_count * rows
    me = lax.axis_index("seq")
    bits = list(range(parts.bit_length() - 1))
    copies = max(1, n // HEADS)
    held = max(1, HEADS // n)
    owners = n // copies
    cos_np, sin_np = angle_tables(n * rows)
    cos_all, sin_all = jnp.asarray(cos_np), jnp.asarray(sin_np)
    cos = lax.dynamic_slice_in_dim(cos_all, me * rows, rows, 0)[:, None, :]
    sin = lax.dynamic_slice_in_dim(sin_all, me * rows, rows, 0)[:, None, :]
    gain_rows = gains.astype(F32)
    state, embedded = state.reshape(tokens, width), embedded.reshape(tokens, width)

    def to_heads(flat):
        return flat.reshape(tokens, HEADS, HEAD_DIM)

    def to_owner(parts_in):
        sent = jnp.stack(parts_in).reshape(len(parts_in), tokens, owners, held, HEAD_DIM)
        sent = sent.transpose(2, 3, 0, 1, 4)
        if copies > 1:
            sent = jnp.repeat(sent, copies, axis=0)
        return lax.all_to_all(sent, "seq", 0, 0)

    def from_owner(value):
        back = lax.all_to_all(value, "seq", 0, 0)[::copies]
        back = back.reshape(HEADS, -1, tokens, HEAD_DIM)
        return back.transpose(2, 1, 0, 3).reshape(tokens, -1)

    table = jnp.asarray(np.concatenate([cos_np, sin_np], axis=1))
    if n == HEADS and seq_count == 1 and parts == 4:
        resid, normed, attended, qkv, attended_t, logsum, left_n, left_j = front(
            state, embedded, w_adapt, w_qkv, gains, table
        )
        qkv, attended_t, logsum = qkv[:, None], attended_t[:, None], logsum[:, None]
    else:
        resid = dot(state, w_adapt[:width]) + dot(embedded, w_adapt[width:])
        normed = mean_norm(resid, gain_rows[0]).astype(BF16)
        packed = dot(normed, w_qkv)
        queries = rotate(to_heads(packed[:, :width]), cos, sin).astype(BF16)
        keys = rotate(to_heads(packed[:, width : 2 * width]), cos, sin).astype(BF16)
        values = to_heads(packed[:, 2 * width :]).astype(BF16)
        qkv = to_owner((queries, keys, values))
        attended, attended_t, logsum = attention(qkv)
        attended = from_owner(attended[:, :, None])
    shape = (seq_count, rows, width)
    if n == HEADS and parts == 4 and seq_count == 1:
        layer_out, middle_grad, gain_parts, packed_low, *kept = middle_block(
            attended,
            resid,
            cotangent.reshape(tokens, width),
            gains,
            w_out,
            w_gate,
            w_up,
            w_down,
            qkv[:, 0],
            attended_t[:, 0],
            logsum[:, 0],
            table,
        )
        grad_state, grad_embedded, grad_adapt, grad_qkv, grad_out, grad_wide, grad_down, gains_sum = tail(
            kept[:4] + [kept[4].reshape(4, width // 4, width // 2)],
            packed_low,
            left_n,
            left_j,
            w_qkv,
            w_adapt,
            resid,
            middle_grad,
            gains,
            gain_parts,
        )
        outs = finish(
            layer_out,
            grad_state,
            grad_embedded,
            grad_adapt,
            grad_qkv,
            grad_out,
            grad_wide,
            grad_down,
            gains_sum,
        )
        return tuple(value.reshape(shape) for value in outs[:3]) + tuple(outs[3:])
    branch = dot(attended, w_out)
    middle = resid + mean_norm(branch, gain_rows[1])
    normed_mid = mean_norm(middle, gain_rows[2]).astype(BF16)
    gate_pre = dot(normed_mid, w_gate)
    up_pre = dot(normed_mid, w_up)
    sigmoid_gate = jax.nn.sigmoid(gate_pre)
    silu_gate = gate_pre * sigmoid_gate
    hidden = (silu_gate * up_pre).astype(BF16)
    down_out = dot(hidden, w_down)
    layer_out = middle + mean_norm(down_out, gain_rows[3])
    out_grad = cotangent.astype(F32).reshape(tokens, width)
    down_grad, gain_grad3 = norm_back(down_out, gain_rows[3], out_grad)
    down_low = down_grad.astype(BF16)
    hidden_grad = dot_nt(down_low, w_down)
    gate_low = (
        hidden_grad * up_pre * sigmoid_gate * (1.0 + gate_pre * (1.0 - sigmoid_gate))
    ).astype(BF16)
    up_low = (hidden_grad * silu_gate).astype(BF16)
    mid_norm_grad = dot_nt(gate_low, w_gate) + dot_nt(up_low, w_up)
    middle_part, gain_grad2 = norm_back(middle, gain_rows[2], mid_norm_grad)
    middle_grad = out_grad + middle_part
    branch_grad, gain_grad1 = norm_back(branch, gain_rows[1], middle_grad)
    branch_low = branch_grad.astype(BF16)
    attended_grad = dot_nt(branch_low, w_out).astype(BF16)
    upstream = to_owner((to_heads(attended_grad),))[:, :, 0]
    packed_grad = attention_back(qkv, upstream, attended_t, logsum, cos_all, sin_all)
    packed_low = from_owner(packed_grad)
    normed_grad = dot_nt(packed_low, w_qkv)
    resid_part, gain_grad0 = norm_back(resid, gain_rows[0], normed_grad)
    resid_low = (middle_grad + resid_part).astype(BF16)
    grad_state = dot_nt(resid_low, w_adapt[:width])
    grad_embedded = dot_nt(resid_low, w_adapt[width:])
    flipped = bits[::-1]
    joined = jnp.concatenate([state, embedded], axis=-1)
    grad_down = scattered_sum(hidden, down_low, bits)
    grad_gate = scattered_sum(normed_mid, gate_low, flipped)
    grad_up = scattered_sum(normed_mid, up_low, bits)
    grad_out = scattered_sum(attended, branch_low, flipped)
    grad_qkv = scattered_sum(normed, packed_low, flipped)
    grad_adapt = scattered_sum(joined, resid_low, bits)
    grad_gains = jnp.stack([gain_grad0, gain_grad1, gain_grad2, gain_grad3])
    grad_gains = small_sum(grad_gains)
    return (
        layer_out.reshape(shape).astype(BF16),
        grad_state.reshape(shape),
        grad_embedded.reshape(shape),
        grad_adapt,
        grad_qkv,
        grad_out,
        grad_gate,
        grad_up,
        grad_down,
        grad_gains,
    )


def solution(mesh):
    tokens = P("dp", "seq", None)
    rows = P(("seq", "dp"), None)
    return jax.shard_map(
        local,
        mesh=mesh,
        in_specs=(tokens,) * 3 + (P(),) * 7,
        out_specs=(tokens,) * 3 + (rows,) * 6 + (P(None, ("seq", "dp")),),
        check_vma=False,
    )
```
